32 devices in a mesh: patch: 8 (over z, y), level: 4 (over x, core).
Axes of the slice: x: 2, y: 2, z: 4, core: 2. Of those that a mesh axis runs over, the one named last changes fastest.
Arguments:
- forcing: bfloat16 [4, 64, 2, 128, 128], P('level', 'patch'), may hold values from -24 to 24
- velocity: bfloat16 [4, 64, 2, 128, 128], P('level', 'patch'), may hold values from -18 to 18
- viscosity: float32 [4, 64, 128, 128], P('level', 'patch'), may hold values from 0.3 to 3
- friction: bfloat16 [4, 64, 128, 128], P('level', 'patch'), may hold values from 0.049804688 to 1
- patch_rows: int32 [4, 8], replicated, may hold values from 0 to 8, as said below
Outputs:
- adjoint: float32 [4, 64, 2, 128, 128], P('level', 'patch')
- gradient: bfloat16 [4, 64, 128, 128], P('level', 'patch')
The draws below stay inside these ranges and needn't reach their ends.
Inputs may be any that keep to these rules, and one draw needn't show every extreme that they name: patch_rows[l, p] is the number of live rows of level l on patch index p: at most 8 // 2**l, patch_rows[0, p] >= 1 and patch_rows[l + 1, p] <= 2 * patch_rows[l, p]; in every draw some patch index holds the most rows on every level.
All inputs are finite; a program needn't handle non-finite values.
Results may differ from the reference program's by a relative error of at most 0.0005.
Values may be sent and summed in bfloat16 or wider, within the bound.
No kernel may reach another device: no remote copies, remote signals or barrier semaphores. Data moves between devices by JAX's collectives and lax.ppermute only.
A program may use at most 128 MiB of HBM per device.

```python
import math
import jax
import jax.numpy as jnp

SIDE = 128
SLOTS = 8
SWEEPS = 1
LEVELS = 4
PATCHES = 8


def draw_patch_rows(key, part):
    first_key, chosen_key, tier_key = jax.random.split(key, 3)
    position = jnp.arange(PATCHES, dtype=jnp.int32)
    chosen = jax.random.randint(chosen_key, (), 0, PATCHES)
    current = jax.random.randint(first_key, (PATCHES,), SLOTS // 2, SLOTS + 1)
    current = jnp.where(position == chosen, SLOTS, current)
    stacked = [current]
    for tier_index in range(1, LEVELS):
        capacity = SLOTS // 2 ** tier_index
        upper_bound = jnp.minimum(2 * current, capacity)
        random_bits = jax.random.randint(jax.random.fold_in(tier_key, tier_index), (PATCHES,), 0, 1 << 20)
        current = random_bits * (upper_bound + 1) // (1 << 20)
        current = jnp.where(position == chosen, capacity, current)
        stacked.append(current)
    return jnp.stack(stacked).astype(jnp.int32)


def steps_of(own_key, extent, cuts, low, high):
    factor_of = 1.0
    for dim, parts in cuts:
        draws = jax.random.uniform(jax.random.fold_in(jax.random.fold_in(own_key, 6), dim), (parts,), jnp.float32, low / len(cuts), high / len(cuts))
        factor_of = factor_of * jnp.repeat(jnp.exp(draws), extent[dim] // parts).reshape((-1,) + (1,) * (len(extent) - 1 - dim))
    return factor_of


def bell_draw(rng, extent, spread, reach, cuts=(), held_as=jnp.bfloat16):
    drawn = spread * jax.random.normal(rng, extent, jnp.float32)
    if cuts:
        drawn = drawn * steps_of(rng, extent, cuts, -0.22, 0.18)
    return jnp.clip(drawn, -reach, reach).astype(held_as)


def setup_inputs(seed: int = 0) -> dict:
    key_of = jax.random.split(jax.random.key(seed), 6)
    return {
        "forcing": bell_draw(key_of[0], (LEVELS, PATCHES * SLOTS, 2, SIDE, SIDE), 4.0, 24.0, ((0, 4), (1, 8))),
        "velocity": bell_draw(key_of[1], (LEVELS, PATCHES * SLOTS, 2, SIDE, SIDE), 3.0, 18.0, ((0, 4), (1, 8))),
        "viscosity": jnp.clip(jnp.exp(math.log(3.0) - 2.3025851 * jax.random.uniform(key_of[2], (LEVELS, PATCHES * SLOTS, SIDE, SIDE), jnp.float32) ** steps_of(key_of[2], (LEVELS, PATCHES * SLOTS, SIDE, SIDE), ((0, 4), (1, 8)), -0.2, 0.2)), 0.3, 3.0),
        "friction": jnp.clip(jnp.exp(math.log(1.0) - 2.9996462 * jax.random.uniform(key_of[3], (LEVELS, PATCHES * SLOTS, SIDE, SIDE), jnp.float32) ** steps_of(key_of[3], (LEVELS, PATCHES * SLOTS, SIDE, SIDE), ((0, 4), (1, 8)), -0.2, 0.2)), 0.049804688, 1.0).astype(jnp.bfloat16),
        "patch_rows": draw_patch_rows(jax.random.fold_in(key_of[5], 71), 0),
    }


relaxation = 0.5


def cell_at(grid, row_step, col_step):
    row_total = grid.shape[-2]
    col_total = grid.shape[-1]
    return grid[..., 1 + row_step:row_total - 1 + row_step, 1 + col_step:col_total - 1 + col_step]


def viscosity_faces(visc_loop):
    centre = cell_at(visc_loop, 0, 0)
    east_cell = cell_at(visc_loop, 0, 1)
    west_cell = cell_at(visc_loop, 0, -1)
    north_cell = cell_at(visc_loop, 1, 0)
    south_cell = cell_at(visc_loop, -1, 0)
    return (east_cell, west_cell, north_cell, south_cell,
            0.5 * (centre + east_cell), 0.5 * (centre + west_cell),
            0.5 * (centre + north_cell), 0.5 * (centre + south_cell))


def diagonal_terms(face_values, friction_cells):
    east_cell, west_cell, north_cell, south_cell, face_east, face_west, face_north, face_south = face_values
    diag_u = 4.0 * (face_east + face_west) + face_north + face_south + friction_cells
    diag_v = 4.0 * (face_north + face_south) + face_east + face_west + friction_cells
    return jnp.stack([diag_u, diag_v], axis=1)


def operator_cells(loop_cells, face_values, friction_cells):
    east_cell, west_cell, north_cell, south_cell, face_east, face_west, face_north, face_south = face_values
    u_loop = loop_cells[:, 0]
    v_loop = loop_cells[:, 1]
    u_centre = cell_at(u_loop, 0, 0)
    u_east = cell_at(u_loop, 0, 1)
    u_west = cell_at(u_loop, 0, -1)
    u_north = cell_at(u_loop, 1, 0)
    u_south = cell_at(u_loop, -1, 0)
    u_northeast = cell_at(u_loop, 1, 1)
    u_northwest = cell_at(u_loop, 1, -1)
    u_southeast = cell_at(u_loop, -1, 1)
    u_southwest = cell_at(u_loop, -1, -1)
    v_centre = cell_at(v_loop, 0, 0)
    v_east = cell_at(v_loop, 0, 1)
    v_west = cell_at(v_loop, 0, -1)
    v_north = cell_at(v_loop, 1, 0)
    v_south = cell_at(v_loop, -1, 0)
    v_northeast = cell_at(v_loop, 1, 1)
    v_northwest = cell_at(v_loop, 1, -1)
    v_southeast = cell_at(v_loop, -1, 1)
    v_southwest = cell_at(v_loop, -1, -1)
    cross_u = (east_cell * (0.5 * (v_northeast - v_southeast)) - west_cell * (0.5 * (v_northwest - v_southwest))
               + 0.5 * (north_cell * (0.5 * (v_northeast - v_northwest)) - south_cell * (0.5 * (v_southeast - v_southwest))))
    cross_v = (north_cell * (0.5 * (u_northeast - u_northwest)) - south_cell * (0.5 * (u_southeast - u_southwest))
               + 0.5 * (east_cell * (0.5 * (u_northeast - u_southeast)) - west_cell * (0.5 * (u_northwest - u_southwest))))
    result_u = (-4.0 * (face_east * (u_east - u_centre) - face_west * (u_centre - u_west))
                - (face_north * (u_north - u_centre) - face_south * (u_centre - u_south))
                - cross_u + friction_cells * u_centre)
    result_v = (-4.0 * (face_north * (v_north - v_centre) - face_south * (v_centre - v_south))
                - (face_east * (v_east - v_centre) - face_west * (v_centre - v_west))
                - cross_v + friction_cells * v_centre)
    return jnp.stack([result_u, result_v], axis=1)


def assemble_loop(cells, edge_table, indices):
    south_index, north_index, west_index, east_index, northeast_index, southeast_index, northwest_index, southwest_index = indices
    side_cells = cells.shape[-1]
    south_row = edge_table[south_index]
    north_row = edge_table[north_index]
    west_col = edge_table[west_index]
    east_col = edge_table[east_index]
    corner_northeast = edge_table[northeast_index][:, :, 0]
    corner_southeast = edge_table[southeast_index][:, :, side_cells - 1]
    corner_northwest = edge_table[northwest_index][:, :, 0]
    corner_southwest = edge_table[southwest_index][:, :, side_cells - 1]
    middle = jnp.concatenate([west_col[..., None], cells, east_col[..., None]], axis=-1)
    bottom = jnp.concatenate([corner_southwest[..., None], south_row, corner_southeast[..., None]], axis=-1)
    top_row = jnp.concatenate([corner_northwest[..., None], north_row, corner_northeast[..., None]], axis=-1)
    return jnp.concatenate([bottom[:, :, None], middle, top_row[:, :, None]], axis=2)


def loop_global(cells, indices):
    comps = cells.shape[1]
    side_cells = cells.shape[-1]
    edge_table = jnp.concatenate([cells[:, :, 0, :], cells[:, :, side_cells - 1, :], cells[:, :, :, 0],
                                  cells[:, :, :, side_cells - 1], jnp.zeros((1, comps, side_cells), jnp.float32)], axis=0)
    return assemble_loop(cells, edge_table, indices)


def global_layout(level_rows, columns, slot_count):
    total = level_rows.shape[0] * slot_count
    global_ids = jnp.arange(total, dtype=jnp.int32)
    patch_of = global_ids // slot_count
    slot_of = global_ids % slot_count
    row_ids = slot_of // columns
    col_ids = slot_of % columns
    padded = jnp.concatenate([jnp.zeros((1,), jnp.int32), level_rows.astype(jnp.int32), jnp.zeros((1,), jnp.int32)])
    own_rows = padded[patch_of + 1]
    left_rows = padded[patch_of]
    right_rows = padded[patch_of + 2]
    alive = row_ids < own_rows
    blank = 4 * total
    inside_west = col_ids > 0
    inside_east = col_ids < columns - 1
    has_south = row_ids >= 1
    has_north = row_ids + 1 < own_rows
    left_base = (patch_of - 1) * slot_count
    right_base = (patch_of + 1) * slot_count

    def choose(condition, position):
        return jnp.where(condition & alive, position, blank)

    south_index = choose(has_south, total + global_ids - columns)
    north_index = choose(has_north, global_ids + columns)
    west_index = jnp.where(inside_west, choose(alive, 3 * total + global_ids - 1),
                           choose(row_ids < left_rows, 3 * total + left_base + row_ids * columns + columns - 1))
    east_index = jnp.where(inside_east, choose(alive, 2 * total + global_ids + 1),
                           choose(row_ids < right_rows, 2 * total + right_base + row_ids * columns))
    northeast_index = jnp.where(inside_east, choose(has_north, 2 * total + global_ids + columns + 1),
                                choose(row_ids + 1 < right_rows, 2 * total + right_base + (row_ids + 1) * columns))
    southeast_index = jnp.where(inside_east, choose(has_south, 2 * total + global_ids - columns + 1),
                                choose(has_south & (row_ids - 1 < right_rows), 2 * total + right_base + (row_ids - 1) * columns))
    northwest_index = jnp.where(inside_west, choose(has_north, 3 * total + global_ids + columns - 1),
                                choose(row_ids + 1 < left_rows, 3 * total + left_base + (row_ids + 1) * columns + columns - 1))
    southwest_index = jnp.where(inside_west, choose(has_south, 3 * total + global_ids - columns - 1),
                                choose(has_south & (row_ids - 1 < left_rows), 3 * total + left_base + (row_ids - 1) * columns + columns - 1))
    indices = (south_index, north_index, west_index, east_index, northeast_index, southeast_index, northwest_index, southwest_index)
    return indices, alive, patch_of, row_ids, col_ids


def join_quadrants(south_west, south_east, north_west, north_east):
    bottom = jnp.concatenate([south_west, south_east], axis=-1)
    top_half = jnp.concatenate([north_west, north_east], axis=-1)
    return jnp.concatenate([bottom, top_half], axis=-2)


def reference(forcing, velocity, viscosity, friction, patch_rows):
    slot_count = SLOTS
    total = PATCHES * SLOTS
    half_side = SIDE // 2
    layouts = []
    masks = []
    faces_all = []
    diagonals = []
    frictions = []
    forces = []
    for tier in range(LEVELS):
        layout = global_layout(patch_rows[tier], 2 ** tier, slot_count)
        layouts.append(layout)
        live_mask = layout[1].astype(jnp.float32)[:, None, None, None]
        masks.append(live_mask)
        visc_loop = loop_global(viscosity[tier][:, None], layout[0])[:, 0]
        face_values = viscosity_faces(visc_loop)
        friction_cells = friction[tier].astype(jnp.float32)
        faces_all.append(face_values)
        frictions.append(friction_cells)
        diagonals.append(diagonal_terms(face_values, friction_cells))
        forces.append(forcing[tier].astype(jnp.float32))

    def apply_level(tier, cells):
        return operator_cells(loop_global(cells, layouts[tier][0]), faces_all[tier], frictions[tier])

    def smooth(tier, right_side, start):
        current = start
        for sweep_index in range(SWEEPS):
            current = masks[tier] * (current + relaxation * (right_side - apply_level(tier, current)) / diagonals[tier])
        return current

    zero_cells = jnp.zeros((total, 2, SIDE, SIDE), jnp.float32)
    right_sides = [None] * LEVELS
    solutions = [None] * LEVELS
    right_sides[LEVELS - 1] = masks[LEVELS - 1] * forces[LEVELS - 1]
    for tier in range(LEVELS - 1, 0, -1):
        solutions[tier] = smooth(tier, right_sides[tier], zero_cells)
        residual = masks[tier] * (right_sides[tier] - apply_level(tier, solutions[tier]))
        quads = residual.reshape(total, 2, half_side, 2, half_side, 2).sum(axis=(3, 5))
        quad_table = jnp.concatenate([quads, jnp.zeros((1, 2, half_side, half_side), jnp.float32)], axis=0)
        coarse = tier - 1
        indices, alive, patch_of, row_ids, col_ids = layouts[coarse]
        coarse_columns = 2 ** coarse
        finer_rows = patch_rows[tier].astype(jnp.int32)[patch_of]
        placed = []
        covers = []
        for quad_row in range(2):
            for quad_col in range(2):
                fine_row = 2 * row_ids + quad_row
                valid = alive & (fine_row < finer_rows)
                child = jnp.where(valid, patch_of * slot_count + fine_row * (2 * coarse_columns) + 2 * col_ids + quad_col, total)
                placed.append(quad_table[child])
                covers.append(jnp.broadcast_to(valid.astype(jnp.float32)[:, None, None, None], (total, 1, half_side, half_side)))
        restricted = join_quadrants(placed[0], placed[1], placed[2], placed[3])
        covered = join_quadrants(covers[0], covers[1], covers[2], covers[3])
        right_sides[coarse] = masks[coarse] * ((1.0 - covered) * forces[coarse] + restricted)
    solutions[0] = smooth(0, right_sides[0], zero_cells)
    for tier in range(1, LEVELS):
        indices, alive, patch_of, row_ids, col_ids = layouts[tier]
        parent_ids = patch_of * slot_count + (row_ids // 2) * (2 ** (tier - 1)) + col_ids // 2
        parents = solutions[tier - 1][parent_ids]
        quad_row_of = (row_ids % 2)[:, None, None, None]
        quad_col_of = (col_ids % 2)[:, None, None, None]
        half_rows = jnp.where(quad_row_of == 0, parents[:, :, :half_side, :], parents[:, :, half_side:, :])
        quarter = jnp.where(quad_col_of == 0, half_rows[..., :half_side], half_rows[..., half_side:])
        correction = jnp.repeat(jnp.repeat(quarter, 2, axis=2), 2, axis=3)
        solutions[tier] = smooth(tier, right_sides[tier], solutions[tier] + masks[tier] * correction)
    gradients = []
    for tier in range(LEVELS):
        speed = velocity[tier].astype(jnp.float32)
        product = speed[:, 0] * solutions[tier][:, 0] + speed[:, 1] * solutions[tier][:, 1]
        gradients.append((-(frictions[tier] * product) * masks[tier][:, 0]).astype(jnp.bfloat16))
    return jnp.stack(solutions), jnp.stack(gradients)
```

```python
from typing import Any, NamedTuple

import jax
import jax.numpy as jnp
from jax import lax
from jax.experimental import pallas as pl
from jax.experimental.pallas import tpu as pltpu
from jax.sharding import PartitionSpec as P

relaxation = 0.5
PAD = 8
LOW, HIGH, EDGES = 0, 1, 2
VM, SM, ANY = pltpu.VMEM, pltpu.SMEM, pl.ANY
F32 = jnp.float32
BF16 = jnp.bfloat16
VMEM_BYTES = 48 * 2**20


class Layout:
    def __init__(self, slots, side, levels, patches):
        self.slots = slots
        self.side = side
        self.levels = levels
        self.patches = patches
        self.half_slots = slots // 2
        self.half_side = side // 2
        self.span = 2 * slots

    def columns(self, level):
        return 1 << level

    def patch_rows(self, level):
        return self.slots >> level

    def rows(self, level):
        return self.patch_rows(level) * self.side

    def margin(self, level):
        return 2 << level

    def own(self, level):
        return max(1, (1 << level) // 2)

    def blocks(self, level):
        return self.own(level) + (1 if level > 0 else 0)

    def chunk(self, level):
        return 8 * max(1, 4 // self.blocks(level))


def lane_ids(side):
    return lax.broadcasted_iota(jnp.int32, (1, side), 1)


def near_counts(g, rows_ref, level, patch, odd):
    own = rows_ref[level, patch]
    east = jnp.where(
        patch + 1 < g.patches, rows_ref[level, jnp.minimum(patch + 1, g.patches - 1)], 0
    )
    west = jnp.where(patch > 0, rows_ref[level, jnp.maximum(patch - 1, 0)], 0)
    return own, jnp.where(odd, own, east), jnp.where(odd, west, own)


def lane_limits(g, level, counts, cells):
    own, east, west = (value * cells for value in counts)
    lane = lane_ids(g.side)
    margin = g.margin(level)
    first = 0 if level > 0 else g.half_side
    edges = jnp.where(
        (lane >= first) & (lane < first + margin), east, jnp.where(lane >= g.side - margin, west, 0)
    )
    if level == 0:
        return [jnp.where(lane < g.half_side, own, edges)]
    return [jnp.full((1, g.side), own, jnp.int32)] * g.own(level) + [edges]


def both_sides(g, values):
    count = len(values)
    lane = lax.broadcasted_iota(jnp.int32, values[0].shape, 1)
    toward_east = [pltpu.roll(value, g.side - 1, 1) for value in values]
    toward_west = [pltpu.roll(value, 1, 1) for value in values]
    if count == 1:
        return toward_east, toward_west
    east = [
        jnp.where(lane == g.side - 1, toward_east[(k + 1) % count], toward_east[k])
        for k in range(count)
    ]
    west = [
        jnp.where(lane == 0, toward_west[(k - 1) % count], toward_west[k]) for k in range(count)
    ]
    return east, west


def operator_chunk(g, cells, visc, fric, row, chunk, count):
    fields = []
    for comp in range(2):
        near = []
        for step in (0, 1, -1):
            line = [cells[comp, k, pl.ds(PAD + row + step, chunk), :] for k in range(count)]
            near.append((line, *both_sides(g, line)))
        fields.append(near)
    centre = [visc[k, pl.ds(PAD + row, chunk), :] for k in range(count)]
    visc_east, visc_west = both_sides(g, centre)
    out_u = []
    out_v = []
    for k in range(count):
        (u, u_e, u_w), (u_n, u_ne, u_nw), (u_s, u_se, u_sw) = (
            [value[k] for value in line] for line in fields[0]
        )
        (v, v_e, v_w), (v_n, v_ne, v_nw), (v_s, v_se, v_sw) = (
            [value[k] for value in line] for line in fields[1]
        )
        visc_north = visc[k, pl.ds(PAD + row + 1, chunk), :]
        visc_south = visc[k, pl.ds(PAD + row - 1, chunk), :]
        du_e, du_w, du_n, du_s = u_e - u, u - u_w, u_n - u, u - u_s
        dv_e, dv_w, dv_n, dv_s = v_e - v, v - v_w, v_n - v, v - v_s
        inner_u = (
            centre[k] * (8.0 * (du_e - du_w) + 2.0 * (du_n - du_s))
            + visc_east[k] * (8.0 * du_e + 2.0 * (v_ne - v_se))
            - visc_west[k] * (8.0 * du_w + 2.0 * (v_nw - v_sw))
            + visc_north * (2.0 * du_n + (v_ne - v_nw))
            - visc_south * (2.0 * du_s + (v_se - v_sw))
        )
        inner_v = (
            centre[k] * (8.0 * (dv_n - dv_s) + 2.0 * (dv_e - dv_w))
            + visc_north * (8.0 * dv_n + 2.0 * (u_ne - u_nw))
            - visc_south * (8.0 * dv_s + 2.0 * (u_se - u_sw))
            + visc_east[k] * (2.0 * dv_e + (u_ne - u_se))
            - visc_west[k] * (2.0 * dv_w + (u_nw - u_sw))
        )
        friction = fric[k, pl.ds(row, chunk), :]
        out_u.append(friction * u - inner_u)
        out_v.append(friction * v - inner_v)
    return out_u, out_v


def over_rows(rows, chunk, body):
    def step(index, carry):
        body(pl.multiple_of(index * chunk, chunk))
        return carry

    lax.fori_loop(0, rows // chunk, step, 0)


def clear_pads(ref, lead):
    width = ref.shape[-1]
    last = ref.shape[-2]
    for index in lead:
        ref[index + (slice(0, PAD), slice(None))] = jnp.zeros((PAD, width), F32)
        ref[index + (slice(last - PAD, last), slice(None))] = jnp.zeros((PAD, width), F32)


def first_smooth(g, level, d, limits, rows):
    count = g.blocks(level)
    chunk = g.chunk(level)

    def body(row):
        centre = [d.visc[k, pl.ds(PAD + row, chunk), :] for k in range(count)]
        east, west = both_sides(g, centre)
        for k in range(count):
            north = d.visc[k, pl.ds(PAD + row + 1, chunk), :]
            south = d.visc[k, pl.ds(PAD + row - 1, chunk), :]
            friction = d.fric[k, pl.ds(row, chunk), :]
            twice = 2.0 * centre[k]
            along_row = twice + east[k] + west[k]
            along_col = twice + north + south
            live = jnp.broadcast_to(limits[k] > row, (chunk, g.side))
            diag_u = 8.0 * along_row + 2.0 * along_col + friction
            diag_v = 8.0 * along_col + 2.0 * along_row + friction
            for comp, diag in ((0, diag_u), (1, diag_v)):
                weight = jnp.where(live, relaxation / diag, 0.0)
                d.weight[comp, k, pl.ds(row, chunk), :] = weight
                d.cells[comp, k, pl.ds(PAD + row, chunk), :] = (
                    weight * d.right[comp, k, pl.ds(row, chunk), :]
                )

    over_rows(rows, chunk, body)


def residual_step(g, level, d, rows, add=False):
    count = g.blocks(level)
    chunk = g.chunk(level)

    def body(row):
        applied = operator_chunk(g, d.cells, d.visc, d.fric, row, chunk, count)
        for comp in range(2):
            for k in range(count):
                weight = d.weight[comp, k, pl.ds(row, chunk), :]
                left = d.right[comp, k, pl.ds(row, chunk), :] - applied[comp][k]
                left = jnp.where(weight > 0.0, left, 0.0)
                d.right[comp, k, pl.ds(row, chunk), :] = left
                value = d.cells[comp, k, pl.ds(PAD + row, chunk), :] + weight * left
                if add:
                    value = value + d.held[comp, k, pl.ds(row, chunk), :]
                d.held[comp, k, pl.ds(row, chunk), :] = value

    over_rows(rows, chunk, body)


def corrected_step(g, level, d, rows):
    count = g.blocks(level)
    chunk = g.chunk(level)

    def body(row):
        applied = operator_chunk(g, d.cells, d.visc, d.fric, row, chunk, count)
        for comp in range(2):
            for k in range(count):
                weight = d.weight[comp, k, pl.ds(row, chunk), :]
                d.held[comp, k, pl.ds(row, chunk), :] = (
                    d.held[comp, k, pl.ds(row, chunk), :]
                    + d.cells[comp, k, pl.ds(PAD + row, chunk), :]
                    - weight * applied[comp][k]
                )

    over_rows(rows, chunk, body)


def pairings(g, fine):
    if fine == 1:
        return [[(0, LOW), (1, HIGH)]]
    parts = [[(2 * k, LOW), (2 * k + 1, HIGH)] for k in range(g.own(fine) // 2)]
    return parts + [[(g.own(fine), EDGES)]]


def target_lane(g, part, fine_lane):
    halved = jnp.right_shift(fine_lane, 1)
    if part == LOW:
        return halved
    if part == HIGH:
        return g.half_side + halved
    return halved + jnp.where(fine_lane >= g.half_side, g.half_side, 0)


def sum_matrix(g, part):
    fine = lax.broadcasted_iota(jnp.int32, (g.side, g.side), 0)
    coarse = lax.broadcasted_iota(jnp.int32, (g.side, g.side), 1)
    return jnp.where(target_lane(g, part, fine) == coarse, 1.0, 0.0).astype(BF16)


def copy_matrix(g, part):
    coarse = lax.broadcasted_iota(jnp.int32, (g.side, g.side), 0)
    fine = lax.broadcasted_iota(jnp.int32, (g.side, g.side), 1)
    return jnp.where(target_lane(g, part, fine) == coarse, 1.0, 0.0).astype(BF16)


def split_dot(values, matrix):
    high = values.astype(BF16)
    rest = (values - high.astype(F32)).astype(BF16)
    return jnp.dot(high, matrix, preferred_element_type=F32) + jnp.dot(
        rest, matrix, preferred_element_type=F32
    )


def restrict_into(g, fine, d, rows, store):
    chunk = min(rows // 2, g.half_side)
    if (rows // 2) % chunk:
        chunk = rows // 2
    parts = pairings(g, fine)
    matrices = {part: sum_matrix(g, part) for members in parts for _, part in members}

    def body(row):
        for comp in range(2):
            for coarse, members in enumerate(parts):
                total = None
                for k, part in members:
                    first = d.right[comp, k, pl.ds(2 * row, chunk, stride=2), :]
                    second = d.right[comp, k, pl.ds(2 * row + 1, chunk, stride=2), :]
                    term = split_dot(first + second, matrices[part])
                    total = term if total is None else total + term
                store(comp, coarse, row, chunk, total)

    over_rows(rows // 2, chunk, body)


def prolong_from(g, fine, d, limits, rows, load):
    chunk = min(rows // 2, g.half_side)
    if (rows // 2) % chunk:
        chunk = rows // 2
    parts = pairings(g, fine)
    matrices = {part: copy_matrix(g, part) for members in parts for _, part in members}

    def body(row):
        ids = 2 * (row + lax.broadcasted_iota(jnp.int32, (chunk, g.side), 0))
        for comp in range(2):
            for coarse, members in enumerate(parts):
                value = load(comp, coarse, row, chunk)
                for k, part in members:
                    spread = jnp.where(ids < limits[k], split_dot(value, matrices[part]), 0.0)
                    d.cells[comp, k, pl.ds(PAD + 2 * row, chunk, stride=2), :] = spread
                    d.cells[comp, k, pl.ds(PAD + 2 * row + 1, chunk, stride=2), :] = spread

    over_rows(rows // 2, chunk, body)


def pack_kernel(g, force, visc, fric, swap, edge_own, edge_other):
    level_here = lax.axis_index("level")
    side = g.side

    def plane(q, slot):
        if q < 2:
            return force[slot, q].astype(F32)
        if q == 2:
            return fric[slot].astype(F32)
        return visc[slot]

    def packed_edge(level, column, start):
        lane = lane_ids(side)
        margin = g.margin(level)
        total = jnp.zeros((side, side), F32)
        for r in range(g.patch_rows(level)):
            slot = r * g.columns(level) + column
            for q in range(4):
                base = q * g.span + r * margin
                moved = plane(q, slot)
                if (base - start) % side:
                    moved = pltpu.roll(moved, (base - start) % side, 1)
                total = jnp.where((lane >= base) & (lane < base + margin), moved, total)
        return total

    def pack_level(level):
        west_type = level % 2 == 1
        margin = g.margin(level)
        last = g.columns(level) - 1
        west_edge = packed_edge(level, 0, 0)
        east_edge = packed_edge(level, last, side - margin)
        edge_own[...] = east_edge if west_type else west_edge
        edge_other[...] = west_edge if west_type else east_edge
        if level == 0:
            lane = lane_ids(side)
            for q in range(4):
                for k in range(g.half_slots):
                    swap[q * g.half_slots + k] = jnp.where(
                        lane < g.half_side,
                        plane(q, k),
                        pltpu.roll(plane(q, k + g.half_slots), g.half_side, 1),
                    )
            swap[4 * g.half_slots] = packed_edge(0, 0, g.half_side)
            return
        own = g.own(level)
        first = own if west_type else 0
        for r in range(g.patch_rows(level)):
            for k in range(own):
                for q in range(4):
                    swap[q * g.half_slots + r * own + k] = plane(
                        q, r * g.columns(level) + first + k
                    )
        if west_type:
            swap[4 * g.half_slots] = packed_edge(level, own - 1, side - margin)
        else:
            swap[4 * g.half_slots] = packed_edge(level, own, 0)

    for level in range(g.levels):
        pl.when(level_here == level)(lambda level=level: pack_level(level))


def fill_level(g, level, west_type, d, limits, raw, got):
    force, visc, fric = raw
    swap, edge_own, edge_other = got
    side = g.side
    home = (level % 2 == 1) == west_type
    margin = g.margin(level)
    own = g.own(level)
    columns = g.columns(level)
    lane = lane_ids(side)
    edges = edge_own if home else edge_other

    def plane(q, slot):
        if q < 2:
            return force[slot, q].astype(F32)
        if q == 2:
            return fric[slot].astype(F32)
        return visc[slot]

    def unpacked(packed, q, r, place):
        shift = (place - (q * g.span + r * margin)) % side
        return pltpu.roll(packed, shift, 1) if shift else packed

    def store(q, k, r, value):
        here = pl.ds(r * side, side)
        if q < 2:
            d.right[q, k, here, :] = value
        elif q == 2:
            d.fric[k, here, :] = value
        else:
            d.visc[k, pl.ds(PAD + r * side, side), :] = jnp.where(
                limits[k] > r * side, 0.25 * value, 0.0
            )

    clear_pads(d.visc, [(k,) for k in range(g.blocks(level))])
    clear_pads(d.cells, [(c, k) for c in range(2) for k in range(g.blocks(level))])
    inner = swap[4 * g.half_slots]
    outer = edges[...]
    for r in range(g.patch_rows(level)):
        for q in range(4):
            if level == 0:
                if home:
                    value = pltpu.roll(plane(q, r), g.half_side, 1)
                    east = unpacked(outer, q, r, g.half_side)
                    value = jnp.where(
                        (lane >= g.half_side) & (lane < g.half_side + margin), east, value
                    )
                else:
                    value = swap[q * g.half_slots + r % g.half_slots]
                    if r >= g.half_slots:
                        value = pltpu.roll(value, g.half_side, 1)
                    east = unpacked(inner, q, r, g.half_side)
                    west = unpacked(outer, q, r, side - margin)
                    value = jnp.where(lane < g.half_side, value, east)
                    value = jnp.where(lane >= side - margin, west, value)
                store(q, 0, r, value)
                continue
            for k in range(own):
                if home:
                    value = plane(q, r * columns + k + (0 if west_type else own))
                else:
                    value = swap[q * g.half_slots + r * own + k]
                store(q, k, r, value)
            if west_type:
                if home:
                    east = plane(q, r * columns + own)
                else:
                    east = unpacked(inner, q, r, 0)
                west = unpacked(outer, q, r, side - margin)
            else:
                east = unpacked(outer, q, r, 0)
                if home:
                    west = plane(q, r * columns + own - 1)
                else:
                    west = unpacked(inner, q, r, side - margin)
            store(q, own, r, jnp.where(lane < g.half_side, east, west))


def joined_edges(g, edge_u, edge_v):
    lane = lane_ids(g.side)
    quarter = g.side // 4
    middle = (lane >= quarter) & (lane < g.side - quarter)
    return jnp.where(middle, pltpu.roll(edge_v, g.half_side, 1), edge_u)


class Level(NamedTuple):
    visc: Any
    fric: Any
    weight: Any
    held: Any
    right: Any = None
    cells: Any = None


def level_arrays(g, count, rows, make, working):
    shapes = [
        (count, rows + 2 * PAD, g.side),
        (count, rows, g.side),
        (2, count, rows, g.side),
        (2, count, rows, g.side),
    ]
    if working:
        shapes += [(2, count, rows, g.side), (2, count, rows + 2 * PAD, g.side)]
    return Level(*[make(shape, F32) for shape in shapes])


def level_scratch(g, level):
    return level_arrays(g, g.blocks(level), g.rows(level), pltpu.VMEM, True)


def level_state(g, level):
    return level_arrays(g, g.blocks(level), g.rows(level), jax.ShapeDtypeStruct, False)


class Copies:
    def __init__(self, sems, first=0):
        self.sems = sems
        self.used = first
        self.open = []

    def start(self, source, target):
        copy = pltpu.make_async_copy(source, target, self.sems.at[self.used])
        self.used += 1
        copy.start()
        self.open.append(copy)

    def finish(self):
        for copy in self.open:
            copy.wait()
        self.open = []


def half_of_level(g, level, held, out, copies):
    own = g.own(level)
    for r in range(g.patch_rows(level)):
        for k in range(own):
            for comp in range(2):
                copies.start(
                    held.at[comp, k, pl.ds(r * g.side, g.side)], out.at[r * own + k, comp]
                )


def down_kernel(
    g, rows_ref, force, visc, fric, swap, edge_own, edge_other, sums, mine, theirs, out, sems, edges,
    packed, levels,
):
    level_here = lax.axis_index("level")
    patch = lax.axis_index("patch")
    raw = (force, visc, fric)
    got = (swap, edge_own, edge_other)
    side = g.side
    top = g.levels - 1
    odd = level_here % 2 == 1

    def limits_of(level):
        return lane_limits(g, level, near_counts(g, rows_ref, level, patch, odd), side)

    def covered_of(level):
        return lane_limits(g, level, near_counts(g, rows_ref, level + 1, patch, odd), g.half_side)

    def filled(wanted):
        for west_type in (True, False):

            @pl.when(odd if west_type else jnp.logical_not(odd))
            def _():
                for level in wanted:
                    fill_level(g, level, west_type, levels[level], limits_of(level), raw, got)

    def set_right(level):
        covered = covered_of(level)

        def store(comp, k, row, chunk, value):
            here = pl.ds(row, chunk)
            ids = row + lax.broadcasted_iota(jnp.int32, (chunk, side), 0)
            old = levels[level].right[comp, k, here, :]
            levels[level].right[comp, k, here, :] = jnp.where(ids < covered[k], value, old)

        return store

    @pl.when(level_here >= top - 1)
    def _():
        copies = Copies(sems)
        filled((top, top - 1))
        for level in (top, top - 1):
            d = levels[level]
            first_smooth(g, level, d, limits_of(level), g.rows(level))
            residual_step(g, level, d, g.rows(level))
            for source, target in zip(d[:4], out[level]):
                copies.start(source, target)
            if level == top:
                restrict_into(g, level, d, g.rows(level), set_right(level - 1))

        def keep(comp, k, row, chunk, value):
            if k == 0:
                sums[comp, pl.ds(row, chunk), :] = value
            else:
                edges[comp, pl.ds(row, chunk), :] = value

        restrict_into(g, top - 1, levels[top - 1], g.rows(top - 1), keep)
        sums[2] = joined_edges(g, edges[0], edges[1])
        copies.finish()

    @pl.when(level_here < top - 1)
    def _():
        copies = Copies(sems)
        filled((1, 0))
        d, coarse = levels[1], levels[0]
        covered = covered_of(1)

        def uncovered(row):
            for comp in range(2):
                for k in range(g.blocks(1)):
                    here = pl.ds(row, g.chunk(1))
                    old = d.right[comp, k, here, :]
                    d.right[comp, k, here, :] = jnp.where(covered[k] > row, 0.0, old)

        over_rows(g.rows(2) // 2, g.chunk(1), uncovered)
        first_smooth(g, 1, d, limits_of(1), g.rows(1))
        residual_step(g, 1, d, g.rows(1))
        restrict_into(g, 1, d, g.rows(1), set_right(0))
        first_smooth(g, 0, coarse, limits_of(0), g.rows(0))

        def load(comp, k, row, chunk):
            return coarse.cells[comp, k, pl.ds(PAD + row, chunk), :]

        prolong_from(g, 1, d, limits_of(1), g.rows(1), load)
        corrected_step(g, 1, d, g.rows(1))
        lane = lane_ids(side)
        for comp in range(2):
            for k in range(g.half_slots):
                low = coarse.cells[comp, 0, pl.ds(PAD + k * side, side), :]
                high = coarse.cells[comp, 0, pl.ds(PAD + (k + g.half_slots) * side, side), :]
                packed[k, comp] = jnp.where(
                    lane < g.half_side, low, pltpu.roll(high, g.half_side, 1)
                )
        rows = bottom_rows(g)
        copies.start(d.visc.at[:, pl.ds(0, rows + 2 * PAD)], out[1].visc)
        copies.start(d.fric.at[:, pl.ds(0, rows)], out[1].fric)
        copies.start(d.weight.at[:, :, pl.ds(0, rows)], out[1].weight)
        copies.start(d.held.at[:, :, pl.ds(0, rows)], out[1].held)
        copies.start(coarse.weight.at[:, :, pl.ds(0, rows // 2)], out[0])

        def write(first, second):
            more = Copies(sems, copies.used)
            half_of_level(g, 1, d.held, first, more)
            more.start(packed, second)
            more.finish()

        pl.when(odd)(lambda: write(mine, theirs))
        pl.when(jnp.logical_not(odd))(lambda: write(theirs, mine))
        copies.finish()


def bottom_rows(g):
    return g.rows(2) // 2 + 2 * PAD


def bottom_kernel(
    g, rows_ref, sums, mine, theirs, state, coarse_weight, adjoint, mine_out, theirs_out, sems,
    packed, d, coarse_state, coarse_cells,
):
    level_here = lax.axis_index("level")
    patch = lax.axis_index("patch")
    side = g.side
    rows = bottom_rows(g)
    reach = g.rows(2) // 2
    top = g.levels - 1
    odd = level_here % 2 == 1

    @pl.when(level_here < top - 1)
    def _():
        copies = Copies(sems)
        for source, target in zip(state, d[:4]):
            copies.start(source, target)
        copies.start(coarse_weight, coarse_state)

        def read(source, sem):
            one = Copies(sems, sem)
            one.start(source.at[0], packed)
            one.finish()

        pl.when(odd)(lambda: read(theirs, 30))
        pl.when(jnp.logical_not(odd))(lambda: read(mine, 31))
        clear_pads(d.cells, [(c, k) for c in range(2) for k in range(2)])
        both = sums[2]
        swapped = pltpu.roll(both, g.half_side, 1)
        copies.finish()
        for comp in range(2):
            for k in range(2):
                rest = jnp.zeros((rows - reach, side), F32)
                d.right[comp, k, pl.ds(reach, rows - reach), :] = rest
                d.cells[comp, k, pl.ds(PAD + reach, rows - reach), :] = rest
                value = sums[comp] if k == 0 else (both, swapped)[comp]
                weight = d.weight[comp, k, pl.ds(0, reach), :]
                value = jnp.where(weight > 0.0, value, 0.0)
                d.right[comp, k, pl.ds(0, reach), :] = value
                d.cells[comp, k, pl.ds(PAD, reach), :] = weight * value
        residual_step(g, 1, d, rows, add=True)
        near = near_counts(g, rows_ref, 1, patch, odd)
        covered = lane_limits(g, 0, near, g.half_side)
        lane = lane_ids(side)

        def store(comp, k, row, size, value):
            here = pl.ds(row, size)
            ids = row + lax.broadcasted_iota(jnp.int32, (size, side), 0)
            change = coarse_state[comp, 0, here, :] * jnp.where(ids < covered[0], value, 0.0)
            coarse_cells[comp, here, :] = change
            packed[comp, here, :] = packed[comp, here, :] + jnp.where(
                lane < g.half_side, change, 0.0
            )

        restrict_into(g, 1, d, rows, store)

        def load(comp, k, row, size):
            return coarse_cells[comp, pl.ds(row, size), :]

        prolong_from(g, 1, d, lane_limits(g, 1, near, side), rows, load)
        corrected_step(g, 1, d, rows)
        held = d.held
        adjoint[0] = held[0, 0, pl.ds(0, side), :]
        adjoint[1] = held[1, 0, pl.ds(0, side), :]
        adjoint[2] = joined_edges(
            g, held[0, 1, pl.ds(0, side), :], held[1, 1, pl.ds(0, side), :]
        )

        def write(first, second, base):
            out = Copies(sems, base)
            for comp in range(2):
                for done in range(0, rows, side):
                    size = min(side, rows - done)
                    out.start(
                        held.at[comp, 0, pl.ds(done, size)],
                        first.at[done // side, comp, pl.ds(0, size)],
                    )
            out.start(packed, second.at[0])
            out.finish()

        pl.when(odd)(lambda: write(mine_out, theirs_out, 10))
        pl.when(jnp.logical_not(odd))(lambda: write(theirs_out, mine_out, 20))


def up_kernel(
    g, rows_ref, adjoint, mine, theirs, state, mine_out, theirs_out, sems, edges, levels
):
    level_here = lax.axis_index("level")
    patch = lax.axis_index("patch")
    side = g.side
    top = g.levels - 1
    odd = level_here % 2 == 1

    @pl.when(level_here >= top - 1)
    def _():
        copies = Copies(sems)
        for level in (top - 1, top):
            for source, target in zip(state[level], levels[level][:4]):
                copies.start(source, target)
            clear_pads(
                levels[level].cells, [(c, k) for c in range(2) for k in range(g.blocks(level))]
            )
        both = adjoint[2]
        edges[0] = both
        edges[1] = pltpu.roll(both, g.half_side, 1)

        def load_given(comp, k, row, chunk):
            return (adjoint if k == 0 else edges)[comp, pl.ds(row, chunk), :]

        def load_held(comp, k, row, chunk):
            return levels[top - 1].held[comp, k, pl.ds(row, chunk), :]

        copies.finish()
        for level, load in ((top - 1, load_given), (top, load_held)):
            near = near_counts(g, rows_ref, level, patch, odd)
            limits = lane_limits(g, level, near, side)
            prolong_from(g, level, levels[level], limits, g.rows(level), load)
            corrected_step(g, level, levels[level], g.rows(level))

        def write(first, second):
            out = Copies(sems)
            half_of_level(g, top - 1, levels[top - 1].held, second, out)
            half_of_level(g, top, levels[top].held, first, out)
            out.finish()

        pl.when(odd)(lambda: write(mine_out, theirs_out))
        pl.when(jnp.logical_not(odd))(lambda: write(theirs_out, mine_out))


def join_kernel(g, mine, given, speed, fric, adjoint, gradient):
    level_here = lax.axis_index("level")
    lane = lane_ids(g.side)

    def put(slot, parts):
        for comp in range(2):
            adjoint[slot, comp] = parts[comp]
        total = speed[slot, 0].astype(F32) * parts[0] + speed[slot, 1].astype(F32) * parts[1]
        gradient[slot] = (-(fric[slot].astype(F32) * total)).astype(BF16)

    def join_level(level):
        if level == 0:
            for k in range(g.half_slots):
                low = []
                high = []
                for comp in range(2):
                    west, east = given[k, comp], mine[k, comp]
                    low.append(
                        jnp.where(lane < g.half_side, west, pltpu.roll(east, g.half_side, 1))
                    )
                    high.append(
                        jnp.where(lane < g.half_side, pltpu.roll(west, g.half_side, 1), east)
                    )
                put(k, low)
                put(k + g.half_slots, high)
            return
        own = g.own(level)
        west_half, east_half = (mine, given) if level % 2 == 1 else (given, mine)
        for r in range(g.patch_rows(level)):
            for k in range(2 * own):
                source = west_half if k < own else east_half
                put(
                    r * g.columns(level) + k,
                    [source[r * own + k % own, comp] for comp in range(2)],
                )

    for level in range(g.levels):
        pl.when(level_here == level)(lambda level=level: join_level(level))


def run_kernel(body, ins, outs, scratch, aliases=()):
    in_trees = [jax.tree.flatten(tree) for tree, _ in ins]
    out_trees = [jax.tree.flatten(tree) for tree, _ in outs]
    scratch_trees = [jax.tree.flatten(tree) for tree in scratch]
    sizes = [len(leaves) for leaves, _ in in_trees + out_trees + scratch_trees]
    shapes = [tree for _, tree in in_trees + out_trees + scratch_trees]

    def kernel(*refs):
        given = []
        first = 0
        for size, shape in zip(sizes, shapes):
            given.append(jax.tree.unflatten(shape, refs[first : first + size]))
            first += size
        body(*given)

    def specs(groups, trees):
        return [
            pl.BlockSpec(memory_space=space)
            for (_, space), (leaves, _) in zip(groups, trees)
            for _ in leaves
        ]

    def place(trees, index):
        return sum(len(leaves) for leaves, _ in trees[:index])

    results = pl.pallas_call(
        kernel,
        out_shape=[leaf for leaves, _ in out_trees for leaf in leaves],
        in_specs=specs(ins, in_trees),
        out_specs=specs(outs, out_trees),
        scratch_shapes=[leaf for leaves, _ in scratch_trees for leaf in leaves],
        input_output_aliases={place(in_trees, a): place(out_trees, b) for a, b in aliases},
        compiler_params=pltpu.CompilerParams(vmem_limit_bytes=VMEM_BYTES),
    )(*[leaf for leaves, _ in in_trees for leaf in leaves])
    answer = []
    first = 0
    for leaves, shape in out_trees:
        answer.append(jax.tree.unflatten(shape, results[first : first + len(leaves)]))
        first += len(leaves)
    return answer


def moved(value, g, step):
    pairs = []
    for patch in range(g.patches):
        for level in range(g.levels):
            to_patch, to_level = step(patch, level)
            if 0 <= to_patch < g.patches and 0 <= to_level < g.levels:
                pairs.append((patch * g.levels + level, to_patch * g.levels + to_level))
    return lax.ppermute(value, ("patch", "level"), pairs)


def per_device(forcing, velocity, viscosity, friction, patch_rows):
    g = Layout(
        forcing.shape[1], forcing.shape[-1], lax.axis_size("level"), lax.axis_size("patch")
    )
    side = g.side
    top = g.levels - 1
    force, speed, visc, fric = forcing[0], velocity[0], viscosity[0], friction[0]
    block = jax.ShapeDtypeStruct((side, side), F32)
    half = jax.ShapeDtypeStruct((g.half_slots, 2, side, side), F32)
    three = jax.ShapeDtypeStruct((3, side, side), F32)
    sems = pltpu.SemaphoreType.DMA((40,))

    swap, edge_own, edge_other = run_kernel(
        lambda *refs: pack_kernel(g, *refs),
        [(force, VM), (visc, VM), (fric, VM)],
        [
            (jax.ShapeDtypeStruct((4 * g.half_slots + 1, side, side), F32), VM),
            (block, VM),
            (block, VM),
        ],
        [],
    )
    swap = moved(swap, g, lambda p, l: (p, l ^ 1))
    edge_own = moved(edge_own, g, lambda p, l: (p + (1 if l % 2 else -1), l))
    edge_other = moved(edge_other, g, lambda p, l: (p + (-1 if l % 2 else 1), l ^ 1))

    rows = bottom_rows(g)
    down_state = [
        jax.ShapeDtypeStruct((2, 1, rows // 2, side), F32),
        level_arrays(g, 2, rows, jax.ShapeDtypeStruct, False),
        level_state(g, top - 1),
        level_state(g, top),
    ]
    sums, mine, theirs, state = run_kernel(
        lambda *refs: down_kernel(g, *refs),
        [
            (patch_rows, SM),
            (force, VM),
            (visc, VM),
            (fric, VM),
            (swap, VM),
            (edge_own, VM),
            (edge_other, VM),
        ],
        [(three, VM), (half, ANY), (half, ANY), (down_state, ANY)],
        [
            sems,
            pltpu.VMEM((2, side, side), F32),
            pltpu.VMEM(half.shape, F32),
            [level_scratch(g, level) for level in range(g.levels)],
        ],
    )
    sums = moved(sums, g, lambda p, l: (p, l - 2))
    adjoint, mine, theirs = run_kernel(
        lambda *refs: bottom_kernel(g, *refs),
        [(patch_rows, SM), (sums, VM), (mine, ANY), (theirs, ANY), (state[1], ANY), (state[0], ANY)],
        [(three, VM), (half, ANY), (half, ANY)],
        [
            sems,
            pltpu.VMEM((2, side, side), F32),
            level_arrays(g, 2, rows, pltpu.VMEM, True),
            pltpu.VMEM((2, 1, rows // 2, side), F32),
            pltpu.VMEM((2, rows // 2, side), F32),
        ],
        [(2, 1), (3, 2)],
    )
    adjoint = moved(adjoint, g, lambda p, l: (p, l + 2))
    mine, theirs = run_kernel(
        lambda rows_ref, a, m, t, *refs: up_kernel(
            g, rows_ref, a, m, t, {top - 1: refs[0], top: refs[1]}, *refs[2:6],
            {top - 1: refs[6], top: refs[7]},
        ),
        [
            (patch_rows, SM),
            (adjoint, VM),
            (mine, ANY),
            (theirs, ANY),
            (state[top - 1], ANY),
            (state[top], ANY),
        ],
        [(half, ANY), (half, ANY)],
        [
            sems,
            pltpu.VMEM((2, side, side), F32),
            level_scratch(g, top - 1),
            level_scratch(g, top),
        ],
        [(2, 0), (3, 1)],
    )
    given = moved(theirs, g, lambda p, l: (p, l ^ 1))
    adjoint, gradient = run_kernel(
        lambda *refs: join_kernel(g, *refs),
        [(mine, VM), (given, VM), (speed, VM), (fric, VM)],
        [
            (jax.ShapeDtypeStruct((g.slots, 2, side, side), F32), VM),
            (jax.ShapeDtypeStruct((g.slots, side, side), BF16), VM),
        ],
        [],
    )
    return (adjoint[None], gradient[None])


def solution(mesh):
    fields = P("level", "patch")
    return jax.shard_map(
        per_device,
        mesh=mesh,
        in_specs=(fields, fields, fields, fields, P()),
        out_specs=(fields, fields),
        check_vma=False,
    )
```

```python
from typing import Any, NamedTuple

import jax
import jax.numpy as jnp
from jax import lax
from jax.experimental import pallas as pl
from jax.experimental.pallas import tpu as pltpu
from jax.sharding import PartitionSpec as P

relaxation = 0.5
PAD = 8
LOW, HIGH, EDGES = 0, 1, 2
VM, SM, HBM = pltpu.VMEM, pltpu.SMEM, pltpu.HBM
F32 = jnp.float32
BF16 = jnp.bfloat16
VMEM_BYTES = 30 * 2**20


class Layout:
    def __init__(self, slots, side, levels, patches):
        self.slots = slots
        self.side = side
        self.levels = levels
        self.patches = patches
        self.half_slots = slots // 2
        self.half_side = side // 2
        self.span = 2 * slots

    def columns(self, level):
        return 1 << level

    def patch_rows(self, level):
        return self.slots >> level

    def rows(self, level):
        return self.patch_rows(level) * self.side

    def margin(self, level):
        return 2 << level

    def own(self, level):
        return max(1, (1 << level) // 2)

    def blocks(self, level):
        return self.own(level) + (1 if level > 0 else 0)

    def chunk(self, level, rows):
        size = 8 * max(1, 14 // self.blocks(level))
        while rows % size or (rows % self.side == 0 and self.side % size):
            size -= 8
        return size


def lane_ids(side):
    return lax.broadcasted_iota(jnp.int32, (1, side), 1)


def near_counts(g, rows_ref, level, patch, odd):
    own = rows_ref[level, patch]
    east = jnp.where(
        patch + 1 < g.patches, rows_ref[level, jnp.minimum(patch + 1, g.patches - 1)], 0
    )
    west = jnp.where(patch > 0, rows_ref[level, jnp.maximum(patch - 1, 0)], 0)
    return own, jnp.where(odd, own, east), jnp.where(odd, west, own)


def lane_limits(g, level, counts, cells):
    own, east, west = (value * cells for value in counts)
    lane = lane_ids(g.side)
    margin = g.margin(level)
    first = 0 if level > 0 else g.half_side
    edges = jnp.where(
        (lane >= first) & (lane < first + margin), east, jnp.where(lane >= g.side - margin, west, 0)
    )
    if level == 0:
        return [jnp.where(lane < g.half_side, own, edges)]
    return [jnp.full((1, g.side), own, jnp.int32)] * g.own(level) + [edges]


def one_side(g, values, east):
    count = len(values)
    turned = [pltpu.roll(value, g.side - 1 if east else 1, 1) for value in values]
    if count == 1:
        return turned
    lane = lax.broadcasted_iota(jnp.int32, values[0].shape, 1)
    last = lane == (g.side - 1 if east else 0)
    step = 1 if east else -1
    return [jnp.where(last, turned[(k + step) % count], turned[k]) for k in range(count)]


def both_sides(g, values):
    return one_side(g, values, True), one_side(g, values, False)


def over_rows(rows, chunk, body):
    def step(index, carry):
        body(pl.multiple_of(index * chunk, chunk))
        return carry

    lax.fori_loop(0, rows // chunk, step, 0)


def clear_pads(ref, lead):
    width = ref.shape[-1]
    last = ref.shape[-2]
    for index in lead:
        ref[index + (slice(0, PAD), slice(None))] = jnp.zeros((PAD, width), F32)
        ref[index + (slice(last - PAD, last), slice(None))] = jnp.zeros((PAD, width), F32)


def off_diagonal_step(g, level, d, start, stop):
    count = g.blocks(level)
    chunk = g.chunk(level, stop - start)

    def body(row):
        row = row + start
        here = pl.ds(row, chunk)
        inner = pl.ds(PAD + row, chunk)

        def line(comp, step):
            rows = pl.ds(PAD + row + step, chunk)
            return [d.cells[comp, k, rows, :] for k in range(count)]

        centre = [line(comp, 0) for comp in range(2)]
        beside = [both_sides(g, centre[comp]) for comp in range(2)]
        products = []
        for k in range(count):
            visc = d.visc[k, inner, :]
            half = 0.5 * visc
            (u, v) = (centre[comp][k] for comp in range(2))
            (u_e, u_w), (v_e, v_w) = ((beside[c][0][k], beside[c][1][k]) for c in range(2))
            u_n, v_n = (d.cells[c, k, pl.ds(PAD + row + 1, chunk), :] for c in range(2))
            u_s, v_s = (d.cells[c, k, pl.ds(PAD + row - 1, chunk), :] for c in range(2))
            one_u, one_v = visc * u, visc * v
            four_u, four_v = 4.0 * one_u, 4.0 * one_v
            cross_u, cross_v = half * (v_e - v_w), visc * (u_e - u_w)
            d.north[0, k, inner, :] = one_u + cross_u
            d.south[0, k, inner, :] = one_u - cross_u
            d.north[1, k, inner, :] = four_v + cross_v
            d.south[1, k, inner, :] = four_v - cross_v
            cross_u, cross_v = visc * (v_n - v_s), half * (u_n - u_s)
            products.append(
                (
                    four_u + cross_u,
                    four_u - cross_u,
                    one_v + cross_v,
                    one_v - cross_v,
                    visc * (4.0 * (u_e + u_w) + (u_n + u_s)),
                    visc * (4.0 * (v_n + v_s) + (v_e + v_w)),
                )
            )
        for comp in range(2):
            east = one_side(g, [item[2 * comp] for item in products], True)
            west = one_side(g, [item[2 * comp + 1] for item in products], False)
            for k in range(count):
                d.part[comp, k, here, :] = products[k][4 + comp] + east[k] + west[k]

    over_rows(stop - start, chunk, body)


def off_diagonal(d, comp, k, row, chunk):
    return (
        d.part[comp, k, pl.ds(row, chunk), :]
        + d.north[comp, k, pl.ds(PAD + row + 1, chunk), :]
        + d.south[comp, k, pl.ds(PAD + row - 1, chunk), :]
    )


def smooth_weights(g, level, d, limits, rows, from_zero):
    count = g.blocks(level)
    chunk = g.chunk(level, rows)

    def body(row):
        here = pl.ds(row, chunk)
        inner = pl.ds(PAD + row, chunk)
        centre = [d.visc[k, inner, :] for k in range(count)]
        east, west = both_sides(g, centre)
        for k in range(count):
            north = d.visc[k, pl.ds(PAD + row + 1, chunk), :]
            south = d.visc[k, pl.ds(PAD + row - 1, chunk), :]
            friction = d.fric[k, here, :]
            twice = 2.0 * centre[k]
            along_row = twice + east[k] + west[k]
            along_col = twice + north + south
            ids = row + lax.broadcasted_iota(jnp.int32, (chunk, g.side), 0)
            live = ids < limits[k]
            diag_u = 4.0 * along_row + along_col + friction
            diag_v = 4.0 * along_col + along_row + friction
            for comp, diag in ((0, diag_u), (1, diag_v)):
                weight = jnp.where(live, relaxation / diag, 0.0)
                d.weight[comp, k, here, :] = weight
                if from_zero:
                    d.cells[comp, k, inner, :] = weight * d.right[comp, k, here, :]

    over_rows(rows, chunk, body)


def residual_step(g, level, d, start, stop):
    count = g.blocks(level)
    chunk = g.chunk(level, stop - start)
    off_diagonal_step(g, level, d, start, stop)

    def body(row):
        row = row + start
        here = pl.ds(row, chunk)
        for comp in range(2):
            for k in range(count):
                weight = d.weight[comp, k, here, :]
                left = (1.0 - relaxation) * d.right[comp, k, here, :] + off_diagonal(
                    d, comp, k, row, chunk
                )
                left = jnp.where(weight > 0.0, left, 0.0)
                d.left[comp, k, here, :] = left
                d.held[comp, k, here, :] = (
                    d.cells[comp, k, pl.ds(PAD + row, chunk), :] + weight * left
                )

    over_rows(stop - start, chunk, body)


def corrected_step(g, level, d, start, stop, store):
    count = g.blocks(level)
    chunk = g.chunk(level, stop - start)
    off_diagonal_step(g, level, d, start, stop)

    def body(row):
        row = row + start
        here = pl.ds(row, chunk)
        for comp in range(2):
            for k in range(count):
                value = (
                    d.held[comp, k, here, :]
                    + (1.0 - relaxation) * d.cells[comp, k, pl.ds(PAD + row, chunk), :]
                    + d.weight[comp, k, here, :] * off_diagonal(d, comp, k, row, chunk)
                )
                store(comp, k, row, chunk, value)

    over_rows(stop - start, chunk, body)


def pairings(g, fine):
    if fine == 1:
        return [[(0, LOW), (1, HIGH)]]
    parts = [[(2 * k, LOW), (2 * k + 1, HIGH)] for k in range(g.own(fine) // 2)]
    return parts + [[(g.own(fine), EDGES)]]


def target_lane(g, part, fine_lane):
    halved = jnp.right_shift(fine_lane, 1)
    if part == LOW:
        return halved
    if part == HIGH:
        return g.half_side + halved
    return halved + jnp.where(fine_lane >= g.half_side, g.half_side, 0)


def sum_matrix(g, part):
    fine = lax.broadcasted_iota(jnp.int32, (g.side, g.side), 0)
    coarse = lax.broadcasted_iota(jnp.int32, (g.side, g.side), 1)
    return jnp.where(target_lane(g, part, fine) == coarse, 1.0, 0.0).astype(BF16)


def copy_matrix(g, part):
    coarse = lax.broadcasted_iota(jnp.int32, (g.side, g.side), 0)
    fine = lax.broadcasted_iota(jnp.int32, (g.side, g.side), 1)
    return jnp.where(target_lane(g, part, fine) == coarse, 1.0, 0.0).astype(BF16)


def split_dot(values, matrix):
    high = values.astype(BF16)
    rest = (values - high.astype(F32)).astype(BF16)
    return jnp.dot(high, matrix, preferred_element_type=F32) + jnp.dot(
        rest, matrix, preferred_element_type=F32
    )


def restrict_into(g, fine, d, start, stop, store):
    rows = stop - start
    chunk = min(rows // 2, g.half_side)
    if (rows // 2) % chunk:
        chunk = rows // 2
    parts = pairings(g, fine)
    matrices = {part: sum_matrix(g, part) for members in parts for _, part in members}

    def body(row):
        row = row + start // 2
        for comp in range(2):
            for coarse, members in enumerate(parts):
                total = None
                for k, part in members:
                    first = d.left[comp, k, pl.ds(2 * row, chunk, stride=2), :]
                    second = d.left[comp, k, pl.ds(2 * row + 1, chunk, stride=2), :]
                    term = split_dot(first + second, matrices[part])
                    total = term if total is None else total + term
                store(comp, coarse, row, chunk, total)

    over_rows(rows // 2, chunk, body)


def prolong_from(g, fine, d, limits, start, stop, load):
    rows = stop - start
    chunk = min(rows // 2, g.half_side)
    if (rows // 2) % chunk:
        chunk = rows // 2
    parts = pairings(g, fine)
    matrices = {part: copy_matrix(g, part) for members in parts for _, part in members}

    def body(row):
        row = row + start // 2
        ids = 2 * (row + lax.broadcasted_iota(jnp.int32, (chunk, g.side), 0))
        for comp in range(2):
            for coarse, members in enumerate(parts):
                value = load(comp, coarse, row, chunk)
                for k, part in members:
                    spread = jnp.where(ids < limits[k], split_dot(value, matrices[part]), 0.0)
                    d.cells[comp, k, pl.ds(PAD + 2 * row, chunk, stride=2), :] = spread
                    d.cells[comp, k, pl.ds(PAD + 2 * row + 1, chunk, stride=2), :] = spread

    over_rows(rows // 2, chunk, body)


def pack_kernel(g, force_in, visc_in, fric_in, swap, edge_own, edge_other, force, visc, fric, sems):
    level_here = lax.axis_index("level")
    copies = Copies(sems)
    for source, target in ((force_in, force), (visc_in, visc), (fric_in, fric)):
        copies.start(source, target)
    copies.finish()
    side = g.side

    def plane(q, slot):
        if q < 2:
            return force[slot, q].astype(F32)
        if q == 2:
            return fric[slot].astype(F32)
        return visc[slot]

    def packed_edge(level, column, start):
        lane = lane_ids(side)
        margin = g.margin(level)
        total = jnp.zeros((side, side), F32)
        for r in range(g.patch_rows(level)):
            slot = r * g.columns(level) + column
            for q in range(4):
                base = q * g.span + r * margin
                moved = plane(q, slot)
                if (base - start) % side:
                    moved = pltpu.roll(moved, (base - start) % side, 1)
                total = jnp.where((lane >= base) & (lane < base + margin), moved, total)
        return total

    def pack_level(level):
        west_type = level % 2 == 1
        margin = g.margin(level)
        last = g.columns(level) - 1
        west_edge = packed_edge(level, 0, 0)
        east_edge = packed_edge(level, last, side - margin)
        edge_own[...] = east_edge if west_type else west_edge
        edge_other[...] = west_edge if west_type else east_edge
        if level == 0:
            lane = lane_ids(side)
            for q in range(4):
                for k in range(g.half_slots):
                    swap[q * g.half_slots + k] = jnp.where(
                        lane < g.half_side,
                        plane(q, k),
                        pltpu.roll(plane(q, k + g.half_slots), g.half_side, 1),
                    )
            swap[4 * g.half_slots] = packed_edge(0, 0, g.half_side)
            return
        own = g.own(level)
        first = own if west_type else 0
        for r in range(g.patch_rows(level)):
            for k in range(own):
                for q in range(4):
                    swap[q * g.half_slots + r * own + k] = plane(
                        q, r * g.columns(level) + first + k
                    )
        if west_type:
            swap[4 * g.half_slots] = packed_edge(level, own - 1, side - margin)
        else:
            swap[4 * g.half_slots] = packed_edge(level, own, 0)

    for level in range(g.levels):
        pl.when(level_here == level)(lambda level=level: pack_level(level))


def fill_level(g, level, west_type, d, limits, covered, raw, got):
    force, visc, fric = raw
    swap, edge_own, edge_other = got
    side = g.side
    home = (level % 2 == 1) == west_type
    margin = g.margin(level)
    own = g.own(level)
    columns = g.columns(level)
    lane = lane_ids(side)
    edges = edge_own if home else edge_other

    def plane(q, slot):
        if q < 2:
            return force[slot, q].astype(F32)
        if q == 2:
            return fric[slot].astype(F32)
        return visc[slot]

    def unpacked(packed, q, r, place):
        shift = (place - (q * g.span + r * margin)) % side
        return pltpu.roll(packed, shift, 1) if shift else packed

    def store(q, k, r, value):
        here = pl.ds(r * side, side)
        if q < 2:
            if covered is not None:
                ids = r * side + lax.broadcasted_iota(jnp.int32, (side, side), 0)
                value = jnp.where(ids < covered[k], 0.0, value)
            d.right[q, k, here, :] = value
        elif q == 2:
            d.fric[k, here, :] = value
        else:
            d.visc[k, pl.ds(PAD + r * side, side), :] = jnp.where(
                limits[k] > r * side, 0.5 * value, 0.0
            )

    inner = swap[4 * g.half_slots]
    outer = edges[...]
    for r in range(g.patch_rows(level)):
        for q in range(4):
            if level == 0:
                if home:
                    value = pltpu.roll(plane(q, r), g.half_side, 1)
                    east = unpacked(outer, q, r, g.half_side)
                    value = jnp.where(
                        (lane >= g.half_side) & (lane < g.half_side + margin), east, value
                    )
                else:
                    value = swap[q * g.half_slots + r % g.half_slots]
                    if r >= g.half_slots:
                        value = pltpu.roll(value, g.half_side, 1)
                    east = unpacked(inner, q, r, g.half_side)
                    west = unpacked(outer, q, r, side - margin)
                    value = jnp.where(lane < g.half_side, value, east)
                    value = jnp.where(lane >= side - margin, west, value)
                store(q, 0, r, value)
                continue
            for k in range(own):
                if home:
                    value = plane(q, r * columns + k + (0 if west_type else own))
                else:
                    value = swap[q * g.half_slots + r * own + k]
                store(q, k, r, value)
            if west_type:
                if home:
                    east = plane(q, r * columns + own)
                else:
                    east = unpacked(inner, q, r, 0)
                west = unpacked(outer, q, r, side - margin)
            else:
                east = unpacked(outer, q, r, 0)
                if home:
                    west = plane(q, r * columns + own - 1)
                else:
                    west = unpacked(inner, q, r, side - margin)
            store(q, own, r, jnp.where(lane < g.half_side, east, west))


def joined_edges(g, edge_u, edge_v):
    lane = lane_ids(g.side)
    quarter = g.side // 4
    middle = (lane >= quarter) & (lane < g.side - quarter)
    return jnp.where(middle, pltpu.roll(edge_v, g.half_side, 1), edge_u)


class Level(NamedTuple):
    visc: Any
    weight: Any
    right: Any = None
    held: Any = None
    fric: Any = None
    cells: Any = None
    part: Any = None
    north: Any = None
    south: Any = None
    left: Any = None


def level_array(g, count, rows, make, comps, pad):
    shape = (count, rows + (2 * PAD if pad else 0), g.side)
    return make((2, *shape) if comps else shape, F32)


def kept_arrays(g, level, make, held):
    count, rows = g.blocks(level), g.rows(level)
    visc = level_array(g, count, rows, make, False, True)
    two = level_array(g, count, rows, make, True, False)
    return Level(visc, two, held=two) if held else Level(visc, two, right=two)


def step_arrays(g, level, rows):
    count = g.blocks(level)
    padded = level_array(g, count, rows, pltpu.VMEM, True, True)
    return dict(
        cells=padded,
        part=level_array(g, count, rows, pltpu.VMEM, True, False),
        north=padded,
        south=padded,
    )


def clear_level(g, level, d):
    blocks = range(g.blocks(level))
    both = [(c, k) for c in range(2) for k in blocks]
    for ref in (d.cells, d.north, d.south):
        clear_pads(ref, both)


def merged(first, second):
    return Level(*[b if a is None else a for a, b in zip(first, second)])


class Copies:
    def __init__(self, sems, first=0):
        self.sems = sems
        self.used = first
        self.open = []

    def start(self, source, target):
        copy = pltpu.make_async_copy(source, target, self.sems.at[self.used])
        self.used += 1
        copy.start()
        self.open.append(copy)

    def finish(self):
        for copy in self.open:
            copy.wait()
        self.open = []


def bottom_rows(g):
    return g.rows(2) // 2 + 4 * PAD


def kept_rows(g):
    return g.rows(2) // 2 + 2 * PAD


def down_kernel(
    g, rows_ref, force, visc, fric, swap, edge_own, edge_other, sums, kept, edges, scratch
):
    level_here = lax.axis_index("level")
    patch = lax.axis_index("patch")
    raw = (force, visc, fric)
    got = (swap, edge_own, edge_other)
    side = g.side
    top = g.levels - 1
    odd = level_here % 2 == 1
    levels = [merged(a, b) for a, b in zip(kept, scratch)]

    def limits_of(level):
        return lane_limits(g, level, near_counts(g, rows_ref, level, patch, odd), side)

    def covered_of(level):
        return lane_limits(g, level, near_counts(g, rows_ref, level + 1, patch, odd), g.half_side)

    def filled(wanted, covered):
        for level in wanted:
            clear_pads(levels[level].visc, [(k,) for k in range(g.blocks(level))])
        for west_type in (True, False):

            @pl.when(odd if west_type else jnp.logical_not(odd))
            def _():
                for level in wanted:
                    fill_level(
                        g, level, west_type, levels[level], limits_of(level),
                        covered.get(level), raw, got,
                    )

    @pl.when(level_here >= top - 1)
    def _():
        filled((top, top - 1), {})
        covered = covered_of(top - 1)

        def set_right(comp, k, row, chunk, value):
            here = pl.ds(row, chunk)
            ids = row + lax.broadcasted_iota(jnp.int32, (chunk, side), 0)
            old = levels[top - 1].right[comp, k, here, :]
            levels[top - 1].right[comp, k, here, :] = jnp.where(ids < covered[k], value, old)

        def keep(comp, k, row, chunk, value):
            (sums if k == 0 else edges)[comp, pl.ds(row, chunk), :] = value

        for level in (top, top - 1):
            d = levels[level]
            clear_level(g, level, d)
            smooth_weights(g, level, d, limits_of(level), g.rows(level), True)
            residual_step(g, level, d, 0, g.rows(level))
            restrict_into(g, level, d, 0, g.rows(level), set_right if level == top else keep)
        sums[2] = joined_edges(g, edges[0], edges[1])

    @pl.when(level_here < top - 1)
    def _():
        filled((1, 0), {1: covered_of(1)})
        for level in (1, 0):
            smooth_weights(g, level, levels[level], limits_of(level), g.rows(level), False)


def bottom_levels(g, rows_ref, patch, odd, start, stop, fine, coarse, new_sums, store_fine, store_coarse):
    side = g.side
    count, chunk = g.blocks(1), g.chunk(1, stop - start)
    clear_level(g, 1, fine)
    if new_sums is not None:
        reach = g.rows(2) // 2
        for comp in range(2):
            for k in range(count):
                here = pl.ds(0, reach)
                fine.right[comp, k, here, :] = fine.right[comp, k, here, :] + new_sums(comp, k)

    def body(row):
        here = pl.ds(start + row, chunk)
        for comp in range(2):
            for k in range(count):
                fine.cells[comp, k, pl.ds(PAD + start + row, chunk), :] = (
                    fine.weight[comp, k, here, :] * fine.right[comp, k, here, :]
                )

    over_rows(stop - start, chunk, body)
    residual_step(g, 1, fine, start, stop)
    near = near_counts(g, rows_ref, 1, patch, odd)
    covered = lane_limits(g, 0, near, g.half_side)

    def smooth_coarse(comp, k, row, size, value):
        here = pl.ds(row, size)
        ids = row + lax.broadcasted_iota(jnp.int32, (size, side), 0)
        value = jnp.where(ids < covered[0], value, coarse.right[comp, 0, here, :])
        value = coarse.weight[comp, 0, here, :] * value
        coarse.cells[comp, 0, here, :] = value
        store_coarse(comp, row, size, value)

    restrict_into(g, 1, fine, start, stop, smooth_coarse)

    def load(comp, k, row, size):
        return coarse.cells[comp, 0, pl.ds(row, size), :]

    prolong_from(g, 1, fine, lane_limits(g, 1, near, side), start, stop, load)
    corrected_step(g, 1, fine, start, stop, store_fine)


def bottom_kernel(g, rows_ref, sums, kept, coarse_kept, adjoint, own_rows, coarse_rows, edges, scratch, coarse_cells):
    level_here = lax.axis_index("level")
    patch = lax.axis_index("patch")
    side = g.side
    rows = bottom_rows(g)
    top = g.levels - 1
    odd = level_here % 2 == 1

    @pl.when(level_here < top - 1)
    def _():
        reach = g.rows(2) // 2
        both = sums[2]
        swapped = pltpu.roll(both, g.half_side, 1)
        fine = merged(Level(kept.visc, kept.weight), scratch)
        for comp in range(2):
            for k in range(g.blocks(1)):
                fine.right[comp, k] = kept.right[comp, k, pl.ds(0, rows), :]

        def new_sums(comp, k):
            value = sums[comp] if k == 0 else (both, swapped)[comp]
            return jnp.where(kept.weight[comp, k, pl.ds(0, reach), :] > 0.0, value, 0.0)

        def store_fine(comp, k, row, chunk, value):
            (own_rows if k == 0 else edges)[comp, pl.ds(row, chunk), :] = value

        def store_coarse(comp, row, size, value):
            coarse_rows[comp, pl.ds(row, size), :] = value

        coarse = Level(None, coarse_kept.weight, coarse_kept.right, cells=coarse_cells)
        bottom_levels(
            g, rows_ref, patch, odd, 0, rows, fine, coarse, new_sums, store_fine, store_coarse
        )
        adjoint[0] = own_rows[0, pl.ds(0, side), :]
        adjoint[1] = own_rows[1, pl.ds(0, side), :]
        adjoint[2] = joined_edges(g, edges[0, pl.ds(0, side), :], edges[1, pl.ds(0, side), :])


def up_kernel(
    g, rows_ref, adjoint, own_rows, coarse_rows, kept, mine, theirs, edges, scratch, coarse_cells, finer,
    coarser,
):
    level_here = lax.axis_index("level")
    patch = lax.axis_index("patch")
    side = g.side
    top = g.levels - 1
    odd = level_here % 2 == 1
    levels = [merged(a, b) for a, b in zip(kept, scratch)]

    def hand_out():
        def write(first, second):
            for k in range(g.half_slots):
                for comp in range(2):
                    first[k, comp] = finer[k, comp]
                    second[k, comp] = coarser[k, comp]

        pl.when(odd)(lambda: write(mine, theirs))
        pl.when(jnp.logical_not(odd))(lambda: write(theirs, mine))

    @pl.when(level_here >= top - 1)
    def _():
        both = adjoint[2]
        edges[0] = both
        edges[1] = pltpu.roll(both, g.half_side, 1)

        def load_given(comp, k, row, chunk):
            return (adjoint if k == 0 else edges)[comp, pl.ds(row, chunk), :]

        def load_held(comp, k, row, chunk):
            return levels[top - 1].held[comp, k, pl.ds(row, chunk), :]

        def store_in(level, out, hold):
            own = g.own(level)

            def store(comp, k, row, chunk, value):
                if hold:
                    levels[level].held[comp, k, pl.ds(row, chunk), :] = value
                if k < own:
                    group, place = row // side, row % side
                    out[group * own + k, comp, pl.ds(pl.multiple_of(place, 8), chunk), :] = value

            return store

        for level, load, out in ((top - 1, load_given, coarser), (top, load_held, finer)):
            d = levels[level]
            clear_level(g, level, d)
            near = near_counts(g, rows_ref, level, patch, odd)
            rows = g.rows(level)
            prolong_from(g, level, d, lane_limits(g, level, near, side), 0, rows, load)
            corrected_step(g, level, d, 0, rows, store_in(level, out, level < top))
        hand_out()

    @pl.when(level_here < top - 1)
    def _():
        rows = g.rows(1)
        first = g.rows(2) // 2
        done = kept_rows(g)
        fine, coarse = levels[1], levels[0]._replace(cells=coarse_cells)

        def store_fine(comp, k, row, chunk, value):
            if k == 0:
                group, place = row // side, row % side
                finer[group, comp, pl.ds(pl.multiple_of(place, 8), chunk), :] = value

        def store_coarse(comp, row, size, value):
            pass

        bottom_levels(
            g, rows_ref, patch, odd, first, rows, fine, coarse, None, store_fine, store_coarse
        )
        lane = lane_ids(side)
        for comp in range(2):
            finer[0, comp] = own_rows[comp, pl.ds(0, side), :]
            finer[1, comp, pl.ds(0, done - side), :] = own_rows[comp, pl.ds(side, done - side), :]
            coarse_cells[comp, 0, pl.ds(0, done // 2), :] = coarse_rows[
                comp, pl.ds(0, done // 2), :
            ]
            for k in range(g.half_slots):
                parts = []
                for group in (k, k + g.half_slots):
                    here = pl.ds(group * side, side)
                    if group * side < rows // 2:
                        parts.append(coarse_cells[comp, 0, here, :])
                    else:
                        parts.append(
                            coarse.weight[comp, 0, here, :] * coarse.right[comp, 0, here, :]
                        )
                coarser[k, comp] = jnp.where(
                    lane < g.half_side, parts[0], pltpu.roll(parts[1], g.half_side, 1)
                )
        hand_out()


def join_kernel(g, mine, given, speed, fric, adjoint, gradient):
    level_here = lax.axis_index("level")
    lane = lane_ids(g.side)

    def put(slot, parts):
        for comp in range(2):
            adjoint[slot, comp] = parts[comp]
        total = speed[slot, 0].astype(F32) * parts[0] + speed[slot, 1].astype(F32) * parts[1]
        gradient[slot] = (-(fric[slot].astype(F32) * total)).astype(BF16)

    def join_level(level):
        if level == 0:
            for k in range(g.half_slots):
                low = []
                high = []
                for comp in range(2):
                    west, east = given[k, comp], mine[k, comp]
                    low.append(
                        jnp.where(lane < g.half_side, west, pltpu.roll(east, g.half_side, 1))
                    )
                    high.append(
                        jnp.where(lane < g.half_side, pltpu.roll(west, g.half_side, 1), east)
                    )
                put(k, low)
                put(k + g.half_slots, high)
            return
        own = g.own(level)
        west_half, east_half = (mine, given) if level % 2 == 1 else (given, mine)
        for r in range(g.patch_rows(level)):
            for k in range(2 * own):
                source = west_half if k < own else east_half
                put(
                    r * g.columns(level) + k,
                    [source[r * own + k % own, comp] for comp in range(2)],
                )

    for level in range(g.levels):
        pl.when(level_here == level)(lambda level=level: join_level(level))


def run_kernel(body, ins, outs, scratch):
    in_trees = [jax.tree.flatten(tree) for tree, _ in ins]
    out_trees = [jax.tree.flatten(tree) for tree, _ in outs]
    scratch_trees = [jax.tree.flatten(tree) for tree in scratch]
    sizes = [len(leaves) for leaves, _ in in_trees + out_trees + scratch_trees]
    shapes = [tree for _, tree in in_trees + out_trees + scratch_trees]

    def kernel(*refs):
        given = []
        first = 0
        for size, shape in zip(sizes, shapes):
            given.append(jax.tree.unflatten(shape, refs[first : first + size]))
            first += size
        body(*given)

    def specs(groups, trees):
        return [
            pl.BlockSpec(memory_space=space)
            for (_, space), (leaves, _) in zip(groups, trees)
            for _ in leaves
        ]

    results = pl.pallas_call(
        kernel,
        out_shape=[leaf for leaves, _ in out_trees for leaf in leaves],
        in_specs=specs(ins, in_trees),
        out_specs=specs(outs, out_trees),
        scratch_shapes=[leaf for leaves, _ in scratch_trees for leaf in leaves],
        compiler_params=pltpu.CompilerParams(vmem_limit_bytes=VMEM_BYTES),
    )(*[leaf for leaves, _ in in_trees for leaf in leaves])
    answer = []
    first = 0
    for leaves, shape in out_trees:
        answer.append(jax.tree.unflatten(shape, results[first : first + len(leaves)]))
        first += len(leaves)
    return answer


def moved(value, g, step):
    pairs = []
    for patch in range(g.patches):
        for level in range(g.levels):
            to_patch, to_level = step(patch, level)
            if 0 <= to_patch < g.patches and 0 <= to_level < g.levels:
                pairs.append((patch * g.levels + level, to_patch * g.levels + to_level))
    return lax.ppermute(value, ("patch", "level"), pairs)


def per_device(forcing, velocity, viscosity, friction, patch_rows):
    g = Layout(
        forcing.shape[1], forcing.shape[-1], lax.axis_size("level"), lax.axis_size("patch")
    )
    side = g.side
    top = g.levels - 1
    force, speed, visc, fric = forcing[0], velocity[0], viscosity[0], friction[0]
    make = jax.ShapeDtypeStruct
    block = make((side, side), F32)
    half = make((g.half_slots, 2, side, side), F32)
    three = make((3, side, side), F32)
    two = pltpu.VMEM((2, side, side), F32)
    sems = pltpu.SemaphoreType.DMA((4,))

    swap, edge_own, edge_other, force, visc, fric = run_kernel(
        lambda *refs: pack_kernel(g, *refs),
        [(force, HBM), (visc, HBM), (fric, HBM)],
        [
            (make((4 * g.half_slots + 1, side, side), F32), VM),
            (block, VM),
            (block, VM),
            (make(force.shape, force.dtype), VM),
            (make(visc.shape, visc.dtype), VM),
            (make(fric.shape, fric.dtype), VM),
        ],
        [sems],
    )
    swap = moved(swap, g, lambda p, l: (p, l ^ 1))
    edge_own = moved(edge_own, g, lambda p, l: (p + (1 if l % 2 else -1), l))
    edge_other = moved(edge_other, g, lambda p, l: (p + (-1 if l % 2 else 1), l ^ 1))

    def down_scratch(level):
        count, rows = g.blocks(level), g.rows(level)
        fric_here = level_array(g, count, rows, pltpu.VMEM, False, False)
        if level < top - 1:
            return Level(None, None, fric=fric_here)
        both = level_array(g, count, rows, pltpu.VMEM, True, False)
        return Level(None, None, right=both, fric=fric_here, left=both, **step_arrays(g, level, rows))

    sums, kept = run_kernel(
        lambda *refs: down_kernel(g, *refs),
        [
            (patch_rows, SM),
            (force, VM),
            (visc, VM),
            (fric, VM),
            (swap, VM),
            (edge_own, VM),
            (edge_other, VM),
        ],
        [
            (three, VM),
            ([kept_arrays(g, level, make, level >= top - 1) for level in range(g.levels)], VM),
        ],
        [two, [down_scratch(level) for level in range(g.levels)]],
    )
    sums = moved(sums, g, lambda p, l: (p, l - 2))
    rows = bottom_rows(g)
    part = level_array(g, g.blocks(1), rows, pltpu.VMEM, True, False)
    adjoint, own_rows, coarse_rows = run_kernel(
        lambda *refs: bottom_kernel(g, *refs),
        [(patch_rows, SM), (sums, VM), (kept[1], VM), (kept[0], VM)],
        [
            (three, VM),
            (make((2, rows, side), F32), VM),
            (make((2, rows // 2, side), F32), VM),
        ],
        [
            pltpu.VMEM((2, rows, side), F32),
            Level(None, None, right=part, held=part, left=part, **step_arrays(g, 1, rows)),
            pltpu.VMEM((2, 1, rows // 2, side), F32),
        ],
    )
    adjoint = moved(adjoint, g, lambda p, l: (p, l + 2))

    def up_scratch(level):
        if level == 0:
            return Level(None, None)
        rows = g.rows(level)
        both = level_array(g, g.blocks(level), rows, pltpu.VMEM, True, False)
        more = dict(held=both, left=both) if level == 1 else {}
        return Level(None, None, **more, **step_arrays(g, level, rows))

    mine, theirs = run_kernel(
        lambda *refs: up_kernel(g, *refs),
        [(patch_rows, SM), (adjoint, VM), (own_rows, VM), (coarse_rows, VM), (kept, VM)],
        [(half, VM), (half, VM)],
        [
            two,
            [up_scratch(level) for level in range(g.levels)],
            pltpu.VMEM((2, 1, g.rows(1) // 2, side), F32),
            pltpu.VMEM(half.shape, F32),
            pltpu.VMEM(half.shape, F32),
        ],
    )
    given = moved(theirs, g, lambda p, l: (p, l ^ 1))
    adjoint, gradient = run_kernel(
        lambda *refs: join_kernel(g, *refs),
        [(mine, VM), (given, VM), (speed, VM), (fric, VM)],
        [
            (make((g.slots, 2, side, side), F32), VM),
            (make((g.slots, side, side), BF16), VM),
        ],
        [],
    )
    return (adjoint[None], gradient[None])


def solution(mesh):
    fields = P("level", "patch")
    return jax.shard_map(
        per_device,
        mesh=mesh,
        in_specs=(fields, fields, fields, fields, P()),
        out_specs=(fields, fields),
        check_vma=False,
    )
```

```python
from typing import Any, NamedTuple

import jax
import jax.numpy as jnp
from jax import lax
from jax.experimental import pallas as pl
from jax.experimental.pallas import tpu as pltpu
from jax.sharding import PartitionSpec as P

relaxation = 0.5
PAD = 8
LOW, HIGH, EDGES = 0, 1, 2
VM, SM, HBM = pltpu.VMEM, pltpu.SMEM, pltpu.HBM
F32 = jnp.float32
BF16 = jnp.bfloat16
VMEM_BYTES = 30 * 2**20
FIRST_BYTES = 60 * 2**20


class Layout:
    def __init__(self, slots, side, levels, patches):
        self.slots = slots
        self.side = side
        self.levels = levels
        self.patches = patches
        self.half_slots = slots // 2
        self.half_side = side // 2
        self.span = 2 * slots

    def columns(self, level):
        return 1 << level

    def patch_rows(self, level):
        return self.slots >> level

    def rows(self, level):
        return self.patch_rows(level) * self.side

    def margin(self, level):
        return 2 << level

    def own(self, level):
        return max(1, (1 << level) // 2)

    def blocks(self, level):
        return self.own(level) + (1 if level > 0 else 0)

    def chunk(self, level, rows):
        size = 8 * max(1, 14 // self.blocks(level))
        while rows % size or (rows % self.side == 0 and self.side % size):
            size -= 8
        return size


def lane_ids(side):
    return lax.broadcasted_iota(jnp.int32, (1, side), 1)


def near_counts(g, rows_ref, level, patch, odd):
    own = rows_ref[level, patch]
    east = jnp.where(
        patch + 1 < g.patches, rows_ref[level, jnp.minimum(patch + 1, g.patches - 1)], 0
    )
    west = jnp.where(patch > 0, rows_ref[level, jnp.maximum(patch - 1, 0)], 0)
    return own, jnp.where(odd, own, east), jnp.where(odd, west, own)


def lane_limits(g, level, counts, cells):
    own, east, west = (value * cells for value in counts)
    lane = lane_ids(g.side)
    margin = g.margin(level)
    first = 0 if level > 0 else g.half_side
    edges = jnp.where(
        (lane >= first) & (lane < first + margin), east, jnp.where(lane >= g.side - margin, west, 0)
    )
    if level == 0:
        return [jnp.where(lane < g.half_side, own, edges)]
    return [jnp.full((1, g.side), own, jnp.int32)] * g.own(level) + [edges]


def one_side(g, values, east):
    count = len(values)
    turned = [pltpu.roll(value, g.side - 1 if east else 1, 1) for value in values]
    if count == 1:
        return turned
    lane = lax.broadcasted_iota(jnp.int32, values[0].shape, 1)
    last = lane == (g.side - 1 if east else 0)
    step = 1 if east else -1
    return [jnp.where(last, turned[(k + step) % count], turned[k]) for k in range(count)]


def both_sides(g, values):
    return one_side(g, values, True), one_side(g, values, False)


def over_rows(rows, chunk, body):
    def step(index, carry):
        body(pl.multiple_of(index * chunk, chunk))
        return carry

    lax.fori_loop(0, rows // chunk, step, 0)


def clear_pads(ref, lead):
    width = ref.shape[-1]
    last = ref.shape[-2]
    for index in lead:
        ref[index + (slice(0, PAD), slice(None))] = jnp.zeros((PAD, width), F32)
        ref[index + (slice(last - PAD, last), slice(None))] = jnp.zeros((PAD, width), F32)


def off_diagonal_step(g, level, d, start, stop):
    count = g.blocks(level)
    chunk = g.chunk(level, stop - start)

    def body(row):
        row = row + start
        here = pl.ds(row, chunk)
        inner = pl.ds(PAD + row, chunk)

        def line(comp, step):
            rows = pl.ds(PAD + row + step, chunk)
            return [d.cells[comp, k, rows, :] for k in range(count)]

        centre = [line(comp, 0) for comp in range(2)]
        beside = [both_sides(g, centre[comp]) for comp in range(2)]
        products = []
        for k in range(count):
            visc = d.visc[k, inner, :]
            half = 0.5 * visc
            (u, v) = (centre[comp][k] for comp in range(2))
            (u_e, u_w), (v_e, v_w) = ((beside[c][0][k], beside[c][1][k]) for c in range(2))
            u_n, v_n = (d.cells[c, k, pl.ds(PAD + row + 1, chunk), :] for c in range(2))
            u_s, v_s = (d.cells[c, k, pl.ds(PAD + row - 1, chunk), :] for c in range(2))
            one_u, one_v = visc * u, visc * v
            four_u, four_v = 4.0 * one_u, 4.0 * one_v
            cross_u, cross_v = half * (v_e - v_w), visc * (u_e - u_w)
            d.north[0, k, inner, :] = one_u + cross_u
            d.south[0, k, inner, :] = one_u - cross_u
            d.north[1, k, inner, :] = four_v + cross_v
            d.south[1, k, inner, :] = four_v - cross_v
            cross_u, cross_v = visc * (v_n - v_s), half * (u_n - u_s)
            products.append(
                (
                    four_u + cross_u,
                    four_u - cross_u,
                    one_v + cross_v,
                    one_v - cross_v,
                    visc * (4.0 * (u_e + u_w) + (u_n + u_s)),
                    visc * (4.0 * (v_n + v_s) + (v_e + v_w)),
                )
            )
        for comp in range(2):
            east = one_side(g, [item[2 * comp] for item in products], True)
            west = one_side(g, [item[2 * comp + 1] for item in products], False)
            for k in range(count):
                d.part[comp, k, here, :] = products[k][4 + comp] + east[k] + west[k]

    over_rows(stop - start, chunk, body)


def off_diagonal(d, comp, k, row, chunk):
    return (
        d.part[comp, k, pl.ds(row, chunk), :]
        + d.north[comp, k, pl.ds(PAD + row + 1, chunk), :]
        + d.south[comp, k, pl.ds(PAD + row - 1, chunk), :]
    )


def smooth_weights(g, level, d, limits, rows, from_zero):
    count = g.blocks(level)
    chunk = g.chunk(level, rows)

    def body(row):
        here = pl.ds(row, chunk)
        inner = pl.ds(PAD + row, chunk)
        centre = [d.visc[k, inner, :] for k in range(count)]
        east, west = both_sides(g, centre)
        for k in range(count):
            north = d.visc[k, pl.ds(PAD + row + 1, chunk), :]
            south = d.visc[k, pl.ds(PAD + row - 1, chunk), :]
            friction = d.fric[k, here, :]
            twice = 2.0 * centre[k]
            along_row = twice + east[k] + west[k]
            along_col = twice + north + south
            ids = row + lax.broadcasted_iota(jnp.int32, (chunk, g.side), 0)
            live = ids < limits[k]
            diag_u = 4.0 * along_row + along_col + friction
            diag_v = 4.0 * along_col + along_row + friction
            for comp, diag in ((0, diag_u), (1, diag_v)):
                weight = jnp.where(live, relaxation / diag, 0.0)
                d.weight[comp, k, here, :] = weight
                if from_zero:
                    d.cells[comp, k, inner, :] = weight * d.right[comp, k, here, :]

    over_rows(rows, chunk, body)


def residual_step(g, level, d, start, stop):
    count = g.blocks(level)
    chunk = g.chunk(level, stop - start)
    off_diagonal_step(g, level, d, start, stop)

    def body(row):
        row = row + start
        here = pl.ds(row, chunk)
        for comp in range(2):
            for k in range(count):
                weight = d.weight[comp, k, here, :]
                left = (1.0 - relaxation) * d.right[comp, k, here, :] + off_diagonal(
                    d, comp, k, row, chunk
                )
                left = jnp.where(weight > 0.0, left, 0.0)
                d.left[comp, k, here, :] = left
                d.held[comp, k, here, :] = (
                    d.cells[comp, k, pl.ds(PAD + row, chunk), :] + weight * left
                )

    over_rows(stop - start, chunk, body)


def corrected_step(g, level, d, start, stop, store):
    count = g.blocks(level)
    chunk = g.chunk(level, stop - start)
    off_diagonal_step(g, level, d, start, stop)

    def body(row):
        row = row + start
        here = pl.ds(row, chunk)
        for comp in range(2):
            for k in range(count):
                value = (
                    d.held[comp, k, here, :]
                    + (1.0 - relaxation) * d.cells[comp, k, pl.ds(PAD + row, chunk), :]
                    + d.weight[comp, k, here, :] * off_diagonal(d, comp, k, row, chunk)
                )
                store(comp, k, row, chunk, value)

    over_rows(stop - start, chunk, body)


def pairings(g, fine):
    if fine == 1:
        return [[(0, LOW), (1, HIGH)]]
    parts = [[(2 * k, LOW), (2 * k + 1, HIGH)] for k in range(g.own(fine) // 2)]
    return parts + [[(g.own(fine), EDGES)]]


def target_lane(g, part, fine_lane):
    halved = jnp.right_shift(fine_lane, 1)
    if part == LOW:
        return halved
    if part == HIGH:
        return g.half_side + halved
    return halved + jnp.where(fine_lane >= g.half_side, g.half_side, 0)


def sum_matrix(g, part):
    fine = lax.broadcasted_iota(jnp.int32, (g.side, g.side), 0)
    coarse = lax.broadcasted_iota(jnp.int32, (g.side, g.side), 1)
    return jnp.where(target_lane(g, part, fine) == coarse, 1.0, 0.0).astype(BF16)


def copy_matrix(g, part):
    coarse = lax.broadcasted_iota(jnp.int32, (g.side, g.side), 0)
    fine = lax.broadcasted_iota(jnp.int32, (g.side, g.side), 1)
    return jnp.where(target_lane(g, part, fine) == coarse, 1.0, 0.0).astype(BF16)


def split_dot(values, matrix):
    high = values.astype(BF16)
    rest = (values - high.astype(F32)).astype(BF16)
    return jnp.dot(high, matrix, preferred_element_type=F32) + jnp.dot(
        rest, matrix, preferred_element_type=F32
    )


def restrict_into(g, fine, d, start, stop, store):
    rows = stop - start
    chunk = min(rows // 2, g.half_side)
    if (rows // 2) % chunk:
        chunk = rows // 2
    parts = pairings(g, fine)
    matrices = {part: sum_matrix(g, part) for members in parts for _, part in members}

    def body(row):
        row = row + start // 2
        for comp in range(2):
            for coarse, members in enumerate(parts):
                total = None
                for k, part in members:
                    first = d.left[comp, k, pl.ds(2 * row, chunk, stride=2), :]
                    second = d.left[comp, k, pl.ds(2 * row + 1, chunk, stride=2), :]
                    term = split_dot(first + second, matrices[part])
                    total = term if total is None else total + term
                store(comp, coarse, row, chunk, total)

    over_rows(rows // 2, chunk, body)


def prolong_from(g, fine, d, limits, start, stop, load):
    rows = stop - start
    chunk = min(rows // 2, g.half_side)
    if (rows // 2) % chunk:
        chunk = rows // 2
    parts = pairings(g, fine)
    matrices = {part: copy_matrix(g, part) for members in parts for _, part in members}

    def body(row):
        row = row + start // 2
        ids = 2 * (row + lax.broadcasted_iota(jnp.int32, (chunk, g.side), 0))
        for comp in range(2):
            for coarse, members in enumerate(parts):
                value = load(comp, coarse, row, chunk)
                for k, part in members:
                    spread = jnp.where(ids < limits[k], split_dot(value, matrices[part]), 0.0)
                    d.cells[comp, k, pl.ds(PAD + 2 * row, chunk, stride=2), :] = spread
                    d.cells[comp, k, pl.ds(PAD + 2 * row + 1, chunk, stride=2), :] = spread

    over_rows(rows // 2, chunk, body)


def pack_kernel(g, force_in, visc_in, fric_in, swap, edge_own, edge_other, sems, force, visc, fric):
    level_here = lax.axis_index("level")
    copies = Copies(sems)
    for source, target in ((force_in, force), (visc_in, visc), (fric_in, fric)):
        copies.start(source, target)
    copies.finish()
    side = g.side

    def plane(q, slot):
        if q < 2:
            return force[slot, q].astype(F32)
        if q == 2:
            return fric[slot].astype(F32)
        return visc[slot]

    def packed_edge(level, column, start):
        lane = lane_ids(side)
        margin = g.margin(level)
        total = jnp.zeros((side, side), F32)
        for r in range(g.patch_rows(level)):
            slot = r * g.columns(level) + column
            for q in range(4):
                base = q * g.span + r * margin
                moved = plane(q, slot)
                if (base - start) % side:
                    moved = pltpu.roll(moved, (base - start) % side, 1)
                total = jnp.where((lane >= base) & (lane < base + margin), moved, total)
        return total

    def pack_level(level):
        west_type = level % 2 == 1
        margin = g.margin(level)
        last = g.columns(level) - 1
        west_edge = packed_edge(level, 0, 0)
        east_edge = packed_edge(level, last, side - margin)
        edge_own[...] = east_edge if west_type else west_edge
        edge_other[...] = west_edge if west_type else east_edge
        if level == 0:
            lane = lane_ids(side)
            for q in range(4):
                for k in range(g.half_slots):
                    swap[q * g.half_slots + k] = jnp.where(
                        lane < g.half_side,
                        plane(q, k),
                        pltpu.roll(plane(q, k + g.half_slots), g.half_side, 1),
                    )
            swap[4 * g.half_slots] = packed_edge(0, 0, g.half_side)
            return
        own = g.own(level)
        first = own if west_type else 0
        for r in range(g.patch_rows(level)):
            for k in range(own):
                for q in range(4):
                    swap[q * g.half_slots + r * own + k] = plane(
                        q, r * g.columns(level) + first + k
                    )
        if west_type:
            swap[4 * g.half_slots] = packed_edge(level, own - 1, side - margin)
        else:
            swap[4 * g.half_slots] = packed_edge(level, own, 0)

    for level in range(g.levels):
        pl.when(level_here == level)(lambda level=level: pack_level(level))


def fill_level(g, level, west_type, d, limits, covered, raw, got):
    force, visc, fric = raw
    swap, edge_own, edge_other = got
    side = g.side
    home = (level % 2 == 1) == west_type
    margin = g.margin(level)
    own = g.own(level)
    columns = g.columns(level)
    lane = lane_ids(side)
    edges = edge_own if home else edge_other

    def plane(q, slot):
        if q < 2:
            return force[slot, q].astype(F32)
        if q == 2:
            return fric[slot].astype(F32)
        return visc[slot]

    def unpacked(packed, q, r, place):
        shift = (place - (q * g.span + r * margin)) % side
        return pltpu.roll(packed, shift, 1) if shift else packed

    def store(q, k, r, value):
        here = pl.ds(r * side, side)
        if q < 2:
            if covered is not None:
                ids = r * side + lax.broadcasted_iota(jnp.int32, (side, side), 0)
                value = jnp.where(ids < covered[k], 0.0, value)
            d.right[q, k, here, :] = value
        elif q == 2:
            d.fric[k, here, :] = value
        else:
            d.visc[k, pl.ds(PAD + r * side, side), :] = jnp.where(
                limits[k] > r * side, 0.5 * value, 0.0
            )

    inner = swap[4 * g.half_slots]
    outer = edges[...]
    for r in range(g.patch_rows(level)):
        for q in range(4):
            if level == 0:
                if home:
                    value = pltpu.roll(plane(q, r), g.half_side, 1)
                    east = unpacked(outer, q, r, g.half_side)
                    value = jnp.where(
                        (lane >= g.half_side) & (lane < g.half_side + margin), east, value
                    )
                else:
                    value = swap[q * g.half_slots + r % g.half_slots]
                    if r >= g.half_slots:
                        value = pltpu.roll(value, g.half_side, 1)
                    east = unpacked(inner, q, r, g.half_side)
                    west = unpacked(outer, q, r, side - margin)
                    value = jnp.where(lane < g.half_side, value, east)
                    value = jnp.where(lane >= side - margin, west, value)
                store(q, 0, r, value)
                continue
            for k in range(own):
                if home:
                    value = plane(q, r * columns + k + (0 if west_type else own))
                else:
                    value = swap[q * g.half_slots + r * own + k]
                store(q, k, r, value)
            if west_type:
                if home:
                    east = plane(q, r * columns + own)
                else:
                    east = unpacked(inner, q, r, 0)
                west = unpacked(outer, q, r, side - margin)
            else:
                east = unpacked(outer, q, r, 0)
                if home:
                    west = plane(q, r * columns + own - 1)
                else:
                    west = unpacked(inner, q, r, side - margin)
            store(q, own, r, jnp.where(lane < g.half_side, east, west))


def joined_edges(g, edge_u, edge_v):
    lane = lane_ids(g.side)
    quarter = g.side // 4
    middle = (lane >= quarter) & (lane < g.side - quarter)
    return jnp.where(middle, pltpu.roll(edge_v, g.half_side, 1), edge_u)


class Level(NamedTuple):
    visc: Any
    weight: Any
    right: Any = None
    held: Any = None
    fric: Any = None
    cells: Any = None
    part: Any = None
    north: Any = None
    south: Any = None
    left: Any = None


def level_array(g, count, rows, make, comps, pad):
    shape = (count, rows + (2 * PAD if pad else 0), g.side)
    return make((2, *shape) if comps else shape, F32)


def step_arrays(g, level, rows):
    count = g.blocks(level)
    padded = level_array(g, count, rows, pltpu.VMEM, True, True)
    return dict(
        cells=padded,
        part=level_array(g, count, rows, pltpu.VMEM, True, False),
        north=padded,
        south=padded,
    )


def clear_level(g, level, d):
    blocks = range(g.blocks(level))
    both = [(c, k) for c in range(2) for k in blocks]
    for ref in (d.cells, d.north, d.south):
        clear_pads(ref, both)


def merged(first, second):
    return Level(*[b if a is None else a for a, b in zip(first, second)])


class Copies:
    def __init__(self, sems, first=0):
        self.sems = sems
        self.used = first
        self.open = []

    def start(self, source, target):
        copy = pltpu.make_async_copy(source, target, self.sems.at[self.used])
        self.used += 1
        copy.start()
        self.open.append(copy)

    def finish(self):
        for copy in self.open:
            copy.wait()
        self.open = []


def low_rows(g):
    return g.rows(2) // 2 + 2 * PAD


def kept_rows(g):
    return g.rows(2) // 2 + PAD


def lent_rows(g):
    return low_rows(g), -(-low_rows(g) // 2 // 16) * 16


def lent_planes(level):
    visc = level[3]
    high = visc.astype(BF16)
    return [value.astype(BF16) for value in level[:3]] + [
        high,
        (visc - high.astype(F32)).astype(BF16),
    ]


def lend(g, fine, coarse, out):
    rows, less = lent_rows(g)
    side, margin = g.side, g.margin(1)
    lane = lane_ids(side)

    def block(level, k, size):
        here = pl.ds(0, size)
        return (
            level.right[0, k, here, :],
            level.right[1, k, here, :],
            level.fric[k, here, :],
            level.visc[k, pl.ds(PAD, size), :],
        )

    planes = lent_planes(block(fine, 0, rows))
    for index, value in enumerate(planes):
        out[pl.ds(index * rows, rows), :] = value
    first = len(planes) * rows
    for index, value in enumerate(lent_planes(block(coarse, 0, less))):
        out[pl.ds(first + index * less, less), :] = value
    first += len(planes) * less
    total = jnp.zeros((rows, side), F32)
    for index, value in enumerate(lent_planes(block(fine, 1, rows))):
        base = 2 * margin * index
        value = pltpu.roll(value.astype(F32), margin + base, 1)
        total = jnp.where((lane >= base) & (lane < base + 2 * margin), value, total)
    out[pl.ds(first, rows), :] = total.astype(BF16)


def borrow(g, lent, limits, fine, coarse):
    rows, less = lent_rows(g)
    side, margin = g.side, g.margin(1)

    def put(level, number, k, size, values):
        here = pl.ds(0, size)
        ids = lax.broadcasted_iota(jnp.int32, (size, side), 0)
        level.right[0, k, here, :] = values[0]
        level.right[1, k, here, :] = values[1]
        level.fric[k, here, :] = values[2]
        level.visc[k, pl.ds(PAD, size), :] = jnp.where(
            ids < limits[number][k], values[3] + values[4], 0.0
        )

    def planes(first, size):
        return [lent[pl.ds(first + index * size, size), :].astype(F32) for index in range(5)]

    put(fine, 1, 0, rows, planes(0, rows))
    put(coarse, 0, 0, less, planes(5 * rows, less))
    packed = lent[pl.ds(5 * (rows + less), rows), :].astype(F32)
    values = [pltpu.roll(packed, side - margin - 2 * margin * index, 1) for index in range(5)]
    put(fine, 1, 1, rows, values)


def fill_kernel(
    g, rows_ref, force, visc, fric, swap, edge_own, edge_other, levels, lent
):
    level_here = lax.axis_index("level")
    patch = lax.axis_index("patch")
    raw = (force, visc, fric)
    got = (swap, edge_own, edge_other)
    odd = level_here % 2 == 1
    top = g.levels - 1

    def filled(wanted, covered):
        for level in wanted:
            clear_pads(levels[level].visc, [(k,) for k in range(g.blocks(level))])
        for west_type in (True, False):

            @pl.when(odd if west_type else jnp.logical_not(odd))
            def _():
                for level in wanted:
                    near = near_counts(g, rows_ref, level, patch, odd)
                    limits = lane_limits(g, level, near, g.side)
                    fill_level(
                        g, level, west_type, levels[level], limits, covered.get(level), raw, got
                    )

    pl.when(level_here >= top - 1)(lambda: filled((top, top - 1), {}))

    @pl.when(level_here < top - 1)
    def _():
        near = near_counts(g, rows_ref, 2, patch, odd)
        filled((1, 0), {1: lane_limits(g, 1, near, g.half_side)})
        lend(g, levels[1], levels[0], lent)


def down_kernel(g, rows_ref, filled, sums, kept, edges, scratch):
    level_here = lax.axis_index("level")
    patch = lax.axis_index("patch")
    side = g.side
    top = g.levels - 1
    odd = level_here % 2 == 1
    levels = [merged(merged(a, b), c) for a, b, c in zip(scratch, kept, filled)]

    def limits_of(level):
        return lane_limits(g, level, near_counts(g, rows_ref, level, patch, odd), side)

    @pl.when(level_here >= top - 1)
    def _():
        near = near_counts(g, rows_ref, top, patch, odd)
        covered = lane_limits(g, top - 1, near, g.half_side)
        given = filled[top - 1].right
        for comp in range(2):
            for k in range(g.blocks(top - 1)):
                rest = pl.ds(g.half_side, g.rows(top - 1) - g.half_side)
                levels[top - 1].right[comp, k, rest, :] = given[comp, k, rest, :]

        def set_right(comp, k, row, chunk, value):
            here = pl.ds(row, chunk)
            ids = row + lax.broadcasted_iota(jnp.int32, (chunk, side), 0)
            levels[top - 1].right[comp, k, here, :] = jnp.where(
                ids < covered[k], value, given[comp, k, here, :]
            )

        def keep(comp, k, row, chunk, value):
            (sums if k == 0 else edges)[comp, pl.ds(row, chunk), :] = value

        for level in (top, top - 1):
            d = levels[level]
            clear_level(g, level, d)
            smooth_weights(g, level, d, limits_of(level), g.rows(level), True)
            residual_step(g, level, d, 0, g.rows(level))
            restrict_into(g, level, d, 0, g.rows(level), set_right if level == top else keep)
        sums[2] = joined_edges(g, edges[0], edges[1])

    @pl.when(level_here < top - 1)
    def _():
        for level in (1, 0):
            smooth_weights(g, level, levels[level], limits_of(level), g.rows(level), False)


def bottom_levels(g, rows_ref, patch, odd, start, stop, fine, coarse, new_sums, store_fine):
    side = g.side
    count, chunk = g.blocks(1), g.chunk(1, stop - start)
    clear_level(g, 1, fine)
    if new_sums is not None:
        reach = g.rows(2) // 2
        for comp in range(2):
            for k in range(count):
                here = pl.ds(0, reach)
                fine.right[comp, k, here, :] = fine.right[comp, k, here, :] + new_sums(comp, k)

    def body(row):
        here = pl.ds(start + row, chunk)
        for comp in range(2):
            for k in range(count):
                fine.cells[comp, k, pl.ds(PAD + start + row, chunk), :] = (
                    fine.weight[comp, k, here, :] * fine.right[comp, k, here, :]
                )

    over_rows(stop - start, chunk, body)
    residual_step(g, 1, fine, start, stop)
    near = near_counts(g, rows_ref, 1, patch, odd)
    covered = lane_limits(g, 0, near, g.half_side)

    def smooth_coarse(comp, k, row, size, value):
        here = pl.ds(row, size)
        ids = row + lax.broadcasted_iota(jnp.int32, (size, side), 0)
        value = jnp.where(ids < covered[0], value, coarse.right[comp, 0, here, :])
        value = coarse.weight[comp, 0, here, :] * value
        coarse.cells[comp, 0, here, :] = value

    restrict_into(g, 1, fine, start, stop, smooth_coarse)

    def load(comp, k, row, size):
        return coarse.cells[comp, 0, pl.ds(row, size), :]

    prolong_from(g, 1, fine, lane_limits(g, 1, near, side), start, stop, load)
    corrected_step(g, 1, fine, start, stop, store_fine)


def up_kernel(
    g, rows_ref, sums, lent, filled, kept, mine, theirs, edges, scratch, low, low_fine, low_coarse, finer, coarser
):
    level_here = lax.axis_index("level")
    patch = lax.axis_index("patch")
    side = g.side
    top = g.levels - 1
    odd = level_here % 2 == 1
    levels = [merged(merged(a, b), c) for a, b, c in zip(scratch, kept, filled)]

    def limits_of(level):
        return lane_limits(g, level, near_counts(g, rows_ref, level, patch, odd), side)

    def hand_out():
        def write(first, second):
            for k in range(g.half_slots):
                for comp in range(2):
                    first[k, comp] = finer[k, comp]
                    second[k, comp] = coarser[k, comp]

        pl.when(odd)(lambda: write(mine, theirs))
        pl.when(jnp.logical_not(odd))(lambda: write(theirs, mine))

    @pl.when(level_here >= top - 1)
    def _():
        rows, less = lent_rows(g)
        limits = {level: limits_of(level) for level in (0, 1)}
        clear_pads(low_fine.visc, [(k,) for k in range(g.blocks(1))])
        clear_pads(low_coarse.visc, [(k,) for k in range(g.blocks(0))])
        borrow(g, lent, limits, low_fine, low_coarse)
        smooth_weights(g, 1, low_fine, limits[1], rows, False)
        smooth_weights(g, 0, low_coarse, limits[0], less, False)

        def store_fine(comp, k, row, chunk, value):
            low[comp, k, pl.ds(row, chunk), :] = value

        bottom_levels(
            g, rows_ref, patch, odd, 0, rows, low_fine, low_coarse,
            level_sums(g, sums, low_fine.weight), store_fine,
        )

        def load_low(comp, k, row, chunk):
            return low[comp, k, pl.ds(row, chunk), :]

        def load_held(comp, k, row, chunk):
            return edges[comp, k, pl.ds(row, chunk), :]

        def store_in(level, out, hold):
            own = g.own(level)

            def store(comp, k, row, chunk, value):
                if hold:
                    edges[comp, k, pl.ds(row, chunk), :] = value
                if k < own:
                    group, place = row // side, row % side
                    out[group * own + k, comp, pl.ds(pl.multiple_of(place, 8), chunk), :] = value

            return store

        for level, load, out in ((top - 1, load_low, coarser), (top, load_held, finer)):
            d = levels[level]
            clear_level(g, level, d)
            rows = g.rows(level)
            prolong_from(g, level, d, limits_of(level), 0, rows, load)
            corrected_step(g, level, d, 0, rows, store_in(level, out, level < top))
        hand_out()

    @pl.when(level_here < top - 1)
    def _():
        rows = g.rows(1)
        first = g.rows(2) // 2
        fine, coarse = levels[1], levels[0]

        def store_fine(comp, k, row, chunk, value):
            if k == 0:
                group, place = row // side, row % side
                finer[group, comp, pl.ds(pl.multiple_of(place, 8), chunk), :] = value

        bottom_levels(g, rows_ref, patch, odd, first, rows, fine, coarse, None, store_fine)
        lane = lane_ids(side)
        for comp in range(2):
            for k in range(g.half_slots):
                parts = []
                for group in (k, k + g.half_slots):
                    here = pl.ds(group * side, side)
                    if group * side < rows // 2:
                        parts.append(coarse.cells[comp, 0, here, :])
                    else:
                        parts.append(
                            coarse.weight[comp, 0, here, :] * coarse.right[comp, 0, here, :]
                        )
                coarser[k, comp] = jnp.where(
                    lane < g.half_side, parts[0], pltpu.roll(parts[1], g.half_side, 1)
                )
        hand_out()


def level_sums(g, sums, weight):
    reach = g.rows(2) // 2

    def value(comp, k):
        found = sums[comp] if k == 0 else sums[2]
        if k and comp:
            found = pltpu.roll(found, g.half_side, 1)
        return jnp.where(weight[comp, k, pl.ds(0, reach), :] > 0.0, found, 0.0)

    return value


def low_kernel(
    g, rows_ref, sums, filled, kept, mine_in, theirs_in, mine, theirs, scratch, low_coarse, own_rows
):
    level_here = lax.axis_index("level")
    patch = lax.axis_index("patch")
    side = g.side
    top = g.levels - 1
    odd = level_here % 2 == 1
    for k in range(g.half_slots):
        for comp in range(2):
            mine[k, comp] = mine_in[k, comp]
            theirs[k, comp] = theirs_in[k, comp]

    @pl.when(level_here < top - 1)
    def _():
        rows, _ = lent_rows(g)
        done = kept_rows(g)
        fine = merged(Level(filled[1].visc, kept[1].weight), scratch)
        coarse = merged(Level(None, kept[0].weight, filled[0].right), low_coarse)
        for comp in range(2):
            for k in range(g.blocks(1)):
                fine.right[comp, k] = filled[1].right[comp, k, pl.ds(0, rows), :]

        def store_fine(comp, k, row, chunk, value):
            if k == 0:
                own_rows[comp, pl.ds(row, chunk), :] = value

        bottom_levels(
            g, rows_ref, patch, odd, 0, rows, fine, coarse,
            level_sums(g, sums, fine.weight), store_fine,
        )
        lane = lane_ids(side)
        size = rows // 2
        ids = lax.broadcasted_iota(jnp.int32, (size, side), 0)
        ours = (ids < done // 2) & (lane < g.half_side)

        def write(first, second):
            for comp in range(2):
                first[0, comp] = own_rows[comp, pl.ds(0, side), :]
                first[1, comp, pl.ds(0, done - side), :] = own_rows[
                    comp, pl.ds(side, done - side), :
                ]
                here = pl.ds(0, size)
                second[0, comp, here, :] = jnp.where(
                    ours, coarse.cells[comp, 0, here, :], second[0, comp, here, :]
                )

        pl.when(odd)(lambda: write(mine, theirs))
        pl.when(jnp.logical_not(odd))(lambda: write(theirs, mine))


def join_kernel(g, mine, given, speed, fric, adjoint, gradient):
    level_here = lax.axis_index("level")
    lane = lane_ids(g.side)

    def put(slot, parts):
        for comp in range(2):
            adjoint[slot, comp] = parts[comp]
        total = speed[slot, 0].astype(F32) * parts[0] + speed[slot, 1].astype(F32) * parts[1]
        gradient[slot] = (-(fric[slot].astype(F32) * total)).astype(BF16)

    def join_level(level):
        if level == 0:
            for k in range(g.half_slots):
                low = []
                high = []
                for comp in range(2):
                    west, east = given[k, comp], mine[k, comp]
                    low.append(
                        jnp.where(lane < g.half_side, west, pltpu.roll(east, g.half_side, 1))
                    )
                    high.append(
                        jnp.where(lane < g.half_side, pltpu.roll(west, g.half_side, 1), east)
                    )
                put(k, low)
                put(k + g.half_slots, high)
            return
        own = g.own(level)
        west_half, east_half = (mine, given) if level % 2 == 1 else (given, mine)
        for r in range(g.patch_rows(level)):
            for k in range(2 * own):
                source = west_half if k < own else east_half
                put(
                    r * g.columns(level) + k,
                    [source[r * own + k % own, comp] for comp in range(2)],
                )

    for level in range(g.levels):
        pl.when(level_here == level)(lambda level=level: join_level(level))


def run_kernel(body, ins, outs, scratch, grant=VMEM_BYTES):
    in_trees = [jax.tree.flatten(tree) for tree, _ in ins]
    out_trees = [jax.tree.flatten(tree) for tree, _ in outs]
    scratch_trees = [jax.tree.flatten(tree) for tree in scratch]
    sizes = [len(leaves) for leaves, _ in in_trees + out_trees + scratch_trees]
    shapes = [tree for _, tree in in_trees + out_trees + scratch_trees]

    def kernel(*refs):
        given = []
        first = 0
        for size, shape in zip(sizes, shapes):
            given.append(jax.tree.unflatten(shape, refs[first : first + size]))
            first += size
        body(*given)

    def specs(groups, trees):
        return [
            pl.BlockSpec(memory_space=space)
            for (_, space), (leaves, _) in zip(groups, trees)
            for _ in leaves
        ]

    results = pl.pallas_call(
        kernel,
        out_shape=[leaf for leaves, _ in out_trees for leaf in leaves],
        in_specs=specs(ins, in_trees),
        out_specs=specs(outs, out_trees),
        scratch_shapes=[leaf for leaves, _ in scratch_trees for leaf in leaves],
        compiler_params=pltpu.CompilerParams(vmem_limit_bytes=grant),
    )(*[leaf for leaves, _ in in_trees for leaf in leaves])
    answer = []
    first = 0
    for leaves, shape in out_trees:
        answer.append(jax.tree.unflatten(shape, results[first : first + len(leaves)]))
        first += len(leaves)
    return answer


def moved(value, g, step):
    pairs = []
    for patch in range(g.patches):
        for level in range(g.levels):
            to_patch, to_level = step(patch, level)
            if 0 <= to_patch < g.patches and 0 <= to_level < g.levels:
                pairs.append((patch * g.levels + level, to_patch * g.levels + to_level))
    return lax.ppermute(value, ("patch", "level"), pairs)


def per_device(forcing, velocity, viscosity, friction, patch_rows):
    g = Layout(
        forcing.shape[1], forcing.shape[-1], lax.axis_size("level"), lax.axis_size("patch")
    )
    side = g.side
    top = g.levels - 1
    force, speed, visc, fric = forcing[0], velocity[0], viscosity[0], friction[0]
    make = jax.ShapeDtypeStruct
    vmem = pltpu.VMEM
    block = make((side, side), F32)
    half = make((g.half_slots, 2, side, side), F32)
    three = make((3, side, side), F32)

    def array(level, rows, kind, comps, pad):
        return level_array(g, g.blocks(level), rows, kind, comps, pad)

    swap, edge_own, edge_other = run_kernel(
        lambda *refs: pack_kernel(g, *refs),
        [(force, HBM), (visc, HBM), (fric, HBM)],
        [(make((4 * g.half_slots + 1, side, side), F32), VM), (block, VM), (block, VM)],
        [
            pltpu.SemaphoreType.DMA((4,)),
            vmem(force.shape, force.dtype),
            vmem(visc.shape, visc.dtype),
            vmem(fric.shape, fric.dtype),
        ],
        FIRST_BYTES,
    )
    swap = moved(swap, g, lambda p, l: (p, l ^ 1))
    edge_own = moved(edge_own, g, lambda p, l: (p + (1 if l % 2 else -1), l))
    edge_other = moved(edge_other, g, lambda p, l: (p + (-1 if l % 2 else 1), l ^ 1))

    fields = [
        Level(
            array(level, g.rows(level), make, False, True),
            None,
            right=array(level, g.rows(level), make, True, False),
            fric=array(level, g.rows(level), make, False, False),
        )
        for level in range(g.levels)
    ]
    rows, less = lent_rows(g)
    filled, lent = run_kernel(
        lambda *refs: fill_kernel(g, *refs),
        [
            (patch_rows, SM),
            (force, VM),
            (visc, VM),
            (fric, VM),
            (swap, VM),
            (edge_own, VM),
            (edge_other, VM),
        ],
        [(fields, VM), (make((5 * (rows + less) + rows, side), BF16), VM)],
        [],
    )
    lent = moved(lent, g, lambda p, l: (p, l + 2))

    def kept_of(level):
        two = array(level, g.rows(level), make, True, False)
        return Level(None, two, held=two if level >= top - 1 else None)

    def down_scratch(level):
        if level < top - 1:
            return Level(None, None)
        both = array(level, g.rows(level), vmem, True, False)
        more = dict(right=both) if level < top else {}
        return Level(None, None, left=both, **more, **step_arrays(g, level, g.rows(level)))

    sums, kept = run_kernel(
        lambda *refs: down_kernel(g, *refs),
        [(patch_rows, SM), (filled, VM)],
        [(three, VM), ([kept_of(level) for level in range(g.levels)], VM)],
        [vmem((2, side, side), F32), [down_scratch(level) for level in range(g.levels)]],
    )
    sums_there = moved(sums, g, lambda p, l: (p, l - 2))

    def up_scratch(level):
        if level == 0:
            return Level(None, None, cells=vmem((2, 1, g.rows(1) // 2, side), F32))
        both = array(level, g.rows(level), vmem, True, False)
        more = dict(held=both, left=both) if level == 1 else {}
        return Level(None, None, **more, **step_arrays(g, level, g.rows(level)))

    low_both = array(1, rows, vmem, True, False)
    low_steps = dict(held=low_both, left=low_both, right=low_both, **step_arrays(g, 1, rows))
    mine, theirs = run_kernel(
        lambda *refs: up_kernel(g, *refs),
        [(patch_rows, SM), (sums, VM), (lent, VM), (filled, VM), (kept, VM)],
        [(half, VM), (half, VM)],
        [
            array(top - 1, g.rows(top - 1), vmem, True, False),
            [up_scratch(level) for level in range(g.levels)],
            low_both,
            Level(
                array(1, rows, vmem, False, True),
                low_both,
                fric=array(1, rows, vmem, False, False),
                **low_steps,
            ),
            Level(
                array(0, less, vmem, False, True),
                array(0, less, vmem, True, False),
                right=array(0, less, vmem, True, False),
                fric=array(0, less, vmem, False, False),
                cells=array(0, less, vmem, True, False),
            ),
            vmem(half.shape, F32),
            vmem(half.shape, F32),
        ],
    )
    mine, theirs = run_kernel(
        lambda *refs: low_kernel(g, *refs),
        [
            (patch_rows, SM),
            (sums_there, VM),
            (filled[:2], VM),
            (kept[:2], VM),
            (mine, VM),
            (theirs, VM),
        ],
        [(half, VM), (half, VM)],
        [
            Level(None, None, **low_steps),
            Level(None, None, cells=array(0, less, vmem, True, False)),
            vmem((2, rows, side), F32),
        ],
    )
    given = moved(theirs, g, lambda p, l: (p, l ^ 1))
    adjoint, gradient = run_kernel(
        lambda *refs: join_kernel(g, *refs),
        [(mine, VM), (given, VM), (speed, VM), (fric, VM)],
        [
            (make((g.slots, 2, side, side), F32), VM),
            (make((g.slots, side, side), BF16), VM),
        ],
        [],
    )
    return (adjoint[None], gradient[None])


def solution(mesh):
    fields = P("level", "patch")
    return jax.shard_map(
        per_device,
        mesh=mesh,
        in_specs=(fields, fields, fields, fields, P()),
        out_specs=(fields, fields),
        check_vma=False,
    )
```

```python
from typing import Any, NamedTuple

import jax
import jax.numpy as jnp
from jax import lax
from jax.experimental import pallas as pl
from jax.experimental.pallas import tpu as pltpu
from jax.sharding import PartitionSpec as P

relaxation = 0.5
PAD = 8
LOW, HIGH, EDGES = 0, 1, 2
VM, SM = pltpu.VMEM, pltpu.SMEM
F32 = jnp.float32
BF16 = jnp.bfloat16
VMEM_BYTES = 30 * 2**20


class Layout:
    def __init__(self, slots, side, levels, patches):
        self.slots = slots
        self.side = side
        self.levels = levels
        self.patches = patches
        self.half_slots = slots // 2
        self.half_side = side // 2
        self.span = 2 * slots

    def columns(self, level):
        return 1 << level

    def patch_rows(self, level):
        return self.slots >> level

    def rows(self, level):
        return self.patch_rows(level) * self.side

    def margin(self, level):
        return 2 << level

    def own(self, level):
        return max(1, (1 << level) // 2)

    def blocks(self, level):
        return self.own(level) + (1 if level > 0 else 0)

    def chunk(self, level, rows):
        size = 8 * max(1, 28 // self.blocks(level))
        while rows % size or (rows % self.side == 0 and self.side % size):
            size -= 8
        return size


def lane_ids(side):
    return lax.broadcasted_iota(jnp.int32, (1, side), 1)


def near_counts(g, rows_ref, level, patch, odd):
    own = rows_ref[level, patch]
    east = jnp.where(
        patch + 1 < g.patches, rows_ref[level, jnp.minimum(patch + 1, g.patches - 1)], 0
    )
    west = jnp.where(patch > 0, rows_ref[level, jnp.maximum(patch - 1, 0)], 0)
    return own, jnp.where(odd, own, east), jnp.where(odd, west, own)


def lane_limits(g, level, counts, cells):
    own, east, west = (value * cells for value in counts)
    lane = lane_ids(g.side)
    margin = g.margin(level)
    first = 0 if level > 0 else g.half_side
    edges = jnp.where(
        (lane >= first) & (lane < first + margin), east, jnp.where(lane >= g.side - margin, west, 0)
    )
    if level == 0:
        return [jnp.where(lane < g.half_side, own, edges)]
    return [jnp.full((1, g.side), own, jnp.int32)] * g.own(level) + [edges]


def one_side(g, values, east):
    count = len(values)
    turned = [pltpu.roll(value, g.side - 1 if east else 1, 1) for value in values]
    if count == 1:
        return turned
    lane = lax.broadcasted_iota(jnp.int32, values[0].shape, 1)
    last = lane == (g.side - 1 if east else 0)
    step = 1 if east else -1
    return [jnp.where(last, turned[(k + step) % count], turned[k]) for k in range(count)]


def both_sides(g, values):
    return one_side(g, values, True), one_side(g, values, False)


def over_rows(rows, chunk, body):
    def step(index, carry):
        body(pl.multiple_of(index * chunk, chunk))
        return carry

    lax.fori_loop(0, rows // chunk, step, 0)


def clear_pads(ref, lead):
    width = ref.shape[-1]
    last = ref.shape[-2]
    for index in lead:
        ref[index + (slice(0, PAD), slice(None))] = jnp.zeros((PAD, width), F32)
        ref[index + (slice(last - PAD, last), slice(None))] = jnp.zeros((PAD, width), F32)


def off_diagonal_step(g, level, d, start, stop):
    count = g.blocks(level)
    chunk = g.chunk(level, stop - start)

    def body(row):
        row = row + start
        here = pl.ds(row, chunk)
        inner = pl.ds(PAD + row, chunk)

        def line(comp, step):
            rows = pl.ds(PAD + row + step, chunk)
            return [d.cells[comp, k, rows, :] for k in range(count)]

        centre = [line(comp, 0) for comp in range(2)]
        beside = [both_sides(g, centre[comp]) for comp in range(2)]
        products = []
        for k in range(count):
            visc = d.visc[k, inner, :]
            half = 0.5 * visc
            (u, v) = (centre[comp][k] for comp in range(2))
            (u_e, u_w), (v_e, v_w) = ((beside[c][0][k], beside[c][1][k]) for c in range(2))
            u_n, v_n = (d.cells[c, k, pl.ds(PAD + row + 1, chunk), :] for c in range(2))
            u_s, v_s = (d.cells[c, k, pl.ds(PAD + row - 1, chunk), :] for c in range(2))
            one_u, one_v = visc * u, visc * v
            four_u, four_v = 4.0 * one_u, 4.0 * one_v
            cross_u, cross_v = half * (v_e - v_w), visc * (u_e - u_w)
            d.north[0, k, inner, :] = one_u + cross_u
            d.south[0, k, inner, :] = one_u - cross_u
            d.north[1, k, inner, :] = four_v + cross_v
            d.south[1, k, inner, :] = four_v - cross_v
            cross_u, cross_v = visc * (v_n - v_s), half * (u_n - u_s)
            products.append(
                (
                    four_u + cross_u,
                    four_u - cross_u,
                    one_v + cross_v,
                    one_v - cross_v,
                    visc * (4.0 * (u_e + u_w) + (u_n + u_s)),
                    visc * (4.0 * (v_n + v_s) + (v_e + v_w)),
                )
            )
        for comp in range(2):
            east = one_side(g, [item[2 * comp] for item in products], True)
            west = one_side(g, [item[2 * comp + 1] for item in products], False)
            for k in range(count):
                d.part[comp, k, here, :] = products[k][4 + comp] + east[k] + west[k]

    over_rows(stop - start, chunk, body)


def off_diagonal(d, comp, k, row, chunk):
    return (
        d.part[comp, k, pl.ds(row, chunk), :]
        + d.north[comp, k, pl.ds(PAD + row + 1, chunk), :]
        + d.south[comp, k, pl.ds(PAD + row - 1, chunk), :]
    )


def smooth_weights(g, level, d, limits, rows, from_zero):
    count = g.blocks(level)
    chunk = g.chunk(level, rows)

    def body(row):
        here = pl.ds(row, chunk)
        inner = pl.ds(PAD + row, chunk)
        centre = [d.visc[k, inner, :] for k in range(count)]
        east, west = both_sides(g, centre)
        for k in range(count):
            north = d.visc[k, pl.ds(PAD + row + 1, chunk), :]
            south = d.visc[k, pl.ds(PAD + row - 1, chunk), :]
            friction = d.fric[k, here, :]
            twice = 2.0 * centre[k]
            along_row = twice + east[k] + west[k]
            along_col = twice + north + south
            ids = row + lax.broadcasted_iota(jnp.int32, (chunk, g.side), 0)
            live = ids < limits[k]
            diag_u = 4.0 * along_row + along_col + friction
            diag_v = 4.0 * along_col + along_row + friction
            for comp, diag in ((0, diag_u), (1, diag_v)):
                weight = jnp.where(live, relaxation / diag, 0.0)
                d.weight[comp, k, here, :] = weight
                if from_zero:
                    d.cells[comp, k, inner, :] = weight * d.right[comp, k, here, :]

    over_rows(rows, chunk, body)


def residual_step(g, level, d, start, stop):
    count = g.blocks(level)
    chunk = g.chunk(level, stop - start)
    off_diagonal_step(g, level, d, start, stop)

    def body(row):
        row = row + start
        here = pl.ds(row, chunk)
        for comp in range(2):
            for k in range(count):
                weight = d.weight[comp, k, here, :]
                left = (1.0 - relaxation) * d.right[comp, k, here, :] + off_diagonal(
                    d, comp, k, row, chunk
                )
                left = jnp.where(weight > 0.0, left, 0.0)
                d.left[comp, k, here, :] = left
                d.held[comp, k, here, :] = (
                    d.cells[comp, k, pl.ds(PAD + row, chunk), :] + weight * left
                )

    over_rows(stop - start, chunk, body)


def corrected_step(g, level, d, start, stop, store):
    count = g.blocks(level)
    chunk = g.chunk(level, stop - start)
    off_diagonal_step(g, level, d, start, stop)

    def body(row):
        row = row + start
        here = pl.ds(row, chunk)
        for comp in range(2):
            for k in range(count):
                value = (
                    d.held[comp, k, here, :]
                    + (1.0 - relaxation) * d.cells[comp, k, pl.ds(PAD + row, chunk), :]
                    + d.weight[comp, k, here, :] * off_diagonal(d, comp, k, row, chunk)
                )
                store(comp, k, row, chunk, value)

    over_rows(stop - start, chunk, body)


def pairings(g, fine):
    if fine == 1:
        return [[(0, LOW), (1, HIGH)]]
    parts = [[(2 * k, LOW), (2 * k + 1, HIGH)] for k in range(g.own(fine) // 2)]
    return parts + [[(g.own(fine), EDGES)]]


def target_lane(g, part, fine_lane):
    halved = jnp.right_shift(fine_lane, 1)
    if part == LOW:
        return halved
    if part == HIGH:
        return g.half_side + halved
    return halved + jnp.where(fine_lane >= g.half_side, g.half_side, 0)


def sum_matrix(g, part):
    fine = lax.broadcasted_iota(jnp.int32, (g.side, g.side), 0)
    coarse = lax.broadcasted_iota(jnp.int32, (g.side, g.side), 1)
    return jnp.where(target_lane(g, part, fine) == coarse, 1.0, 0.0).astype(BF16)


def copy_matrix(g, part):
    coarse = lax.broadcasted_iota(jnp.int32, (g.side, g.side), 0)
    fine = lax.broadcasted_iota(jnp.int32, (g.side, g.side), 1)
    return jnp.where(target_lane(g, part, fine) == coarse, 1.0, 0.0).astype(BF16)


def split_dot(values, matrix):
    high = values.astype(BF16)
    rest = (values - high.astype(F32)).astype(BF16)
    return jnp.dot(high, matrix, preferred_element_type=F32) + jnp.dot(
        rest, matrix, preferred_element_type=F32
    )


def restrict_into(g, fine, d, start, stop, store):
    rows = stop - start
    chunk = min(rows // 2, g.half_side)
    if (rows // 2) % chunk:
        chunk = rows // 2
    parts = pairings(g, fine)
    matrices = {part: sum_matrix(g, part) for members in parts for _, part in members}

    def body(row):
        row = row + start // 2
        for comp in range(2):
            for coarse, members in enumerate(parts):
                total = None
                for k, part in members:
                    first = d.left[comp, k, pl.ds(2 * row, chunk, stride=2), :]
                    second = d.left[comp, k, pl.ds(2 * row + 1, chunk, stride=2), :]
                    term = split_dot(first + second, matrices[part])
                    total = term if total is None else total + term
                store(comp, coarse, row, chunk, total)

    over_rows(rows // 2, chunk, body)


def prolong_from(g, fine, d, limits, start, stop, load):
    rows = stop - start
    chunk = min(rows // 2, g.half_side)
    if (rows // 2) % chunk:
        chunk = rows // 2
    parts = pairings(g, fine)
    matrices = {part: copy_matrix(g, part) for members in parts for _, part in members}

    def body(row):
        row = row + start // 2
        ids = 2 * (row + lax.broadcasted_iota(jnp.int32, (chunk, g.side), 0))
        for comp in range(2):
            for coarse, members in enumerate(parts):
                value = load(comp, coarse, row, chunk)
                for k, part in members:
                    spread = jnp.where(ids < limits[k], split_dot(value, matrices[part]), 0.0)
                    d.cells[comp, k, pl.ds(PAD + 2 * row, chunk, stride=2), :] = spread
                    d.cells[comp, k, pl.ds(PAD + 2 * row + 1, chunk, stride=2), :] = spread

    over_rows(rows // 2, chunk, body)


def joined_edges(g, edge_u, edge_v):
    lane = lane_ids(g.side)
    quarter = g.side // 4
    middle = (lane >= quarter) & (lane < g.side - quarter)
    return jnp.where(middle, pltpu.roll(edge_v, g.half_side, 1), edge_u)


def plane(raw, q, slot):
    force, visc, fric = raw
    if q < 2:
        return force[slot, q].astype(F32)
    return (fric if q == 2 else visc)[slot].astype(F32)


def edge_lane(g, level, q, r):
    return (0 if level % 2 else g.half_side) + q * g.span + r * g.margin(level)


def edge_kernel(g, own, other, edge):
    level_here = lax.axis_index("level")
    side = g.side

    def pack(here):
        lane = lane_ids(side)
        total = jnp.zeros((side, side), F32)
        for level in (here | 1, here & ~1):
            raw = own if level == here else other
            margin = g.margin(level)
            column, start = (0, 0) if here % 2 else (g.columns(level) - 1, side - margin)
            for r in range(g.patch_rows(level)):
                for q in range(4):
                    base = edge_lane(g, level, q, r)
                    value = plane(raw, q, r * g.columns(level) + column)
                    if (base - start) % side:
                        value = pltpu.roll(value, (base - start) % side, 1)
                    total = jnp.where((lane >= base) & (lane < base + margin), value, total)
        edge[...] = total

    for here in range(g.levels):
        pl.when(level_here == here)(lambda here=here: pack(here))


def fill_level(g, level, west_type, d, limits, covered, raw, edge, groups):
    side = g.side
    margin = g.margin(level)
    own = g.own(level)
    columns = g.columns(level)
    lane = lane_ids(side)

    def outer(q, r, place):
        shift = (place - edge_lane(g, level, q, r)) % side
        return pltpu.roll(edge[...], shift, 1) if shift else edge[...]

    def store(q, k, r, value):
        here = pl.ds(r * side, side)
        if q < 2:
            if covered is not None:
                ids = r * side + lax.broadcasted_iota(jnp.int32, (side, side), 0)
                value = jnp.where(ids < covered[k], 0.0, value)
            d.right[q, k, here, :] = value
        elif q == 2:
            d.fric[k, here, :] = value
        else:
            d.visc[k, pl.ds(PAD + r * side, side), :] = jnp.where(
                limits[k] > r * side, 0.5 * value, 0.0
            )

    clear_pads(d.visc, [(k,) for k in range(g.blocks(level))])
    for r in range(groups):
        for q in range(4):
            if level == 0 and west_type:
                west = outer(q, r, side - margin)
                store(q, 0, r, jnp.where(lane >= side - margin, west, plane(raw, q, r)))
            elif level == 0:
                value = pltpu.roll(plane(raw, q, r), g.half_side, 1)
                here = (lane >= g.half_side) & (lane < g.half_side + margin)
                store(q, 0, r, jnp.where(here, outer(q, r, g.half_side), value))
            else:
                for k in range(own):
                    store(q, k, r, plane(raw, q, r * columns + k + (0 if west_type else own)))
                if west_type:
                    east = plane(raw, q, r * columns + own)
                    west = outer(q, r, side - margin)
                else:
                    east = outer(q, r, 0)
                    west = plane(raw, q, r * columns + own - 1)
                store(q, own, r, jnp.where(lane < g.half_side, east, west))


class Level(NamedTuple):
    visc: Any
    weight: Any
    right: Any = None
    held: Any = None
    fric: Any = None
    cells: Any = None
    part: Any = None
    north: Any = None
    south: Any = None
    left: Any = None


def level_array(g, count, rows, make, comps, pad):
    shape = (count, rows + (2 * PAD if pad else 0), g.side)
    return make((2, *shape) if comps else shape, F32)


def step_arrays(g, level, rows):
    count = g.blocks(level)
    padded = level_array(g, count, rows, pltpu.VMEM, True, True)
    return dict(
        cells=padded,
        part=level_array(g, count, rows, pltpu.VMEM, True, False),
        north=padded,
        south=padded,
    )


def clear_level(g, level, d):
    blocks = range(g.blocks(level))
    both = [(c, k) for c in range(2) for k in blocks]
    for ref in (d.cells, d.north, d.south):
        clear_pads(ref, both)


def merged(first, second):
    return Level(*[b if a is None else a for a, b in zip(first, second)])


class Copies:
    def __init__(self, sems, first=0):
        self.sems = sems
        self.used = first
        self.open = []

    def start(self, source, target):
        copy = pltpu.make_async_copy(source, target, self.sems.at[self.used])
        self.used += 1
        copy.start()
        self.open.append(copy)

    def finish(self):
        for copy in self.open:
            copy.wait()
        self.open = []


def low_rows(g):
    return g.rows(2) // 2 + 2 * PAD


def kept_rows(g):
    return g.rows(2) // 2 + PAD


def lent_rows(g):
    return low_rows(g), -(-low_rows(g) // 2 // 16) * 16


def lent_planes(level):
    visc = level[3]
    high = visc.astype(BF16)
    return [value.astype(BF16) for value in level[:3]] + [
        high,
        (visc - high.astype(F32)).astype(BF16),
    ]


def lend(g, fine, coarse, out):
    rows, less = lent_rows(g)
    side, margin = g.side, g.margin(1)
    lane = lane_ids(side)

    def block(level, k, size):
        here = pl.ds(0, size)
        return (
            level.right[0, k, here, :],
            level.right[1, k, here, :],
            level.fric[k, here, :],
            level.visc[k, pl.ds(PAD, size), :],
        )

    planes = lent_planes(block(fine, 0, rows))
    for index, value in enumerate(planes):
        out[pl.ds(index * rows, rows), :] = value
    first = len(planes) * rows
    for index, value in enumerate(lent_planes(block(coarse, 0, less))):
        out[pl.ds(first + index * less, less), :] = value
    first += len(planes) * less
    total = jnp.zeros((rows, side), F32)
    for index, value in enumerate(lent_planes(block(fine, 1, rows))):
        base = 2 * margin * index
        value = pltpu.roll(value.astype(F32), margin + base, 1)
        total = jnp.where((lane >= base) & (lane < base + 2 * margin), value, total)
    out[pl.ds(first, rows), :] = total.astype(BF16)


def borrow(g, lent, limits, fine, coarse):
    rows, less = lent_rows(g)
    side, margin = g.side, g.margin(1)

    def put(level, number, k, size, values):
        here = pl.ds(0, size)
        ids = lax.broadcasted_iota(jnp.int32, (size, side), 0)
        level.right[0, k, here, :] = values[0]
        level.right[1, k, here, :] = values[1]
        level.fric[k, here, :] = values[2]
        level.visc[k, pl.ds(PAD, size), :] = jnp.where(
            ids < limits[number][k], values[3] + values[4], 0.0
        )

    def planes(first, size):
        return [lent[pl.ds(first + index * size, size), :].astype(F32) for index in range(5)]

    put(fine, 1, 0, rows, planes(0, rows))
    put(coarse, 0, 0, less, planes(5 * rows, less))
    packed = lent[pl.ds(5 * (rows + less), rows), :].astype(F32)
    values = [pltpu.roll(packed, side - margin - 2 * margin * index, 1) for index in range(5)]
    put(fine, 1, 1, rows, values)


def fill_pair(g, rows_ref, own, other, edge, levels, wanted, groups):
    level_here = lax.axis_index("level")
    patch = lax.axis_index("patch")
    odd = level_here % 2 == 1
    for west_type in (True, False):

        @pl.when(odd if west_type else jnp.logical_not(odd))
        def _():
            for level in wanted:
                near = near_counts(g, rows_ref, level, patch, odd)
                limits = lane_limits(g, level, near, g.side)
                covered = None
                if level == 1:
                    finer = near_counts(g, rows_ref, 2, patch, odd)
                    covered = lane_limits(g, 1, finer, g.half_side)
                home = (level % 2 == 1) == west_type
                raw = own if home else other
                fill_level(
                    g, level, west_type, levels[level], limits, covered, raw, edge, groups(level)
                )


def fill_kernel(g, rows_ref, own, other, edge, filled, lent, low):
    level_here = lax.axis_index("level")
    top = g.levels - 1

    @pl.when(level_here >= top - 1)
    def _():
        levels = dict(zip((top - 1, top), filled))
        fill_pair(g, rows_ref, own, other, edge, levels, (top, top - 1), g.patch_rows)

    @pl.when(level_here < top - 1)
    def _():
        fill_pair(g, rows_ref, own, other, edge, low, (1, 0), lambda level: low_groups(g, level))
        lend(g, low[1], low[0], lent)


def low_groups(g, level):
    return -(-lent_rows(g)[1 - level] // g.side)


def down_kernel(g, rows_ref, own, other, edge, upper, sums, kept, lower, edges, scratch):
    level_here = lax.axis_index("level")
    patch = lax.axis_index("patch")
    side = g.side
    top = g.levels - 1
    odd = level_here % 2 == 1
    filled = [*lower, *upper]
    levels = [merged(merged(a, b), c) for a, b, c in zip(scratch, kept, filled)]

    def limits_of(level):
        return lane_limits(g, level, near_counts(g, rows_ref, level, patch, odd), side)

    @pl.when(level_here >= top - 1)
    def _():
        near = near_counts(g, rows_ref, top, patch, odd)
        covered = lane_limits(g, top - 1, near, g.half_side)
        given = filled[top - 1].right
        for comp in range(2):
            for k in range(g.blocks(top - 1)):
                rest = pl.ds(g.half_side, g.rows(top - 1) - g.half_side)
                levels[top - 1].right[comp, k, rest, :] = given[comp, k, rest, :]

        def set_right(comp, k, row, chunk, value):
            here = pl.ds(row, chunk)
            ids = row + lax.broadcasted_iota(jnp.int32, (chunk, side), 0)
            levels[top - 1].right[comp, k, here, :] = jnp.where(
                ids < covered[k], value, given[comp, k, here, :]
            )

        def keep(comp, k, row, chunk, value):
            (sums if k == 0 else edges)[comp, pl.ds(row, chunk), :] = value

        for level in (top, top - 1):
            d = levels[level]
            clear_level(g, level, d)
            smooth_weights(g, level, d, limits_of(level), g.rows(level), True)
            residual_step(g, level, d, 0, g.rows(level))
            restrict_into(g, level, d, 0, g.rows(level), set_right if level == top else keep)
        sums[2] = joined_edges(g, edges[0], edges[1])

    @pl.when(level_here < top - 1)
    def _():
        fill_pair(g, rows_ref, own, other, edge, levels, (1, 0), g.patch_rows)
        for level in (1, 0):
            smooth_weights(g, level, levels[level], limits_of(level), g.rows(level), False)


def bottom_levels(g, rows_ref, patch, odd, start, stop, fine, coarse, new_sums, store_fine):
    side = g.side
    count, chunk = g.blocks(1), g.chunk(1, stop - start)
    clear_level(g, 1, fine)
    if new_sums is not None:
        reach = g.rows(2) // 2
        for comp in range(2):
            for k in range(count):
                here = pl.ds(0, reach)
                fine.right[comp, k, here, :] = fine.right[comp, k, here, :] + new_sums(comp, k)

    def body(row):
        here = pl.ds(start + row, chunk)
        for comp in range(2):
            for k in range(count):
                fine.cells[comp, k, pl.ds(PAD + start + row, chunk), :] = (
                    fine.weight[comp, k, here, :] * fine.right[comp, k, here, :]
                )

    over_rows(stop - start, chunk, body)
    residual_step(g, 1, fine, start, stop)
    near = near_counts(g, rows_ref, 1, patch, odd)
    covered = lane_limits(g, 0, near, g.half_side)

    def smooth_coarse(comp, k, row, size, value):
        here = pl.ds(row, size)
        ids = row + lax.broadcasted_iota(jnp.int32, (size, side), 0)
        value = jnp.where(ids < covered[0], value, coarse.right[comp, 0, here, :])
        value = coarse.weight[comp, 0, here, :] * value
        coarse.cells[comp, 0, here, :] = value

    restrict_into(g, 1, fine, start, stop, smooth_coarse)

    def load(comp, k, row, size):
        return coarse.cells[comp, 0, pl.ds(row, size), :]

    prolong_from(g, 1, fine, lane_limits(g, 1, near, side), start, stop, load)
    corrected_step(g, 1, fine, start, stop, store_fine)


def up_kernel(
    g, rows_ref, sums, lent, filled, kept, mine, theirs, edges, scratch, low, low_fine, low_coarse, finer, coarser
):
    level_here = lax.axis_index("level")
    patch = lax.axis_index("patch")
    side = g.side
    top = g.levels - 1
    odd = level_here % 2 == 1
    levels = [merged(merged(a, b), c) for a, b, c in zip(scratch, kept, filled)]

    def limits_of(level):
        return lane_limits(g, level, near_counts(g, rows_ref, level, patch, odd), side)

    def hand_out():
        def write(first, second):
            for k in range(g.half_slots):
                for comp in range(2):
                    first[k, comp] = finer[k, comp]
                    second[k, comp] = coarser[k, comp]

        pl.when(odd)(lambda: write(mine, theirs))
        pl.when(jnp.logical_not(odd))(lambda: write(theirs, mine))

    @pl.when(level_here >= top - 1)
    def _():
        rows, less = lent_rows(g)
        limits = {level: limits_of(level) for level in (0, 1)}
        clear_pads(low_fine.visc, [(k,) for k in range(g.blocks(1))])
        clear_pads(low_coarse.visc, [(k,) for k in range(g.blocks(0))])
        borrow(g, lent, limits, low_fine, low_coarse)
        smooth_weights(g, 1, low_fine, limits[1], rows, False)
        smooth_weights(g, 0, low_coarse, limits[0], less, False)

        def store_fine(comp, k, row, chunk, value):
            low[comp, k, pl.ds(row, chunk), :] = value

        bottom_levels(
            g, rows_ref, patch, odd, 0, rows, low_fine, low_coarse,
            level_sums(g, sums, low_fine.weight), store_fine,
        )

        def load_low(comp, k, row, chunk):
            return low[comp, k, pl.ds(row, chunk), :]

        def load_held(comp, k, row, chunk):
            return edges[comp, k, pl.ds(row, chunk), :]

        def store_in(level, out, hold):
            own = g.own(level)

            def store(comp, k, row, chunk, value):
                if hold:
                    edges[comp, k, pl.ds(row, chunk), :] = value
                if k < own:
                    group, place = row // side, row % side
                    out[group * own + k, comp, pl.ds(pl.multiple_of(place, 8), chunk), :] = value

            return store

        for level, load, out in ((top - 1, load_low, coarser), (top, load_held, finer)):
            d = levels[level]
            clear_level(g, level, d)
            rows = g.rows(level)
            prolong_from(g, level, d, limits_of(level), 0, rows, load)
            corrected_step(g, level, d, 0, rows, store_in(level, out, level < top))
        hand_out()

    @pl.when(level_here < top - 1)
    def _():
        rows = g.rows(1)
        first = g.rows(2) // 2
        fine, coarse = levels[1], levels[0]

        def store_fine(comp, k, row, chunk, value):
            if k == 0:
                group, place = row // side, row % side
                finer[group, comp, pl.ds(pl.multiple_of(place, 8), chunk), :] = value

        bottom_levels(g, rows_ref, patch, odd, first, rows, fine, coarse, None, store_fine)
        lane = lane_ids(side)
        for comp in range(2):
            for k in range(g.half_slots):
                parts = []
                for group in (k, k + g.half_slots):
                    here = pl.ds(group * side, side)
                    if group * side < rows // 2:
                        parts.append(coarse.cells[comp, 0, here, :])
                    else:
                        parts.append(
                            coarse.weight[comp, 0, here, :] * coarse.right[comp, 0, here, :]
                        )
                coarser[k, comp] = jnp.where(
                    lane < g.half_side, parts[0], pltpu.roll(parts[1], g.half_side, 1)
                )
        hand_out()


def level_sums(g, sums, weight):
    reach = g.rows(2) // 2

    def value(comp, k):
        found = sums[comp] if k == 0 else sums[2]
        if k and comp:
            found = pltpu.roll(found, g.half_side, 1)
        return jnp.where(weight[comp, k, pl.ds(0, reach), :] > 0.0, found, 0.0)

    return value


def low_kernel(
    g, rows_ref, sums, filled, kept, mine_in, theirs_in, mine, theirs, scratch, low_coarse, own_rows
):
    level_here = lax.axis_index("level")
    patch = lax.axis_index("patch")
    side = g.side
    top = g.levels - 1
    odd = level_here % 2 == 1
    for k in range(g.half_slots):
        for comp in range(2):
            mine[k, comp] = mine_in[k, comp]
            theirs[k, comp] = theirs_in[k, comp]

    @pl.when(level_here < top - 1)
    def _():
        rows, _ = lent_rows(g)
        done = kept_rows(g)
        fine = merged(Level(filled[1].visc, kept[1].weight), scratch)
        coarse = merged(Level(None, kept[0].weight, filled[0].right), low_coarse)
        for comp in range(2):
            for k in range(g.blocks(1)):
                fine.right[comp, k] = filled[1].right[comp, k, pl.ds(0, rows), :]

        def store_fine(comp, k, row, chunk, value):
            if k == 0:
                own_rows[comp, pl.ds(row, chunk), :] = value

        bottom_levels(
            g, rows_ref, patch, odd, 0, rows, fine, coarse,
            level_sums(g, sums, fine.weight), store_fine,
        )
        lane = lane_ids(side)
        size = rows // 2
        ids = lax.broadcasted_iota(jnp.int32, (size, side), 0)
        ours = (ids < done // 2) & (lane < g.half_side)

        def write(first, second):
            for comp in range(2):
                first[0, comp] = own_rows[comp, pl.ds(0, side), :]
                first[1, comp, pl.ds(0, done - side), :] = own_rows[
                    comp, pl.ds(side, done - side), :
                ]
                here = pl.ds(0, size)
                second[0, comp, here, :] = jnp.where(
                    ours, coarse.cells[comp, 0, here, :], second[0, comp, here, :]
                )

        pl.when(odd)(lambda: write(mine, theirs))
        pl.when(jnp.logical_not(odd))(lambda: write(theirs, mine))


def join_kernel(g, mine, given, speed, fric, adjoint, gradient):
    level_here = lax.axis_index("level")
    lane = lane_ids(g.side)

    def put(slot, parts):
        for comp in range(2):
            adjoint[slot, comp] = parts[comp]
        total = speed[slot, 0].astype(F32) * parts[0] + speed[slot, 1].astype(F32) * parts[1]
        gradient[slot] = (-(fric[slot].astype(F32) * total)).astype(BF16)

    def join_level(level):
        if level == 0:
            for k in range(g.half_slots):
                low = []
                high = []
                for comp in range(2):
                    west, east = given[k, comp], mine[k, comp]
                    low.append(
                        jnp.where(lane < g.half_side, west, pltpu.roll(east, g.half_side, 1))
                    )
                    high.append(
                        jnp.where(lane < g.half_side, pltpu.roll(west, g.half_side, 1), east)
                    )
                put(k, low)
                put(k + g.half_slots, high)
            return
        own = g.own(level)
        west_half, east_half = (mine, given) if level % 2 == 1 else (given, mine)
        for r in range(g.patch_rows(level)):
            for k in range(2 * own):
                source = west_half if k < own else east_half
                put(
                    r * g.columns(level) + k,
                    [source[r * own + k % own, comp] for comp in range(2)],
                )

    for level in range(g.levels):
        pl.when(level_here == level)(lambda level=level: join_level(level))


def run_kernel(body, ins, outs, scratch, grant=VMEM_BYTES):
    in_trees = [jax.tree.flatten(tree) for tree, _ in ins]
    out_trees = [jax.tree.flatten(tree) for tree, _ in outs]
    scratch_trees = [jax.tree.flatten(tree) for tree in scratch]
    sizes = [len(leaves) for leaves, _ in in_trees + out_trees + scratch_trees]
    shapes = [tree for _, tree in in_trees + out_trees + scratch_trees]

    def kernel(*refs):
        given = []
        first = 0
        for size, shape in zip(sizes, shapes):
            given.append(jax.tree.unflatten(shape, refs[first : first + size]))
            first += size
        body(*given)

    def specs(groups, trees):
        return [
            pl.BlockSpec(memory_space=space)
            for (_, space), (leaves, _) in zip(groups, trees)
            for _ in leaves
        ]

    results = pl.pallas_call(
        kernel,
        out_shape=[leaf for leaves, _ in out_trees for leaf in leaves],
        in_specs=specs(ins, in_trees),
        out_specs=specs(outs, out_trees),
        scratch_shapes=[leaf for leaves, _ in scratch_trees for leaf in leaves],
        compiler_params=pltpu.CompilerParams(vmem_limit_bytes=grant),
    )(*[leaf for leaves, _ in in_trees for leaf in leaves])
    answer = []
    first = 0
    for leaves, shape in out_trees:
        answer.append(jax.tree.unflatten(shape, results[first : first + len(leaves)]))
        first += len(leaves)
    return answer


def moved(value, g, step):
    pairs = []
    for patch in range(g.patches):
        for level in range(g.levels):
            to_patch, to_level = step(patch, level)
            if 0 <= to_patch < g.patches and 0 <= to_level < g.levels:
                pairs.append((patch * g.levels + level, to_patch * g.levels + to_level))
    return lax.ppermute(value, ("patch", "level"), pairs)


def per_device(forcing, velocity, viscosity, friction, patch_rows):
    g = Layout(
        forcing.shape[1], forcing.shape[-1], lax.axis_size("level"), lax.axis_size("patch")
    )
    side = g.side
    top = g.levels - 1
    force, speed, visc, fric = forcing[0], velocity[0], viscosity[0], friction[0]
    make = jax.ShapeDtypeStruct
    vmem = pltpu.VMEM
    block = make((side, side), F32)
    half = make((g.half_slots, 2, side, side), F32)
    three = make((3, side, side), F32)

    def array(level, rows, kind, comps, pad):
        return level_array(g, g.blocks(level), rows, kind, comps, pad)

    own = (force, visc, fric)
    other = tuple(moved(value, g, lambda p, l: (p, l ^ 1)) for value in own)
    (edge,) = run_kernel(
        lambda *refs: edge_kernel(g, *refs), [(own, VM), (other, VM)], [(block, VM)], []
    )
    edge = moved(edge, g, lambda p, l: (p + (-1 if l % 2 else 1), l ^ 1))

    fields = [
        Level(
            array(level, g.rows(level), make, False, True),
            None,
            right=array(level, g.rows(level), make, True, False),
            fric=array(level, g.rows(level), make, False, False),
        )
        for level in range(g.levels)
    ]
    rows, less = lent_rows(g)
    given = [(patch_rows, SM), (own, VM), (other, VM), (edge, VM)]

    def low_scratch(level):
        size = low_groups(g, level) * side
        return Level(
            array(level, size, vmem, False, True),
            None,
            right=array(level, size, vmem, True, False),
            fric=array(level, size, vmem, False, False),
        )

    upper, lent = run_kernel(
        lambda *refs: fill_kernel(g, *refs),
        given,
        [(fields[top - 1 :], VM), (make((5 * (rows + less) + rows, side), BF16), VM)],
        [[low_scratch(level) for level in (0, 1)]],
    )
    lent = moved(lent, g, lambda p, l: (p, l + 2))

    def kept_of(level):
        two = array(level, g.rows(level), make, True, False)
        return Level(None, two, held=two if level >= top - 1 else None)

    def down_scratch(level):
        if level < top - 1:
            return Level(None, None)
        both = array(level, g.rows(level), vmem, True, False)
        more = dict(right=both) if level < top else {}
        return Level(None, None, left=both, **more, **step_arrays(g, level, g.rows(level)))

    sums, kept, lower = run_kernel(
        lambda *refs: down_kernel(g, *refs),
        [*given, (upper, VM)],
        [
            (three, VM),
            ([kept_of(level) for level in range(g.levels)], VM),
            (fields[: top - 1], VM),
        ],
        [vmem((2, side, side), F32), [down_scratch(level) for level in range(g.levels)]],
    )
    filled = [*lower, *upper]
    sums_there = moved(sums, g, lambda p, l: (p, l - 2))

    def up_scratch(level):
        if level == 0:
            return Level(None, None, cells=vmem((2, 1, g.rows(1) // 2, side), F32))
        both = array(level, g.rows(level), vmem, True, False)
        more = dict(held=both, left=both) if level == 1 else {}
        return Level(None, None, **more, **step_arrays(g, level, g.rows(level)))

    low_both = array(1, rows, vmem, True, False)
    low_steps = dict(held=low_both, left=low_both, right=low_both, **step_arrays(g, 1, rows))
    mine, theirs = run_kernel(
        lambda *refs: up_kernel(g, *refs),
        [(patch_rows, SM), (sums, VM), (lent, VM), (filled, VM), (kept, VM)],
        [(half, VM), (half, VM)],
        [
            array(top - 1, g.rows(top - 1), vmem, True, False),
            [up_scratch(level) for level in range(g.levels)],
            low_both,
            Level(
                array(1, rows, vmem, False, True),
                low_both,
                fric=array(1, rows, vmem, False, False),
                **low_steps,
            ),
            Level(
                array(0, less, vmem, False, True),
                array(0, less, vmem, True, False),
                right=array(0, less, vmem, True, False),
                fric=array(0, less, vmem, False, False),
                cells=array(0, less, vmem, True, False),
            ),
            vmem(half.shape, F32),
            vmem(half.shape, F32),
        ],
    )
    mine, theirs = run_kernel(
        lambda *refs: low_kernel(g, *refs),
        [
            (patch_rows, SM),
            (sums_there, VM),
            (filled[:2], VM),
            (kept[:2], VM),
            (mine, VM),
            (theirs, VM),
        ],
        [(half, VM), (half, VM)],
        [
            Level(None, None, **low_steps),
            Level(None, None, cells=array(0, less, vmem, True, False)),
            vmem((2, rows, side), F32),
        ],
    )
    received = moved(theirs, g, lambda p, l: (p, l ^ 1))
    adjoint, gradient = run_kernel(
        lambda *refs: join_kernel(g, *refs),
        [(mine, VM), (received, VM), (speed, VM), (fric, VM)],
        [
            (make((g.slots, 2, side, side), F32), VM),
            (make((g.slots, side, side), BF16), VM),
        ],
        [],
    )
    return (adjoint[None], gradient[None])


def solution(mesh):
    fields = P("level", "patch")
    return jax.shard_map(
        per_device,
        mesh=mesh,
        in_specs=(fields, fields, fields, fields, P()),
        out_specs=(fields, fields),
        check_vma=False,
    )
```

```python
from typing import Any, NamedTuple

import jax
import jax.numpy as jnp
from jax import lax
from jax.experimental import pallas as pl
from jax.experimental.pallas import tpu as pltpu
from jax.sharding import PartitionSpec as P

relaxation = 0.5
PAD = 8
LOW, HIGH, EDGES = 0, 1, 2
VM, SM = pltpu.VMEM, pltpu.SMEM
F32 = jnp.float32
BF16 = jnp.bfloat16
VMEM_BYTES = 30 * 2**20
FIRST_BYTES = 60 * 2**20


class Layout:
    def __init__(self, slots, side, levels, patches):
        self.slots = slots
        self.side = side
        self.levels = levels
        self.patches = patches
        self.half_slots = slots // 2
        self.half_side = side // 2
        self.span = 2 * slots

    def columns(self, level):
        return 1 << level

    def patch_rows(self, level):
        return self.slots >> level

    def rows(self, level):
        return self.patch_rows(level) * self.side

    def margin(self, level):
        return 2 << level

    def own(self, level):
        return max(1, (1 << level) // 2)

    def blocks(self, level):
        return self.own(level) + (1 if level > 0 else 0)

    def chunk(self, level, rows):
        size = 8 * max(1, 28 // self.blocks(level))
        while rows % size or (rows % self.side == 0 and self.side % size):
            size -= 8
        return size


def lane_ids(side):
    return lax.broadcasted_iota(jnp.int32, (1, side), 1)


def near_counts(g, rows_ref, level, patch, odd):
    own = rows_ref[level, patch]
    east = jnp.where(
        patch + 1 < g.patches, rows_ref[level, jnp.minimum(patch + 1, g.patches - 1)], 0
    )
    west = jnp.where(patch > 0, rows_ref[level, jnp.maximum(patch - 1, 0)], 0)
    return own, jnp.where(odd, own, east), jnp.where(odd, west, own)


def lane_limits(g, level, counts, cells):
    own, east, west = (value * cells for value in counts)
    lane = lane_ids(g.side)
    margin = g.margin(level)
    first = 0 if level > 0 else g.half_side
    edges = jnp.where(
        (lane >= first) & (lane < first + margin), east, jnp.where(lane >= g.side - margin, west, 0)
    )
    if level == 0:
        return [jnp.where(lane < g.half_side, own, edges)]
    return [jnp.full((1, g.side), own, jnp.int32)] * g.own(level) + [edges]


def one_side(g, values, east):
    count = len(values)
    turned = [pltpu.roll(value, g.side - 1 if east else 1, 1) for value in values]
    if count == 1:
        return turned
    lane = lax.broadcasted_iota(jnp.int32, values[0].shape, 1)
    last = lane == (g.side - 1 if east else 0)
    step = 1 if east else -1
    return [jnp.where(last, turned[(k + step) % count], turned[k]) for k in range(count)]


def both_sides(g, values):
    return one_side(g, values, True), one_side(g, values, False)


def over_rows(rows, chunk, body):
    def step(index, carry):
        body(pl.multiple_of(index * chunk, chunk))
        return carry

    lax.fori_loop(0, rows // chunk, step, 0)


def clear_pads(ref, lead):
    width = ref.shape[-1]
    last = ref.shape[-2]
    for index in lead:
        ref[index + (slice(0, PAD), slice(None))] = jnp.zeros((PAD, width), F32)
        ref[index + (slice(last - PAD, last), slice(None))] = jnp.zeros((PAD, width), F32)


def off_diagonal_rows(g, d, row, size, count):
    here = pl.ds(row, size)
    inner = pl.ds(PAD + row, size)
    centre = [[d.cells[comp, k, inner, :] for k in range(count)] for comp in range(2)]
    beside = [both_sides(g, centre[comp]) for comp in range(2)]
    products = []
    for k in range(count):
        visc = d.visc[k, inner, :]
        half = 0.5 * visc
        (u, v) = (centre[comp][k] for comp in range(2))
        (u_e, u_w), (v_e, v_w) = ((beside[c][0][k], beside[c][1][k]) for c in range(2))
        u_n, v_n = (d.cells[c, k, pl.ds(PAD + row + 1, size), :] for c in range(2))
        u_s, v_s = (d.cells[c, k, pl.ds(PAD + row - 1, size), :] for c in range(2))
        one_u, one_v = visc * u, visc * v
        four_u, four_v = 4.0 * one_u, 4.0 * one_v
        cross_u, cross_v = half * (v_e - v_w), visc * (u_e - u_w)
        d.north[0, k, inner, :] = one_u + cross_u
        d.south[0, k, inner, :] = one_u - cross_u
        d.north[1, k, inner, :] = four_v + cross_v
        d.south[1, k, inner, :] = four_v - cross_v
        cross_u, cross_v = visc * (v_n - v_s), half * (u_n - u_s)
        products.append(
            (
                four_u + cross_u,
                four_u - cross_u,
                one_v + cross_v,
                one_v - cross_v,
                visc * (4.0 * (u_e + u_w) + (u_n + u_s)),
                visc * (4.0 * (v_n + v_s) + (v_e + v_w)),
            )
        )
    for comp in range(2):
        east = one_side(g, [item[2 * comp] for item in products], True)
        west = one_side(g, [item[2 * comp + 1] for item in products], False)
        for k in range(count):
            d.part[comp, k, here, :] = products[k][4 + comp] + east[k] + west[k]


def off_diagonal_step(g, level, d, start, stop):
    count = g.blocks(level)
    chunk = g.chunk(level, stop - start)

    def body(row):
        for step in range(0, chunk, 8):
            off_diagonal_rows(g, d, start + row + step, 8, count)

    over_rows(stop - start, chunk, body)


def off_diagonal(d, comp, k, row, chunk):
    return (
        d.part[comp, k, pl.ds(row, chunk), :]
        + d.north[comp, k, pl.ds(PAD + row + 1, chunk), :]
        + d.south[comp, k, pl.ds(PAD + row - 1, chunk), :]
    )


def smooth_weights(g, level, d, limits, rows, from_zero):
    count = g.blocks(level)
    chunk = g.chunk(level, rows)

    def some_rows(row):
        here = pl.ds(row, 8)
        inner = pl.ds(PAD + row, 8)
        centre = [d.visc[k, inner, :] for k in range(count)]
        east, west = both_sides(g, centre)
        for k in range(count):
            north = d.visc[k, pl.ds(PAD + row + 1, 8), :]
            south = d.visc[k, pl.ds(PAD + row - 1, 8), :]
            friction = d.fric[k, here, :]
            twice = 2.0 * centre[k]
            along_row = twice + east[k] + west[k]
            along_col = twice + north + south
            live = jnp.broadcast_to(limits[k], (8, g.side)) > row
            diag_u = 4.0 * along_row + along_col + friction
            diag_v = 4.0 * along_col + along_row + friction
            for comp, diag in ((0, diag_u), (1, diag_v)):
                guess = pl.reciprocal(diag, approx=True)
                weight = guess * (2.0 * relaxation - relaxation * diag * guess)
                weight = jnp.where(live, weight, 0.0)
                d.weight[comp, k, here, :] = weight
                if from_zero:
                    d.cells[comp, k, inner, :] = weight * d.right[comp, k, here, :]

    def body(row):
        for step in range(0, chunk, 8):
            some_rows(row + step)

    over_rows(rows, chunk, body)


def residual_step(g, level, d, start, stop):
    count = g.blocks(level)
    chunk = g.chunk(level, stop - start)
    off_diagonal_step(g, level, d, start, stop)

    def body(row):
        row = row + start
        here = pl.ds(row, chunk)
        for comp in range(2):
            for k in range(count):
                weight = d.weight[comp, k, here, :]
                left = (1.0 - relaxation) * d.right[comp, k, here, :] + off_diagonal(
                    d, comp, k, row, chunk
                )
                left = jnp.where(weight > 0.0, left, 0.0)
                d.left[comp, k, here, :] = left
                d.held[comp, k, here, :] = (
                    d.cells[comp, k, pl.ds(PAD + row, chunk), :] + weight * left
                )

    over_rows(stop - start, chunk, body)


def corrected_step(g, level, d, start, stop, store):
    count = g.blocks(level)
    chunk = g.chunk(level, stop - start)
    off_diagonal_step(g, level, d, start, stop)

    def body(row):
        row = row + start
        here = pl.ds(row, chunk)
        for comp in range(2):
            for k in range(count):
                value = (
                    d.held[comp, k, here, :]
                    + (1.0 - relaxation) * d.cells[comp, k, pl.ds(PAD + row, chunk), :]
                    + d.weight[comp, k, here, :] * off_diagonal(d, comp, k, row, chunk)
                )
                store(comp, k, row, chunk, value)

    over_rows(stop - start, chunk, body)


def pairings(g, fine):
    if fine == 1:
        return [[(0, LOW), (1, HIGH)]]
    parts = [[(2 * k, LOW), (2 * k + 1, HIGH)] for k in range(g.own(fine) // 2)]
    return parts + [[(g.own(fine), EDGES)]]


def target_lane(g, part, fine_lane):
    halved = jnp.right_shift(fine_lane, 1)
    if part == LOW:
        return halved
    if part == HIGH:
        return g.half_side + halved
    return halved + jnp.where(fine_lane >= g.half_side, g.half_side, 0)


def sum_matrix(g, part):
    fine = lax.broadcasted_iota(jnp.int32, (g.side, g.side), 0)
    coarse = lax.broadcasted_iota(jnp.int32, (g.side, g.side), 1)
    return jnp.where(target_lane(g, part, fine) == coarse, 1.0, 0.0).astype(BF16)


def copy_matrix(g, part):
    coarse = lax.broadcasted_iota(jnp.int32, (g.side, g.side), 0)
    fine = lax.broadcasted_iota(jnp.int32, (g.side, g.side), 1)
    return jnp.where(target_lane(g, part, fine) == coarse, 1.0, 0.0).astype(BF16)


def split_dot(values, matrix):
    high = values.astype(BF16)
    rest = (values - high.astype(F32)).astype(BF16)
    return jnp.dot(high, matrix, preferred_element_type=F32) + jnp.dot(
        rest, matrix, preferred_element_type=F32
    )


def restrict_into(g, fine, d, start, stop, store):
    rows = stop - start
    chunk = min(rows // 2, g.half_side)
    if (rows // 2) % chunk:
        chunk = rows // 2
    parts = pairings(g, fine)
    matrices = {part: sum_matrix(g, part) for members in parts for _, part in members}

    def body(row):
        row = row + start // 2
        for comp in range(2):
            for coarse, members in enumerate(parts):
                total = None
                for k, part in members:
                    first = d.left[comp, k, pl.ds(2 * row, chunk, stride=2), :]
                    second = d.left[comp, k, pl.ds(2 * row + 1, chunk, stride=2), :]
                    term = split_dot(first + second, matrices[part])
                    total = term if total is None else total + term
                store(comp, coarse, row, chunk, total)

    over_rows(rows // 2, chunk, body)


def prolong_from(g, fine, d, limits, start, stop, load):
    rows = stop - start
    chunk = min(rows // 2, g.half_side)
    if (rows // 2) % chunk:
        chunk = rows // 2
    parts = pairings(g, fine)
    matrices = {part: copy_matrix(g, part) for members in parts for _, part in members}

    def body(row):
        row = row + start // 2
        ids = 2 * (row + lax.broadcasted_iota(jnp.int32, (chunk, g.side), 0))
        for comp in range(2):
            for coarse, members in enumerate(parts):
                value = load(comp, coarse, row, chunk)
                for k, part in members:
                    spread = jnp.where(ids < limits[k], split_dot(value, matrices[part]), 0.0)
                    d.cells[comp, k, pl.ds(PAD + 2 * row, chunk, stride=2), :] = spread
                    d.cells[comp, k, pl.ds(PAD + 2 * row + 1, chunk, stride=2), :] = spread

    over_rows(rows // 2, chunk, body)


def joined_edges(g, edge_u, edge_v):
    lane = lane_ids(g.side)
    quarter = g.side // 4
    middle = (lane >= quarter) & (lane < g.side - quarter)
    return jnp.where(middle, pltpu.roll(edge_v, g.half_side, 1), edge_u)


def plane(raw, q, slot):
    force, visc, fric = raw
    if q < 2:
        return force[slot, q].astype(F32)
    return (fric if q == 2 else visc)[slot].astype(F32)


def edge_lane(g, level, q, r):
    return (0 if level % 2 else g.half_side) + q * g.span + r * g.margin(level)


def packed_edge(g, here, level, patch_of):
    side = g.side
    lane = lane_ids(side)
    margin = g.margin(level)
    start = 0 if here % 2 else side - margin
    total = jnp.zeros((side, side), F32)
    for r in range(g.patch_rows(level)):
        for q in range(4):
            base = edge_lane(g, level, q, r)
            value = patch_of(q, r)
            if (base - start) % side:
                value = pltpu.roll(value, (base - start) % side, 1)
            total = jnp.where((lane >= base) & (lane < base + margin), value, total)
    return total


def edge_column(g, here, level):
    return 0 if here % 2 else g.columns(level) - 1


def first_edge_kernel(g, own, edge, sems, held):
    level_here = lax.axis_index("level")

    def pack(level):
        copies = Copies(sems)
        rows = g.patch_rows(level)
        if g.columns(level) == 1:
            for source, target in zip(own, held):
                copies.start(source, target)
        else:
            for r in range(rows):
                slot = r * g.columns(level) + edge_column(g, level, level)
                for source, target in zip(own, held):
                    copies.start(source.at[slot], target.at[r])
        copies.finish()
        edge[...] = packed_edge(g, level, level, lambda q, r: plane(held, q, r))

    for level in range(g.levels):
        pl.when(level_here == level)(lambda level=level: pack(level))


def edge_kernel(g, first, other, edge):
    level_here = lax.axis_index("level")

    def pack(here):
        level = here ^ 1
        column = edge_column(g, here, level)

        def patch_of(q, r):
            return plane(other, q, r * g.columns(level) + column)

        edge[...] = first[...] + packed_edge(g, here, level, patch_of)

    for here in range(g.levels):
        pl.when(level_here == here)(lambda here=here: pack(here))


def fill_level(g, level, west_type, d, limits, covered, raw, edge, groups):
    side = g.side
    margin = g.margin(level)
    own = g.own(level)
    columns = g.columns(level)
    lane = lane_ids(side)

    def outer(q, r, place):
        shift = (place - edge_lane(g, level, q, r)) % side
        return pltpu.roll(edge[...], shift, 1) if shift else edge[...]

    def store(q, k, r, value):
        here = pl.ds(r * side, side)
        if q < 2:
            if covered is not None:
                ids = r * side + lax.broadcasted_iota(jnp.int32, (side, side), 0)
                value = jnp.where(ids < covered[k], 0.0, value)
            d.right[q, k, here, :] = value
        elif q == 2:
            d.fric[k, here, :] = value
        else:
            d.visc[k, pl.ds(PAD + r * side, side), :] = jnp.where(
                limits[k] > r * side, 0.5 * value, 0.0
            )

    clear_pads(d.visc, [(k,) for k in range(g.blocks(level))])
    for r in range(groups):
        for q in range(4):
            if level == 0 and west_type:
                west = outer(q, r, side - margin)
                store(q, 0, r, jnp.where(lane >= side - margin, west, plane(raw, q, r)))
            elif level == 0:
                value = pltpu.roll(plane(raw, q, r), g.half_side, 1)
                here = (lane >= g.half_side) & (lane < g.half_side + margin)
                store(q, 0, r, jnp.where(here, outer(q, r, g.half_side), value))
            else:
                for k in range(own):
                    store(q, k, r, plane(raw, q, r * columns + k + (0 if west_type else own)))
                if west_type:
                    east = plane(raw, q, r * columns + own)
                    west = outer(q, r, side - margin)
                else:
                    east = outer(q, r, 0)
                    west = plane(raw, q, r * columns + own - 1)
                store(q, own, r, jnp.where(lane < g.half_side, east, west))


class Level(NamedTuple):
    visc: Any
    weight: Any
    right: Any = None
    held: Any = None
    fric: Any = None
    cells: Any = None
    part: Any = None
    north: Any = None
    south: Any = None
    left: Any = None


def level_array(g, count, rows, make, comps, pad):
    shape = (count, rows + (2 * PAD if pad else 0), g.side)
    return make((2, *shape) if comps else shape, F32)


def step_arrays(g, level, rows):
    count = g.blocks(level)
    padded = level_array(g, count, rows, pltpu.VMEM, True, True)
    return dict(
        cells=padded,
        part=level_array(g, count, rows, pltpu.VMEM, True, False),
        north=padded,
        south=padded,
    )


def clear_level(g, level, d):
    blocks = range(g.blocks(level))
    both = [(c, k) for c in range(2) for k in blocks]
    for ref in (d.cells, d.north, d.south):
        clear_pads(ref, both)


def merged(first, second):
    return Level(*[b if a is None else a for a, b in zip(first, second)])


class Copies:
    def __init__(self, sems, first=0):
        self.sems = sems
        self.used = first
        self.open = []

    def start(self, source, target):
        copy = pltpu.make_async_copy(source, target, self.sems.at[self.used])
        self.used += 1
        copy.start()
        self.open.append(copy)

    def finish(self):
        for copy in self.open:
            copy.wait()
        self.open = []


def low_rows(g):
    return g.rows(2) // 2 + 2 * PAD


def kept_rows(g):
    return g.rows(2) // 2 + PAD


def lent_rows(g):
    return low_rows(g), -(-low_rows(g) // 2 // 16) * 16


def lent_forcing(g):
    return [count * g.half_side for count in range(1, g.patch_rows(2) + 1)]


def lent_size(g):
    rows, less = lent_rows(g)
    return 3 * rows + 2 * 16 * len(lent_forcing(g)) + 5 * less


def pair_of(visc):
    high = visc.astype(BF16)
    return [high, (visc - high.astype(F32)).astype(BF16)]


def margin_shift(g, index):
    margin = g.margin(1)
    base = g.half_side + PAD + 2 * margin * index
    return base, (margin + base) % g.side


def lend(g, fine, coarse, out):
    rows, less = lent_rows(g)
    side = g.side
    lane = lane_ids(side)
    place = [0]

    def put(value):
        size = value.shape[0]
        out[pl.ds(place[0], size), :] = value.astype(BF16)
        place[0] += size

    def block(level, k, size):
        here = pl.ds(0, size)
        return [
            level.right[0, k, here, :],
            level.right[1, k, here, :],
            level.fric[k, here, :],
            *pair_of(level.visc[k, pl.ds(PAD, size), :]),
        ]

    put(fine.fric[0, pl.ds(0, rows), :])
    for value in pair_of(fine.visc[0, pl.ds(PAD, rows), :]):
        put(value)
    for comp in range(2):
        for first in lent_forcing(g):
            put(fine.right[comp, 0, pl.ds(first, 16), :])
    total = jnp.zeros((rows, side), F32)
    for index, value in enumerate(block(fine, 1, rows)):
        base, shift = margin_shift(g, index)
        value = pltpu.roll(value.astype(F32), shift, 1)
        total = jnp.where((lane >= base) & (lane < base + 2 * g.margin(1)), value, total)
    spare = (lane >= g.half_side + PAD) & (lane < side - PAD)
    for index, value in enumerate(block(coarse, 0, less)):
        value = value.astype(F32)
        if index == 2:
            value = jnp.where(spare, total[:less], value)
        if index == 3:
            more = rows - less
            put(jnp.where(spare, total[less:], value[:more]))
            value = value[more:]
        put(value)


def borrow(g, lent, limits, fine, coarse):
    rows, less = lent_rows(g)
    side = g.side
    place = [0]

    def take(size):
        value = lent[pl.ds(place[0], size), :].astype(F32)
        place[0] += size
        return value

    def put_visc(level, number, k, first, value):
        size = value.shape[0]
        ids = first + lax.broadcasted_iota(jnp.int32, (size, side), 0)
        level.visc[k, pl.ds(PAD + first, size), :] = jnp.where(ids < limits[number][k], value, 0.0)

    fine.fric[0, pl.ds(0, rows), :] = take(rows)
    high = take(rows)
    put_visc(fine, 1, 0, 0, high + take(rows))
    for comp in range(2):
        fine.right[comp, 0] = jnp.zeros((rows, side), F32)
        for first in lent_forcing(g):
            fine.right[comp, 0, pl.ds(first, 16), :] = take(16)
    planes = [take(less) for _ in range(5)]
    for comp in range(2):
        coarse.right[comp, 0] = planes[comp]
    coarse.fric[0] = planes[2]
    put_visc(coarse, 0, 0, 0, planes[3] + planes[4])
    for first, packed in ((0, planes[2]), (less, planes[3][: rows - less])):
        size = packed.shape[0]
        here = pl.ds(first, size)
        values = [pltpu.roll(packed, side - margin_shift(g, i)[1], 1) for i in range(5)]
        for comp in range(2):
            fine.right[comp, 1, here, :] = values[comp]
        fine.fric[1, here, :] = values[2]
        put_visc(fine, 1, 1, first, values[3] + values[4])


def fill_pair(g, rows_ref, own, other, edge, levels, wanted, groups):
    level_here = lax.axis_index("level")
    patch = lax.axis_index("patch")
    odd = level_here % 2 == 1
    for west_type in (True, False):

        @pl.when(odd if west_type else jnp.logical_not(odd))
        def _():
            for level in wanted:
                near = near_counts(g, rows_ref, level, patch, odd)
                limits = lane_limits(g, level, near, g.side)
                covered = None
                if level == 1:
                    finer = near_counts(g, rows_ref, 2, patch, odd)
                    covered = lane_limits(g, 1, finer, g.half_side)
                home = (level % 2 == 1) == west_type
                raw = own if home else other
                fill_level(
                    g, level, west_type, levels[level], limits, covered, raw, edge, groups(level)
                )


def fill_kernel(g, rows_ref, own, other, edge, filled, lent, low):
    level_here = lax.axis_index("level")
    top = g.levels - 1

    @pl.when(level_here >= top - 1)
    def _():
        levels = dict(zip((top - 1, top), filled))
        fill_pair(g, rows_ref, own, other, edge, levels, (top, top - 1), g.patch_rows)

    @pl.when(level_here < top - 1)
    def _():
        fill_pair(g, rows_ref, own, other, edge, low, (1, 0), lambda level: low_groups(g, level))
        lend(g, low[1], low[0], lent)


def low_groups(g, level):
    return -(-lent_rows(g)[1 - level] // g.side)


def down_kernel(g, rows_ref, own, other, edge, upper, sums, kept, lower, edges, scratch):
    level_here = lax.axis_index("level")
    patch = lax.axis_index("patch")
    side = g.side
    top = g.levels - 1
    odd = level_here % 2 == 1
    filled = [*lower, *upper]
    levels = [merged(merged(a, b), c) for a, b, c in zip(scratch, kept, filled)]

    def limits_of(level):
        return lane_limits(g, level, near_counts(g, rows_ref, level, patch, odd), side)

    @pl.when(level_here >= top - 1)
    def _():
        near = near_counts(g, rows_ref, top, patch, odd)
        covered = lane_limits(g, top - 1, near, g.half_side)
        given = filled[top - 1].right
        for comp in range(2):
            for k in range(g.blocks(top - 1)):
                rest = pl.ds(g.half_side, g.rows(top - 1) - g.half_side)
                levels[top - 1].right[comp, k, rest, :] = given[comp, k, rest, :]

        def set_right(comp, k, row, chunk, value):
            here = pl.ds(row, chunk)
            ids = row + lax.broadcasted_iota(jnp.int32, (chunk, side), 0)
            levels[top - 1].right[comp, k, here, :] = jnp.where(
                ids < covered[k], value, given[comp, k, here, :]
            )

        def keep(comp, k, row, chunk, value):
            (sums if k == 0 else edges)[comp, pl.ds(row, chunk), :] = value

        for level in (top, top - 1):
            d = levels[level]
            clear_level(g, level, d)
            smooth_weights(g, level, d, limits_of(level), g.rows(level), True)
            residual_step(g, level, d, 0, g.rows(level))
            restrict_into(g, level, d, 0, g.rows(level), set_right if level == top else keep)
        sums[2] = joined_edges(g, edges[0], edges[1])

    @pl.when(level_here < top - 1)
    def _():
        fill_pair(g, rows_ref, own, other, edge, levels, (1, 0), g.patch_rows)
        for level in (1, 0):
            smooth_weights(g, level, levels[level], limits_of(level), g.rows(level), False)


def bottom_levels(g, rows_ref, patch, odd, start, stop, fine, coarse, new_sums, store_fine):
    side = g.side
    count, chunk = g.blocks(1), g.chunk(1, stop - start)
    clear_level(g, 1, fine)
    if new_sums is not None:
        reach = g.rows(2) // 2
        for comp in range(2):
            for k in range(count):
                here = pl.ds(0, reach)
                fine.right[comp, k, here, :] = fine.right[comp, k, here, :] + new_sums(comp, k)

    def body(row):
        here = pl.ds(start + row, chunk)
        for comp in range(2):
            for k in range(count):
                fine.cells[comp, k, pl.ds(PAD + start + row, chunk), :] = (
                    fine.weight[comp, k, here, :] * fine.right[comp, k, here, :]
                )

    over_rows(stop - start, chunk, body)
    residual_step(g, 1, fine, start, stop)
    near = near_counts(g, rows_ref, 1, patch, odd)
    covered = lane_limits(g, 0, near, g.half_side)

    def smooth_coarse(comp, k, row, size, value):
        here = pl.ds(row, size)
        ids = row + lax.broadcasted_iota(jnp.int32, (size, side), 0)
        value = jnp.where(ids < covered[0], value, coarse.right[comp, 0, here, :])
        value = coarse.weight[comp, 0, here, :] * value
        coarse.cells[comp, 0, here, :] = value

    restrict_into(g, 1, fine, start, stop, smooth_coarse)

    def load(comp, k, row, size):
        return coarse.cells[comp, 0, pl.ds(row, size), :]

    prolong_from(g, 1, fine, lane_limits(g, 1, near, side), start, stop, load)
    corrected_step(g, 1, fine, start, stop, store_fine)


def up_kernel(
    g, rows_ref, sums, lent, filled, kept, mine, theirs, edges, scratch, low, low_fine, low_coarse, finer, coarser
):
    level_here = lax.axis_index("level")
    patch = lax.axis_index("patch")
    side = g.side
    top = g.levels - 1
    odd = level_here % 2 == 1
    levels = [merged(merged(a, b), c) for a, b, c in zip(scratch, kept, filled)]

    def limits_of(level):
        return lane_limits(g, level, near_counts(g, rows_ref, level, patch, odd), side)

    def hand_out():
        def write(first, second):
            for k in range(g.half_slots):
                for comp in range(2):
                    first[k, comp] = finer[k, comp]
                    second[k, comp] = coarser[k, comp]

        pl.when(odd)(lambda: write(mine, theirs))
        pl.when(jnp.logical_not(odd))(lambda: write(theirs, mine))

    @pl.when(level_here >= top - 1)
    def _():
        rows, less = lent_rows(g)
        limits = {level: limits_of(level) for level in (0, 1)}
        clear_pads(low_fine.visc, [(k,) for k in range(g.blocks(1))])
        clear_pads(low_coarse.visc, [(k,) for k in range(g.blocks(0))])
        borrow(g, lent, limits, low_fine, low_coarse)
        smooth_weights(g, 1, low_fine, limits[1], rows, False)
        smooth_weights(g, 0, low_coarse, limits[0], less, False)

        def store_fine(comp, k, row, chunk, value):
            low[comp, k, pl.ds(row, chunk), :] = value

        bottom_levels(
            g, rows_ref, patch, odd, 0, rows, low_fine, low_coarse,
            level_sums(g, sums, low_fine.weight), store_fine,
        )

        def load_low(comp, k, row, chunk):
            return low[comp, k, pl.ds(row, chunk), :]

        def load_held(comp, k, row, chunk):
            return edges[comp, k, pl.ds(row, chunk), :]

        def store_in(level, out, hold):
            own = g.own(level)

            def store(comp, k, row, chunk, value):
                if hold:
                    edges[comp, k, pl.ds(row, chunk), :] = value
                if k < own:
                    group, place = row // side, row % side
                    out[group * own + k, comp, pl.ds(pl.multiple_of(place, 8), chunk), :] = value

            return store

        for level, load, out in ((top - 1, load_low, coarser), (top, load_held, finer)):
            d = levels[level]
            clear_level(g, level, d)
            rows = g.rows(level)
            prolong_from(g, level, d, limits_of(level), 0, rows, load)
            corrected_step(g, level, d, 0, rows, store_in(level, out, level < top))
        hand_out()

    @pl.when(level_here < top - 1)
    def _():
        rows = g.rows(1)
        first = g.rows(2) // 2
        fine, coarse = levels[1], levels[0]

        def store_fine(comp, k, row, chunk, value):
            if k == 0:
                group, place = row // side, row % side
                finer[group, comp, pl.ds(pl.multiple_of(place, 8), chunk), :] = value

        bottom_levels(g, rows_ref, patch, odd, first, rows, fine, coarse, None, store_fine)
        lane = lane_ids(side)
        for comp in range(2):
            for k in range(g.half_slots):
                parts = []
                for group in (k, k + g.half_slots):
                    here = pl.ds(group * side, side)
                    if group * side < rows // 2:
                        parts.append(coarse.cells[comp, 0, here, :])
                    else:
                        parts.append(
                            coarse.weight[comp, 0, here, :] * coarse.right[comp, 0, here, :]
                        )
                coarser[k, comp] = jnp.where(
                    lane < g.half_side, parts[0], pltpu.roll(parts[1], g.half_side, 1)
                )
        hand_out()


def level_sums(g, sums, weight):
    reach = g.rows(2) // 2

    def value(comp, k):
        found = sums[comp] if k == 0 else sums[2]
        if k and comp:
            found = pltpu.roll(found, g.half_side, 1)
        return jnp.where(weight[comp, k, pl.ds(0, reach), :] > 0.0, found, 0.0)

    return value


def low_kernel(
    g, rows_ref, sums, filled, kept, mine_in, theirs_in, mine, theirs, scratch, low_coarse, own_rows
):
    level_here = lax.axis_index("level")
    patch = lax.axis_index("patch")
    side = g.side
    top = g.levels - 1
    odd = level_here % 2 == 1
    for k in range(g.half_slots):
        for comp in range(2):
            mine[k, comp] = mine_in[k, comp]
            theirs[k, comp] = theirs_in[k, comp]

    @pl.when(level_here < top - 1)
    def _():
        rows, _ = lent_rows(g)
        done = kept_rows(g)
        fine = merged(Level(filled[1].visc, kept[1].weight), scratch)
        coarse = merged(Level(None, kept[0].weight, filled[0].right), low_coarse)
        for comp in range(2):
            for k in range(g.blocks(1)):
                fine.right[comp, k] = filled[1].right[comp, k, pl.ds(0, rows), :]

        def store_fine(comp, k, row, chunk, value):
            if k == 0:
                own_rows[comp, pl.ds(row, chunk), :] = value

        bottom_levels(
            g, rows_ref, patch, odd, 0, rows, fine, coarse,
            level_sums(g, sums, fine.weight), store_fine,
        )
        lane = lane_ids(side)
        size = rows // 2
        ids = lax.broadcasted_iota(jnp.int32, (size, side), 0)
        ours = (ids < done // 2) & (lane < g.half_side)

        def write(first, second):
            for comp in range(2):
                first[0, comp] = own_rows[comp, pl.ds(0, side), :]
                first[1, comp, pl.ds(0, done - side), :] = own_rows[
                    comp, pl.ds(side, done - side), :
                ]
                here = pl.ds(0, size)
                second[0, comp, here, :] = jnp.where(
                    ours, coarse.cells[comp, 0, here, :], second[0, comp, here, :]
                )

        pl.when(odd)(lambda: write(mine, theirs))
        pl.when(jnp.logical_not(odd))(lambda: write(theirs, mine))


def join_kernel(g, mine, given, speed, fric, adjoint, gradient):
    level_here = lax.axis_index("level")
    lane = lane_ids(g.side)

    def put(slot, parts):
        for comp in range(2):
            adjoint[slot, comp] = parts[comp]
        total = speed[slot, 0].astype(F32) * parts[0] + speed[slot, 1].astype(F32) * parts[1]
        gradient[slot] = (-(fric[slot].astype(F32) * total)).astype(BF16)

    def join_level(level):
        if level == 0:
            for k in range(g.half_slots):
                low = []
                high = []
                for comp in range(2):
                    west, east = given[k, comp], mine[k, comp]
                    low.append(
                        jnp.where(lane < g.half_side, west, pltpu.roll(east, g.half_side, 1))
                    )
                    high.append(
                        jnp.where(lane < g.half_side, pltpu.roll(west, g.half_side, 1), east)
                    )
                put(k, low)
                put(k + g.half_slots, high)
            return
        own = g.own(level)
        west_half, east_half = (mine, given) if level % 2 == 1 else (given, mine)
        for r in range(g.patch_rows(level)):
            for k in range(2 * own):
                source = west_half if k < own else east_half
                put(
                    r * g.columns(level) + k,
                    [source[r * own + k % own, comp] for comp in range(2)],
                )

    for level in range(g.levels):
        pl.when(level_here == level)(lambda level=level: join_level(level))


def run_kernel(body, ins, outs, scratch, grant=VMEM_BYTES):
    in_trees = [jax.tree.flatten(tree) for tree, _ in ins]
    out_trees = [jax.tree.flatten(tree) for tree, _ in outs]
    scratch_trees = [jax.tree.flatten(tree) for tree in scratch]
    sizes = [len(leaves) for leaves, _ in in_trees + out_trees + scratch_trees]
    shapes = [tree for _, tree in in_trees + out_trees + scratch_trees]

    def kernel(*refs):
        given = []
        first = 0
        for size, shape in zip(sizes, shapes):
            given.append(jax.tree.unflatten(shape, refs[first : first + size]))
            first += size
        body(*given)

    def specs(groups, trees):
        return [
            pl.BlockSpec(memory_space=space)
            for (_, space), (leaves, _) in zip(groups, trees)
            for _ in leaves
        ]

    results = pl.pallas_call(
        kernel,
        out_shape=[leaf for leaves, _ in out_trees for leaf in leaves],
        in_specs=specs(ins, in_trees),
        out_specs=specs(outs, out_trees),
        scratch_shapes=[leaf for leaves, _ in scratch_trees for leaf in leaves],
        compiler_params=pltpu.CompilerParams(vmem_limit_bytes=grant),
    )(*[leaf for leaves, _ in in_trees for leaf in leaves])
    answer = []
    first = 0
    for leaves, shape in out_trees:
        answer.append(jax.tree.unflatten(shape, results[first : first + len(leaves)]))
        first += len(leaves)
    return answer


def moved(value, g, step):
    pairs = []
    for patch in range(g.patches):
        for level in range(g.levels):
            to_patch, to_level = step(patch, level)
            if 0 <= to_patch < g.patches and 0 <= to_level < g.levels:
                pairs.append((patch * g.levels + level, to_patch * g.levels + to_level))
    return lax.ppermute(value, ("patch", "level"), pairs)


def per_device(forcing, velocity, viscosity, friction, patch_rows):
    g = Layout(
        forcing.shape[1], forcing.shape[-1], lax.axis_size("level"), lax.axis_size("patch")
    )
    side = g.side
    top = g.levels - 1
    force, speed, visc, fric = forcing[0], velocity[0], viscosity[0], friction[0]
    make = jax.ShapeDtypeStruct
    vmem = pltpu.VMEM
    block = make((side, side), F32)
    half = make((g.half_slots, 2, side, side), F32)
    three = make((3, side, side), F32)

    def array(level, rows, kind, comps, pad):
        return level_array(g, g.blocks(level), rows, kind, comps, pad)

    own = (force, visc, fric)
    other = tuple(moved(value, g, lambda p, l: (p, l ^ 1)) for value in own)
    (edge,) = run_kernel(
        lambda *refs: first_edge_kernel(g, *refs),
        [(own, pltpu.HBM)],
        [(block, VM)],
        [
            pltpu.SemaphoreType.DMA((3 * g.slots,)),
            tuple(vmem(value.shape, value.dtype) for value in own),
        ],
        FIRST_BYTES,
    )
    (edge,) = run_kernel(
        lambda *refs: edge_kernel(g, *refs), [(edge, VM), (other, VM)], [(block, VM)], []
    )
    edge = moved(edge, g, lambda p, l: (p + (-1 if l % 2 else 1), l ^ 1))

    fields = [
        Level(
            array(level, g.rows(level), make, False, True),
            None,
            right=array(level, g.rows(level), make, True, False),
            fric=array(level, g.rows(level), make, False, False),
        )
        for level in range(g.levels)
    ]
    rows, less = lent_rows(g)
    given = [(patch_rows, SM), (own, VM), (other, VM), (edge, VM)]

    def low_scratch(level):
        size = low_groups(g, level) * side
        return Level(
            array(level, size, vmem, False, True),
            None,
            right=array(level, size, vmem, True, False),
            fric=array(level, size, vmem, False, False),
        )

    upper, lent = run_kernel(
        lambda *refs: fill_kernel(g, *refs),
        given,
        [(fields[top - 1 :], VM), (make((lent_size(g), side), BF16), VM)],
        [[low_scratch(level) for level in (0, 1)]],
    )
    lent = moved(lent, g, lambda p, l: (p, l + 2))

    def kept_of(level):
        two = array(level, g.rows(level), make, True, False)
        return Level(None, two, held=two if level >= top - 1 else None)

    def down_scratch(level):
        if level < top - 1:
            return Level(None, None)
        both = array(level, g.rows(level), vmem, True, False)
        more = dict(right=both) if level < top else {}
        return Level(None, None, left=both, **more, **step_arrays(g, level, g.rows(level)))

    sums, kept, lower = run_kernel(
        lambda *refs: down_kernel(g, *refs),
        [*given, (upper, VM)],
        [
            (three, VM),
            ([kept_of(level) for level in range(g.levels)], VM),
            (fields[: top - 1], VM),
        ],
        [vmem((2, side, side), F32), [down_scratch(level) for level in range(g.levels)]],
    )
    filled = [*lower, *upper]
    sums_there = moved(sums, g, lambda p, l: (p, l - 2))

    def up_scratch(level):
        if level == 0:
            return Level(None, None, cells=vmem((2, 1, g.rows(1) // 2, side), F32))
        both = array(level, g.rows(level), vmem, True, False)
        more = dict(held=both, left=both) if level == 1 else {}
        return Level(None, None, **more, **step_arrays(g, level, g.rows(level)))

    low_both = array(1, rows, vmem, True, False)
    low_steps = dict(held=low_both, left=low_both, right=low_both, **step_arrays(g, 1, rows))
    mine, theirs = run_kernel(
        lambda *refs: up_kernel(g, *refs),
        [(patch_rows, SM), (sums, VM), (lent, VM), (filled, VM), (kept, VM)],
        [(half, VM), (half, VM)],
        [
            array(top - 1, g.rows(top - 1), vmem, True, False),
            [up_scratch(level) for level in range(g.levels)],
            low_both,
            Level(
                array(1, rows, vmem, False, True),
                low_both,
                fric=array(1, rows, vmem, False, False),
                **low_steps,
            ),
            Level(
                array(0, less, vmem, False, True),
                array(0, less, vmem, True, False),
                right=array(0, less, vmem, True, False),
                fric=array(0, less, vmem, False, False),
                cells=array(0, less, vmem, True, False),
            ),
            vmem(half.shape, F32),
            vmem(half.shape, F32),
        ],
    )
    mine, theirs = run_kernel(
        lambda *refs: low_kernel(g, *refs),
        [
            (patch_rows, SM),
            (sums_there, VM),
            (filled[:2], VM),
            (kept[:2], VM),
            (mine, VM),
            (theirs, VM),
        ],
        [(half, VM), (half, VM)],
        [
            Level(None, None, **low_steps),
            Level(None, None, cells=array(0, less, vmem, True, False)),
            vmem((2, rows, side), F32),
        ],
    )
    received = moved(theirs, g, lambda p, l: (p, l ^ 1))
    adjoint, gradient = run_kernel(
        lambda *refs: join_kernel(g, *refs),
        [(mine, VM), (received, VM), (speed, VM), (fric, VM)],
        [
            (make((g.slots, 2, side, side), F32), VM),
            (make((g.slots, side, side), BF16), VM),
        ],
        [],
    )
    return (adjoint[None], gradient[None])


def solution(mesh):
    fields = P("level", "patch")
    return jax.shard_map(
        per_device,
        mesh=mesh,
        in_specs=(fields, fields, fields, fields, P()),
        out_specs=(fields, fields),
        check_vma=False,
    )
```

```python
from typing import Any, NamedTuple

import jax
import jax.numpy as jnp
from jax import lax
from jax.experimental import pallas as pl
from jax.experimental.pallas import tpu as pltpu
from jax.sharding import PartitionSpec as P

relaxation = 0.5
PAD = 8
LOW, HIGH, EDGES = 0, 1, 2
VM, SM = pltpu.VMEM, pltpu.SMEM
F32 = jnp.float32
BF16 = jnp.bfloat16
VMEM_BYTES = 30 * 2**20
FIRST_BYTES = 60 * 2**20


class Layout:
    def __init__(self, slots, side, levels, patches):
        self.slots = slots
        self.side = side
        self.levels = levels
        self.patches = patches
        self.half_slots = slots // 2
        self.half_side = side // 2
        self.span = 2 * slots

    def columns(self, level):
        return 1 << level

    def patch_rows(self, level):
        return self.slots >> level

    def rows(self, level):
        return self.patch_rows(level) * self.side

    def margin(self, level):
        return 2 << level

    def own(self, level):
        return max(1, (1 << level) // 2)

    def blocks(self, level):
        return self.own(level) + (1 if level > 0 else 0)

    def chunk(self, level, rows):
        size = 8 * max(1, 56 // self.blocks(level))
        while rows % size or (rows % self.side == 0 and self.side % size):
            size -= 8
        return size


def lane_ids(side):
    return lax.broadcasted_iota(jnp.int32, (1, side), 1)


def near_counts(g, rows_ref, level, patch, odd):
    own = rows_ref[level, patch]
    east = jnp.where(
        patch + 1 < g.patches, rows_ref[level, jnp.minimum(patch + 1, g.patches - 1)], 0
    )
    west = jnp.where(patch > 0, rows_ref[level, jnp.maximum(patch - 1, 0)], 0)
    return own, jnp.where(odd, own, east), jnp.where(odd, west, own)


def lane_limits(g, level, counts, cells):
    own, east, west = (value * cells for value in counts)
    lane = lane_ids(g.side)
    margin = g.margin(level)
    first = 0 if level > 0 else g.half_side
    edges = jnp.where(
        (lane >= first) & (lane < first + margin), east, jnp.where(lane >= g.side - margin, west, 0)
    )
    if level == 0:
        return [jnp.where(lane < g.half_side, own, edges)]
    return [jnp.full((1, g.side), own, jnp.int32)] * g.own(level) + [edges]


def one_side(g, values, east):
    count = len(values)
    turned = [pltpu.roll(value, g.side - 1 if east else 1, 1) for value in values]
    if count == 1:
        return turned
    lane = lax.broadcasted_iota(jnp.int32, values[0].shape, 1)
    last = lane == (g.side - 1 if east else 0)
    step = 1 if east else -1
    return [jnp.where(last, turned[(k + step) % count], turned[k]) for k in range(count)]


def both_sides(g, values):
    return one_side(g, values, True), one_side(g, values, False)


def over_rows(rows, chunk, body):
    def step(index, carry):
        body(pl.multiple_of(index * chunk, chunk))
        return carry

    lax.fori_loop(0, rows // chunk, step, 0)


def clear_pads(ref, lead):
    width = ref.shape[-1]
    last = ref.shape[-2]
    for index in lead:
        ref[index + (slice(0, PAD), slice(None))] = jnp.zeros((PAD, width), F32)
        ref[index + (slice(last - PAD, last), slice(None))] = jnp.zeros((PAD, width), F32)


def off_diagonal_rows(g, d, row, size, count):
    here = pl.ds(row, size)
    inner = pl.ds(PAD + row, size)
    centre = [[d.cells[comp, k, inner, :] for k in range(count)] for comp in range(2)]
    beside = [both_sides(g, centre[comp]) for comp in range(2)]
    products = []
    for k in range(count):
        visc = d.visc[k, inner, :]
        half = 0.5 * visc
        (u, v) = (centre[comp][k] for comp in range(2))
        (u_e, u_w), (v_e, v_w) = ((beside[c][0][k], beside[c][1][k]) for c in range(2))
        u_n, v_n = (d.cells[c, k, pl.ds(PAD + row + 1, size), :] for c in range(2))
        u_s, v_s = (d.cells[c, k, pl.ds(PAD + row - 1, size), :] for c in range(2))
        one_u, one_v = visc * u, visc * v
        four_u, four_v = 4.0 * one_u, 4.0 * one_v
        cross_u, cross_v = half * (v_e - v_w), visc * (u_e - u_w)
        d.north[0, k, inner, :] = one_u + cross_u
        d.south[0, k, inner, :] = one_u - cross_u
        d.north[1, k, inner, :] = four_v + cross_v
        d.south[1, k, inner, :] = four_v - cross_v
        cross_u, cross_v = visc * (v_n - v_s), half * (u_n - u_s)
        products.append(
            (
                four_u + cross_u,
                four_u - cross_u,
                one_v + cross_v,
                one_v - cross_v,
                visc * (4.0 * (u_e + u_w) + (u_n + u_s)),
                visc * (4.0 * (v_n + v_s) + (v_e + v_w)),
            )
        )
    for comp in range(2):
        east = one_side(g, [item[2 * comp] for item in products], True)
        west = one_side(g, [item[2 * comp + 1] for item in products], False)
        for k in range(count):
            d.part[comp, k, here, :] = products[k][4 + comp] + east[k] + west[k]


def off_diagonal_step(g, level, d, start, stop):
    count = g.blocks(level)
    chunk = g.chunk(level, stop - start)

    def body(row):
        for step in range(0, chunk, 8):
            off_diagonal_rows(g, d, start + row + step, 8, count)

    over_rows(stop - start, chunk, body)


def off_diagonal(d, comp, k, row, chunk):
    return (
        d.part[comp, k, pl.ds(row, chunk), :]
        + d.north[comp, k, pl.ds(PAD + row + 1, chunk), :]
        + d.south[comp, k, pl.ds(PAD + row - 1, chunk), :]
    )


def smooth_weights(g, level, d, limits, rows, from_zero):
    count = g.blocks(level)
    chunk = g.chunk(level, rows)

    def some_rows(row):
        here = pl.ds(row, 8)
        inner = pl.ds(PAD + row, 8)
        centre = [d.visc[k, inner, :] for k in range(count)]
        east, west = both_sides(g, centre)
        for k in range(count):
            north = d.visc[k, pl.ds(PAD + row + 1, 8), :]
            south = d.visc[k, pl.ds(PAD + row - 1, 8), :]
            friction = d.fric[k, here, :]
            twice = 2.0 * centre[k]
            along_row = twice + east[k] + west[k]
            along_col = twice + north + south
            live = jnp.broadcast_to(limits[k], (8, g.side)) > row
            diag_u = 4.0 * along_row + along_col + friction
            diag_v = 4.0 * along_col + along_row + friction
            for comp, diag in ((0, diag_u), (1, diag_v)):
                guess = pl.reciprocal(diag, approx=True)
                weight = guess * (2.0 * relaxation - relaxation * diag * guess)
                weight = jnp.where(live, weight, 0.0)
                d.weight[comp, k, here, :] = weight
                if from_zero:
                    d.cells[comp, k, inner, :] = weight * d.right[comp, k, here, :]

    def body(row):
        for step in range(0, chunk, 8):
            some_rows(row + step)

    over_rows(rows, chunk, body)


def residual_step(g, level, d, start, stop):
    count = g.blocks(level)
    chunk = g.chunk(level, stop - start)
    off_diagonal_step(g, level, d, start, stop)

    def body(row):
        row = row + start
        here = pl.ds(row, chunk)
        for comp in range(2):
            for k in range(count):
                weight = d.weight[comp, k, here, :]
                left = (1.0 - relaxation) * d.right[comp, k, here, :] + off_diagonal(
                    d, comp, k, row, chunk
                )
                left = jnp.where(weight > 0.0, left, 0.0)
                d.left[comp, k, here, :] = left
                d.held[comp, k, here, :] = (
                    d.cells[comp, k, pl.ds(PAD + row, chunk), :] + weight * left
                )

    over_rows(stop - start, chunk, body)


def corrected_step(g, level, d, start, stop, store):
    count = g.blocks(level)
    chunk = g.chunk(level, stop - start)
    off_diagonal_step(g, level, d, start, stop)

    def body(row):
        row = row + start
        here = pl.ds(row, chunk)
        for comp in range(2):
            for k in range(count):
                value = (
                    d.held[comp, k, here, :]
                    + (1.0 - relaxation) * d.cells[comp, k, pl.ds(PAD + row, chunk), :]
                    + d.weight[comp, k, here, :] * off_diagonal(d, comp, k, row, chunk)
                )
                store(comp, k, row, chunk, value)

    over_rows(stop - start, chunk, body)


def pairings(g, fine):
    if fine == 1:
        return [[(0, LOW), (1, HIGH)]]
    parts = [[(2 * k, LOW), (2 * k + 1, HIGH)] for k in range(g.own(fine) // 2)]
    return parts + [[(g.own(fine), EDGES)]]


def target_lane(g, part, fine_lane):
    halved = jnp.right_shift(fine_lane, 1)
    if part == LOW:
        return halved
    if part == HIGH:
        return g.half_side + halved
    return halved + jnp.where(fine_lane >= g.half_side, g.half_side, 0)


def sum_matrix(g, part):
    fine = lax.broadcasted_iota(jnp.int32, (g.side, g.side), 0)
    coarse = lax.broadcasted_iota(jnp.int32, (g.side, g.side), 1)
    return jnp.where(target_lane(g, part, fine) == coarse, 1.0, 0.0).astype(BF16)


def copy_matrix(g, part):
    coarse = lax.broadcasted_iota(jnp.int32, (g.side, g.side), 0)
    fine = lax.broadcasted_iota(jnp.int32, (g.side, g.side), 1)
    return jnp.where(target_lane(g, part, fine) == coarse, 1.0, 0.0).astype(BF16)


def split_dot(values, matrix):
    high = values.astype(BF16)
    rest = (values - high.astype(F32)).astype(BF16)
    return jnp.dot(high, matrix, preferred_element_type=F32) + jnp.dot(
        rest, matrix, preferred_element_type=F32
    )


def restrict_into(g, fine, d, start, stop, store):
    rows = stop - start
    chunk = min(rows // 2, g.half_side)
    if (rows // 2) % chunk:
        chunk = rows // 2
    parts = pairings(g, fine)
    matrices = {part: sum_matrix(g, part) for members in parts for _, part in members}

    def body(row):
        row = row + start // 2
        for comp in range(2):
            for coarse, members in enumerate(parts):
                total = None
                for k, part in members:
                    first = d.left[comp, k, pl.ds(2 * row, chunk, stride=2), :]
                    second = d.left[comp, k, pl.ds(2 * row + 1, chunk, stride=2), :]
                    term = split_dot(first + second, matrices[part])
                    total = term if total is None else total + term
                store(comp, coarse, row, chunk, total)

    over_rows(rows // 2, chunk, body)


def prolong_from(g, fine, d, limits, start, stop, load):
    rows = stop - start
    chunk = min(rows // 2, g.half_side)
    if (rows // 2) % chunk:
        chunk = rows // 2
    parts = pairings(g, fine)
    matrices = {part: copy_matrix(g, part) for members in parts for _, part in members}

    def body(row):
        row = row + start // 2
        ids = 2 * (row + lax.broadcasted_iota(jnp.int32, (chunk, g.side), 0))
        for comp in range(2):
            for coarse, members in enumerate(parts):
                value = load(comp, coarse, row, chunk)
                for k, part in members:
                    spread = jnp.where(ids < limits[k], split_dot(value, matrices[part]), 0.0)
                    d.cells[comp, k, pl.ds(PAD + 2 * row, chunk, stride=2), :] = spread
                    d.cells[comp, k, pl.ds(PAD + 2 * row + 1, chunk, stride=2), :] = spread

    over_rows(rows // 2, chunk, body)


def joined_edges(g, edge_u, edge_v):
    lane = lane_ids(g.side)
    quarter = g.side // 4
    middle = (lane >= quarter) & (lane < g.side - quarter)
    return jnp.where(middle, pltpu.roll(edge_v, g.half_side, 1), edge_u)


def plane(raw, q, slot):
    force, visc, fric = raw
    if q < 2:
        return force[slot, q].astype(F32)
    return (fric if q == 2 else visc)[slot].astype(F32)


def edge_lane(g, level, q, r):
    return (0 if level % 2 else g.half_side) + q * g.span + r * g.margin(level)


def packed_edge(g, here, level, patch_of):
    side = g.side
    lane = lane_ids(side)
    margin = g.margin(level)
    start = 0 if here % 2 else side - margin
    total = jnp.zeros((side, side), F32)
    for r in range(g.patch_rows(level)):
        for q in range(4):
            base = edge_lane(g, level, q, r)
            value = patch_of(q, r)
            if (base - start) % side:
                value = pltpu.roll(value, (base - start) % side, 1)
            total = jnp.where((lane >= base) & (lane < base + margin), value, total)
    return total


def edge_column(g, here, level):
    return 0 if here % 2 else g.columns(level) - 1


def first_edge_kernel(g, own, edge, sems, held):
    level_here = lax.axis_index("level")

    def pack(level):
        copies = Copies(sems)
        rows = g.patch_rows(level)
        if g.columns(level) == 1:
            for source, target in zip(own, held):
                copies.start(source, target)
        else:
            for r in range(rows):
                slot = r * g.columns(level) + edge_column(g, level, level)
                for source, target in zip(own, held):
                    copies.start(source.at[slot], target.at[r])
        copies.finish()
        edge[...] = packed_edge(g, level, level, lambda q, r: plane(held, q, r))

    for level in range(g.levels):
        pl.when(level_here == level)(lambda level=level: pack(level))


def edge_kernel(g, first, other, edge):
    level_here = lax.axis_index("level")

    def pack(here):
        level = here ^ 1
        column = edge_column(g, here, level)

        def patch_of(q, r):
            return plane(other, q, r * g.columns(level) + column)

        edge[...] = first[...] + packed_edge(g, here, level, patch_of)

    for here in range(g.levels):
        pl.when(level_here == here)(lambda here=here: pack(here))


def fill_level(g, level, west_type, d, limits, covered, raw, edge, groups):
    side = g.side
    margin = g.margin(level)
    own = g.own(level)
    columns = g.columns(level)
    lane = lane_ids(side)

    def outer(q, r, place):
        shift = (place - edge_lane(g, level, q, r)) % side
        return pltpu.roll(edge[...], shift, 1) if shift else edge[...]

    def store(q, k, r, value):
        here = pl.ds(r * side, side)
        if q < 2:
            if covered is not None:
                ids = r * side + lax.broadcasted_iota(jnp.int32, (side, side), 0)
                value = jnp.where(ids < covered[k], 0.0, value)
            d.right[q, k, here, :] = value
        elif q == 2:
            d.fric[k, here, :] = value
        else:
            d.visc[k, pl.ds(PAD + r * side, side), :] = jnp.where(
                limits[k] > r * side, 0.5 * value, 0.0
            )

    clear_pads(d.visc, [(k,) for k in range(g.blocks(level))])
    for r in range(groups):
        for q in range(4):
            if level == 0 and west_type:
                west = outer(q, r, side - margin)
                store(q, 0, r, jnp.where(lane >= side - margin, west, plane(raw, q, r)))
            elif level == 0:
                value = pltpu.roll(plane(raw, q, r), g.half_side, 1)
                here = (lane >= g.half_side) & (lane < g.half_side + margin)
                store(q, 0, r, jnp.where(here, outer(q, r, g.half_side), value))
            else:
                for k in range(own):
                    store(q, k, r, plane(raw, q, r * columns + k + (0 if west_type else own)))
                if west_type:
                    east = plane(raw, q, r * columns + own)
                    west = outer(q, r, side - margin)
                else:
                    east = outer(q, r, 0)
                    west = plane(raw, q, r * columns + own - 1)
                store(q, own, r, jnp.where(lane < g.half_side, east, west))


class Level(NamedTuple):
    visc: Any
    weight: Any
    right: Any = None
    held: Any = None
    fric: Any = None
    cells: Any = None
    part: Any = None
    north: Any = None
    south: Any = None
    left: Any = None


def level_array(g, count, rows, make, comps, pad):
    shape = (count, rows + (2 * PAD if pad else 0), g.side)
    return make((2, *shape) if comps else shape, F32)


def step_arrays(g, level, rows):
    count = g.blocks(level)
    padded = level_array(g, count, rows, pltpu.VMEM, True, True)
    return dict(
        cells=padded,
        part=level_array(g, count, rows, pltpu.VMEM, True, False),
        north=padded,
        south=padded,
    )


def clear_level(g, level, d):
    blocks = range(g.blocks(level))
    both = [(c, k) for c in range(2) for k in blocks]
    for ref in (d.cells, d.north, d.south):
        clear_pads(ref, both)


def merged(first, second):
    return Level(*[b if a is None else a for a, b in zip(first, second)])


class Copies:
    def __init__(self, sems, first=0):
        self.sems = sems
        self.used = first
        self.open = []

    def start(self, source, target):
        copy = pltpu.make_async_copy(source, target, self.sems.at[self.used])
        self.used += 1
        copy.start()
        self.open.append(copy)

    def finish(self):
        for copy in self.open:
            copy.wait()
        self.open = []


def low_rows(g):
    return g.rows(2) // 2 + 2 * PAD


def kept_rows(g):
    return g.rows(2) // 2 + PAD


def lent_rows(g):
    return low_rows(g), -(-low_rows(g) // 2 // 16) * 16


def lent_forcing(g):
    return [count * g.half_side for count in range(1, g.patch_rows(2) + 1)]


def lent_size(g):
    rows, less = lent_rows(g)
    return 3 * rows + 2 * 16 * len(lent_forcing(g)) + 5 * less


def pair_of(visc):
    high = visc.astype(BF16)
    return [high, (visc - high.astype(F32)).astype(BF16)]


def margin_shift(g, index):
    margin = g.margin(1)
    base = g.half_side + PAD + 2 * margin * index
    return base, (margin + base) % g.side


def lend(g, fine, coarse, out):
    rows, less = lent_rows(g)
    side = g.side
    lane = lane_ids(side)
    place = [0]

    def put(value):
        size = value.shape[0]
        out[pl.ds(place[0], size), :] = value.astype(BF16)
        place[0] += size

    def block(level, k, size):
        here = pl.ds(0, size)
        return [
            level.right[0, k, here, :],
            level.right[1, k, here, :],
            level.fric[k, here, :],
            *pair_of(level.visc[k, pl.ds(PAD, size), :]),
        ]

    put(fine.fric[0, pl.ds(0, rows), :])
    for value in pair_of(fine.visc[0, pl.ds(PAD, rows), :]):
        put(value)
    for comp in range(2):
        for first in lent_forcing(g):
            put(fine.right[comp, 0, pl.ds(first, 16), :])
    total = jnp.zeros((rows, side), F32)
    for index, value in enumerate(block(fine, 1, rows)):
        base, shift = margin_shift(g, index)
        value = pltpu.roll(value.astype(F32), shift, 1)
        total = jnp.where((lane >= base) & (lane < base + 2 * g.margin(1)), value, total)
    spare = (lane >= g.half_side + PAD) & (lane < side - PAD)
    for index, value in enumerate(block(coarse, 0, less)):
        value = value.astype(F32)
        if index == 2:
            value = jnp.where(spare, total[:less], value)
        if index == 3:
            more = rows - less
            put(jnp.where(spare, total[less:], value[:more]))
            value = value[more:]
        put(value)


def borrow(g, lent, limits, fine, coarse):
    rows, less = lent_rows(g)
    side = g.side
    place = [0]

    def take(size):
        value = lent[pl.ds(place[0], size), :].astype(F32)
        place[0] += size
        return value

    def put_visc(level, number, k, first, value):
        size = value.shape[0]
        ids = first + lax.broadcasted_iota(jnp.int32, (size, side), 0)
        level.visc[k, pl.ds(PAD + first, size), :] = jnp.where(ids < limits[number][k], value, 0.0)

    fine.fric[0, pl.ds(0, rows), :] = take(rows)
    high = take(rows)
    put_visc(fine, 1, 0, 0, high + take(rows))
    for comp in range(2):
        fine.right[comp, 0] = jnp.zeros((rows, side), F32)
        for first in lent_forcing(g):
            fine.right[comp, 0, pl.ds(first, 16), :] = take(16)
    planes = [take(less) for _ in range(5)]
    for comp in range(2):
        coarse.right[comp, 0] = planes[comp]
    coarse.fric[0] = planes[2]
    put_visc(coarse, 0, 0, 0, planes[3] + planes[4])
    for first, packed in ((0, planes[2]), (less, planes[3][: rows - less])):
        size = packed.shape[0]
        here = pl.ds(first, size)
        values = [pltpu.roll(packed, side - margin_shift(g, i)[1], 1) for i in range(5)]
        for comp in range(2):
            fine.right[comp, 1, here, :] = values[comp]
        fine.fric[1, here, :] = values[2]
        put_visc(fine, 1, 1, first, values[3] + values[4])


def fill_pair(g, rows_ref, own, other, edge, levels, wanted, groups):
    level_here = lax.axis_index("level")
    patch = lax.axis_index("patch")
    odd = level_here % 2 == 1
    for west_type in (True, False):

        @pl.when(odd if west_type else jnp.logical_not(odd))
        def _():
            for level in wanted:
                near = near_counts(g, rows_ref, level, patch, odd)
                limits = lane_limits(g, level, near, g.side)
                covered = None
                if level == 1:
                    finer = near_counts(g, rows_ref, 2, patch, odd)
                    covered = lane_limits(g, 1, finer, g.half_side)
                home = (level % 2 == 1) == west_type
                raw = own if home else other
                fill_level(
                    g, level, west_type, levels[level], limits, covered, raw, edge, groups(level)
                )


def fill_kernel(g, rows_ref, own, other, edge, filled, lent, low):
    level_here = lax.axis_index("level")
    top = g.levels - 1

    @pl.when(level_here >= top - 1)
    def _():
        levels = dict(zip((top - 1, top), filled))
        fill_pair(g, rows_ref, own, other, edge, levels, (top, top - 1), g.patch_rows)

    @pl.when(level_here < top - 1)
    def _():
        fill_pair(g, rows_ref, own, other, edge, low, (1, 0), lambda level: low_groups(g, level))
        lend(g, low[1], low[0], lent)


def low_groups(g, level):
    return -(-lent_rows(g)[1 - level] // g.side)


def down_kernel(g, rows_ref, own, other, edge, upper, sums, kept, lower, edges, scratch):
    level_here = lax.axis_index("level")
    patch = lax.axis_index("patch")
    side = g.side
    top = g.levels - 1
    odd = level_here % 2 == 1
    filled = [*lower, *upper]
    levels = [merged(merged(a, b), c) for a, b, c in zip(scratch, kept, filled)]

    def limits_of(level):
        return lane_limits(g, level, near_counts(g, rows_ref, level, patch, odd), side)

    @pl.when(level_here >= top - 1)
    def _():
        near = near_counts(g, rows_ref, top, patch, odd)
        covered = lane_limits(g, top - 1, near, g.half_side)
        given = filled[top - 1].right
        for comp in range(2):
            for k in range(g.blocks(top - 1)):
                rest = pl.ds(g.half_side, g.rows(top - 1) - g.half_side)
                levels[top - 1].right[comp, k, rest, :] = given[comp, k, rest, :]

        def set_right(comp, k, row, chunk, value):
            here = pl.ds(row, chunk)
            ids = row + lax.broadcasted_iota(jnp.int32, (chunk, side), 0)
            levels[top - 1].right[comp, k, here, :] = jnp.where(
                ids < covered[k], value, given[comp, k, here, :]
            )

        def keep(comp, k, row, chunk, value):
            (sums if k == 0 else edges)[comp, pl.ds(row, chunk), :] = value

        for level in (top, top - 1):
            d = levels[level]
            clear_level(g, level, d)
            smooth_weights(g, level, d, limits_of(level), g.rows(level), True)
            residual_step(g, level, d, 0, g.rows(level))
            restrict_into(g, level, d, 0, g.rows(level), set_right if level == top else keep)
        sums[2] = joined_edges(g, edges[0], edges[1])

    @pl.when(level_here < top - 1)
    def _():
        fill_pair(g, rows_ref, own, other, edge, levels, (1, 0), g.patch_rows)
        for level in (1, 0):
            smooth_weights(g, level, levels[level], limits_of(level), g.rows(level), False)


def bottom_levels(g, rows_ref, patch, odd, start, stop, fine, coarse, new_sums, store_fine):
    side = g.side
    count, chunk = g.blocks(1), g.chunk(1, stop - start)
    clear_level(g, 1, fine)
    if new_sums is not None:
        reach = g.rows(2) // 2
        for comp in range(2):
            for k in range(count):
                here = pl.ds(0, reach)
                fine.right[comp, k, here, :] = fine.right[comp, k, here, :] + new_sums(comp, k)

    def body(row):
        here = pl.ds(start + row, chunk)
        for comp in range(2):
            for k in range(count):
                fine.cells[comp, k, pl.ds(PAD + start + row, chunk), :] = (
                    fine.weight[comp, k, here, :] * fine.right[comp, k, here, :]
                )

    over_rows(stop - start, chunk, body)
    residual_step(g, 1, fine, start, stop)
    near = near_counts(g, rows_ref, 1, patch, odd)
    covered = lane_limits(g, 0, near, g.half_side)

    def smooth_coarse(comp, k, row, size, value):
        here = pl.ds(row, size)
        ids = row + lax.broadcasted_iota(jnp.int32, (size, side), 0)
        value = jnp.where(ids < covered[0], value, coarse.right[comp, 0, here, :])
        value = coarse.weight[comp, 0, here, :] * value
        coarse.cells[comp, 0, here, :] = value

    restrict_into(g, 1, fine, start, stop, smooth_coarse)

    def load(comp, k, row, size):
        return coarse.cells[comp, 0, pl.ds(row, size), :]

    prolong_from(g, 1, fine, lane_limits(g, 1, near, side), start, stop, load)
    corrected_step(g, 1, fine, start, stop, store_fine)


def up_kernel(
    g, rows_ref, sums, lent, filled, kept, mine, theirs, edges, scratch, low, low_fine, low_coarse, finer, coarser
):
    level_here = lax.axis_index("level")
    patch = lax.axis_index("patch")
    side = g.side
    top = g.levels - 1
    odd = level_here % 2 == 1
    levels = [merged(merged(a, b), c) for a, b, c in zip(scratch, kept, filled)]

    def limits_of(level):
        return lane_limits(g, level, near_counts(g, rows_ref, level, patch, odd), side)

    def hand_out():
        def write(first, second):
            for k in range(g.half_slots):
                for comp in range(2):
                    first[k, comp] = finer[k, comp]
                    second[k, comp] = coarser[k, comp]

        pl.when(odd)(lambda: write(mine, theirs))
        pl.when(jnp.logical_not(odd))(lambda: write(theirs, mine))

    @pl.when(level_here >= top - 1)
    def _():
        rows, less = lent_rows(g)
        limits = {level: limits_of(level) for level in (0, 1)}
        clear_pads(low_fine.visc, [(k,) for k in range(g.blocks(1))])
        clear_pads(low_coarse.visc, [(k,) for k in range(g.blocks(0))])
        borrow(g, lent, limits, low_fine, low_coarse)
        smooth_weights(g, 1, low_fine, limits[1], rows, False)
        smooth_weights(g, 0, low_coarse, limits[0], less, False)

        def store_fine(comp, k, row, chunk, value):
            low[comp, k, pl.ds(row, chunk), :] = value

        bottom_levels(
            g, rows_ref, patch, odd, 0, rows, low_fine, low_coarse,
            level_sums(g, sums, low_fine.weight), store_fine,
        )

        def load_low(comp, k, row, chunk):
            return low[comp, k, pl.ds(row, chunk), :]

        def load_held(comp, k, row, chunk):
            return edges[comp, k, pl.ds(row, chunk), :]

        def store_in(level, out, hold):
            own = g.own(level)

            def store(comp, k, row, chunk, value):
                if hold:
                    edges[comp, k, pl.ds(row, chunk), :] = value
                if k < own:
                    group, place = row // side, row % side
                    out[group * own + k, comp, pl.ds(pl.multiple_of(place, 8), chunk), :] = value

            return store

        for level, load, out in ((top - 1, load_low, coarser), (top, load_held, finer)):
            d = levels[level]
            clear_level(g, level, d)
            rows = g.rows(level)
            prolong_from(g, level, d, limits_of(level), 0, rows, load)
            corrected_step(g, level, d, 0, rows, store_in(level, out, level < top))
        hand_out()

    @pl.when(level_here < top - 1)
    def _():
        rows = g.rows(1)
        first = g.rows(2) // 2
        fine, coarse = levels[1], levels[0]

        def store_fine(comp, k, row, chunk, value):
            if k == 0:
                group, place = row // side, row % side
                finer[group, comp, pl.ds(pl.multiple_of(place, 8), chunk), :] = value

        bottom_levels(g, rows_ref, patch, odd, first, rows, fine, coarse, None, store_fine)
        lane = lane_ids(side)
        for comp in range(2):
            for k in range(g.half_slots):
                parts = []
                for group in (k, k + g.half_slots):
                    here = pl.ds(group * side, side)
                    if group * side < rows // 2:
                        parts.append(coarse.cells[comp, 0, here, :])
                    else:
                        parts.append(
                            coarse.weight[comp, 0, here, :] * coarse.right[comp, 0, here, :]
                        )
                coarser[k, comp] = jnp.where(
                    lane < g.half_side, parts[0], pltpu.roll(parts[1], g.half_side, 1)
                )
        hand_out()


def level_sums(g, sums, weight):
    reach = g.rows(2) // 2

    def value(comp, k):
        found = sums[comp] if k == 0 else sums[2]
        if k and comp:
            found = pltpu.roll(found, g.half_side, 1)
        return jnp.where(weight[comp, k, pl.ds(0, reach), :] > 0.0, found, 0.0)

    return value


def low_kernel(
    g, rows_ref, sums, filled, kept, mine_in, theirs_in, mine, theirs, scratch, low_coarse, own_rows
):
    level_here = lax.axis_index("level")
    patch = lax.axis_index("patch")
    side = g.side
    top = g.levels - 1
    odd = level_here % 2 == 1

    @pl.when(level_here < top - 1)
    def _():
        for k in range(g.half_slots):
            for comp in range(2):
                mine[k, comp] = mine_in[k, comp]
                theirs[k, comp] = theirs_in[k, comp]
        rows, _ = lent_rows(g)
        done = kept_rows(g)
        fine = merged(Level(filled[1].visc, kept[1].weight), scratch)
        coarse = merged(Level(None, kept[0].weight, filled[0].right), low_coarse)
        for comp in range(2):
            for k in range(g.blocks(1)):
                fine.right[comp, k] = filled[1].right[comp, k, pl.ds(0, rows), :]

        def store_fine(comp, k, row, chunk, value):
            if k == 0:
                own_rows[comp, pl.ds(row, chunk), :] = value

        bottom_levels(
            g, rows_ref, patch, odd, 0, rows, fine, coarse,
            level_sums(g, sums, fine.weight), store_fine,
        )
        lane = lane_ids(side)
        size = rows // 2
        ids = lax.broadcasted_iota(jnp.int32, (size, side), 0)
        ours = (ids < done // 2) & (lane < g.half_side)

        def write(first, second):
            for comp in range(2):
                first[0, comp] = own_rows[comp, pl.ds(0, side), :]
                first[1, comp, pl.ds(0, done - side), :] = own_rows[
                    comp, pl.ds(side, done - side), :
                ]
                here = pl.ds(0, size)
                second[0, comp, here, :] = jnp.where(
                    ours, coarse.cells[comp, 0, here, :], second[0, comp, here, :]
                )

        pl.when(odd)(lambda: write(mine, theirs))
        pl.when(jnp.logical_not(odd))(lambda: write(theirs, mine))


def join_kernel(g, mine_up, given_up, mine_low, given_low, speed, fric, adjoint, gradient):
    level_here = lax.axis_index("level")
    lane = lane_ids(g.side)

    def put(slot, parts):
        for comp in range(2):
            adjoint[slot, comp] = parts[comp]
        total = speed[slot, 0].astype(F32) * parts[0] + speed[slot, 1].astype(F32) * parts[1]
        gradient[slot] = (-(fric[slot].astype(F32) * total)).astype(BF16)

    def join_level(level):
        upper = level >= g.levels - 2
        mine, given = (mine_up, given_up) if upper else (mine_low, given_low)
        if level == 0:
            for k in range(g.half_slots):
                low = []
                high = []
                for comp in range(2):
                    west, east = given[k, comp], mine[k, comp]
                    low.append(
                        jnp.where(lane < g.half_side, west, pltpu.roll(east, g.half_side, 1))
                    )
                    high.append(
                        jnp.where(lane < g.half_side, pltpu.roll(west, g.half_side, 1), east)
                    )
                put(k, low)
                put(k + g.half_slots, high)
            return
        own = g.own(level)
        west_half, east_half = (mine, given) if level % 2 == 1 else (given, mine)
        for r in range(g.patch_rows(level)):
            for k in range(2 * own):
                source = west_half if k < own else east_half
                put(
                    r * g.columns(level) + k,
                    [source[r * own + k % own, comp] for comp in range(2)],
                )

    for level in range(g.levels):
        pl.when(level_here == level)(lambda level=level: join_level(level))


def run_kernel(body, ins, outs, scratch, grant=VMEM_BYTES):
    in_trees = [jax.tree.flatten(tree) for tree, _ in ins]
    out_trees = [jax.tree.flatten(tree) for tree, _ in outs]
    scratch_trees = [jax.tree.flatten(tree) for tree in scratch]
    sizes = [len(leaves) for leaves, _ in in_trees + out_trees + scratch_trees]
    shapes = [tree for _, tree in in_trees + out_trees + scratch_trees]

    def kernel(*refs):
        given = []
        first = 0
        for size, shape in zip(sizes, shapes):
            given.append(jax.tree.unflatten(shape, refs[first : first + size]))
            first += size
        body(*given)

    def specs(groups, trees):
        return [
            pl.BlockSpec(memory_space=space)
            for (_, space), (leaves, _) in zip(groups, trees)
            for _ in leaves
        ]

    results = pl.pallas_call(
        kernel,
        out_shape=[leaf for leaves, _ in out_trees for leaf in leaves],
        in_specs=specs(ins, in_trees),
        out_specs=specs(outs, out_trees),
        scratch_shapes=[leaf for leaves, _ in scratch_trees for leaf in leaves],
        compiler_params=pltpu.CompilerParams(vmem_limit_bytes=grant),
    )(*[leaf for leaves, _ in in_trees for leaf in leaves])
    answer = []
    first = 0
    for leaves, shape in out_trees:
        answer.append(jax.tree.unflatten(shape, results[first : first + len(leaves)]))
        first += len(leaves)
    return answer


def moved(value, g, step):
    pairs = []
    for patch in range(g.patches):
        for level in range(g.levels):
            to_patch, to_level = step(patch, level)
            if 0 <= to_patch < g.patches and 0 <= to_level < g.levels:
                pairs.append((patch * g.levels + level, to_patch * g.levels + to_level))
    return lax.ppermute(value, ("patch", "level"), pairs)


def per_device(forcing, velocity, viscosity, friction, patch_rows):
    g = Layout(
        forcing.shape[1], forcing.shape[-1], lax.axis_size("level"), lax.axis_size("patch")
    )
    side = g.side
    top = g.levels - 1
    force, speed, visc, fric = forcing[0], velocity[0], viscosity[0], friction[0]
    make = jax.ShapeDtypeStruct
    vmem = pltpu.VMEM
    block = make((side, side), F32)
    half = make((g.half_slots, 2, side, side), F32)
    three = make((3, side, side), F32)

    def array(level, rows, kind, comps, pad):
        return level_array(g, g.blocks(level), rows, kind, comps, pad)

    own = (force, visc, fric)
    other = tuple(moved(value, g, lambda p, l: (p, l ^ 1)) for value in own)
    (edge,) = run_kernel(
        lambda *refs: first_edge_kernel(g, *refs),
        [(own, pltpu.HBM)],
        [(block, VM)],
        [
            pltpu.SemaphoreType.DMA((3 * g.slots,)),
            tuple(vmem(value.shape, value.dtype) for value in own),
        ],
        FIRST_BYTES,
    )
    (edge,) = run_kernel(
        lambda *refs: edge_kernel(g, *refs), [(edge, VM), (other, VM)], [(block, VM)], []
    )
    edge = moved(edge, g, lambda p, l: (p + (-1 if l % 2 else 1), l ^ 1))

    fields = [
        Level(
            array(level, g.rows(level), make, False, True),
            None,
            right=array(level, g.rows(level), make, True, False),
            fric=array(level, g.rows(level), make, False, False),
        )
        for level in range(g.levels)
    ]
    rows, less = lent_rows(g)
    given = [(patch_rows, SM), (own, VM), (other, VM), (edge, VM)]

    def low_scratch(level):
        size = low_groups(g, level) * side
        return Level(
            array(level, size, vmem, False, True),
            None,
            right=array(level, size, vmem, True, False),
            fric=array(level, size, vmem, False, False),
        )

    upper, lent = run_kernel(
        lambda *refs: fill_kernel(g, *refs),
        given,
        [(fields[top - 1 :], VM), (make((lent_size(g), side), BF16), VM)],
        [[low_scratch(level) for level in (0, 1)]],
    )
    lent = moved(lent, g, lambda p, l: (p, l + 2))

    def kept_of(level):
        two = array(level, g.rows(level), make, True, False)
        return Level(None, two, held=two if level >= top - 1 else None)

    def down_scratch(level):
        if level < top - 1:
            return Level(None, None)
        both = array(level, g.rows(level), vmem, True, False)
        more = dict(right=both) if level < top else {}
        return Level(None, None, left=both, **more, **step_arrays(g, level, g.rows(level)))

    sums, kept, lower = run_kernel(
        lambda *refs: down_kernel(g, *refs),
        [*given, (upper, VM)],
        [
            (three, VM),
            ([kept_of(level) for level in range(g.levels)], VM),
            (fields[: top - 1], VM),
        ],
        [vmem((2, side, side), F32), [down_scratch(level) for level in range(g.levels)]],
    )
    filled = [*lower, *upper]
    sums_there = moved(sums, g, lambda p, l: (p, l - 2))

    def up_scratch(level):
        if level == 0:
            return Level(None, None, cells=vmem((2, 1, g.rows(1) // 2, side), F32))
        both = array(level, g.rows(level), vmem, True, False)
        more = dict(held=both, left=both) if level == 1 else {}
        return Level(None, None, **more, **step_arrays(g, level, g.rows(level)))

    low_both = array(1, rows, vmem, True, False)
    low_steps = dict(held=low_both, left=low_both, right=low_both, **step_arrays(g, 1, rows))
    mine_up, theirs_up = run_kernel(
        lambda *refs: up_kernel(g, *refs),
        [(patch_rows, SM), (sums, VM), (lent, VM), (filled, VM), (kept, VM)],
        [(half, VM), (half, VM)],
        [
            array(top - 1, g.rows(top - 1), vmem, True, False),
            [up_scratch(level) for level in range(g.levels)],
            low_both,
            Level(
                array(1, rows, vmem, False, True),
                low_both,
                fric=array(1, rows, vmem, False, False),
                **low_steps,
            ),
            Level(
                array(0, less, vmem, False, True),
                array(0, less, vmem, True, False),
                right=array(0, less, vmem, True, False),
                fric=array(0, less, vmem, False, False),
                cells=array(0, less, vmem, True, False),
            ),
            vmem(half.shape, F32),
            vmem(half.shape, F32),
        ],
    )
    received_up = moved(theirs_up, g, lambda p, l: (p, l ^ 1 if l >= top - 1 else -1))
    mine, theirs = run_kernel(
        lambda *refs: low_kernel(g, *refs),
        [
            (patch_rows, SM),
            (sums_there, VM),
            (filled[:2], VM),
            (kept[:2], VM),
            (mine_up, VM),
            (theirs_up, VM),
        ],
        [(half, VM), (half, VM)],
        [
            Level(None, None, **low_steps),
            Level(None, None, cells=array(0, less, vmem, True, False)),
            vmem((2, rows, side), F32),
        ],
    )
    received = moved(theirs, g, lambda p, l: (p, l ^ 1 if l < top - 1 else -1))
    adjoint, gradient = run_kernel(
        lambda *refs: join_kernel(g, *refs),
        [
            (mine_up, VM),
            (received_up, VM),
            (mine, VM),
            (received, VM),
            (speed, VM),
            (fric, VM),
        ],
        [
            (make((g.slots, 2, side, side), F32), VM),
            (make((g.slots, side, side), BF16), VM),
        ],
        [],
    )
    return (adjoint[None], gradient[None])


def solution(mesh):
    fields = P("level", "patch")
    return jax.shard_map(
        per_device,
        mesh=mesh,
        in_specs=(fields, fields, fields, fields, P()),
        out_specs=(fields, fields),
        check_vma=False,
    )
```

```python
from typing import Any, NamedTuple

import jax
import jax.numpy as jnp
from jax import lax
from jax.experimental import pallas as pl
from jax.experimental.pallas import tpu as pltpu
from jax.sharding import PartitionSpec as P

relaxation = 0.5
PAD = 8
LOW, HIGH, EDGES = 0, 1, 2
VM, SM = pltpu.VMEM, pltpu.SMEM
F32 = jnp.float32
BF16 = jnp.bfloat16
VMEM_BYTES = 30 * 2**20
FIRST_BYTES = 60 * 2**20


class Layout:
    def __init__(self, slots, side, levels, patches):
        self.slots = slots
        self.side = side
        self.levels = levels
        self.patches = patches
        self.half_slots = slots // 2
        self.half_side = side // 2
        self.span = 2 * slots

    def columns(self, level):
        return 1 << level

    def patch_rows(self, level):
        return self.slots >> level

    def rows(self, level):
        return self.patch_rows(level) * self.side

    def margin(self, level):
        return 2 << level

    def own(self, level):
        return max(1, (1 << level) // 2)

    def blocks(self, level):
        return self.own(level) + (1 if level > 0 else 0)

    def chunk(self, level, rows):
        size = 8 * max(1, 112 // self.blocks(level))
        while rows % size or (rows % self.side == 0 and self.side % size):
            size -= 8
        return size


def lane_ids(side):
    return lax.broadcasted_iota(jnp.int32, (1, side), 1)


def near_counts(g, rows_ref, level, patch, odd):
    own = rows_ref[level, patch]
    east = jnp.where(
        patch + 1 < g.patches, rows_ref[level, jnp.minimum(patch + 1, g.patches - 1)], 0
    )
    west = jnp.where(patch > 0, rows_ref[level, jnp.maximum(patch - 1, 0)], 0)
    return own, jnp.where(odd, own, east), jnp.where(odd, west, own)


def lane_limits(g, level, counts, cells):
    own, east, west = (value * cells for value in counts)
    lane = lane_ids(g.side)
    margin = g.margin(level)
    first = 0 if level > 0 else g.half_side
    edges = jnp.where(
        (lane >= first) & (lane < first + margin), east, jnp.where(lane >= g.side - margin, west, 0)
    )
    if level == 0:
        return [jnp.where(lane < g.half_side, own, edges)]
    return [jnp.full((1, g.side), own, jnp.int32)] * g.own(level) + [edges]


def one_side(g, values, east):
    count = len(values)
    turned = [pltpu.roll(value, g.side - 1 if east else 1, 1) for value in values]
    if count == 1:
        return turned
    lane = lax.broadcasted_iota(jnp.int32, values[0].shape, 1)
    last = lane == (g.side - 1 if east else 0)
    step = 1 if east else -1
    return [jnp.where(last, turned[(k + step) % count], turned[k]) for k in range(count)]


def both_sides(g, values):
    return one_side(g, values, True), one_side(g, values, False)


def over_rows(rows, chunk, body):
    def step(index, carry):
        body(pl.multiple_of(index * chunk, chunk))
        return carry

    lax.fori_loop(0, rows // chunk, step, 0)


def clear_pads(ref, lead):
    width = ref.shape[-1]
    last = ref.shape[-2]
    for index in lead:
        ref[index + (slice(0, PAD), slice(None))] = jnp.zeros((PAD, width), F32)
        ref[index + (slice(last - PAD, last), slice(None))] = jnp.zeros((PAD, width), F32)


def off_diagonal_rows(g, d, row, size, count):
    here = pl.ds(row, size)
    inner = pl.ds(PAD + row, size)
    centre = [[d.cells[comp, k, inner, :] for k in range(count)] for comp in range(2)]
    beside = [both_sides(g, centre[comp]) for comp in range(2)]
    products = []
    for k in range(count):
        visc = d.visc[k, inner, :]
        half = 0.5 * visc
        (u, v) = (centre[comp][k] for comp in range(2))
        (u_e, u_w), (v_e, v_w) = ((beside[c][0][k], beside[c][1][k]) for c in range(2))
        u_n, v_n = (d.cells[c, k, pl.ds(PAD + row + 1, size), :] for c in range(2))
        u_s, v_s = (d.cells[c, k, pl.ds(PAD + row - 1, size), :] for c in range(2))
        one_u, one_v = visc * u, visc * v
        four_u, four_v = 4.0 * one_u, 4.0 * one_v
        cross_u, cross_v = half * (v_e - v_w), visc * (u_e - u_w)
        d.north[0, k, inner, :] = one_u + cross_u
        d.south[0, k, inner, :] = one_u - cross_u
        d.north[1, k, inner, :] = four_v + cross_v
        d.south[1, k, inner, :] = four_v - cross_v
        cross_u, cross_v = visc * (v_n - v_s), half * (u_n - u_s)
        products.append(
            (
                four_u + cross_u,
                four_u - cross_u,
                one_v + cross_v,
                one_v - cross_v,
                visc * (4.0 * (u_e + u_w) + (u_n + u_s)),
                visc * (4.0 * (v_n + v_s) + (v_e + v_w)),
            )
        )
    for comp in range(2):
        east = one_side(g, [item[2 * comp] for item in products], True)
        west = one_side(g, [item[2 * comp + 1] for item in products], False)
        for k in range(count):
            d.part[comp, k, here, :] = products[k][4 + comp] + east[k] + west[k]


def off_diagonal_step(g, level, d, start, stop):
    count = g.blocks(level)
    chunk = g.chunk(level, stop - start)

    def body(row):
        for step in range(0, chunk, 8):
            off_diagonal_rows(g, d, start + row + step, 8, count)

    over_rows(stop - start, chunk, body)


def off_diagonal(d, comp, k, row, chunk):
    return (
        d.part[comp, k, pl.ds(row, chunk), :]
        + d.north[comp, k, pl.ds(PAD + row + 1, chunk), :]
        + d.south[comp, k, pl.ds(PAD + row - 1, chunk), :]
    )


def smooth_weights(g, level, d, limits, start, stop, from_zero):
    count = g.blocks(level)
    chunk = g.chunk(level, stop - start)

    def some_rows(row):
        here = pl.ds(row, 8)
        inner = pl.ds(PAD + row, 8)
        centre = [d.visc[k, inner, :] for k in range(count)]
        east, west = both_sides(g, centre)
        for k in range(count):
            north = d.visc[k, pl.ds(PAD + row + 1, 8), :]
            south = d.visc[k, pl.ds(PAD + row - 1, 8), :]
            friction = d.fric[k, here, :]
            twice = 2.0 * centre[k]
            along_row = twice + east[k] + west[k]
            along_col = twice + north + south
            live = jnp.broadcast_to(limits[k], (8, g.side)) > row
            diag_u = 4.0 * along_row + along_col + friction
            diag_v = 4.0 * along_col + along_row + friction
            for comp, diag in ((0, diag_u), (1, diag_v)):
                guess = pl.reciprocal(diag, approx=True)
                weight = guess * (2.0 * relaxation - relaxation * diag * guess)
                weight = jnp.where(live, weight, 0.0)
                d.weight[comp, k, here, :] = weight
                if from_zero:
                    d.cells[comp, k, inner, :] = weight * d.right[comp, k, here, :]

    def body(row):
        for step in range(0, chunk, 8):
            some_rows(start + row + step)

    over_rows(stop - start, chunk, body)


def residual_step(g, level, d, start, stop):
    count = g.blocks(level)
    chunk = g.chunk(level, stop - start)
    off_diagonal_step(g, level, d, start, stop)

    def body(row):
        row = row + start
        here = pl.ds(row, chunk)
        for comp in range(2):
            for k in range(count):
                weight = d.weight[comp, k, here, :]
                left = (1.0 - relaxation) * d.right[comp, k, here, :] + off_diagonal(
                    d, comp, k, row, chunk
                )
                left = jnp.where(weight > 0.0, left, 0.0)
                d.left[comp, k, here, :] = left
                d.held[comp, k, here, :] = (
                    d.cells[comp, k, pl.ds(PAD + row, chunk), :] + weight * left
                )

    over_rows(stop - start, chunk, body)


def corrected_step(g, level, d, start, stop, store):
    count = g.blocks(level)
    chunk = g.chunk(level, stop - start)
    off_diagonal_step(g, level, d, start, stop)

    def body(row):
        row = row + start
        here = pl.ds(row, chunk)
        for comp in range(2):
            for k in range(count):
                value = (
                    d.held[comp, k, here, :]
                    + (1.0 - relaxation) * d.cells[comp, k, pl.ds(PAD + row, chunk), :]
                    + d.weight[comp, k, here, :] * off_diagonal(d, comp, k, row, chunk)
                )
                store(comp, k, row, chunk, value)

    over_rows(stop - start, chunk, body)


def pairings(g, fine):
    if fine == 1:
        return [[(0, LOW), (1, HIGH)]]
    parts = [[(2 * k, LOW), (2 * k + 1, HIGH)] for k in range(g.own(fine) // 2)]
    return parts + [[(g.own(fine), EDGES)]]


def target_lane(g, part, fine_lane):
    halved = jnp.right_shift(fine_lane, 1)
    if part == LOW:
        return halved
    if part == HIGH:
        return g.half_side + halved
    return halved + jnp.where(fine_lane >= g.half_side, g.half_side, 0)


def sum_matrix(g, part):
    fine = lax.broadcasted_iota(jnp.int32, (g.side, g.side), 0)
    coarse = lax.broadcasted_iota(jnp.int32, (g.side, g.side), 1)
    return jnp.where(target_lane(g, part, fine) == coarse, 1.0, 0.0).astype(BF16)


def copy_matrix(g, part):
    coarse = lax.broadcasted_iota(jnp.int32, (g.side, g.side), 0)
    fine = lax.broadcasted_iota(jnp.int32, (g.side, g.side), 1)
    return jnp.where(target_lane(g, part, fine) == coarse, 1.0, 0.0).astype(BF16)


def split_dot(values, matrix):
    high = values.astype(BF16)
    rest = (values - high.astype(F32)).astype(BF16)
    return jnp.dot(high, matrix, preferred_element_type=F32) + jnp.dot(
        rest, matrix, preferred_element_type=F32
    )


def restrict_into(g, fine, d, start, stop, store):
    rows = stop - start
    chunk = min(rows // 2, g.half_side)
    if (rows // 2) % chunk:
        chunk = rows // 2
    parts = pairings(g, fine)
    matrices = {part: sum_matrix(g, part) for members in parts for _, part in members}

    def body(row):
        row = row + start // 2
        for comp in range(2):
            for coarse, members in enumerate(parts):
                total = None
                for k, part in members:
                    first = d.left[comp, k, pl.ds(2 * row, chunk, stride=2), :]
                    second = d.left[comp, k, pl.ds(2 * row + 1, chunk, stride=2), :]
                    term = split_dot(first + second, matrices[part])
                    total = term if total is None else total + term
                store(comp, coarse, row, chunk, total)

    over_rows(rows // 2, chunk, body)


def prolong_from(g, fine, d, limits, start, stop, load):
    rows = stop - start
    chunk = min(rows // 2, g.half_side)
    if (rows // 2) % chunk:
        chunk = rows // 2
    parts = pairings(g, fine)
    matrices = {part: copy_matrix(g, part) for members in parts for _, part in members}

    def body(row):
        row = row + start // 2
        ids = 2 * (row + lax.broadcasted_iota(jnp.int32, (chunk, g.side), 0))
        for comp in range(2):
            for coarse, members in enumerate(parts):
                value = load(comp, coarse, row, chunk)
                for k, part in members:
                    spread = jnp.where(ids < limits[k], split_dot(value, matrices[part]), 0.0)
                    d.cells[comp, k, pl.ds(PAD + 2 * row, chunk, stride=2), :] = spread
                    d.cells[comp, k, pl.ds(PAD + 2 * row + 1, chunk, stride=2), :] = spread

    over_rows(rows // 2, chunk, body)


def joined_edges(g, edge_u, edge_v):
    lane = lane_ids(g.side)
    quarter = g.side // 4
    middle = (lane >= quarter) & (lane < g.side - quarter)
    return jnp.where(middle, pltpu.roll(edge_v, g.half_side, 1), edge_u)


def plane(raw, q, slot):
    force, visc, fric = raw
    if q < 2:
        return force[slot, q].astype(F32)
    return (fric if q == 2 else visc)[slot].astype(F32)


def edge_lane(g, level, q, r):
    return (0 if level % 2 else g.half_side) + q * g.span + r * g.margin(level)


def packed_edge(g, here, level, patch_of):
    side = g.side
    lane = lane_ids(side)
    margin = g.margin(level)
    start = 0 if here % 2 else side - margin
    total = jnp.zeros((side, side), F32)
    for r in range(g.patch_rows(level)):
        for q in range(4):
            base = edge_lane(g, level, q, r)
            value = patch_of(q, r)
            if (base - start) % side:
                value = pltpu.roll(value, (base - start) % side, 1)
            total = jnp.where((lane >= base) & (lane < base + margin), value, total)
    return total


def edge_column(g, here, level):
    return 0 if here % 2 else g.columns(level) - 1


def first_edge_kernel(g, own, edge, sems, held):
    level_here = lax.axis_index("level")

    def pack(level):
        copies = Copies(sems)
        rows = g.patch_rows(level)
        if g.columns(level) == 1:
            for source, target in zip(own, held):
                copies.start(source, target)
        else:
            for r in range(rows):
                slot = r * g.columns(level) + edge_column(g, level, level)
                for source, target in zip(own, held):
                    copies.start(source.at[slot], target.at[r])
        copies.finish()
        edge[...] = packed_edge(g, level, level, lambda q, r: plane(held, q, r))

    for level in range(g.levels):
        pl.when(level_here == level)(lambda level=level: pack(level))


def edge_kernel(g, first, other, edge):
    level_here = lax.axis_index("level")

    def pack(here):
        level = here ^ 1
        column = edge_column(g, here, level)

        def patch_of(q, r):
            return plane(other, q, r * g.columns(level) + column)

        edge[...] = first[...] + packed_edge(g, here, level, patch_of)

    for here in range(g.levels):
        pl.when(level_here == here)(lambda here=here: pack(here))


def fill_level(g, level, west_type, d, limits, covered, raw, edge, groups):
    side = g.side
    margin = g.margin(level)
    own = g.own(level)
    columns = g.columns(level)
    lane = lane_ids(side)

    def outer(q, r, place):
        shift = (place - edge_lane(g, level, q, r)) % side
        return pltpu.roll(edge[...], shift, 1) if shift else edge[...]

    def store(q, k, r, value):
        here = pl.ds(r * side, side)
        if q < 2:
            if covered is not None:
                ids = r * side + lax.broadcasted_iota(jnp.int32, (side, side), 0)
                value = jnp.where(ids < covered[k], 0.0, value)
            d.right[q, k, here, :] = value
        elif q == 2:
            d.fric[k, here, :] = value
        else:
            d.visc[k, pl.ds(PAD + r * side, side), :] = jnp.where(
                limits[k] > r * side, 0.5 * value, 0.0
            )

    clear_pads(d.visc, [(k,) for k in range(g.blocks(level))])
    for r in range(groups):
        for q in range(4):
            if level == 0 and west_type:
                west = outer(q, r, side - margin)
                store(q, 0, r, jnp.where(lane >= side - margin, west, plane(raw, q, r)))
            elif level == 0:
                value = pltpu.roll(plane(raw, q, r), g.half_side, 1)
                here = (lane >= g.half_side) & (lane < g.half_side + margin)
                store(q, 0, r, jnp.where(here, outer(q, r, g.half_side), value))
            else:
                for k in range(own):
                    store(q, k, r, plane(raw, q, r * columns + k + (0 if west_type else own)))
                if west_type:
                    east = plane(raw, q, r * columns + own)
                    west = outer(q, r, side - margin)
                else:
                    east = outer(q, r, 0)
                    west = plane(raw, q, r * columns + own - 1)
                store(q, own, r, jnp.where(lane < g.half_side, east, west))


class Level(NamedTuple):
    visc: Any
    weight: Any
    right: Any = None
    held: Any = None
    fric: Any = None
    cells: Any = None
    part: Any = None
    north: Any = None
    south: Any = None
    left: Any = None


def level_array(g, count, rows, make, comps, pad):
    shape = (count, rows + (2 * PAD if pad else 0), g.side)
    return make((2, *shape) if comps else shape, F32)


def step_arrays(g, level, rows):
    count = g.blocks(level)
    padded = level_array(g, count, rows, pltpu.VMEM, True, True)
    return dict(
        cells=padded,
        part=level_array(g, count, rows, pltpu.VMEM, True, False),
        north=padded,
        south=padded,
    )


def clear_level(g, level, d):
    blocks = range(g.blocks(level))
    both = [(c, k) for c in range(2) for k in blocks]
    for ref in (d.cells, d.north, d.south):
        clear_pads(ref, both)


def merged(first, second):
    return Level(*[b if a is None else a for a, b in zip(first, second)])


class Copies:
    def __init__(self, sems, first=0):
        self.sems = sems
        self.used = first
        self.open = []

    def start(self, source, target):
        copy = pltpu.make_async_copy(source, target, self.sems.at[self.used])
        self.used += 1
        copy.start()
        self.open.append(copy)

    def finish(self):
        for copy in self.open:
            copy.wait()
        self.open = []


def low_rows(g):
    return g.rows(2) // 2 + 2 * PAD


def kept_rows(g):
    return g.rows(2) // 2 + PAD


def lent_rows(g):
    return low_rows(g), -(-low_rows(g) // 2 // 16) * 16


def lent_forcing(g):
    return [count * g.half_side for count in range(1, g.patch_rows(2) + 1)]


def lent_size(g):
    rows, less = lent_rows(g)
    return 3 * rows + 2 * 16 * len(lent_forcing(g)) + 5 * less


def pair_of(visc):
    high = visc.astype(BF16)
    return [high, (visc - high.astype(F32)).astype(BF16)]


def margin_shift(g, index):
    margin = g.margin(1)
    base = g.half_side + PAD + 2 * margin * index
    return base, (margin + base) % g.side


def lend(g, fine, coarse, out):
    rows, less = lent_rows(g)
    side = g.side
    lane = lane_ids(side)
    place = [0]

    def put(value):
        size = value.shape[0]
        out[pl.ds(place[0], size), :] = value.astype(BF16)
        place[0] += size

    def block(level, k, size):
        here = pl.ds(0, size)
        return [
            level.right[0, k, here, :],
            level.right[1, k, here, :],
            level.fric[k, here, :],
            *pair_of(level.visc[k, pl.ds(PAD, size), :]),
        ]

    put(fine.fric[0, pl.ds(0, rows), :])
    for value in pair_of(fine.visc[0, pl.ds(PAD, rows), :]):
        put(value)
    for comp in range(2):
        for first in lent_forcing(g):
            put(fine.right[comp, 0, pl.ds(first, 16), :])
    total = jnp.zeros((rows, side), F32)
    for index, value in enumerate(block(fine, 1, rows)):
        base, shift = margin_shift(g, index)
        value = pltpu.roll(value.astype(F32), shift, 1)
        total = jnp.where((lane >= base) & (lane < base + 2 * g.margin(1)), value, total)
    spare = (lane >= g.half_side + PAD) & (lane < side - PAD)
    for index, value in enumerate(block(coarse, 0, less)):
        value = value.astype(F32)
        if index == 2:
            value = jnp.where(spare, total[:less], value)
        if index == 3:
            more = rows - less
            put(jnp.where(spare, total[less:], value[:more]))
            value = value[more:]
        put(value)


def borrow(g, lent, limits, fine, coarse):
    rows, less = lent_rows(g)
    side = g.side
    place = [0]

    def take(size):
        value = lent[pl.ds(place[0], size), :].astype(F32)
        place[0] += size
        return value

    def put_visc(level, number, k, first, value):
        size = value.shape[0]
        ids = first + lax.broadcasted_iota(jnp.int32, (size, side), 0)
        level.visc[k, pl.ds(PAD + first, size), :] = jnp.where(ids < limits[number][k], value, 0.0)

    fine.fric[0, pl.ds(0, rows), :] = take(rows)
    high = take(rows)
    put_visc(fine, 1, 0, 0, high + take(rows))
    for comp in range(2):
        fine.right[comp, 0] = jnp.zeros((rows, side), F32)
        for first in lent_forcing(g):
            fine.right[comp, 0, pl.ds(first, 16), :] = take(16)
    planes = [take(less) for _ in range(5)]
    for comp in range(2):
        coarse.right[comp, 0] = planes[comp]
    coarse.fric[0] = planes[2]
    put_visc(coarse, 0, 0, 0, planes[3] + planes[4])
    for first, packed in ((0, planes[2]), (less, planes[3][: rows - less])):
        size = packed.shape[0]
        here = pl.ds(first, size)
        values = [pltpu.roll(packed, side - margin_shift(g, i)[1], 1) for i in range(5)]
        for comp in range(2):
            fine.right[comp, 1, here, :] = values[comp]
        fine.fric[1, here, :] = values[2]
        put_visc(fine, 1, 1, first, values[3] + values[4])


def fill_pair(g, rows_ref, own, other, edge, levels, wanted, groups):
    level_here = lax.axis_index("level")
    patch = lax.axis_index("patch")
    odd = level_here % 2 == 1
    for west_type in (True, False):

        @pl.when(odd if west_type else jnp.logical_not(odd))
        def _():
            for level in wanted:
                near = near_counts(g, rows_ref, level, patch, odd)
                limits = lane_limits(g, level, near, g.side)
                covered = None
                if level == 1:
                    finer = near_counts(g, rows_ref, 2, patch, odd)
                    covered = lane_limits(g, 1, finer, g.half_side)
                home = (level % 2 == 1) == west_type
                raw = own if home else other
                fill_level(
                    g, level, west_type, levels[level], limits, covered, raw, edge, groups(level)
                )


def fill_kernel(g, rows_ref, own, other, edge, filled, lent, low):
    level_here = lax.axis_index("level")
    top = g.levels - 1

    @pl.when(level_here >= top - 1)
    def _():
        levels = dict(zip((top - 1, top), filled))
        fill_pair(g, rows_ref, own, other, edge, levels, (top, top - 1), g.patch_rows)

    @pl.when(level_here < top - 1)
    def _():
        fill_pair(g, rows_ref, own, other, edge, low, (1, 0), lambda level: low_groups(g, level))
        lend(g, low[1], low[0], lent)


def low_groups(g, level):
    return -(-lent_rows(g)[1 - level] // g.side)


def down_kernel(
    g, rows_ref, own, other, edge, upper, sums, kept, low_kept, lower, edges, scratch
):
    level_here = lax.axis_index("level")
    patch = lax.axis_index("patch")
    side = g.side
    top = g.levels - 1
    odd = level_here % 2 == 1
    filled = [*lower, *upper]
    kept = [*(Level(None, weight) for weight in low_kept), *kept]
    levels = [merged(merged(a, b), c) for a, b, c in zip(scratch, kept, filled)]

    def limits_of(level):
        return lane_limits(g, level, near_counts(g, rows_ref, level, patch, odd), side)

    @pl.when(level_here >= top - 1)
    def _():
        near = near_counts(g, rows_ref, top, patch, odd)
        covered = lane_limits(g, top - 1, near, g.half_side)
        given = filled[top - 1].right
        for comp in range(2):
            for k in range(g.blocks(top - 1)):
                rest = pl.ds(g.half_side, g.rows(top - 1) - g.half_side)
                levels[top - 1].right[comp, k, rest, :] = given[comp, k, rest, :]

        def set_right(comp, k, row, chunk, value):
            here = pl.ds(row, chunk)
            ids = row + lax.broadcasted_iota(jnp.int32, (chunk, side), 0)
            levels[top - 1].right[comp, k, here, :] = jnp.where(
                ids < covered[k], value, given[comp, k, here, :]
            )

        def keep(comp, k, row, chunk, value):
            (sums if k == 0 else edges)[comp, pl.ds(row, chunk), :] = value

        for level in (top, top - 1):
            d = levels[level]
            clear_level(g, level, d)
            smooth_weights(g, level, d, limits_of(level), 0, g.rows(level), True)
            residual_step(g, level, d, 0, g.rows(level))
            restrict_into(g, level, d, 0, g.rows(level), set_right if level == top else keep)
        sums[2] = joined_edges(g, edges[0], edges[1])

    @pl.when(level_here < top - 1)
    def _():
        fill_pair(g, rows_ref, own, other, edge, levels, (1, 0), g.patch_rows)
        for level, size in zip((1, 0), lent_rows(g)):
            smooth_weights(g, level, levels[level], limits_of(level), 0, size, False)


def bottom_levels(g, rows_ref, patch, odd, start, stop, fine, coarse, new_sums, store_fine):
    side = g.side
    count, chunk = g.blocks(1), g.chunk(1, stop - start)
    clear_level(g, 1, fine)
    if new_sums is not None:
        reach = g.rows(2) // 2
        for comp in range(2):
            for k in range(count):
                here = pl.ds(0, reach)
                fine.right[comp, k, here, :] = fine.right[comp, k, here, :] + new_sums(comp, k)

    def body(row):
        here = pl.ds(start + row, chunk)
        for comp in range(2):
            for k in range(count):
                fine.cells[comp, k, pl.ds(PAD + start + row, chunk), :] = (
                    fine.weight[comp, k, here, :] * fine.right[comp, k, here, :]
                )

    over_rows(stop - start, chunk, body)
    residual_step(g, 1, fine, start, stop)
    near = near_counts(g, rows_ref, 1, patch, odd)
    covered = lane_limits(g, 0, near, g.half_side)

    def smooth_coarse(comp, k, row, size, value):
        here = pl.ds(row, size)
        ids = row + lax.broadcasted_iota(jnp.int32, (size, side), 0)
        value = jnp.where(ids < covered[0], value, coarse.right[comp, 0, here, :])
        value = coarse.weight[comp, 0, here, :] * value
        coarse.cells[comp, 0, here, :] = value

    restrict_into(g, 1, fine, start, stop, smooth_coarse)

    def load(comp, k, row, size):
        return coarse.cells[comp, 0, pl.ds(row, size), :]

    prolong_from(g, 1, fine, lane_limits(g, 1, near, side), start, stop, load)
    corrected_step(g, 1, fine, start, stop, store_fine)


def up_kernel(
    g, rows_ref, sums, lent, filled, kept, mine, theirs, own_rows, coarse_rows, edges, scratch, low, low_fine,
    low_coarse, finer, coarser,
):
    level_here = lax.axis_index("level")
    patch = lax.axis_index("patch")
    side = g.side
    top = g.levels - 1
    odd = level_here % 2 == 1
    levels = [merged(a, b) for a, b in zip(scratch, filled)]
    for level in (top - 1, top):
        levels[level] = merged(levels[level], kept[level - top + 1])

    def limits_of(level):
        return lane_limits(g, level, near_counts(g, rows_ref, level, patch, odd), side)

    def hand_out():
        def write(first, second):
            for k in range(g.half_slots):
                for comp in range(2):
                    first[k, comp] = finer[k, comp]
                    second[k, comp] = coarser[k, comp]

        pl.when(odd)(lambda: write(mine, theirs))
        pl.when(jnp.logical_not(odd))(lambda: write(theirs, mine))

    @pl.when(level_here >= top - 1)
    def _():
        rows, less = lent_rows(g)
        limits = {level: limits_of(level) for level in (0, 1)}
        clear_pads(low_fine.visc, [(k,) for k in range(g.blocks(1))])
        clear_pads(low_coarse.visc, [(k,) for k in range(g.blocks(0))])
        borrow(g, lent, limits, low_fine, low_coarse)
        smooth_weights(g, 1, low_fine, limits[1], 0, rows, False)
        smooth_weights(g, 0, low_coarse, limits[0], 0, less, False)

        def store_fine(comp, k, row, chunk, value):
            low[comp, k, pl.ds(row, chunk), :] = value

        bottom_levels(
            g, rows_ref, patch, odd, 0, rows, low_fine, low_coarse,
            level_sums(g, sums, low_fine.weight), store_fine,
        )

        def load_low(comp, k, row, chunk):
            return low[comp, k, pl.ds(row, chunk), :]

        def load_held(comp, k, row, chunk):
            return edges[comp, k, pl.ds(row, chunk), :]

        def store_in(level, out, hold):
            own = g.own(level)

            def store(comp, k, row, chunk, value):
                if hold:
                    edges[comp, k, pl.ds(row, chunk), :] = value
                if k < own:
                    group, place = row // side, row % side
                    out[group * own + k, comp, pl.ds(pl.multiple_of(place, 8), chunk), :] = value

            return store

        for level, load, out in ((top - 1, load_low, coarser), (top, load_held, finer)):
            d = levels[level]
            clear_level(g, level, d)
            rows = g.rows(level)
            prolong_from(g, level, d, limits_of(level), 0, rows, load)
            corrected_step(g, level, d, 0, rows, store_in(level, out, level < top))
        hand_out()

    @pl.when(level_here < top - 1)
    def _():
        rows = g.rows(1)
        first = g.rows(2) // 2
        fine, coarse = levels[1], levels[0]._replace(cells=coarse_rows)
        smooth_weights(g, 1, fine, limits_of(1), first, rows, False)
        smooth_weights(g, 0, coarse, limits_of(0), first // 2, g.rows(0), False)

        def store_fine(comp, k, row, chunk, value):
            if k == 0:
                own_rows[comp, pl.ds(row, chunk), :] = value

        bottom_levels(g, rows_ref, patch, odd, first, rows, fine, coarse, None, store_fine)
        for r in range(rows // 2 // side, g.patch_rows(0)):
            here = pl.ds(r * side, side)
            for comp in range(2):
                coarse_rows[comp, 0, here, :] = (
                    coarse.weight[comp, 0, here, :] * coarse.right[comp, 0, here, :]
                )


def level_sums(g, sums, weight):
    reach = g.rows(2) // 2

    def value(comp, k):
        found = sums[comp] if k == 0 else sums[2]
        if k and comp:
            found = pltpu.roll(found, g.half_side, 1)
        return jnp.where(weight[comp, k, pl.ds(0, reach), :] > 0.0, found, 0.0)

    return value


def low_kernel(
    g, rows_ref, sums, filled, kept, mine_in, theirs_in, own_rows, coarse_rows, mine, theirs, scratch, low_coarse, near_rows
):
    level_here = lax.axis_index("level")
    patch = lax.axis_index("patch")
    side = g.side
    top = g.levels - 1
    odd = level_here % 2 == 1

    @pl.when(level_here >= top - 1)
    def _():
        for k in range(g.half_slots):
            for comp in range(2):
                mine[k, comp] = mine_in[k, comp]
                theirs[k, comp] = theirs_in[k, comp]

    @pl.when(level_here < top - 1)
    def _():
        rows, _ = lent_rows(g)
        done = kept_rows(g)
        fine = merged(Level(filled[1].visc, kept[1]), scratch)
        coarse = merged(Level(None, kept[0], filled[0].right), low_coarse)
        for comp in range(2):
            for k in range(g.blocks(1)):
                fine.right[comp, k] = filled[1].right[comp, k, pl.ds(0, rows), :]

        def store_fine(comp, k, row, chunk, value):
            if k == 0:
                near_rows[comp, pl.ds(row, chunk), :] = value

        bottom_levels(
            g, rows_ref, patch, odd, 0, rows, fine, coarse,
            level_sums(g, sums, fine.weight), store_fine,
        )
        lane = lane_ids(side)
        size = rows // 2
        ids = lax.broadcasted_iota(jnp.int32, (size, side), 0)

        def coarse_group(comp, r):
            value = coarse_rows[comp, 0, pl.ds(r * side, side), :]
            if r:
                return value
            near = coarse.cells[comp, 0, pl.ds(0, size), :]
            near = jnp.where(ids < done // 2, near, value[:size])
            return jnp.concatenate([near, value[size:]], axis=0)

        def write(first, second):
            for comp in range(2):
                first[0, comp] = near_rows[comp, pl.ds(0, side), :]
                for r in range(1, g.patch_rows(1)):
                    first[r, comp] = own_rows[comp, pl.ds(r * side, side), :]
                first[1, comp, pl.ds(0, done - side), :] = near_rows[
                    comp, pl.ds(side, done - side), :
                ]
                for k in range(g.half_slots):
                    high = pltpu.roll(coarse_group(comp, k + g.half_slots), g.half_side, 1)
                    second[k, comp] = jnp.where(lane < g.half_side, coarse_group(comp, k), high)

        pl.when(odd)(lambda: write(mine, theirs))
        pl.when(jnp.logical_not(odd))(lambda: write(theirs, mine))


def join_kernel(g, mine, given, speed, fric, adjoint, gradient):
    level_here = lax.axis_index("level")
    lane = lane_ids(g.side)

    def put(slot, parts):
        for comp in range(2):
            adjoint[slot, comp] = parts[comp]
        total = speed[slot, 0].astype(F32) * parts[0] + speed[slot, 1].astype(F32) * parts[1]
        gradient[slot] = (-(fric[slot].astype(F32) * total)).astype(BF16)

    def join_level(level):
        if level == 0:
            for k in range(g.half_slots):
                low = []
                high = []
                for comp in range(2):
                    west, east = given[k, comp], mine[k, comp]
                    low.append(
                        jnp.where(lane < g.half_side, west, pltpu.roll(east, g.half_side, 1))
                    )
                    high.append(
                        jnp.where(lane < g.half_side, pltpu.roll(west, g.half_side, 1), east)
                    )
                put(k, low)
                put(k + g.half_slots, high)
            return
        own = g.own(level)
        west_half, east_half = (mine, given) if level % 2 == 1 else (given, mine)
        for r in range(g.patch_rows(level)):
            for k in range(2 * own):
                source = west_half if k < own else east_half
                put(
                    r * g.columns(level) + k,
                    [source[r * own + k % own, comp] for comp in range(2)],
                )

    for level in range(g.levels):
        pl.when(level_here == level)(lambda level=level: join_level(level))


def run_kernel(body, ins, outs, scratch, grant=VMEM_BYTES):
    in_trees = [jax.tree.flatten(tree) for tree, _ in ins]
    out_trees = [jax.tree.flatten(tree) for tree, _ in outs]
    scratch_trees = [jax.tree.flatten(tree) for tree in scratch]
    sizes = [len(leaves) for leaves, _ in in_trees + out_trees + scratch_trees]
    shapes = [tree for _, tree in in_trees + out_trees + scratch_trees]

    def kernel(*refs):
        given = []
        first = 0
        for size, shape in zip(sizes, shapes):
            given.append(jax.tree.unflatten(shape, refs[first : first + size]))
            first += size
        body(*given)

    def specs(groups, trees):
        return [
            pl.BlockSpec(memory_space=space)
            for (_, space), (leaves, _) in zip(groups, trees)
            for _ in leaves
        ]

    results = pl.pallas_call(
        kernel,
        out_shape=[leaf for leaves, _ in out_trees for leaf in leaves],
        in_specs=specs(ins, in_trees),
        out_specs=specs(outs, out_trees),
        scratch_shapes=[leaf for leaves, _ in scratch_trees for leaf in leaves],
        compiler_params=pltpu.CompilerParams(vmem_limit_bytes=grant),
    )(*[leaf for leaves, _ in in_trees for leaf in leaves])
    answer = []
    first = 0
    for leaves, shape in out_trees:
        answer.append(jax.tree.unflatten(shape, results[first : first + len(leaves)]))
        first += len(leaves)
    return answer


def moved(value, g, step):
    pairs = []
    for patch in range(g.patches):
        for level in range(g.levels):
            to_patch, to_level = step(patch, level)
            if 0 <= to_patch < g.patches and 0 <= to_level < g.levels:
                pairs.append((patch * g.levels + level, to_patch * g.levels + to_level))
    return lax.ppermute(value, ("patch", "level"), pairs)


def per_device(forcing, velocity, viscosity, friction, patch_rows):
    g = Layout(
        forcing.shape[1], forcing.shape[-1], lax.axis_size("level"), lax.axis_size("patch")
    )
    side = g.side
    top = g.levels - 1
    force, speed, visc, fric = forcing[0], velocity[0], viscosity[0], friction[0]
    make = jax.ShapeDtypeStruct
    vmem = pltpu.VMEM
    block = make((side, side), F32)
    half = make((g.half_slots, 2, side, side), F32)
    three = make((3, side, side), F32)

    def array(level, rows, kind, comps, pad):
        return level_array(g, g.blocks(level), rows, kind, comps, pad)

    own = (force, visc, fric)
    other = tuple(moved(value, g, lambda p, l: (p, l ^ 1)) for value in own)
    (edge,) = run_kernel(
        lambda *refs: first_edge_kernel(g, *refs),
        [(own, pltpu.HBM)],
        [(block, VM)],
        [
            pltpu.SemaphoreType.DMA((3 * g.slots,)),
            tuple(vmem(value.shape, value.dtype) for value in own),
        ],
        FIRST_BYTES,
    )
    (edge,) = run_kernel(
        lambda *refs: edge_kernel(g, *refs), [(edge, VM), (other, VM)], [(block, VM)], []
    )
    edge = moved(edge, g, lambda p, l: (p + (-1 if l % 2 else 1), l ^ 1))

    fields = [
        Level(
            array(level, g.rows(level), make, False, True),
            None,
            right=array(level, g.rows(level), make, True, False),
            fric=array(level, g.rows(level), make, False, False),
        )
        for level in range(g.levels)
    ]
    rows, less = lent_rows(g)
    given = [(patch_rows, SM), (own, VM), (other, VM), (edge, VM)]

    def low_scratch(level):
        size = low_groups(g, level) * side
        return Level(
            array(level, size, vmem, False, True),
            None,
            right=array(level, size, vmem, True, False),
            fric=array(level, size, vmem, False, False),
        )

    upper, lent = run_kernel(
        lambda *refs: fill_kernel(g, *refs),
        given,
        [(fields[top - 1 :], VM), (make((lent_size(g), side), BF16), VM)],
        [[low_scratch(level) for level in (0, 1)]],
    )
    lent = moved(lent, g, lambda p, l: (p, l + 2))

    def kept_of(level):
        two = array(level, g.rows(level), make, True, False)
        return Level(None, two, held=two)

    low_weights = [array(0, less, make, True, False), array(1, rows, make, True, False)]

    def down_scratch(level):
        if level < top - 1:
            return Level(None, None)
        both = array(level, g.rows(level), vmem, True, False)
        more = dict(right=both) if level < top else {}
        return Level(None, None, left=both, **more, **step_arrays(g, level, g.rows(level)))

    sums, kept, low_kept, lower = run_kernel(
        lambda *refs: down_kernel(g, *refs),
        [*given, (upper, VM)],
        [
            (three, VM),
            ([kept_of(level) for level in (top - 1, top)], VM),
            (low_weights, VM),
            (fields[: top - 1], VM),
        ],
        [vmem((2, side, side), F32), [down_scratch(level) for level in range(g.levels)]],
    )
    filled = [*lower, *upper]
    sums_there = moved(sums, g, lambda p, l: (p, l - 2))

    def up_scratch(level):
        both = array(level, g.rows(level), vmem, True, False)
        if level == 0:
            return Level(None, both)
        steps = step_arrays(g, level, g.rows(level))
        if level == 1:
            return Level(None, both, held=both, left=both, **steps)
        return Level(None, None, **steps)

    low_both = array(1, rows, vmem, True, False)
    low_steps = dict(held=low_both, left=low_both, right=low_both, **step_arrays(g, 1, rows))
    mine, theirs, own_rows, coarse_rows = run_kernel(
        lambda *refs: up_kernel(g, *refs),
        [(patch_rows, SM), (sums, VM), (lent, VM), (filled, VM), (kept, VM)],
        [
            (half, VM),
            (half, VM),
            (make((2, g.rows(1), side), F32), VM),
            (make((2, 1, g.rows(0), side), F32), VM),
        ],
        [
            array(top - 1, g.rows(top - 1), vmem, True, False),
            [up_scratch(level) for level in range(g.levels)],
            low_both,
            Level(
                array(1, rows, vmem, False, True),
                low_both,
                fric=array(1, rows, vmem, False, False),
                **low_steps,
            ),
            Level(
                array(0, less, vmem, False, True),
                array(0, less, vmem, True, False),
                right=array(0, less, vmem, True, False),
                fric=array(0, less, vmem, False, False),
                cells=array(0, less, vmem, True, False),
            ),
            vmem(half.shape, F32),
            vmem(half.shape, F32),
        ],
    )
    mine, theirs = run_kernel(
        lambda *refs: low_kernel(g, *refs),
        [
            (patch_rows, SM),
            (sums_there, VM),
            (filled[:2], VM),
            (low_kept, VM),
            (mine, VM),
            (theirs, VM),
            (own_rows, VM),
            (coarse_rows, VM),
        ],
        [(half, VM), (half, VM)],
        [
            Level(None, None, **low_steps),
            Level(None, None, cells=array(0, less, vmem, True, False)),
            vmem((2, rows, side), F32),
        ],
    )
    received = moved(theirs, g, lambda p, l: (p, l ^ 1))
    adjoint, gradient = run_kernel(
        lambda *refs: join_kernel(g, *refs),
        [(mine, VM), (received, VM), (speed, VM), (fric, VM)],
        [
            (make((g.slots, 2, side, side), F32), VM),
            (make((g.slots, side, side), BF16), VM),
        ],
        [],
    )
    return (adjoint[None], gradient[None])


def solution(mesh):
    fields = P("level", "patch")
    return jax.shard_map(
        per_device,
        mesh=mesh,
        in_specs=(fields, fields, fields, fields, P()),
        out_specs=(fields, fields),
        check_vma=False,
    )
```

```python
from typing import Any, NamedTuple

import jax
import jax.numpy as jnp
from jax import lax
from jax.experimental import pallas as pl
from jax.experimental.pallas import tpu as pltpu
from jax.sharding import PartitionSpec as P

relaxation = 0.5
PAD = 8
LOW, HIGH, EDGES = 0, 1, 2
VM, SM = pltpu.VMEM, pltpu.SMEM
F32 = jnp.float32
BF16 = jnp.bfloat16
VMEM_BYTES = 30 * 2**20
FIRST_BYTES = 60 * 2**20


class Layout:
    def __init__(self, slots, side, levels, patches):
        self.slots = slots
        self.side = side
        self.levels = levels
        self.patches = patches
        self.half_slots = slots // 2
        self.half_side = side // 2
        self.span = 2 * slots

    def columns(self, level):
        return 1 << level

    def patch_rows(self, level):
        return self.slots >> level

    def rows(self, level):
        return self.patch_rows(level) * self.side

    def margin(self, level):
        return 2 << level

    def own(self, level):
        return max(1, (1 << level) // 2)

    def blocks(self, level):
        return self.own(level) + (1 if level > 0 else 0)

    def chunk(self, level, rows):
        size = 8 * max(1, 112 // self.blocks(level))
        while rows % size or (rows % self.side == 0 and self.side % size):
            size -= 8
        return size


def lane_ids(side):
    return lax.broadcasted_iota(jnp.int32, (1, side), 1)


def near_counts(g, rows_ref, level, patch, odd):
    own = rows_ref[level, patch]
    east = jnp.where(
        patch + 1 < g.patches, rows_ref[level, jnp.minimum(patch + 1, g.patches - 1)], 0
    )
    west = jnp.where(patch > 0, rows_ref[level, jnp.maximum(patch - 1, 0)], 0)
    return own, jnp.where(odd, own, east), jnp.where(odd, west, own)


def lane_limits(g, level, counts, cells):
    own, east, west = (value * cells for value in counts)
    lane = lane_ids(g.side)
    margin = g.margin(level)
    first = 0 if level > 0 else g.half_side
    edges = jnp.where(
        (lane >= first) & (lane < first + margin), east, jnp.where(lane >= g.side - margin, west, 0)
    )
    if level == 0:
        return [jnp.where(lane < g.half_side, own, edges)]
    return [jnp.full((1, g.side), own, jnp.int32)] * g.own(level) + [edges]


def one_side(g, values, east):
    count = len(values)
    turned = [pltpu.roll(value, g.side - 1 if east else 1, 1) for value in values]
    if count == 1:
        return turned
    lane = lax.broadcasted_iota(jnp.int32, values[0].shape, 1)
    last = lane == (g.side - 1 if east else 0)
    step = 1 if east else -1
    return [jnp.where(last, turned[(k + step) % count], turned[k]) for k in range(count)]


def both_sides(g, values):
    return one_side(g, values, True), one_side(g, values, False)


def over_rows(rows, chunk, body):
    def step(index, carry):
        body(pl.multiple_of(index * chunk, chunk))
        return carry

    lax.fori_loop(0, rows // chunk, step, 0)


def clear_pads(ref, lead):
    width = ref.shape[-1]
    last = ref.shape[-2]
    for index in lead:
        ref[index + (slice(0, PAD), slice(None))] = jnp.zeros((PAD, width), F32)
        ref[index + (slice(last - PAD, last), slice(None))] = jnp.zeros((PAD, width), F32)


def off_diagonal_rows(g, d, row, size, count):
    here = pl.ds(row, size)
    inner = pl.ds(PAD + row, size)
    centre = [[d.cells[comp, k, inner, :] for k in range(count)] for comp in range(2)]
    beside = [both_sides(g, centre[comp]) for comp in range(2)]
    products = []
    for k in range(count):
        visc = d.visc[k, inner, :]
        half = 0.5 * visc
        (u, v) = (centre[comp][k] for comp in range(2))
        (u_e, u_w), (v_e, v_w) = ((beside[c][0][k], beside[c][1][k]) for c in range(2))
        u_n, v_n = (d.cells[c, k, pl.ds(PAD + row + 1, size), :] for c in range(2))
        u_s, v_s = (d.cells[c, k, pl.ds(PAD + row - 1, size), :] for c in range(2))
        one_u, one_v = visc * u, visc * v
        four_u, four_v = 4.0 * one_u, 4.0 * one_v
        cross_u, cross_v = half * (v_e - v_w), visc * (u_e - u_w)
        d.north[0, k, inner, :] = one_u + cross_u
        d.south[0, k, inner, :] = one_u - cross_u
        d.north[1, k, inner, :] = four_v + cross_v
        d.south[1, k, inner, :] = four_v - cross_v
        cross_u, cross_v = visc * (v_n - v_s), half * (u_n - u_s)
        products.append(
            (
                four_u + cross_u,
                four_u - cross_u,
                one_v + cross_v,
                one_v - cross_v,
                visc * (4.0 * (u_e + u_w) + (u_n + u_s)),
                visc * (4.0 * (v_n + v_s) + (v_e + v_w)),
            )
        )
    for comp in range(2):
        east = one_side(g, [item[2 * comp] for item in products], True)
        west = one_side(g, [item[2 * comp + 1] for item in products], False)
        for k in range(count):
            d.part[comp, k, here, :] = products[k][4 + comp] + east[k] + west[k]


def off_diagonal_step(g, level, d, start, stop):
    count = g.blocks(level)
    chunk = g.chunk(level, stop - start)

    def body(row):
        for step in range(0, chunk, 8):
            off_diagonal_rows(g, d, start + row + step, 8, count)

    over_rows(stop - start, chunk, body)


def off_diagonal(d, comp, k, row, chunk):
    return (
        d.part[comp, k, pl.ds(row, chunk), :]
        + d.north[comp, k, pl.ds(PAD + row + 1, chunk), :]
        + d.south[comp, k, pl.ds(PAD + row - 1, chunk), :]
    )


def smooth_weights(g, level, d, limits, start, stop, from_zero):
    count = g.blocks(level)
    chunk = g.chunk(level, stop - start)

    def some_rows(row):
        here = pl.ds(row, 8)
        inner = pl.ds(PAD + row, 8)
        centre = [d.visc[k, inner, :] for k in range(count)]
        east, west = both_sides(g, centre)
        for k in range(count):
            north = d.visc[k, pl.ds(PAD + row + 1, 8), :]
            south = d.visc[k, pl.ds(PAD + row - 1, 8), :]
            friction = d.fric[k, here, :]
            twice = 2.0 * centre[k]
            along_row = twice + east[k] + west[k]
            along_col = twice + north + south
            live = jnp.broadcast_to(limits[k], (8, g.side)) > row
            diag_u = 4.0 * along_row + along_col + friction
            diag_v = 4.0 * along_col + along_row + friction
            for comp, diag in ((0, diag_u), (1, diag_v)):
                guess = pl.reciprocal(diag, approx=True)
                weight = guess * (2.0 * relaxation - relaxation * diag * guess)
                weight = jnp.where(live, weight, 0.0)
                d.weight[comp, k, here, :] = weight
                if from_zero:
                    d.cells[comp, k, inner, :] = weight * d.right[comp, k, here, :]

    def body(row):
        for step in range(0, chunk, 8):
            some_rows(start + row + step)

    over_rows(stop - start, chunk, body)


def residual_step(g, level, d, start, stop):
    count = g.blocks(level)
    chunk = g.chunk(level, stop - start)
    off_diagonal_step(g, level, d, start, stop)

    def body(row):
        row = row + start
        here = pl.ds(row, chunk)
        for comp in range(2):
            for k in range(count):
                weight = d.weight[comp, k, here, :]
                left = (1.0 - relaxation) * d.right[comp, k, here, :] + off_diagonal(
                    d, comp, k, row, chunk
                )
                left = jnp.where(weight > 0.0, left, 0.0)
                d.left[comp, k, here, :] = left
                d.held[comp, k, here, :] = (
                    d.cells[comp, k, pl.ds(PAD + row, chunk), :] + weight * left
                )

    over_rows(stop - start, chunk, body)


def corrected_step(g, level, d, start, stop, store):
    count = g.blocks(level)
    chunk = g.chunk(level, stop - start)
    off_diagonal_step(g, level, d, start, stop)

    def body(row):
        row = row + start
        here = pl.ds(row, chunk)
        for comp in range(2):
            for k in range(count):
                value = (
                    d.held[comp, k, here, :]
                    + (1.0 - relaxation) * d.cells[comp, k, pl.ds(PAD + row, chunk), :]
                    + d.weight[comp, k, here, :] * off_diagonal(d, comp, k, row, chunk)
                )
                store(comp, k, row, chunk, value)

    over_rows(stop - start, chunk, body)


def pairings(g, fine):
    if fine == 1:
        return [[(0, LOW), (1, HIGH)]]
    parts = [[(2 * k, LOW), (2 * k + 1, HIGH)] for k in range(g.own(fine) // 2)]
    return parts + [[(g.own(fine), EDGES)]]


def target_lane(g, part, fine_lane):
    halved = jnp.right_shift(fine_lane, 1)
    if part == LOW:
        return halved
    if part == HIGH:
        return g.half_side + halved
    return halved + jnp.where(fine_lane >= g.half_side, g.half_side, 0)


def sum_matrix(g, part):
    fine = lax.broadcasted_iota(jnp.int32, (g.side, g.side), 0)
    coarse = lax.broadcasted_iota(jnp.int32, (g.side, g.side), 1)
    return jnp.where(target_lane(g, part, fine) == coarse, 1.0, 0.0).astype(BF16)


def copy_matrix(g, part):
    coarse = lax.broadcasted_iota(jnp.int32, (g.side, g.side), 0)
    fine = lax.broadcasted_iota(jnp.int32, (g.side, g.side), 1)
    return jnp.where(target_lane(g, part, fine) == coarse, 1.0, 0.0).astype(BF16)


def split_dot(values, matrix):
    high = values.astype(BF16)
    rest = (values - high.astype(F32)).astype(BF16)
    return jnp.dot(high, matrix, preferred_element_type=F32) + jnp.dot(
        rest, matrix, preferred_element_type=F32
    )


def restrict_into(g, fine, d, start, stop, store):
    rows = stop - start
    chunk = min(rows // 2, g.half_side)
    if (rows // 2) % chunk:
        chunk = rows // 2
    parts = pairings(g, fine)
    matrices = {part: sum_matrix(g, part) for members in parts for _, part in members}

    def body(row):
        row = row + start // 2
        for comp in range(2):
            for coarse, members in enumerate(parts):
                total = None
                for k, part in members:
                    first = d.left[comp, k, pl.ds(2 * row, chunk, stride=2), :]
                    second = d.left[comp, k, pl.ds(2 * row + 1, chunk, stride=2), :]
                    term = split_dot(first + second, matrices[part])
                    total = term if total is None else total + term
                store(comp, coarse, row, chunk, total)

    over_rows(rows // 2, chunk, body)


def prolong_from(g, fine, d, limits, start, stop, load):
    rows = stop - start
    chunk = min(rows // 2, g.half_side)
    if (rows // 2) % chunk:
        chunk = rows // 2
    parts = pairings(g, fine)
    matrices = {part: copy_matrix(g, part) for members in parts for _, part in members}

    def body(row):
        row = row + start // 2
        ids = 2 * (row + lax.broadcasted_iota(jnp.int32, (chunk, g.side), 0))
        for comp in range(2):
            for coarse, members in enumerate(parts):
                value = load(comp, coarse, row, chunk)
                for k, part in members:
                    spread = jnp.where(ids < limits[k], split_dot(value, matrices[part]), 0.0)
                    d.cells[comp, k, pl.ds(PAD + 2 * row, chunk, stride=2), :] = spread
                    d.cells[comp, k, pl.ds(PAD + 2 * row + 1, chunk, stride=2), :] = spread

    over_rows(rows // 2, chunk, body)


def joined_edges(g, edge_u, edge_v):
    lane = lane_ids(g.side)
    quarter = g.side // 4
    middle = (lane >= quarter) & (lane < g.side - quarter)
    return jnp.where(middle, pltpu.roll(edge_v, g.half_side, 1), edge_u)


def plane(raw, q, slot):
    force, visc, fric = raw
    if q < 2:
        return force[slot, q].astype(F32)
    return (fric if q == 2 else visc)[slot].astype(F32)


def edge_lane(g, level, q, r):
    return (0 if level % 2 else g.half_side) + q * g.span + r * g.margin(level)


def packed_edge(g, here, level, patch_of):
    side = g.side
    lane = lane_ids(side)
    margin = g.margin(level)
    start = 0 if here % 2 else side - margin
    total = jnp.zeros((side, side), F32)
    for r in range(g.patch_rows(level)):
        for q in range(4):
            base = edge_lane(g, level, q, r)
            value = patch_of(q, r)
            if (base - start) % side:
                value = pltpu.roll(value, (base - start) % side, 1)
            total = jnp.where((lane >= base) & (lane < base + margin), value, total)
    return total


def edge_column(g, here, level):
    return 0 if here % 2 else g.columns(level) - 1


def first_edge_kernel(g, own, edge, sems, held):
    level_here = lax.axis_index("level")

    def pack(level):
        copies = Copies(sems)
        rows = g.patch_rows(level)
        if g.columns(level) == 1:
            for source, target in zip(own, held):
                copies.start(source, target)
        else:
            for r in range(rows):
                slot = r * g.columns(level) + edge_column(g, level, level)
                for source, target in zip(own, held):
                    copies.start(source.at[slot], target.at[r])
        copies.finish()
        edge[...] = packed_edge(g, level, level, lambda q, r: plane(held, q, r))

    for level in range(g.levels):
        pl.when(level_here == level)(lambda level=level: pack(level))


def edge_kernel(g, first, other, edge):
    level_here = lax.axis_index("level")

    def pack(here):
        level = here ^ 1
        column = edge_column(g, here, level)

        def patch_of(q, r):
            return plane(other, q, r * g.columns(level) + column)

        edge[...] = first[...] + packed_edge(g, here, level, patch_of)

    for here in range(g.levels):
        pl.when(level_here == here)(lambda here=here: pack(here))


def fill_level(g, level, west_type, d, limits, covered, raw, edge, groups):
    side = g.side
    margin = g.margin(level)
    own = g.own(level)
    columns = g.columns(level)
    lane = lane_ids(side)

    def outer(q, r, place):
        shift = (place - edge_lane(g, level, q, r)) % side
        return pltpu.roll(edge[...], shift, 1) if shift else edge[...]

    def store(q, k, r, value):
        here = pl.ds(r * side, side)
        if q < 2:
            if covered is not None:
                ids = r * side + lax.broadcasted_iota(jnp.int32, (side, side), 0)
                value = jnp.where(ids < covered[k], 0.0, value)
            d.right[q, k, here, :] = value
        elif q == 2:
            d.fric[k, here, :] = value
        else:
            d.visc[k, pl.ds(PAD + r * side, side), :] = jnp.where(
                limits[k] > r * side, 0.5 * value, 0.0
            )

    clear_pads(d.visc, [(k,) for k in range(g.blocks(level))])
    for r in range(groups):
        for q in range(4):
            if level == 0 and west_type:
                west = outer(q, r, side - margin)
                store(q, 0, r, jnp.where(lane >= side - margin, west, plane(raw, q, r)))
            elif level == 0:
                value = pltpu.roll(plane(raw, q, r), g.half_side, 1)
                here = (lane >= g.half_side) & (lane < g.half_side + margin)
                store(q, 0, r, jnp.where(here, outer(q, r, g.half_side), value))
            else:
                for k in range(own):
                    store(q, k, r, plane(raw, q, r * columns + k + (0 if west_type else own)))
                if west_type:
                    east = plane(raw, q, r * columns + own)
                    west = outer(q, r, side - margin)
                else:
                    east = outer(q, r, 0)
                    west = plane(raw, q, r * columns + own - 1)
                store(q, own, r, jnp.where(lane < g.half_side, east, west))


class Level(NamedTuple):
    visc: Any
    weight: Any
    right: Any = None
    held: Any = None
    fric: Any = None
    cells: Any = None
    part: Any = None
    north: Any = None
    south: Any = None
    left: Any = None


def level_array(g, count, rows, make, comps, pad):
    shape = (count, rows + (2 * PAD if pad else 0), g.side)
    return make((2, *shape) if comps else shape, F32)


def step_arrays(g, level, rows):
    count = g.blocks(level)
    padded = level_array(g, count, rows, pltpu.VMEM, True, True)
    return dict(
        cells=padded,
        part=level_array(g, count, rows, pltpu.VMEM, True, False),
        north=padded,
        south=padded,
    )


def clear_level(g, level, d):
    blocks = range(g.blocks(level))
    both = [(c, k) for c in range(2) for k in blocks]
    for ref in (d.cells, d.north, d.south):
        clear_pads(ref, both)


def merged(first, second):
    return Level(*[b if a is None else a for a, b in zip(first, second)])


class Copies:
    def __init__(self, sems, first=0):
        self.sems = sems
        self.used = first
        self.open = []

    def start(self, source, target):
        copy = pltpu.make_async_copy(source, target, self.sems.at[self.used])
        self.used += 1
        copy.start()
        self.open.append(copy)

    def finish(self):
        for copy in self.open:
            copy.wait()
        self.open = []


def low_rows(g):
    return g.rows(2) // 2 + 2 * PAD


def kept_rows(g):
    return g.rows(2) // 2 + PAD


def lent_rows(g):
    return low_rows(g), -(-low_rows(g) // 2 // 16) * 16


def lent_forcing(g):
    return [count * g.half_side for count in range(1, g.patch_rows(2) + 1)]


def lent_size(g):
    rows, less = lent_rows(g)
    return 4 * rows + 2 * 16 * len(lent_forcing(g)) + 2 * less + 16


def pair_of(visc):
    high = visc.astype(BF16)
    return [high, (visc - high.astype(F32)).astype(BF16)]


class Rows:
    def __init__(self, ref):
        self.ref = ref
        self.place = 0

    def put(self, value):
        size = value.shape[0]
        self.ref[pl.ds(self.place, size), :] = value.astype(BF16)
        self.place += size

    def take(self, size):
        value = self.ref[pl.ds(self.place, size), :].astype(F32)
        self.place += size
        return value


def side_by_side(g, low, high):
    lane = lane_ids(g.side)
    return jnp.where(
        lane < g.half_side, low.astype(F32), pltpu.roll(high.astype(F32), g.half_side, 1)
    )


def lend(g, west_type, own, other, out):
    rows, less = lent_rows(g)
    side = g.side
    fine, coarse = (own, other) if west_type else (other, own)
    target = Rows(out)

    def some_rows(raw, q, slot, first, size):
        here = pl.ds(first, size)
        force, visc, fric = raw
        value = force[slot, q, here, :] if q < 2 else (fric if q == 2 else visc)[slot, here, :]
        return 0.5 * value if q == 3 else value

    def fine_rows(q, first, size, column=0 if west_type else g.own(1)):
        parts = []
        while size:
            group, place = first // side, first % side
            part = min(size, side - place)
            slot = group * g.columns(1) + column
            parts.append(some_rows(fine, q, slot, place, part))
            first, size = first + part, size - part
        return parts

    for part in fine_rows(2, 0, rows):
        target.put(part)
    pairs = [pair_of(part) for part in fine_rows(3, 0, rows)]
    for index in range(2):
        for pair in pairs:
            target.put(pair[index])
    for comp in range(2):
        for first in lent_forcing(g):
            for part in fine_rows(comp, first, 16):
                target.put(part)

    def coarse_rows(q, first, size):
        value = some_rows(coarse, q, 0, first, size).astype(F32)
        return value if west_type else pltpu.roll(value, g.half_side, 1)

    high, rest = pair_of(coarse_rows(3, 0, less))
    target.put(side_by_side(g, coarse_rows(2, 0, less), high))
    target.put(rest)
    target.put(
        side_by_side(g, coarse_rows(0, g.half_side, 16), coarse_rows(1, g.half_side, 16))
    )
    lane = lane_ids(side)

    def inner(level, size):
        column = g.own(1) if west_type else g.own(1) - 1
        total = jnp.zeros((size, side), F32)
        for q in range(4):
            if level:
                parts = fine_rows(q, 0, size, column)
                value = jnp.concatenate([part.astype(F32) for part in parts], axis=0)
            else:
                value = coarse_rows(q, 0, size)
            for offset, plane_value in enumerate(pair_of(value) if q == 3 else [value]):
                place, target_lane = margin_moves(g, level, q + offset)[1 if west_type else 0]
                shifted = pltpu.roll(plane_value.astype(F32), (target_lane - place) % side, 1)
                here = (lane >= target_lane) & (lane < target_lane + g.margin(level))
                total = jnp.where(here, shifted, total)
        return total

    fine_part = inner(1, rows)
    target.put(fine_part[:less] + inner(0, less))
    target.put(fine_part[less:])


def margin_moves(g, level, index):
    margin = g.margin(level)
    base = 2 * margin * index + (0 if level else 2 * g.margin(1) * 5)
    return (g.side - margin, base), ((0 if level else g.half_side), base + margin)


def edges_of(g, level, west, east):
    lane = lane_ids(g.side)
    middle = g.side - g.half_side // 2 if level == 0 else g.half_side
    return jnp.where(lane < middle, east, west)


def borrow(g, rows_ref, patch, odd, lent, edge, limits, covered, fine, coarse):
    rows, less = lent_rows(g)
    side = g.side
    lane = lane_ids(side)
    source = Rows(lent)

    def masked(value, bounds, inside):
        ids = lax.broadcasted_iota(jnp.int32, value.shape, 0)
        return jnp.where((ids < bounds) == inside, value, 0.0)

    fine.fric[0] = source.take(rows)
    high = source.take(rows)
    fine.visc[0, pl.ds(PAD, rows), :] = masked(high + source.take(rows), limits[1][0], True)
    for comp in range(2):
        fine.right[comp, 0] = jnp.zeros((rows, side), F32)
        for first in lent_forcing(g):
            value = masked(source.take(16), covered[0] - first, False)
            fine.right[comp, 0, pl.ds(first, 16), :] = value
    first, rest, window = source.take(less), source.take(less), source.take(16)
    inner = source.take(rows)

    def margins(level, q, size):
        indices = (q,) if q < 3 else (3, 4)
        moves = [margin_moves(g, level, index) for index in indices]

        def one(west):
            near = sum(
                pltpu.roll(inner[:size], (places[0] - places[1]) % side, 1)
                for places in (move[0 if west else 1] for move in moves)
            )
            far = []
            for r in range(-(-size // side)):
                part = edge[pl.ds(0, min(side, size - r * side)), :]
                place = moves[0][0 if west else 1][0]
                shift = (place - edge_lane(g, level, q, r)) % side
                far.append(pltpu.roll(part, shift, 1) if shift else part)
            far = jnp.concatenate(far, axis=0) if len(far) > 1 else far[0]
            far = 0.5 * far if q == 3 else far
            return near, far

        (near_west, far_west), (near_east, far_east) = one(True), one(False)
        return edges_of(
            g, level, jnp.where(odd, far_west, near_west), jnp.where(odd, near_east, far_east)
        )

    for comp in range(2):
        fine.right[comp, 1] = masked(margins(1, comp, rows), covered[1], False)
    fine.fric[1] = margins(1, 2, rows)
    fine.visc[1, pl.ds(PAD, rows), :] = masked(margins(1, 3, rows), limits[1][1], True)

    def with_margins(value, q):
        return jnp.where(lane < g.half_side, value, margins(0, q, less))

    coarse.fric[0] = with_margins(first, 2)
    value = with_margins(pltpu.roll(first, g.half_side, 1) + rest, 3)
    coarse.visc[0, pl.ds(PAD, less), :] = masked(value, limits[0][0], True)
    for comp in range(2):
        value = pltpu.roll(window, g.half_side, 1) if comp else window
        value = jnp.concatenate([jnp.zeros((g.half_side, side), F32), value], axis=0)
        coarse.right[comp, 0] = with_margins(value, comp)


def lend_kernel(g, own, other, edge, lent):
    level_here = lax.axis_index("level")
    top = g.levels - 1
    for level in range(top - 1):
        pl.when(level_here == level)(
            lambda level=level: lend(g, level % 2 == 1, own, other, lent)
        )


def fill_pair(g, rows_ref, own, other, edge, levels, wanted, groups):
    level_here = lax.axis_index("level")
    patch = lax.axis_index("patch")
    odd = level_here % 2 == 1
    for west_type in (True, False):

        @pl.when(odd if west_type else jnp.logical_not(odd))
        def _():
            for level in wanted:
                near = near_counts(g, rows_ref, level, patch, odd)
                limits = lane_limits(g, level, near, g.side)
                covered = None
                if level == 1:
                    finer = near_counts(g, rows_ref, 2, patch, odd)
                    covered = lane_limits(g, 1, finer, g.half_side)
                home = (level % 2 == 1) == west_type
                raw = own if home else other
                fill_level(
                    g, level, west_type, levels[level], limits, covered, raw, edge, groups(level)
                )


def fill_kernel(g, rows_ref, own, other, edge, _, __, filled):
    level_here = lax.axis_index("level")
    top = g.levels - 1

    @pl.when(level_here >= top - 1)
    def _():
        levels = dict(zip((top - 1, top), filled))
        fill_pair(g, rows_ref, own, other, edge, levels, (top, top - 1), g.patch_rows)


def down_kernel(
    g, rows_ref, own, other, edge, upper, sums, kept, low_kept, lower, edges, scratch
):
    level_here = lax.axis_index("level")
    patch = lax.axis_index("patch")
    side = g.side
    top = g.levels - 1
    odd = level_here % 2 == 1
    filled = [*lower, *upper]
    kept = [*(Level(None, weight) for weight in low_kept), *kept]
    levels = [merged(merged(a, b), c) for a, b, c in zip(scratch, kept, filled)]

    def limits_of(level):
        return lane_limits(g, level, near_counts(g, rows_ref, level, patch, odd), side)

    @pl.when(level_here >= top - 1)
    def _():
        near = near_counts(g, rows_ref, top, patch, odd)
        covered = lane_limits(g, top - 1, near, g.half_side)
        given = filled[top - 1].right
        for comp in range(2):
            for k in range(g.blocks(top - 1)):
                rest = pl.ds(g.half_side, g.rows(top - 1) - g.half_side)
                levels[top - 1].right[comp, k, rest, :] = given[comp, k, rest, :]

        def set_right(comp, k, row, chunk, value):
            here = pl.ds(row, chunk)
            ids = row + lax.broadcasted_iota(jnp.int32, (chunk, side), 0)
            levels[top - 1].right[comp, k, here, :] = jnp.where(
                ids < covered[k], value, given[comp, k, here, :]
            )

        def keep(comp, k, row, chunk, value):
            (sums if k == 0 else edges)[comp, pl.ds(row, chunk), :] = value

        for level in (top, top - 1):
            d = levels[level]
            clear_level(g, level, d)
            smooth_weights(g, level, d, limits_of(level), 0, g.rows(level), True)
            residual_step(g, level, d, 0, g.rows(level))
            restrict_into(g, level, d, 0, g.rows(level), set_right if level == top else keep)
        sums[2] = joined_edges(g, edges[0], edges[1])

    @pl.when(level_here < top - 1)
    def _():
        fill_pair(g, rows_ref, own, other, edge, levels, (1, 0), g.patch_rows)
        for level, size in zip((1, 0), lent_rows(g)):
            smooth_weights(g, level, levels[level], limits_of(level), 0, size, False)


def bottom_levels(g, rows_ref, patch, odd, start, stop, fine, coarse, new_sums, store_fine):
    side = g.side
    count, chunk = g.blocks(1), g.chunk(1, stop - start)
    clear_level(g, 1, fine)
    if new_sums is not None:
        reach = g.rows(2) // 2
        for comp in range(2):
            for k in range(count):
                here = pl.ds(0, reach)
                fine.right[comp, k, here, :] = fine.right[comp, k, here, :] + new_sums(comp, k)

    def body(row):
        here = pl.ds(start + row, chunk)
        for comp in range(2):
            for k in range(count):
                fine.cells[comp, k, pl.ds(PAD + start + row, chunk), :] = (
                    fine.weight[comp, k, here, :] * fine.right[comp, k, here, :]
                )

    over_rows(stop - start, chunk, body)
    residual_step(g, 1, fine, start, stop)
    near = near_counts(g, rows_ref, 1, patch, odd)
    covered = lane_limits(g, 0, near, g.half_side)

    def smooth_coarse(comp, k, row, size, value):
        here = pl.ds(row, size)
        ids = row + lax.broadcasted_iota(jnp.int32, (size, side), 0)
        value = jnp.where(ids < covered[0], value, coarse.right[comp, 0, here, :])
        value = coarse.weight[comp, 0, here, :] * value
        coarse.cells[comp, 0, here, :] = value

    restrict_into(g, 1, fine, start, stop, smooth_coarse)

    def load(comp, k, row, size):
        return coarse.cells[comp, 0, pl.ds(row, size), :]

    prolong_from(g, 1, fine, lane_limits(g, 1, near, side), start, stop, load)
    corrected_step(g, 1, fine, start, stop, store_fine)


def up_kernel(
    g, rows_ref, sums, lent, edge, filled, kept, mine, theirs, own_rows, coarse_rows, edges, scratch, low, low_fine,
    low_coarse, finer, coarser,
):
    level_here = lax.axis_index("level")
    patch = lax.axis_index("patch")
    side = g.side
    top = g.levels - 1
    odd = level_here % 2 == 1
    levels = [merged(a, b) for a, b in zip(scratch, filled)]
    for level in (top - 1, top):
        levels[level] = merged(levels[level], kept[level - top + 1])

    def limits_of(level):
        return lane_limits(g, level, near_counts(g, rows_ref, level, patch, odd), side)

    def hand_out():
        def write(first, second):
            for k in range(g.half_slots):
                for comp in range(2):
                    first[k, comp] = finer[k, comp]
                    second[k, comp] = coarser[k, comp]

        pl.when(odd)(lambda: write(mine, theirs))
        pl.when(jnp.logical_not(odd))(lambda: write(theirs, mine))

    @pl.when(level_here >= top - 1)
    def _():
        rows, less = lent_rows(g)
        limits = {level: limits_of(level) for level in (0, 1)}
        clear_pads(low_fine.visc, [(k,) for k in range(g.blocks(1))])
        clear_pads(low_coarse.visc, [(k,) for k in range(g.blocks(0))])
        finer_near = near_counts(g, rows_ref, 2, patch, odd)
        covered = lane_limits(g, 1, finer_near, g.half_side)
        borrow(g, rows_ref, patch, odd, lent, edge, limits, covered, low_fine, low_coarse)
        smooth_weights(g, 1, low_fine, limits[1], 0, rows, False)
        smooth_weights(g, 0, low_coarse, limits[0], 0, less, False)

        def store_fine(comp, k, row, chunk, value):
            low[comp, k, pl.ds(row, chunk), :] = value

        bottom_levels(
            g, rows_ref, patch, odd, 0, rows, low_fine, low_coarse,
            level_sums(g, sums, low_fine.weight), store_fine,
        )

        def load_low(comp, k, row, chunk):
            return low[comp, k, pl.ds(row, chunk), :]

        def load_held(comp, k, row, chunk):
            return edges[comp, k, pl.ds(row, chunk), :]

        def store_in(level, out, hold):
            own = g.own(level)

            def store(comp, k, row, chunk, value):
                if hold:
                    edges[comp, k, pl.ds(row, chunk), :] = value
                if k < own:
                    group, place = row // side, row % side
                    out[group * own + k, comp, pl.ds(pl.multiple_of(place, 8), chunk), :] = value

            return store

        for level, load, out in ((top - 1, load_low, coarser), (top, load_held, finer)):
            d = levels[level]
            clear_level(g, level, d)
            rows = g.rows(level)
            prolong_from(g, level, d, limits_of(level), 0, rows, load)
            corrected_step(g, level, d, 0, rows, store_in(level, out, level < top))
        hand_out()

    @pl.when(level_here < top - 1)
    def _():
        rows = g.rows(1)
        first = g.rows(2) // 2
        fine, coarse = levels[1], levels[0]._replace(cells=coarse_rows)
        smooth_weights(g, 1, fine, limits_of(1), first, rows, False)
        smooth_weights(g, 0, coarse, limits_of(0), first // 2, g.rows(0), False)

        def store_fine(comp, k, row, chunk, value):
            if k == 0:
                own_rows[comp, pl.ds(row, chunk), :] = value

        bottom_levels(g, rows_ref, patch, odd, first, rows, fine, coarse, None, store_fine)
        for r in range(rows // 2 // side, g.patch_rows(0)):
            here = pl.ds(r * side, side)
            for comp in range(2):
                coarse_rows[comp, 0, here, :] = (
                    coarse.weight[comp, 0, here, :] * coarse.right[comp, 0, here, :]
                )


def level_sums(g, sums, weight):
    reach = g.rows(2) // 2

    def value(comp, k):
        found = sums[comp] if k == 0 else sums[2]
        if k and comp:
            found = pltpu.roll(found, g.half_side, 1)
        return jnp.where(weight[comp, k, pl.ds(0, reach), :] > 0.0, found, 0.0)

    return value


def low_kernel(
    g, rows_ref, sums, filled, kept, mine_in, theirs_in, own_rows, coarse_rows, mine, theirs, scratch, low_coarse, near_rows
):
    level_here = lax.axis_index("level")
    patch = lax.axis_index("patch")
    side = g.side
    top = g.levels - 1
    odd = level_here % 2 == 1

    @pl.when(level_here >= top - 1)
    def _():
        for k in range(g.half_slots):
            for comp in range(2):
                mine[k, comp] = mine_in[k, comp]
                theirs[k, comp] = theirs_in[k, comp]

    @pl.when(level_here < top - 1)
    def _():
        rows, _ = lent_rows(g)
        done = kept_rows(g)
        fine = merged(Level(filled[1].visc, kept[1]), scratch)
        coarse = merged(Level(None, kept[0], filled[0].right), low_coarse)
        for comp in range(2):
            for k in range(g.blocks(1)):
                fine.right[comp, k] = filled[1].right[comp, k, pl.ds(0, rows), :]

        def store_fine(comp, k, row, chunk, value):
            if k == 0:
                near_rows[comp, pl.ds(row, chunk), :] = value

        bottom_levels(
            g, rows_ref, patch, odd, 0, rows, fine, coarse,
            level_sums(g, sums, fine.weight), store_fine,
        )
        lane = lane_ids(side)
        size = rows // 2
        ids = lax.broadcasted_iota(jnp.int32, (size, side), 0)

        def coarse_group(comp, r):
            value = coarse_rows[comp, 0, pl.ds(r * side, side), :]
            if r:
                return value
            near = coarse.cells[comp, 0, pl.ds(0, size), :]
            near = jnp.where(ids < done // 2, near, value[:size])
            return jnp.concatenate([near, value[size:]], axis=0)

        def write(first, second):
            for comp in range(2):
                first[0, comp] = near_rows[comp, pl.ds(0, side), :]
                for r in range(1, g.patch_rows(1)):
                    first[r, comp] = own_rows[comp, pl.ds(r * side, side), :]
                first[1, comp, pl.ds(0, done - side), :] = near_rows[
                    comp, pl.ds(side, done - side), :
                ]
                for k in range(g.half_slots):
                    high = pltpu.roll(coarse_group(comp, k + g.half_slots), g.half_side, 1)
                    second[k, comp] = jnp.where(lane < g.half_side, coarse_group(comp, k), high)

        pl.when(odd)(lambda: write(mine, theirs))
        pl.when(jnp.logical_not(odd))(lambda: write(theirs, mine))


def join_kernel(g, mine, given, speed, fric, adjoint, gradient):
    level_here = lax.axis_index("level")
    lane = lane_ids(g.side)

    def put(slot, parts):
        for comp in range(2):
            adjoint[slot, comp] = parts[comp]
        total = speed[slot, 0].astype(F32) * parts[0] + speed[slot, 1].astype(F32) * parts[1]
        gradient[slot] = (-(fric[slot].astype(F32) * total)).astype(BF16)

    def join_level(level):
        if level == 0:
            for k in range(g.half_slots):
                low = []
                high = []
                for comp in range(2):
                    west, east = given[k, comp], mine[k, comp]
                    low.append(
                        jnp.where(lane < g.half_side, west, pltpu.roll(east, g.half_side, 1))
                    )
                    high.append(
                        jnp.where(lane < g.half_side, pltpu.roll(west, g.half_side, 1), east)
                    )
                put(k, low)
                put(k + g.half_slots, high)
            return
        own = g.own(level)
        west_half, east_half = (mine, given) if level % 2 == 1 else (given, mine)
        for r in range(g.patch_rows(level)):
            for k in range(2 * own):
                source = west_half if k < own else east_half
                put(
                    r * g.columns(level) + k,
                    [source[r * own + k % own, comp] for comp in range(2)],
                )

    for level in range(g.levels):
        pl.when(level_here == level)(lambda level=level: join_level(level))


def run_kernel(body, ins, outs, scratch, grant=VMEM_BYTES):
    in_trees = [jax.tree.flatten(tree) for tree, _ in ins]
    out_trees = [jax.tree.flatten(tree) for tree, _ in outs]
    scratch_trees = [jax.tree.flatten(tree) for tree in scratch]
    sizes = [len(leaves) for leaves, _ in in_trees + out_trees + scratch_trees]
    shapes = [tree for _, tree in in_trees + out_trees + scratch_trees]

    def kernel(*refs):
        given = []
        first = 0
        for size, shape in zip(sizes, shapes):
            given.append(jax.tree.unflatten(shape, refs[first : first + size]))
            first += size
        body(*given)

    def specs(groups, trees):
        return [
            pl.BlockSpec(memory_space=space)
            for (_, space), (leaves, _) in zip(groups, trees)
            for _ in leaves
        ]

    results = pl.pallas_call(
        kernel,
        out_shape=[leaf for leaves, _ in out_trees for leaf in leaves],
        in_specs=specs(ins, in_trees),
        out_specs=specs(outs, out_trees),
        scratch_shapes=[leaf for leaves, _ in scratch_trees for leaf in leaves],
        compiler_params=pltpu.CompilerParams(vmem_limit_bytes=grant),
    )(*[leaf for leaves, _ in in_trees for leaf in leaves])
    answer = []
    first = 0
    for leaves, shape in out_trees:
        answer.append(jax.tree.unflatten(shape, results[first : first + len(leaves)]))
        first += len(leaves)
    return answer


def moved(value, g, step):
    pairs = []
    for patch in range(g.patches):
        for level in range(g.levels):
            to_patch, to_level = step(patch, level)
            if 0 <= to_patch < g.patches and 0 <= to_level < g.levels:
                pairs.append((patch * g.levels + level, to_patch * g.levels + to_level))
    return lax.ppermute(value, ("patch", "level"), pairs)


def per_device(forcing, velocity, viscosity, friction, patch_rows):
    g = Layout(
        forcing.shape[1], forcing.shape[-1], lax.axis_size("level"), lax.axis_size("patch")
    )
    side = g.side
    top = g.levels - 1
    force, speed, visc, fric = forcing[0], velocity[0], viscosity[0], friction[0]
    make = jax.ShapeDtypeStruct
    vmem = pltpu.VMEM
    block = make((side, side), F32)
    half = make((g.half_slots, 2, side, side), F32)
    three = make((3, side, side), F32)

    def array(level, rows, kind, comps, pad):
        return level_array(g, g.blocks(level), rows, kind, comps, pad)

    own = (force, visc, fric)
    other = tuple(moved(value, g, lambda p, l: (p, l ^ 1)) for value in own)
    (edge,) = run_kernel(
        lambda *refs: first_edge_kernel(g, *refs),
        [(own, pltpu.HBM)],
        [(block, VM)],
        [
            pltpu.SemaphoreType.DMA((3 * g.slots,)),
            tuple(vmem(value.shape, value.dtype) for value in own),
        ],
        FIRST_BYTES,
    )
    (edge,) = run_kernel(
        lambda *refs: edge_kernel(g, *refs), [(edge, VM), (other, VM)], [(block, VM)], []
    )
    (lent_here,) = run_kernel(
        lambda *refs: lend_kernel(g, *refs),
        [(own, VM), (other, VM), (edge, VM)],
        [(make((lent_size(g), side), BF16), VM)],
        [],
    )
    edge_here = edge
    step = lambda l: -1 if l % 2 else 1
    edge = moved(edge_here, g, lambda p, l: (p + step(l), l ^ 1))
    edge_low = moved(edge_here, g, lambda p, l: (p + step(l), (l ^ 1) + 2))
    lent = moved(lent_here, g, lambda p, l: (p, l + 2))

    fields = [
        Level(
            array(level, g.rows(level), make, False, True),
            None,
            right=array(level, g.rows(level), make, True, False),
            fric=array(level, g.rows(level), make, False, False),
        )
        for level in range(g.levels)
    ]
    rows, less = lent_rows(g)
    given = [(patch_rows, SM), (own, VM), (other, VM), (edge, VM)]

    (upper,) = run_kernel(
        lambda *refs: fill_kernel(g, *refs),
        [*given, (edge_low, VM), (lent_here, VM)],
        [(fields[top - 1 :], VM)],
        [],
    )

    def kept_of(level):
        two = array(level, g.rows(level), make, True, False)
        return Level(None, two, held=two)

    low_weights = [array(0, less, make, True, False), array(1, rows, make, True, False)]

    def down_scratch(level):
        if level < top - 1:
            return Level(None, None)
        both = array(level, g.rows(level), vmem, True, False)
        more = dict(right=both) if level < top else {}
        return Level(None, None, left=both, **more, **step_arrays(g, level, g.rows(level)))

    sums, kept, low_kept, lower = run_kernel(
        lambda *refs: down_kernel(g, *refs),
        [*given, (upper, VM)],
        [
            (three, VM),
            ([kept_of(level) for level in (top - 1, top)], VM),
            (low_weights, VM),
            (fields[: top - 1], VM),
        ],
        [vmem((2, side, side), F32), [down_scratch(level) for level in range(g.levels)]],
    )
    filled = [*lower, *upper]
    sums_there = moved(sums, g, lambda p, l: (p, l - 2))

    def up_scratch(level):
        both = array(level, g.rows(level), vmem, True, False)
        if level == 0:
            return Level(None, both)
        steps = step_arrays(g, level, g.rows(level))
        if level == 1:
            return Level(None, both, held=both, left=both, **steps)
        return Level(None, None, **steps)

    low_both = array(1, rows, vmem, True, False)
    low_steps = dict(held=low_both, left=low_both, right=low_both, **step_arrays(g, 1, rows))
    mine, theirs, own_rows, coarse_rows = run_kernel(
        lambda *refs: up_kernel(g, *refs),
        [
            (patch_rows, SM),
            (sums, VM),
            (lent, VM),
            (edge_low, VM),
            (filled, VM),
            (kept, VM),
        ],
        [
            (half, VM),
            (half, VM),
            (make((2, g.rows(1), side), F32), VM),
            (make((2, 1, g.rows(0), side), F32), VM),
        ],
        [
            array(top - 1, g.rows(top - 1), vmem, True, False),
            [up_scratch(level) for level in range(g.levels)],
            low_both,
            Level(
                array(1, rows, vmem, False, True),
                low_both,
                fric=array(1, rows, vmem, False, False),
                **low_steps,
            ),
            Level(
                array(0, less, vmem, False, True),
                array(0, less, vmem, True, False),
                right=array(0, less, vmem, True, False),
                fric=array(0, less, vmem, False, False),
                cells=array(0, less, vmem, True, False),
            ),
            vmem(half.shape, F32),
            vmem(half.shape, F32),
        ],
    )
    mine, theirs = run_kernel(
        lambda *refs: low_kernel(g, *refs),
        [
            (patch_rows, SM),
            (sums_there, VM),
            (filled[:2], VM),
            (low_kept, VM),
            (mine, VM),
            (theirs, VM),
            (own_rows, VM),
            (coarse_rows, VM),
        ],
        [(half, VM), (half, VM)],
        [
            Level(None, None, **low_steps),
            Level(None, None, cells=array(0, less, vmem, True, False)),
            vmem((2, rows, side), F32),
        ],
    )
    received = moved(theirs, g, lambda p, l: (p, l ^ 1))
    adjoint, gradient = run_kernel(
        lambda *refs: join_kernel(g, *refs),
        [(mine, VM), (received, VM), (speed, VM), (fric, VM)],
        [
            (make((g.slots, 2, side, side), F32), VM),
            (make((g.slots, side, side), BF16), VM),
        ],
        [],
    )
    return (adjoint[None], gradient[None])


def solution(mesh):
    fields = P("level", "patch")
    return jax.shard_map(
        per_device,
        mesh=mesh,
        in_specs=(fields, fields, fields, fields, P()),
        out_specs=(fields, fields),
        check_vma=False,
    )
```

```python
from typing import Any, NamedTuple

import jax
import jax.numpy as jnp
from jax import lax
from jax.experimental import pallas as pl
from jax.experimental.pallas import tpu as pltpu
from jax.sharding import PartitionSpec as P

relaxation = 0.5
PAD = 8
LOW, HIGH, EDGES = 0, 1, 2
VM, SM = pltpu.VMEM, pltpu.SMEM
F32 = jnp.float32
BF16 = jnp.bfloat16
VMEM_BYTES = 30 * 2**20
FIRST_BYTES = 60 * 2**20


class Layout:
    def __init__(self, slots, side, levels, patches):
        self.slots = slots
        self.side = side
        self.levels = levels
        self.patches = patches
        self.half_slots = slots // 2
        self.half_side = side // 2
        self.span = 2 * slots

    def columns(self, level):
        return 1 << level

    def patch_rows(self, level):
        return self.slots >> level

    def rows(self, level):
        return self.patch_rows(level) * self.side

    def margin(self, level):
        return 2 << level

    def own(self, level):
        return max(1, (1 << level) // 2)

    def blocks(self, level):
        return self.own(level) + (1 if level > 0 else 0)

    def chunk(self, level, rows):
        size = 8 * max(1, 112 // self.blocks(level))
        while rows % size or (rows % self.side == 0 and self.side % size):
            size -= 8
        return size


def lane_ids(side):
    return lax.broadcasted_iota(jnp.int32, (1, side), 1)


def near_counts(g, rows_ref, level, patch, odd):
    own = rows_ref[level, patch]
    east = jnp.where(
        patch + 1 < g.patches, rows_ref[level, jnp.minimum(patch + 1, g.patches - 1)], 0
    )
    west = jnp.where(patch > 0, rows_ref[level, jnp.maximum(patch - 1, 0)], 0)
    return own, jnp.where(odd, own, east), jnp.where(odd, west, own)


def lane_limits(g, level, counts, cells):
    own, east, west = (value * cells for value in counts)
    lane = lane_ids(g.side)
    margin = g.margin(level)
    first = 0 if level > 0 else g.half_side
    edges = jnp.where(
        (lane >= first) & (lane < first + margin), east, jnp.where(lane >= g.side - margin, west, 0)
    )
    if level == 0:
        return [jnp.where(lane < g.half_side, own, edges)]
    return [jnp.full((1, g.side), own, jnp.int32)] * g.own(level) + [edges]


def one_side(g, values, east):
    count = len(values)
    turned = [pltpu.roll(value, g.side - 1 if east else 1, 1) for value in values]
    if count == 1:
        return turned
    lane = lax.broadcasted_iota(jnp.int32, values[0].shape, 1)
    last = lane == (g.side - 1 if east else 0)
    step = 1 if east else -1
    return [jnp.where(last, turned[(k + step) % count], turned[k]) for k in range(count)]


def both_sides(g, values):
    return one_side(g, values, True), one_side(g, values, False)


def over_rows(rows, chunk, body):
    def step(index, carry):
        body(pl.multiple_of(index * chunk, chunk))
        return carry

    lax.fori_loop(0, rows // chunk, step, 0)


def clear_pads(ref, lead):
    width = ref.shape[-1]
    last = ref.shape[-2]
    for index in lead:
        ref[index + (slice(0, PAD), slice(None))] = jnp.zeros((PAD, width), F32)
        ref[index + (slice(last - PAD, last), slice(None))] = jnp.zeros((PAD, width), F32)


def off_diagonal_rows(g, d, row, size, count):
    here = pl.ds(row, size)
    inner = pl.ds(PAD + row, size)
    centre = [[d.cells[comp, k, inner, :] for k in range(count)] for comp in range(2)]
    beside = [both_sides(g, centre[comp]) for comp in range(2)]
    products = []
    for k in range(count):
        visc = d.visc[k, inner, :]
        half = 0.5 * visc
        (u, v) = (centre[comp][k] for comp in range(2))
        (u_e, u_w), (v_e, v_w) = ((beside[c][0][k], beside[c][1][k]) for c in range(2))
        u_n, v_n = (d.cells[c, k, pl.ds(PAD + row + 1, size), :] for c in range(2))
        u_s, v_s = (d.cells[c, k, pl.ds(PAD + row - 1, size), :] for c in range(2))
        one_u, one_v = visc * u, visc * v
        four_u, four_v = 4.0 * one_u, 4.0 * one_v
        cross_u, cross_v = half * (v_e - v_w), visc * (u_e - u_w)
        d.north[0, k, inner, :] = one_u + cross_u
        d.south[0, k, inner, :] = one_u - cross_u
        d.north[1, k, inner, :] = four_v + cross_v
        d.south[1, k, inner, :] = four_v - cross_v
        cross_u, cross_v = visc * (v_n - v_s), half * (u_n - u_s)
        products.append(
            (
                four_u + cross_u,
                four_u - cross_u,
                one_v + cross_v,
                one_v - cross_v,
                visc * (4.0 * (u_e + u_w) + (u_n + u_s)),
                visc * (4.0 * (v_n + v_s) + (v_e + v_w)),
            )
        )
    for comp in range(2):
        east = one_side(g, [item[2 * comp] for item in products], True)
        west = one_side(g, [item[2 * comp + 1] for item in products], False)
        for k in range(count):
            d.part[comp, k, here, :] = products[k][4 + comp] + east[k] + west[k]


def off_diagonal_step(g, level, d, start, stop):
    count = g.blocks(level)
    chunk = g.chunk(level, stop - start)

    def body(row):
        for step in range(0, chunk, 8):
            off_diagonal_rows(g, d, start + row + step, 8, count)

    over_rows(stop - start, chunk, body)


def off_diagonal(d, comp, k, row, chunk):
    return (
        d.part[comp, k, pl.ds(row, chunk), :]
        + d.north[comp, k, pl.ds(PAD + row + 1, chunk), :]
        + d.south[comp, k, pl.ds(PAD + row - 1, chunk), :]
    )


def smooth_weights(g, level, d, limits, start, stop, from_zero):
    count = g.blocks(level)
    chunk = g.chunk(level, stop - start)

    def some_rows(row):
        here = pl.ds(row, 8)
        inner = pl.ds(PAD + row, 8)
        centre = [d.visc[k, inner, :] for k in range(count)]
        east, west = both_sides(g, centre)
        for k in range(count):
            north = d.visc[k, pl.ds(PAD + row + 1, 8), :]
            south = d.visc[k, pl.ds(PAD + row - 1, 8), :]
            friction = d.fric[k, here, :]
            twice = 2.0 * centre[k]
            along_row = twice + east[k] + west[k]
            along_col = twice + north + south
            live = jnp.broadcast_to(limits[k], (8, g.side)) > row
            diag_u = 4.0 * along_row + along_col + friction
            diag_v = 4.0 * along_col + along_row + friction
            for comp, diag in ((0, diag_u), (1, diag_v)):
                guess = pl.reciprocal(diag, approx=True)
                weight = guess * (2.0 * relaxation - relaxation * diag * guess)
                weight = jnp.where(live, weight, 0.0)
                d.weight[comp, k, here, :] = weight
                if from_zero:
                    d.cells[comp, k, inner, :] = weight * d.right[comp, k, here, :]

    def body(row):
        for step in range(0, chunk, 8):
            some_rows(start + row + step)

    over_rows(stop - start, chunk, body)


def residual_step(g, level, d, start, stop):
    count = g.blocks(level)
    chunk = g.chunk(level, stop - start)
    off_diagonal_step(g, level, d, start, stop)

    def body(row):
        row = row + start
        here = pl.ds(row, chunk)
        for comp in range(2):
            for k in range(count):
                weight = d.weight[comp, k, here, :]
                left = (1.0 - relaxation) * d.right[comp, k, here, :] + off_diagonal(
                    d, comp, k, row, chunk
                )
                left = jnp.where(weight > 0.0, left, 0.0)
                d.left[comp, k, here, :] = left
                d.held[comp, k, here, :] = (
                    d.cells[comp, k, pl.ds(PAD + row, chunk), :] + weight * left
                )

    over_rows(stop - start, chunk, body)


def corrected_step(g, level, d, start, stop, store):
    count = g.blocks(level)
    chunk = g.chunk(level, stop - start)
    off_diagonal_step(g, level, d, start, stop)

    def body(row):
        row = row + start
        here = pl.ds(row, chunk)
        for comp in range(2):
            for k in range(count):
                value = (
                    d.held[comp, k, here, :]
                    + (1.0 - relaxation) * d.cells[comp, k, pl.ds(PAD + row, chunk), :]
                    + d.weight[comp, k, here, :] * off_diagonal(d, comp, k, row, chunk)
                )
                store(comp, k, row, chunk, value)

    over_rows(stop - start, chunk, body)


def pairings(g, fine):
    if fine == 1:
        return [[(0, LOW), (1, HIGH)]]
    parts = [[(2 * k, LOW), (2 * k + 1, HIGH)] for k in range(g.own(fine) // 2)]
    return parts + [[(g.own(fine), EDGES)]]


def target_lane(g, part, fine_lane):
    halved = jnp.right_shift(fine_lane, 1)
    if part == LOW:
        return halved
    if part == HIGH:
        return g.half_side + halved
    return halved + jnp.where(fine_lane >= g.half_side, g.half_side, 0)


def sum_matrix(g, part):
    fine = lax.broadcasted_iota(jnp.int32, (g.side, g.side), 0)
    coarse = lax.broadcasted_iota(jnp.int32, (g.side, g.side), 1)
    return jnp.where(target_lane(g, part, fine) == coarse, 1.0, 0.0).astype(BF16)


def copy_matrix(g, part):
    coarse = lax.broadcasted_iota(jnp.int32, (g.side, g.side), 0)
    fine = lax.broadcasted_iota(jnp.int32, (g.side, g.side), 1)
    return jnp.where(target_lane(g, part, fine) == coarse, 1.0, 0.0).astype(BF16)


def split_dot(values, matrix):
    high = values.astype(BF16)
    rest = (values - high.astype(F32)).astype(BF16)
    return jnp.dot(high, matrix, preferred_element_type=F32) + jnp.dot(
        rest, matrix, preferred_element_type=F32
    )


def restrict_into(g, fine, d, start, stop, store):
    rows = stop - start
    chunk = min(rows // 2, g.half_side)
    if (rows // 2) % chunk:
        chunk = rows // 2
    parts = pairings(g, fine)
    matrices = {part: sum_matrix(g, part) for members in parts for _, part in members}

    def body(row):
        row = row + start // 2
        for comp in range(2):
            for coarse, members in enumerate(parts):
                total = None
                for k, part in members:
                    first = d.left[comp, k, pl.ds(2 * row, chunk, stride=2), :]
                    second = d.left[comp, k, pl.ds(2 * row + 1, chunk, stride=2), :]
                    term = split_dot(first + second, matrices[part])
                    total = term if total is None else total + term
                store(comp, coarse, row, chunk, total)

    over_rows(rows // 2, chunk, body)


def prolong_from(g, fine, d, limits, start, stop, load):
    rows = stop - start
    chunk = min(rows // 2, g.half_side)
    if (rows // 2) % chunk:
        chunk = rows // 2
    parts = pairings(g, fine)
    matrices = {part: copy_matrix(g, part) for members in parts for _, part in members}

    def body(row):
        row = row + start // 2
        ids = 2 * (row + lax.broadcasted_iota(jnp.int32, (chunk, g.side), 0))
        for comp in range(2):
            for coarse, members in enumerate(parts):
                value = load(comp, coarse, row, chunk)
                for k, part in members:
                    spread = jnp.where(ids < limits[k], split_dot(value, matrices[part]), 0.0)
                    d.cells[comp, k, pl.ds(PAD + 2 * row, chunk, stride=2), :] = spread
                    d.cells[comp, k, pl.ds(PAD + 2 * row + 1, chunk, stride=2), :] = spread

    over_rows(rows // 2, chunk, body)


def sums_groups(g):
    count = g.side // (4 * g.margin(1))
    return count, g.rows(2) // 2 // count


def sums_moves(g, group):
    margin = g.margin(1)
    base = 4 * margin * group
    return (base + margin, base), (base + 3 * margin, base + 2 * margin)


def packed_sums(g, edges):
    lane = lane_ids(g.side)
    count, size = sums_groups(g)
    total = jnp.zeros((size, g.side), F32)
    for group in range(count):
        for comp, (shift, first) in enumerate(sums_moves(g, group)):
            value = pltpu.roll(edges[comp, pl.ds(group * size, size), :], shift % g.side, 1)
            inside = (lane >= first) & (lane < first + 2 * g.margin(1))
            total = jnp.where(inside, value, total)
    return total


def plane(raw, q, slot):
    force, visc, fric = raw
    if q < 2:
        return force[slot, q].astype(F32)
    return (fric if q == 2 else visc)[slot].astype(F32)


def edge_lane(g, level, q, r):
    return (0 if level % 2 else g.half_side) + q * g.span + r * g.margin(level)


def packed_edge(g, here, level, patch_of):
    side = g.side
    lane = lane_ids(side)
    margin = g.margin(level)
    start = 0 if here % 2 else side - margin
    total = jnp.zeros((side, side), F32)
    for r in range(g.patch_rows(level)):
        for q in range(4):
            base = edge_lane(g, level, q, r)
            value = patch_of(q, r)
            if (base - start) % side:
                value = pltpu.roll(value, (base - start) % side, 1)
            total = jnp.where((lane >= base) & (lane < base + margin), value, total)
    return total


def edge_column(g, here, level):
    return 0 if here % 2 else g.columns(level) - 1


def first_edge_kernel(g, own, edge, sems, held):
    level_here = lax.axis_index("level")

    def pack(level):
        copies = Copies(sems)
        rows = g.patch_rows(level)
        if g.columns(level) == 1:
            for source, target in zip(own, held):
                copies.start(source, target)
        else:
            for r in range(rows):
                slot = r * g.columns(level) + edge_column(g, level, level)
                for source, target in zip(own, held):
                    copies.start(source.at[slot], target.at[r])
        copies.finish()
        edge[...] = packed_edge(g, level, level, lambda q, r: plane(held, q, r))

    for level in range(g.levels):
        pl.when(level_here == level)(lambda level=level: pack(level))


def edge_kernel(g, first, other, edge):
    level_here = lax.axis_index("level")

    def pack(here):
        level = here ^ 1
        column = edge_column(g, here, level)

        def patch_of(q, r):
            return plane(other, q, r * g.columns(level) + column)

        edge[...] = first[...] + packed_edge(g, here, level, patch_of)

    for here in range(g.levels):
        pl.when(level_here == here)(lambda here=here: pack(here))


def fill_level(g, level, west_type, d, limits, covered, raw, edge, groups):
    side = g.side
    margin = g.margin(level)
    own = g.own(level)
    columns = g.columns(level)
    lane = lane_ids(side)

    def outer(q, r, place):
        shift = (place - edge_lane(g, level, q, r)) % side
        return pltpu.roll(edge[...], shift, 1) if shift else edge[...]

    def store(q, k, r, value):
        here = pl.ds(r * side, side)
        if q < 2:
            if covered is not None:
                ids = r * side + lax.broadcasted_iota(jnp.int32, (side, side), 0)
                value = jnp.where(ids < covered[k], 0.0, value)
            d.right[q, k, here, :] = value
        elif q == 2:
            d.fric[k, here, :] = value
        else:
            d.visc[k, pl.ds(PAD + r * side, side), :] = jnp.where(
                limits[k] > r * side, 0.5 * value, 0.0
            )

    clear_pads(d.visc, [(k,) for k in range(g.blocks(level))])
    for r in range(groups):
        for q in range(4):
            if level == 0 and west_type:
                west = outer(q, r, side - margin)
                store(q, 0, r, jnp.where(lane >= side - margin, west, plane(raw, q, r)))
            elif level == 0:
                value = pltpu.roll(plane(raw, q, r), g.half_side, 1)
                here = (lane >= g.half_side) & (lane < g.half_side + margin)
                store(q, 0, r, jnp.where(here, outer(q, r, g.half_side), value))
            else:
                for k in range(own):
                    store(q, k, r, plane(raw, q, r * columns + k + (0 if west_type else own)))
                if west_type:
                    east = plane(raw, q, r * columns + own)
                    west = outer(q, r, side - margin)
                else:
                    east = outer(q, r, 0)
                    west = plane(raw, q, r * columns + own - 1)
                store(q, own, r, jnp.where(lane < g.half_side, east, west))


class Level(NamedTuple):
    visc: Any
    weight: Any
    right: Any = None
    held: Any = None
    fric: Any = None
    cells: Any = None
    part: Any = None
    north: Any = None
    south: Any = None
    left: Any = None


def level_array(g, count, rows, make, comps, pad):
    shape = (count, rows + (2 * PAD if pad else 0), g.side)
    return make((2, *shape) if comps else shape, F32)


def step_arrays(g, level, rows):
    count = g.blocks(level)
    padded = level_array(g, count, rows, pltpu.VMEM, True, True)
    return dict(
        cells=padded,
        part=level_array(g, count, rows, pltpu.VMEM, True, False),
        north=padded,
        south=padded,
    )


def clear_level(g, level, d):
    blocks = range(g.blocks(level))
    both = [(c, k) for c in range(2) for k in blocks]
    for ref in (d.cells, d.north, d.south):
        clear_pads(ref, both)


def merged(first, second):
    return Level(*[b if a is None else a for a, b in zip(first, second)])


class Copies:
    def __init__(self, sems, first=0):
        self.sems = sems
        self.used = first
        self.open = []

    def start(self, source, target):
        copy = pltpu.make_async_copy(source, target, self.sems.at[self.used])
        self.used += 1
        copy.start()
        self.open.append(copy)

    def finish(self):
        for copy in self.open:
            copy.wait()
        self.open = []


def low_rows(g):
    return g.rows(2) // 2 + 2 * PAD


def kept_rows(g):
    return g.rows(2) // 2 + PAD


def lent_rows(g):
    return low_rows(g), -(-low_rows(g) // 2 // 16) * 16


def lent_forcing(g):
    return [count * g.half_side for count in range(1, g.patch_rows(2) + 1)]


def lent_size(g):
    rows, less = lent_rows(g)
    return 4 * rows + 2 * 16 * len(lent_forcing(g)) + 2 * less + 16


def pair_of(visc):
    high = visc.astype(BF16)
    return [high, (visc - high.astype(F32)).astype(BF16)]


class Rows:
    def __init__(self, ref):
        self.ref = ref
        self.place = 0

    def put(self, value):
        size = value.shape[0]
        self.ref[pl.ds(self.place, size), :] = value.astype(BF16)
        self.place += size

    def take(self, size):
        value = self.ref[pl.ds(self.place, size), :].astype(F32)
        self.place += size
        return value


def side_by_side(g, low, high):
    lane = lane_ids(g.side)
    return jnp.where(
        lane < g.half_side, low.astype(F32), pltpu.roll(high.astype(F32), g.half_side, 1)
    )


def lend(g, west_type, own, other, out):
    rows, less = lent_rows(g)
    side = g.side
    fine, coarse = (own, other) if west_type else (other, own)
    target = Rows(out)

    def some_rows(raw, q, slot, first, size):
        here = pl.ds(first, size)
        force, visc, fric = raw
        value = force[slot, q, here, :] if q < 2 else (fric if q == 2 else visc)[slot, here, :]
        return 0.5 * value if q == 3 else value

    def fine_rows(q, first, size, column=0 if west_type else g.own(1)):
        parts = []
        while size:
            group, place = first // side, first % side
            part = min(size, side - place)
            slot = group * g.columns(1) + column
            parts.append(some_rows(fine, q, slot, place, part))
            first, size = first + part, size - part
        return parts

    for part in fine_rows(2, 0, rows):
        target.put(part)
    pairs = [pair_of(part) for part in fine_rows(3, 0, rows)]
    for index in range(2):
        for pair in pairs:
            target.put(pair[index])
    for comp in range(2):
        for first in lent_forcing(g):
            for part in fine_rows(comp, first, 16):
                target.put(part)

    def coarse_rows(q, first, size):
        value = some_rows(coarse, q, 0, first, size).astype(F32)
        return value if west_type else pltpu.roll(value, g.half_side, 1)

    high, rest = pair_of(coarse_rows(3, 0, less))
    target.put(side_by_side(g, coarse_rows(2, 0, less), high))
    target.put(rest)
    target.put(
        side_by_side(g, coarse_rows(0, g.half_side, 16), coarse_rows(1, g.half_side, 16))
    )
    lane = lane_ids(side)

    def inner(level, size):
        column = g.own(1) if west_type else g.own(1) - 1
        total = jnp.zeros((size, side), F32)
        for q in range(4):
            if level:
                parts = fine_rows(q, 0, size, column)
                value = jnp.concatenate([part.astype(F32) for part in parts], axis=0)
            else:
                value = coarse_rows(q, 0, size)
            for offset, plane_value in enumerate(pair_of(value) if q == 3 else [value]):
                place, target_lane = margin_moves(g, level, q + offset)[1 if west_type else 0]
                shifted = pltpu.roll(plane_value.astype(F32), (target_lane - place) % side, 1)
                here = (lane >= target_lane) & (lane < target_lane + g.margin(level))
                total = jnp.where(here, shifted, total)
        return total

    fine_part = inner(1, rows)
    target.put(fine_part[:less] + inner(0, less))
    target.put(fine_part[less:])


def margin_moves(g, level, index):
    margin = g.margin(level)
    base = 2 * margin * index + (0 if level else 2 * g.margin(1) * 5)
    return (g.side - margin, base), ((0 if level else g.half_side), base + margin)


def edges_of(g, level, west, east):
    lane = lane_ids(g.side)
    middle = g.side - g.half_side // 2 if level == 0 else g.half_side
    return jnp.where(lane < middle, east, west)


def borrow(g, rows_ref, patch, odd, lent, edge, limits, covered, fine, coarse):
    rows, less = lent_rows(g)
    side = g.side
    lane = lane_ids(side)
    source = Rows(lent)

    def masked(value, bounds, inside):
        ids = lax.broadcasted_iota(jnp.int32, value.shape, 0)
        return jnp.where((ids < bounds) == inside, value, 0.0)

    fine.fric[0] = source.take(rows)
    high = source.take(rows)
    fine.visc[0, pl.ds(PAD, rows), :] = masked(high + source.take(rows), limits[1][0], True)
    for comp in range(2):
        fine.right[comp, 0] = jnp.zeros((rows, side), F32)
        for first in lent_forcing(g):
            value = masked(source.take(16), covered[0] - first, False)
            fine.right[comp, 0, pl.ds(first, 16), :] = value
    first, rest, window = source.take(less), source.take(less), source.take(16)
    inner = source.take(rows)

    def margins(level, q, size):
        indices = (q,) if q < 3 else (3, 4)
        moves = [margin_moves(g, level, index) for index in indices]

        def one(west):
            near = sum(
                pltpu.roll(inner[:size], (places[0] - places[1]) % side, 1)
                for places in (move[0 if west else 1] for move in moves)
            )
            far = []
            for r in range(-(-size // side)):
                part = edge[pl.ds(0, min(side, size - r * side)), :]
                place = moves[0][0 if west else 1][0]
                shift = (place - edge_lane(g, level, q, r)) % side
                far.append(pltpu.roll(part, shift, 1) if shift else part)
            far = jnp.concatenate(far, axis=0) if len(far) > 1 else far[0]
            far = 0.5 * far if q == 3 else far
            return near, far

        (near_west, far_west), (near_east, far_east) = one(True), one(False)
        return edges_of(
            g, level, jnp.where(odd, far_west, near_west), jnp.where(odd, near_east, far_east)
        )

    for comp in range(2):
        fine.right[comp, 1] = masked(margins(1, comp, rows), covered[1], False)
    fine.fric[1] = margins(1, 2, rows)
    fine.visc[1, pl.ds(PAD, rows), :] = masked(margins(1, 3, rows), limits[1][1], True)

    def with_margins(value, q):
        return jnp.where(lane < g.half_side, value, margins(0, q, less))

    coarse.fric[0] = with_margins(first, 2)
    value = with_margins(pltpu.roll(first, g.half_side, 1) + rest, 3)
    coarse.visc[0, pl.ds(PAD, less), :] = masked(value, limits[0][0], True)
    for comp in range(2):
        value = pltpu.roll(window, g.half_side, 1) if comp else window
        value = jnp.concatenate([jnp.zeros((g.half_side, side), F32), value], axis=0)
        coarse.right[comp, 0] = with_margins(value, comp)


def lend_kernel(g, own, other, edge, lent):
    level_here = lax.axis_index("level")
    top = g.levels - 1
    for level in range(top - 1):
        pl.when(level_here == level)(
            lambda level=level: lend(g, level % 2 == 1, own, other, lent)
        )


def fill_pair(g, rows_ref, own, other, edge, levels, wanted, groups):
    level_here = lax.axis_index("level")
    patch = lax.axis_index("patch")
    odd = level_here % 2 == 1
    for west_type in (True, False):

        @pl.when(odd if west_type else jnp.logical_not(odd))
        def _():
            for level in wanted:
                near = near_counts(g, rows_ref, level, patch, odd)
                limits = lane_limits(g, level, near, g.side)
                covered = None
                if level == 1:
                    finer = near_counts(g, rows_ref, 2, patch, odd)
                    covered = lane_limits(g, 1, finer, g.half_side)
                home = (level % 2 == 1) == west_type
                raw = own if home else other
                fill_level(
                    g, level, west_type, levels[level], limits, covered, raw, edge, groups(level)
                )


def fill_kernel(g, rows_ref, own, other, edge, _, __, filled):
    level_here = lax.axis_index("level")
    top = g.levels - 1

    @pl.when(level_here >= top - 1)
    def _():
        levels = dict(zip((top - 1, top), filled))
        fill_pair(g, rows_ref, own, other, edge, levels, (top, top - 1), g.patch_rows)


def down_kernel(
    g, rows_ref, own, other, edge, upper, sums, kept, low_kept, lower, edges, scratch
):
    level_here = lax.axis_index("level")
    patch = lax.axis_index("patch")
    side = g.side
    top = g.levels - 1
    odd = level_here % 2 == 1
    filled = [*lower, *upper]
    kept = [*(Level(None, weight) for weight in low_kept), *kept]
    levels = [merged(merged(a, b), c) for a, b, c in zip(scratch, kept, filled)]

    def limits_of(level):
        return lane_limits(g, level, near_counts(g, rows_ref, level, patch, odd), side)

    @pl.when(level_here >= top - 1)
    def _():
        near = near_counts(g, rows_ref, top, patch, odd)
        covered = lane_limits(g, top - 1, near, g.half_side)
        given = filled[top - 1].right
        reach = g.rows(2) // 2
        for comp in range(2):
            for k in range(g.blocks(top - 1)):
                rest = pl.ds(g.half_side, g.rows(top - 1) - g.half_side)
                levels[top - 1].right[comp, k, rest, :] = given[comp, k, rest, :]

        def set_right(comp, k, row, chunk, value):
            here = pl.ds(row, chunk)
            ids = row + lax.broadcasted_iota(jnp.int32, (chunk, side), 0)
            levels[top - 1].right[comp, k, here, :] = jnp.where(
                ids < covered[k], value, given[comp, k, here, :]
            )

        def keep(comp, k, row, chunk, value):
            if k == 0:
                sums[pl.ds(comp * reach + row, chunk), :] = value
            else:
                edges[comp, pl.ds(row, chunk), :] = value

        for level in (top, top - 1):
            d = levels[level]
            clear_level(g, level, d)
            smooth_weights(g, level, d, limits_of(level), 0, g.rows(level), True)
            residual_step(g, level, d, 0, g.rows(level))
            restrict_into(g, level, d, 0, g.rows(level), set_right if level == top else keep)
        packed = packed_sums(g, edges)
        sums[pl.ds(2 * reach, packed.shape[0]), :] = packed

    @pl.when(level_here < top - 1)
    def _():
        fill_pair(g, rows_ref, own, other, edge, levels, (1, 0), g.patch_rows)
        for level, size in zip((1, 0), lent_rows(g)):
            smooth_weights(g, level, levels[level], limits_of(level), 0, size, False)


def bottom_levels(g, rows_ref, patch, odd, start, stop, fine, coarse, new_sums, store_fine):
    side = g.side
    count, chunk = g.blocks(1), g.chunk(1, stop - start)
    clear_level(g, 1, fine)
    if new_sums is not None:
        reach = g.rows(2) // 2
        for comp in range(2):
            for k in range(count):
                here = pl.ds(0, reach)
                fine.right[comp, k, here, :] = fine.right[comp, k, here, :] + new_sums(comp, k)

    def body(row):
        here = pl.ds(start + row, chunk)
        for comp in range(2):
            for k in range(count):
                fine.cells[comp, k, pl.ds(PAD + start + row, chunk), :] = (
                    fine.weight[comp, k, here, :] * fine.right[comp, k, here, :]
                )

    over_rows(stop - start, chunk, body)
    residual_step(g, 1, fine, start, stop)
    near = near_counts(g, rows_ref, 1, patch, odd)
    covered = lane_limits(g, 0, near, g.half_side)

    def smooth_coarse(comp, k, row, size, value):
        here = pl.ds(row, size)
        ids = row + lax.broadcasted_iota(jnp.int32, (size, side), 0)
        value = jnp.where(ids < covered[0], value, coarse.right[comp, 0, here, :])
        value = coarse.weight[comp, 0, here, :] * value
        coarse.cells[comp, 0, here, :] = value

    restrict_into(g, 1, fine, start, stop, smooth_coarse)

    def load(comp, k, row, size):
        return coarse.cells[comp, 0, pl.ds(row, size), :]

    prolong_from(g, 1, fine, lane_limits(g, 1, near, side), start, stop, load)
    corrected_step(g, 1, fine, start, stop, store_fine)


def up_kernel(
    g, rows_ref, sums, lent, edge, filled, kept, mine, theirs, own_rows, coarse_rows, edges, scratch, low, low_fine,
    low_coarse, finer, coarser,
):
    level_here = lax.axis_index("level")
    patch = lax.axis_index("patch")
    side = g.side
    top = g.levels - 1
    odd = level_here % 2 == 1
    levels = [merged(a, b) for a, b in zip(scratch, filled)]
    for level in (top - 1, top):
        levels[level] = merged(levels[level], kept[level - top + 1])

    def limits_of(level):
        return lane_limits(g, level, near_counts(g, rows_ref, level, patch, odd), side)

    def hand_out():
        def write(first, second):
            for k in range(g.half_slots):
                for comp in range(2):
                    first[k, comp] = finer[k, comp]
                    second[k, comp] = coarser[k, comp]

        pl.when(odd)(lambda: write(mine, theirs))
        pl.when(jnp.logical_not(odd))(lambda: write(theirs, mine))

    @pl.when(level_here >= top - 1)
    def _():
        rows, less = lent_rows(g)
        limits = {level: limits_of(level) for level in (0, 1)}
        clear_pads(low_fine.visc, [(k,) for k in range(g.blocks(1))])
        clear_pads(low_coarse.visc, [(k,) for k in range(g.blocks(0))])
        finer_near = near_counts(g, rows_ref, 2, patch, odd)
        covered = lane_limits(g, 1, finer_near, g.half_side)
        borrow(g, rows_ref, patch, odd, lent, edge, limits, covered, low_fine, low_coarse)
        smooth_weights(g, 1, low_fine, limits[1], 0, rows, False)
        smooth_weights(g, 0, low_coarse, limits[0], 0, less, False)

        def store_fine(comp, k, row, chunk, value):
            low[comp, k, pl.ds(row, chunk), :] = value

        bottom_levels(
            g, rows_ref, patch, odd, 0, rows, low_fine, low_coarse,
            level_sums(g, sums, low_fine.weight), store_fine,
        )

        def load_low(comp, k, row, chunk):
            return low[comp, k, pl.ds(row, chunk), :]

        def load_held(comp, k, row, chunk):
            return edges[comp, k, pl.ds(row, chunk), :]

        def store_in(level, out, hold):
            own = g.own(level)

            def store(comp, k, row, chunk, value):
                if hold:
                    edges[comp, k, pl.ds(row, chunk), :] = value
                if k < own:
                    group, place = row // side, row % side
                    out[group * own + k, comp, pl.ds(pl.multiple_of(place, 8), chunk), :] = value

            return store

        for level, load, out in ((top - 1, load_low, coarser), (top, load_held, finer)):
            d = levels[level]
            clear_level(g, level, d)
            rows = g.rows(level)
            prolong_from(g, level, d, limits_of(level), 0, rows, load)
            corrected_step(g, level, d, 0, rows, store_in(level, out, level < top))
        hand_out()

    @pl.when(level_here < top - 1)
    def _():
        rows = g.rows(1)
        first = g.rows(2) // 2
        fine, coarse = levels[1], levels[0]._replace(cells=coarse_rows)
        smooth_weights(g, 1, fine, limits_of(1), first, rows, False)
        smooth_weights(g, 0, coarse, limits_of(0), first // 2, g.rows(0), False)

        def store_fine(comp, k, row, chunk, value):
            if k == 0:
                own_rows[comp, pl.ds(row, chunk), :] = value

        bottom_levels(g, rows_ref, patch, odd, first, rows, fine, coarse, None, store_fine)
        for r in range(rows // 2 // side, g.patch_rows(0)):
            here = pl.ds(r * side, side)
            for comp in range(2):
                coarse_rows[comp, 0, here, :] = (
                    coarse.weight[comp, 0, here, :] * coarse.right[comp, 0, here, :]
                )


def level_sums(g, sums, weight):
    reach = g.rows(2) // 2

    def value(comp, k):
        if k == 0:
            found = sums[pl.ds(comp * reach, reach), :]
        else:
            count, size = sums_groups(g)
            packed = sums[pl.ds(2 * reach, size), :]
            shifts = [sums_moves(g, group)[comp][0] for group in range(count)]
            parts = [pltpu.roll(packed, -shift % g.side, 1) for shift in shifts]
            found = jnp.concatenate(parts, axis=0)
        return jnp.where(weight[comp, k, pl.ds(0, reach), :] > 0.0, found, 0.0)

    return value


def low_kernel(
    g, rows_ref, sums, filled, kept, mine_in, theirs_in, own_rows, coarse_rows, mine, theirs, scratch, low_coarse, near_rows
):
    level_here = lax.axis_index("level")
    patch = lax.axis_index("patch")
    side = g.side
    top = g.levels - 1
    odd = level_here % 2 == 1

    @pl.when(level_here >= top - 1)
    def _():
        for k in range(g.half_slots):
            for comp in range(2):
                mine[k, comp] = mine_in[k, comp]
                theirs[k, comp] = theirs_in[k, comp]

    @pl.when(level_here < top - 1)
    def _():
        rows, _ = lent_rows(g)
        done = kept_rows(g)
        fine = merged(Level(filled[1].visc, kept[1]), scratch)
        coarse = merged(Level(None, kept[0], filled[0].right), low_coarse)
        for comp in range(2):
            for k in range(g.blocks(1)):
                fine.right[comp, k] = filled[1].right[comp, k, pl.ds(0, rows), :]

        def store_fine(comp, k, row, chunk, value):
            if k == 0:
                near_rows[comp, pl.ds(row, chunk), :] = value

        bottom_levels(
            g, rows_ref, patch, odd, 0, rows, fine, coarse,
            level_sums(g, sums, fine.weight), store_fine,
        )
        lane = lane_ids(side)
        size = rows // 2
        ids = lax.broadcasted_iota(jnp.int32, (size, side), 0)

        def coarse_group(comp, r):
            value = coarse_rows[comp, 0, pl.ds(r * side, side), :]
            if r:
                return value
            near = coarse.cells[comp, 0, pl.ds(0, size), :]
            near = jnp.where(ids < done // 2, near, value[:size])
            return jnp.concatenate([near, value[size:]], axis=0)

        def write(first, second):
            for comp in range(2):
                first[0, comp] = near_rows[comp, pl.ds(0, side), :]
                for r in range(1, g.patch_rows(1)):
                    first[r, comp] = own_rows[comp, pl.ds(r * side, side), :]
                first[1, comp, pl.ds(0, done - side), :] = near_rows[
                    comp, pl.ds(side, done - side), :
                ]
                for k in range(g.half_slots):
                    high = pltpu.roll(coarse_group(comp, k + g.half_slots), g.half_side, 1)
                    second[k, comp] = jnp.where(lane < g.half_side, coarse_group(comp, k), high)

        pl.when(odd)(lambda: write(mine, theirs))
        pl.when(jnp.logical_not(odd))(lambda: write(theirs, mine))


def join_kernel(g, mine, given, speed, fric, adjoint, gradient):
    level_here = lax.axis_index("level")
    lane = lane_ids(g.side)

    def put(slot, parts):
        for comp in range(2):
            adjoint[slot, comp] = parts[comp]
        total = speed[slot, 0].astype(F32) * parts[0] + speed[slot, 1].astype(F32) * parts[1]
        gradient[slot] = (-(fric[slot].astype(F32) * total)).astype(BF16)

    def join_level(level):
        if level == 0:
            for k in range(g.half_slots):
                low = []
                high = []
                for comp in range(2):
                    west, east = given[k, comp], mine[k, comp]
                    low.append(
                        jnp.where(lane < g.half_side, west, pltpu.roll(east, g.half_side, 1))
                    )
                    high.append(
                        jnp.where(lane < g.half_side, pltpu.roll(west, g.half_side, 1), east)
                    )
                put(k, low)
                put(k + g.half_slots, high)
            return
        own = g.own(level)
        west_half, east_half = (mine, given) if level % 2 == 1 else (given, mine)
        for r in range(g.patch_rows(level)):
            for k in range(2 * own):
                source = west_half if k < own else east_half
                put(
                    r * g.columns(level) + k,
                    [source[r * own + k % own, comp] for comp in range(2)],
                )

    for level in range(g.levels):
        pl.when(level_here == level)(lambda level=level: join_level(level))


def run_kernel(body, ins, outs, scratch, grant=VMEM_BYTES):
    in_trees = [jax.tree.flatten(tree) for tree, _ in ins]
    out_trees = [jax.tree.flatten(tree) for tree, _ in outs]
    scratch_trees = [jax.tree.flatten(tree) for tree in scratch]
    sizes = [len(leaves) for leaves, _ in in_trees + out_trees + scratch_trees]
    shapes = [tree for _, tree in in_trees + out_trees + scratch_trees]

    def kernel(*refs):
        given = []
        first = 0
        for size, shape in zip(sizes, shapes):
            given.append(jax.tree.unflatten(shape, refs[first : first + size]))
            first += size
        body(*given)

    def specs(groups, trees):
        return [
            pl.BlockSpec(memory_space=space)
            for (_, space), (leaves, _) in zip(groups, trees)
            for _ in leaves
        ]

    results = pl.pallas_call(
        kernel,
        out_shape=[leaf for leaves, _ in out_trees for leaf in leaves],
        in_specs=specs(ins, in_trees),
        out_specs=specs(outs, out_trees),
        scratch_shapes=[leaf for leaves, _ in scratch_trees for leaf in leaves],
        compiler_params=pltpu.CompilerParams(vmem_limit_bytes=grant),
    )(*[leaf for leaves, _ in in_trees for leaf in leaves])
    answer = []
    first = 0
    for leaves, shape in out_trees:
        answer.append(jax.tree.unflatten(shape, results[first : first + len(leaves)]))
        first += len(leaves)
    return answer


def moved(value, g, step):
    pairs = []
    for patch in range(g.patches):
        for level in range(g.levels):
            to_patch, to_level = step(patch, level)
            if 0 <= to_patch < g.patches and 0 <= to_level < g.levels:
                pairs.append((patch * g.levels + level, to_patch * g.levels + to_level))
    return lax.ppermute(value, ("patch", "level"), pairs)


def per_device(forcing, velocity, viscosity, friction, patch_rows):
    g = Layout(
        forcing.shape[1], forcing.shape[-1], lax.axis_size("level"), lax.axis_size("patch")
    )
    side = g.side
    top = g.levels - 1
    force, speed, visc, fric = forcing[0], velocity[0], viscosity[0], friction[0]
    make = jax.ShapeDtypeStruct
    vmem = pltpu.VMEM
    block = make((side, side), F32)
    half = make((g.half_slots, 2, side, side), F32)
    sums_rows = g.rows(2) + sums_groups(g)[1]

    def array(level, rows, kind, comps, pad):
        return level_array(g, g.blocks(level), rows, kind, comps, pad)

    own = (force, visc, fric)
    other = tuple(moved(value, g, lambda p, l: (p, l ^ 1)) for value in own)
    (edge,) = run_kernel(
        lambda *refs: first_edge_kernel(g, *refs),
        [(own, pltpu.HBM)],
        [(block, VM)],
        [
            pltpu.SemaphoreType.DMA((3 * g.slots,)),
            tuple(vmem(value.shape, value.dtype) for value in own),
        ],
        FIRST_BYTES,
    )
    (edge,) = run_kernel(
        lambda *refs: edge_kernel(g, *refs), [(edge, VM), (other, VM)], [(block, VM)], []
    )
    (lent_here,) = run_kernel(
        lambda *refs: lend_kernel(g, *refs),
        [(own, VM), (other, VM), (edge, VM)],
        [(make((lent_size(g), side), BF16), VM)],
        [],
    )
    edge_here = edge
    step = lambda l: -1 if l % 2 else 1
    edge = moved(edge_here, g, lambda p, l: (p + step(l), l ^ 1))
    edge_low = moved(edge_here, g, lambda p, l: (p + step(l), (l ^ 1) + 2))
    lent = moved(lent_here, g, lambda p, l: (p, l + 2))

    fields = [
        Level(
            array(level, g.rows(level), make, False, True),
            None,
            right=array(level, g.rows(level), make, True, False),
            fric=array(level, g.rows(level), make, False, False),
        )
        for level in range(g.levels)
    ]
    rows, less = lent_rows(g)
    given = [(patch_rows, SM), (own, VM), (other, VM), (edge, VM)]

    (upper,) = run_kernel(
        lambda *refs: fill_kernel(g, *refs),
        [*given, (edge_low, VM), (lent_here, VM)],
        [(fields[top - 1 :], VM)],
        [],
    )

    def kept_of(level):
        two = array(level, g.rows(level), make, True, False)
        return Level(None, two, held=two)

    low_weights = [array(0, less, make, True, False), array(1, rows, make, True, False)]

    def down_scratch(level):
        if level < top - 1:
            return Level(None, None)
        both = array(level, g.rows(level), vmem, True, False)
        more = dict(right=both) if level < top else {}
        return Level(None, None, left=both, **more, **step_arrays(g, level, g.rows(level)))

    sums, kept, low_kept, lower = run_kernel(
        lambda *refs: down_kernel(g, *refs),
        [*given, (upper, VM)],
        [
            (make((sums_rows, side), F32), VM),
            ([kept_of(level) for level in (top - 1, top)], VM),
            (low_weights, VM),
            (fields[: top - 1], VM),
        ],
        [vmem((2, side, side), F32), [down_scratch(level) for level in range(g.levels)]],
    )
    filled = [*lower, *upper]
    sums_there = moved(sums, g, lambda p, l: (p, l - 2))

    def up_scratch(level):
        both = array(level, g.rows(level), vmem, True, False)
        if level == 0:
            return Level(None, both)
        steps = step_arrays(g, level, g.rows(level))
        if level == 1:
            return Level(None, both, held=both, left=both, **steps)
        return Level(None, None, **steps)

    low_both = array(1, rows, vmem, True, False)
    low_steps = dict(held=low_both, left=low_both, right=low_both, **step_arrays(g, 1, rows))
    mine, theirs, own_rows, coarse_rows = run_kernel(
        lambda *refs: up_kernel(g, *refs),
        [
            (patch_rows, SM),
            (sums, VM),
            (lent, VM),
            (edge_low, VM),
            (filled, VM),
            (kept, VM),
        ],
        [
            (half, VM),
            (half, VM),
            (make((2, g.rows(1), side), F32), VM),
            (make((2, 1, g.rows(0), side), F32), VM),
        ],
        [
            array(top - 1, g.rows(top - 1), vmem, True, False),
            [up_scratch(level) for level in range(g.levels)],
            low_both,
            Level(
                array(1, rows, vmem, False, True),
                low_both,
                fric=array(1, rows, vmem, False, False),
                **low_steps,
            ),
            Level(
                array(0, less, vmem, False, True),
                array(0, less, vmem, True, False),
                right=array(0, less, vmem, True, False),
                fric=array(0, less, vmem, False, False),
                cells=array(0, less, vmem, True, False),
            ),
            vmem(half.shape, F32),
            vmem(half.shape, F32),
        ],
    )
    mine, theirs = run_kernel(
        lambda *refs: low_kernel(g, *refs),
        [
            (patch_rows, SM),
            (sums_there, VM),
            (filled[:2], VM),
            (low_kept, VM),
            (mine, VM),
            (theirs, VM),
            (own_rows, VM),
            (coarse_rows, VM),
        ],
        [(half, VM), (half, VM)],
        [
            Level(None, None, **low_steps),
            Level(None, None, cells=array(0, less, vmem, True, False)),
            vmem((2, rows, side), F32),
        ],
    )
    received = moved(theirs, g, lambda p, l: (p, l ^ 1))
    adjoint, gradient = run_kernel(
        lambda *refs: join_kernel(g, *refs),
        [(mine, VM), (received, VM), (speed, VM), (fric, VM)],
        [
            (make((g.slots, 2, side, side), F32), VM),
            (make((g.slots, side, side), BF16), VM),
        ],
        [],
    )
    return (adjoint[None], gradient[None])


def solution(mesh):
    fields = P("level", "patch")
    return jax.shard_map(
        per_device,
        mesh=mesh,
        in_specs=(fields, fields, fields, fields, P()),
        out_specs=(fields, fields),
        check_vma=False,
    )
```

```python
from typing import Any, NamedTuple

import jax
import jax.numpy as jnp
from jax import lax
from jax.experimental import pallas as pl
from jax.experimental.pallas import tpu as pltpu
from jax.sharding import PartitionSpec as P

relaxation = 0.5
PAD = 8
LOW, HIGH, EDGES = 0, 1, 2
VM, SM = pltpu.VMEM, pltpu.SMEM
F32 = jnp.float32
BF16 = jnp.bfloat16
VMEM_BYTES = 30 * 2**20
FIRST_BYTES = 60 * 2**20


class Layout:
    def __init__(self, slots, side, levels, patches):
        self.slots = slots
        self.side = side
        self.levels = levels
        self.patches = patches
        self.half_slots = slots // 2
        self.half_side = side // 2
        self.span = 2 * slots

    def columns(self, level):
        return 1 << level

    def patch_rows(self, level):
        return self.slots >> level

    def rows(self, level):
        return self.patch_rows(level) * self.side

    def margin(self, level):
        return 2 << level

    def own(self, level):
        return max(1, (1 << level) // 2)

    def blocks(self, level):
        return self.own(level) + (1 if level > 0 else 0)

    def chunk(self, level, rows):
        size = 8 * max(1, 112 // self.blocks(level))
        while rows % size or (rows % self.side == 0 and self.side % size):
            size -= 8
        return size


def lane_ids(side):
    return lax.broadcasted_iota(jnp.int32, (1, side), 1)


def near_counts(g, rows_ref, level, patch, odd):
    own = rows_ref[level, patch]
    east = jnp.where(
        patch + 1 < g.patches, rows_ref[level, jnp.minimum(patch + 1, g.patches - 1)], 0
    )
    west = jnp.where(patch > 0, rows_ref[level, jnp.maximum(patch - 1, 0)], 0)
    return own, jnp.where(odd, own, east), jnp.where(odd, west, own)


def lane_limits(g, level, counts, cells):
    own, east, west = (value * cells for value in counts)
    lane = lane_ids(g.side)
    margin = g.margin(level)
    first = 0 if level > 0 else g.half_side
    edges = jnp.where(
        (lane >= first) & (lane < first + margin), east, jnp.where(lane >= g.side - margin, west, 0)
    )
    if level == 0:
        return [jnp.where(lane < g.half_side, own, edges)]
    return [jnp.full((1, g.side), own, jnp.int32)] * g.own(level) + [edges]


def one_side(g, values, east):
    count = len(values)
    turned = [pltpu.roll(value, g.side - 1 if east else 1, 1) for value in values]
    if count == 1:
        return turned
    lane = lax.broadcasted_iota(jnp.int32, values[0].shape, 1)
    last = lane == (g.side - 1 if east else 0)
    step = 1 if east else -1
    return [jnp.where(last, turned[(k + step) % count], turned[k]) for k in range(count)]


def both_sides(g, values):
    return one_side(g, values, True), one_side(g, values, False)


def over_rows(rows, chunk, body):
    def step(index, carry):
        body(pl.multiple_of(index * chunk, chunk))
        return carry

    lax.fori_loop(0, rows // chunk, step, 0)


def clear_pads(ref, lead):
    width = ref.shape[-1]
    last = ref.shape[-2]
    for index in lead:
        ref[index + (slice(0, PAD), slice(None))] = jnp.zeros((PAD, width), F32)
        ref[index + (slice(last - PAD, last), slice(None))] = jnp.zeros((PAD, width), F32)


def off_diagonal_rows(g, d, row, size, count):
    here = pl.ds(row, size)
    inner = pl.ds(PAD + row, size)
    centre = [[d.cells[comp, k, inner, :] for k in range(count)] for comp in range(2)]
    beside = [both_sides(g, centre[comp]) for comp in range(2)]
    products = []
    for k in range(count):
        visc = d.visc[k, inner, :]
        half = 0.5 * visc
        (u, v) = (centre[comp][k] for comp in range(2))
        (u_e, u_w), (v_e, v_w) = ((beside[c][0][k], beside[c][1][k]) for c in range(2))
        u_n, v_n = (d.cells[c, k, pl.ds(PAD + row + 1, size), :] for c in range(2))
        u_s, v_s = (d.cells[c, k, pl.ds(PAD + row - 1, size), :] for c in range(2))
        one_u, one_v = visc * u, visc * v
        four_u, four_v = 4.0 * one_u, 4.0 * one_v
        cross_u, cross_v = half * (v_e - v_w), visc * (u_e - u_w)
        d.north[0, k, inner, :] = one_u + cross_u
        d.south[0, k, inner, :] = one_u - cross_u
        d.north[1, k, inner, :] = four_v + cross_v
        d.south[1, k, inner, :] = four_v - cross_v
        cross_u, cross_v = visc * (v_n - v_s), half * (u_n - u_s)
        products.append(
            (
                four_u + cross_u,
                four_u - cross_u,
                one_v + cross_v,
                one_v - cross_v,
                visc * (4.0 * (u_e + u_w) + (u_n + u_s)),
                visc * (4.0 * (v_n + v_s) + (v_e + v_w)),
            )
        )
    for comp in range(2):
        east = one_side(g, [item[2 * comp] for item in products], True)
        west = one_side(g, [item[2 * comp + 1] for item in products], False)
        for k in range(count):
            d.part[comp, k, here, :] = products[k][4 + comp] + east[k] + west[k]


def off_diagonal_step(g, level, d, start, stop):
    count = g.blocks(level)
    chunk = g.chunk(level, stop - start)

    def body(row):
        for step in range(0, chunk, 8):
            off_diagonal_rows(g, d, start + row + step, 8, count)

    over_rows(stop - start, chunk, body)


def off_diagonal(d, comp, k, row, chunk):
    return (
        d.part[comp, k, pl.ds(row, chunk), :]
        + d.north[comp, k, pl.ds(PAD + row + 1, chunk), :]
        + d.south[comp, k, pl.ds(PAD + row - 1, chunk), :]
    )


def smooth_weights(g, level, d, limits, start, stop, from_zero):
    count = g.blocks(level)
    chunk = g.chunk(level, stop - start)

    def some_rows(row):
        here = pl.ds(row, 8)
        inner = pl.ds(PAD + row, 8)
        centre = [d.visc[k, inner, :] for k in range(count)]
        east, west = both_sides(g, centre)
        for k in range(count):
            north = d.visc[k, pl.ds(PAD + row + 1, 8), :]
            south = d.visc[k, pl.ds(PAD + row - 1, 8), :]
            friction = d.fric[k, here, :]
            twice = 2.0 * centre[k]
            along_row = twice + east[k] + west[k]
            along_col = twice + north + south
            live = jnp.broadcast_to(limits[k], (8, g.side)) > row
            diag_u = 4.0 * along_row + along_col + friction
            diag_v = 4.0 * along_col + along_row + friction
            for comp, diag in ((0, diag_u), (1, diag_v)):
                guess = pl.reciprocal(diag, approx=True)
                weight = guess * (2.0 * relaxation - relaxation * diag * guess)
                weight = jnp.where(live, weight, 0.0)
                d.weight[comp, k, here, :] = weight
                if from_zero:
                    d.cells[comp, k, inner, :] = weight * d.right[comp, k, here, :]

    def body(row):
        for step in range(0, chunk, 8):
            some_rows(start + row + step)

    over_rows(stop - start, chunk, body)


def residual_step(g, level, d, start, stop):
    count = g.blocks(level)
    chunk = g.chunk(level, stop - start)
    off_diagonal_step(g, level, d, start, stop)

    def body(row):
        row = row + start
        here = pl.ds(row, chunk)
        for comp in range(2):
            for k in range(count):
                weight = d.weight[comp, k, here, :]
                left = (1.0 - relaxation) * d.right[comp, k, here, :] + off_diagonal(
                    d, comp, k, row, chunk
                )
                left = jnp.where(weight > 0.0, left, 0.0)
                d.left[comp, k, here, :] = left
                d.held[comp, k, here, :] = (
                    d.cells[comp, k, pl.ds(PAD + row, chunk), :] + weight * left
                )

    over_rows(stop - start, chunk, body)


def corrected_step(g, level, d, start, stop, store):
    count = g.blocks(level)
    chunk = g.chunk(level, stop - start)
    off_diagonal_step(g, level, d, start, stop)

    def body(row):
        row = row + start
        here = pl.ds(row, chunk)
        for comp in range(2):
            for k in range(count):
                value = (
                    d.held[comp, k, here, :]
                    + (1.0 - relaxation) * d.cells[comp, k, pl.ds(PAD + row, chunk), :]
                    + d.weight[comp, k, here, :] * off_diagonal(d, comp, k, row, chunk)
                )
                store(comp, k, row, chunk, value)

    over_rows(stop - start, chunk, body)


def pairings(g, fine):
    if fine == 1:
        return [[(0, LOW), (1, HIGH)]]
    parts = [[(2 * k, LOW), (2 * k + 1, HIGH)] for k in range(g.own(fine) // 2)]
    return parts + [[(g.own(fine), EDGES)]]


def target_lane(g, part, fine_lane):
    halved = jnp.right_shift(fine_lane, 1)
    if part == LOW:
        return halved
    if part == HIGH:
        return g.half_side + halved
    return halved + jnp.where(fine_lane >= g.half_side, g.half_side, 0)


def sum_matrix(g, part):
    fine = lax.broadcasted_iota(jnp.int32, (g.side, g.side), 0)
    coarse = lax.broadcasted_iota(jnp.int32, (g.side, g.side), 1)
    return jnp.where(target_lane(g, part, fine) == coarse, 1.0, 0.0).astype(BF16)


def copy_matrix(g, part):
    coarse = lax.broadcasted_iota(jnp.int32, (g.side, g.side), 0)
    fine = lax.broadcasted_iota(jnp.int32, (g.side, g.side), 1)
    return jnp.where(target_lane(g, part, fine) == coarse, 1.0, 0.0).astype(BF16)


def split_dot(values, matrix):
    high = values.astype(BF16)
    rest = (values - high.astype(F32)).astype(BF16)
    return jnp.dot(high, matrix, preferred_element_type=F32) + jnp.dot(
        rest, matrix, preferred_element_type=F32
    )


def restrict_into(g, fine, d, start, stop, store):
    rows = stop - start
    chunk = min(rows // 2, g.half_side)
    if (rows // 2) % chunk:
        chunk = rows // 2
    parts = pairings(g, fine)
    matrices = {part: sum_matrix(g, part) for members in parts for _, part in members}

    def body(row):
        row = row + start // 2
        for comp in range(2):
            for coarse, members in enumerate(parts):
                total = None
                for k, part in members:
                    first = d.left[comp, k, pl.ds(2 * row, chunk, stride=2), :]
                    second = d.left[comp, k, pl.ds(2 * row + 1, chunk, stride=2), :]
                    term = split_dot(first + second, matrices[part])
                    total = term if total is None else total + term
                store(comp, coarse, row, chunk, total)

    over_rows(rows // 2, chunk, body)


def prolong_from(g, fine, d, limits, start, stop, load):
    rows = stop - start
    chunk = min(rows // 2, g.half_side)
    if (rows // 2) % chunk:
        chunk = rows // 2
    parts = pairings(g, fine)
    matrices = {part: copy_matrix(g, part) for members in parts for _, part in members}

    def body(row):
        row = row + start // 2
        ids = 2 * (row + lax.broadcasted_iota(jnp.int32, (chunk, g.side), 0))
        for comp in range(2):
            for coarse, members in enumerate(parts):
                value = load(comp, coarse, row, chunk)
                for k, part in members:
                    spread = jnp.where(ids < limits[k], split_dot(value, matrices[part]), 0.0)
                    d.cells[comp, k, pl.ds(PAD + 2 * row, chunk, stride=2), :] = spread
                    d.cells[comp, k, pl.ds(PAD + 2 * row + 1, chunk, stride=2), :] = spread

    over_rows(rows // 2, chunk, body)


def sums_groups(g):
    count = g.side // (4 * g.margin(1))
    return count, g.rows(2) // 2 // count


def sums_moves(g, group):
    margin = g.margin(1)
    base = 4 * margin * group
    return (base + margin, base), (base + 3 * margin, base + 2 * margin)


def packed_sums(g, edges):
    lane = lane_ids(g.side)
    count, size = sums_groups(g)
    total = jnp.zeros((size, g.side), F32)
    for group in range(count):
        for comp, (shift, first) in enumerate(sums_moves(g, group)):
            value = pltpu.roll(edges[comp, pl.ds(group * size, size), :], shift % g.side, 1)
            inside = (lane >= first) & (lane < first + 2 * g.margin(1))
            total = jnp.where(inside, value, total)
    return total


def plane(raw, q, slot):
    force, visc, fric = raw
    if q < 2:
        return force[slot, q].astype(F32)
    return (fric if q == 2 else visc)[slot].astype(F32)


def edge_lane(g, level, q, r):
    return (0 if level % 2 else g.half_side) + q * g.span + r * g.margin(level)


def packed_edge(g, here, level, patch_of):
    side = g.side
    lane = lane_ids(side)
    margin = g.margin(level)
    start = 0 if here % 2 else side - margin
    total = jnp.zeros((side, side), F32)
    for r in range(g.patch_rows(level)):
        for q in range(4):
            base = edge_lane(g, level, q, r)
            value = patch_of(q, r)
            if (base - start) % side:
                value = pltpu.roll(value, (base - start) % side, 1)
            total = jnp.where((lane >= base) & (lane < base + margin), value, total)
    return total


def edge_column(g, here, level):
    return 0 if here % 2 else g.columns(level) - 1


def first_edge_kernel(g, own, edge, sems, held):
    level_here = lax.axis_index("level")

    def pack(level):
        copies = Copies(sems)
        rows = g.patch_rows(level)
        if g.columns(level) == 1:
            for source, target in zip(own, held):
                copies.start(source, target)
        else:
            for r in range(rows):
                slot = r * g.columns(level) + edge_column(g, level, level)
                for source, target in zip(own, held):
                    copies.start(source.at[slot], target.at[r])
        copies.finish()
        edge[...] = packed_edge(g, level, level, lambda q, r: plane(held, q, r))

    for level in range(g.levels):
        pl.when(level_here == level)(lambda level=level: pack(level))


def edge_kernel(g, first, other, edge):
    level_here = lax.axis_index("level")

    def pack(here):
        level = here ^ 1
        column = edge_column(g, here, level)

        def patch_of(q, r):
            return plane(other, q, r * g.columns(level) + column)

        edge[...] = first[...] + packed_edge(g, here, level, patch_of)

    for here in range(g.levels):
        pl.when(level_here == here)(lambda here=here: pack(here))


def fill_level(g, level, west_type, d, limits, covered, raw, edge, groups):
    side = g.side
    margin = g.margin(level)
    own = g.own(level)
    columns = g.columns(level)
    lane = lane_ids(side)

    def outer(q, r, place):
        shift = (place - edge_lane(g, level, q, r)) % side
        return pltpu.roll(edge[...], shift, 1) if shift else edge[...]

    def store(q, k, r, value):
        here = pl.ds(r * side, side)
        if q < 2:
            if covered is not None:
                ids = r * side + lax.broadcasted_iota(jnp.int32, (side, side), 0)
                value = jnp.where(ids < covered[k], 0.0, value)
            d.right[q, k, here, :] = value
        elif q == 2:
            d.fric[k, here, :] = value
        else:
            d.visc[k, pl.ds(PAD + r * side, side), :] = jnp.where(
                limits[k] > r * side, 0.5 * value, 0.0
            )

    clear_pads(d.visc, [(k,) for k in range(g.blocks(level))])
    for r in range(groups):
        for q in range(4):
            if level == 0 and west_type:
                west = outer(q, r, side - margin)
                store(q, 0, r, jnp.where(lane >= side - margin, west, plane(raw, q, r)))
            elif level == 0:
                value = pltpu.roll(plane(raw, q, r), g.half_side, 1)
                here = (lane >= g.half_side) & (lane < g.half_side + margin)
                store(q, 0, r, jnp.where(here, outer(q, r, g.half_side), value))
            else:
                for k in range(own):
                    store(q, k, r, plane(raw, q, r * columns + k + (0 if west_type else own)))
                if west_type:
                    east = plane(raw, q, r * columns + own)
                    west = outer(q, r, side - margin)
                else:
                    east = outer(q, r, 0)
                    west = plane(raw, q, r * columns + own - 1)
                store(q, own, r, jnp.where(lane < g.half_side, east, west))


class Level(NamedTuple):
    visc: Any
    weight: Any
    right: Any = None
    held: Any = None
    fric: Any = None
    cells: Any = None
    part: Any = None
    north: Any = None
    south: Any = None
    left: Any = None


def level_array(g, count, rows, make, comps, pad):
    shape = (count, rows + (2 * PAD if pad else 0), g.side)
    return make((2, *shape) if comps else shape, F32)


def step_arrays(g, level, rows):
    count = g.blocks(level)
    padded = level_array(g, count, rows, pltpu.VMEM, True, True)
    return dict(
        cells=padded,
        part=level_array(g, count, rows, pltpu.VMEM, True, False),
        north=padded,
        south=padded,
    )


def clear_level(g, level, d):
    blocks = range(g.blocks(level))
    both = [(c, k) for c in range(2) for k in blocks]
    for ref in (d.cells, d.north, d.south):
        clear_pads(ref, both)


def merged(first, second):
    return Level(*[b if a is None else a for a, b in zip(first, second)])


class Copies:
    def __init__(self, sems, first=0):
        self.sems = sems
        self.used = first
        self.open = []

    def start(self, source, target):
        copy = pltpu.make_async_copy(source, target, self.sems.at[self.used])
        self.used += 1
        copy.start()
        self.open.append(copy)

    def finish(self):
        for copy in self.open:
            copy.wait()
        self.open = []


def low_rows(g):
    return g.rows(2) // 2 + 2 * PAD


def kept_rows(g):
    return g.rows(2) // 2 + PAD


def lent_rows(g):
    return low_rows(g), -(-low_rows(g) // 2 // 16) * 16


def lent_forcing(g):
    return [count * g.half_side for count in range(1, g.patch_rows(2) + 1)]


def lent_size(g):
    rows, less = lent_rows(g)
    return 4 * rows + 2 * 16 * len(lent_forcing(g)) + 2 * less + 16


def pair_of(visc):
    high = visc.astype(BF16)
    return [high, (visc - high.astype(F32)).astype(BF16)]


class Rows:
    def __init__(self, ref):
        self.ref = ref
        self.place = 0

    def put(self, value):
        size = value.shape[0]
        self.ref[pl.ds(self.place, size), :] = value.astype(BF16)
        self.place += size

    def take(self, size):
        value = self.ref[pl.ds(self.place, size), :].astype(F32)
        self.place += size
        return value


def side_by_side(g, low, high):
    lane = lane_ids(g.side)
    return jnp.where(
        lane < g.half_side, low.astype(F32), pltpu.roll(high.astype(F32), g.half_side, 1)
    )


def lend(g, west_type, own, other, edge, out):
    rows, less = lent_rows(g)
    side = g.side
    fine, coarse = (own, other) if west_type else (other, own)
    target = Rows(out)

    def some_rows(raw, q, slot, first, size):
        here = pl.ds(first, size)
        force, visc, fric = raw
        value = force[slot, q, here, :] if q < 2 else (fric if q == 2 else visc)[slot, here, :]
        return 0.5 * value if q == 3 else value

    def fine_rows(q, first, size, column=0 if west_type else g.own(1)):
        parts = []
        while size:
            group, place = first // side, first % side
            part = min(size, side - place)
            slot = group * g.columns(1) + column
            parts.append(some_rows(fine, q, slot, place, part))
            first, size = first + part, size - part
        return parts

    for part in fine_rows(2, 0, rows):
        target.put(part)
    pairs = [pair_of(part) for part in fine_rows(3, 0, rows)]
    for index in range(2):
        for pair in pairs:
            target.put(pair[index])
    for comp in range(2):
        for first in lent_forcing(g):
            for part in fine_rows(comp, first, 16):
                target.put(part)

    def coarse_rows(q, first, size):
        value = some_rows(coarse, q, 0, first, size).astype(F32)
        return value if west_type else pltpu.roll(value, g.half_side, 1)

    high, rest = pair_of(coarse_rows(3, 0, less))
    target.put(side_by_side(g, coarse_rows(2, 0, less), high))
    target.put(rest)
    target.put(
        side_by_side(g, coarse_rows(0, g.half_side, 16), coarse_rows(1, g.half_side, 16))
    )
    lane = lane_ids(side)

    def outer_plane(level, q, size, place):
        parts = []
        for r in range(-(-size // side)):
            part = edge[pl.ds(0, min(side, size - r * side)), :]
            shift = (place - edge_lane(g, level, q, r)) % side
            parts.append(pltpu.roll(part, shift, 1) if shift else part)
        value = jnp.concatenate(parts, axis=0) if len(parts) > 1 else parts[0]
        return 0.5 * value if q == 3 else value

    def margins(level, size):
        column = g.own(1) if west_type else g.own(1) - 1
        total = jnp.zeros((size, side), F32)
        for q in range(4):
            if level:
                parts = fine_rows(q, 0, size, column)
                inner = jnp.concatenate([part.astype(F32) for part in parts], axis=0)
            else:
                inner = coarse_rows(q, 0, size)
            for west in (True, False):
                if west == west_type:
                    place = margin_moves(g, level, q)[0 if west else 1][0]
                    value = outer_plane(level, q, size, place)
                else:
                    value = inner
                for offset, part in enumerate(pair_of(value) if q == 3 else [value]):
                    place, target_lane = margin_moves(g, level, q + offset)[0 if west else 1]
                    shifted = pltpu.roll(part.astype(F32), (target_lane - place) % side, 1)
                    here = (lane >= target_lane) & (lane < target_lane + g.margin(level))
                    total = jnp.where(here, shifted, total)
        return total

    fine_part = margins(1, rows)
    target.put(fine_part[:less] + margins(0, less))
    target.put(fine_part[less:])


def margin_moves(g, level, index):
    margin = g.margin(level)
    base = 2 * margin * index + (0 if level else 2 * g.margin(1) * 5)
    return (g.side - margin, base), ((0 if level else g.half_side), base + margin)


def edges_of(g, level, west, east):
    lane = lane_ids(g.side)
    middle = g.side - g.half_side // 2 if level == 0 else g.half_side
    return jnp.where(lane < middle, east, west)


def borrow(g, lent, limits, covered, fine, coarse):
    rows, less = lent_rows(g)
    side = g.side
    lane = lane_ids(side)
    source = Rows(lent)

    def masked(value, bounds, inside):
        ids = lax.broadcasted_iota(jnp.int32, value.shape, 0)
        return jnp.where((ids < bounds) == inside, value, 0.0)

    fine.fric[0] = source.take(rows)
    high = source.take(rows)
    fine.visc[0, pl.ds(PAD, rows), :] = masked(high + source.take(rows), limits[1][0], True)
    for comp in range(2):
        fine.right[comp, 0] = jnp.zeros((rows, side), F32)
        for first in lent_forcing(g):
            value = masked(source.take(16), covered[0] - first, False)
            fine.right[comp, 0, pl.ds(first, 16), :] = value
    first, rest, window = source.take(less), source.take(less), source.take(16)
    packed = source.take(rows)

    def margins(level, q, size):
        moves = [margin_moves(g, level, index) for index in ((q,) if q < 3 else (3, 4))]
        west, east = (
            sum(
                pltpu.roll(packed[:size], (move[at][0] - move[at][1]) % side, 1)
                for move in moves
            )
            for at in range(2)
        )
        return edges_of(g, level, west, east)

    for comp in range(2):
        fine.right[comp, 1] = masked(margins(1, comp, rows), covered[1], False)
    fine.fric[1] = margins(1, 2, rows)
    fine.visc[1, pl.ds(PAD, rows), :] = masked(margins(1, 3, rows), limits[1][1], True)

    def with_margins(value, q):
        return jnp.where(lane < g.half_side, value, margins(0, q, less))

    coarse.fric[0] = with_margins(first, 2)
    value = with_margins(pltpu.roll(first, g.half_side, 1) + rest, 3)
    coarse.visc[0, pl.ds(PAD, less), :] = masked(value, limits[0][0], True)
    for comp in range(2):
        value = pltpu.roll(window, g.half_side, 1) if comp else window
        value = jnp.concatenate([jnp.zeros((g.half_side, side), F32), value], axis=0)
        coarse.right[comp, 0] = with_margins(value, comp)


def fill_pair(g, rows_ref, own, other, edge, levels, wanted, groups):
    level_here = lax.axis_index("level")
    patch = lax.axis_index("patch")
    odd = level_here % 2 == 1
    for west_type in (True, False):

        @pl.when(odd if west_type else jnp.logical_not(odd))
        def _():
            for level in wanted:
                near = near_counts(g, rows_ref, level, patch, odd)
                limits = lane_limits(g, level, near, g.side)
                covered = None
                if level == 1:
                    finer = near_counts(g, rows_ref, 2, patch, odd)
                    covered = lane_limits(g, 1, finer, g.half_side)
                home = (level % 2 == 1) == west_type
                raw = own if home else other
                fill_level(
                    g, level, west_type, levels[level], limits, covered, raw, edge, groups(level)
                )


def fill_kernel(g, rows_ref, own, other, edge, filled, lent):
    level_here = lax.axis_index("level")
    top = g.levels - 1

    @pl.when(level_here >= top - 1)
    def _():
        levels = dict(zip((top - 1, top), filled))
        fill_pair(g, rows_ref, own, other, edge, levels, (top, top - 1), g.patch_rows)

    for level in range(top - 1):
        pl.when(level_here == level)(
            lambda level=level: lend(g, level % 2 == 1, own, other, edge, lent)
        )


def down_kernel(
    g, rows_ref, own, other, edge, upper, sums, kept, low_kept, lower, edges, scratch
):
    level_here = lax.axis_index("level")
    patch = lax.axis_index("patch")
    side = g.side
    top = g.levels - 1
    odd = level_here % 2 == 1
    filled = [*lower, *upper]
    kept = [*(Level(None, weight) for weight in low_kept), *kept]
    levels = [merged(merged(a, b), c) for a, b, c in zip(scratch, kept, filled)]

    def limits_of(level):
        return lane_limits(g, level, near_counts(g, rows_ref, level, patch, odd), side)

    @pl.when(level_here >= top - 1)
    def _():
        near = near_counts(g, rows_ref, top, patch, odd)
        covered = lane_limits(g, top - 1, near, g.half_side)
        given = filled[top - 1].right
        reach = g.rows(2) // 2
        for comp in range(2):
            for k in range(g.blocks(top - 1)):
                rest = pl.ds(g.half_side, g.rows(top - 1) - g.half_side)
                levels[top - 1].right[comp, k, rest, :] = given[comp, k, rest, :]

        def set_right(comp, k, row, chunk, value):
            here = pl.ds(row, chunk)
            ids = row + lax.broadcasted_iota(jnp.int32, (chunk, side), 0)
            levels[top - 1].right[comp, k, here, :] = jnp.where(
                ids < covered[k], value, given[comp, k, here, :]
            )

        def keep(comp, k, row, chunk, value):
            if k == 0:
                sums[pl.ds(comp * reach + row, chunk), :] = value
            else:
                edges[comp, pl.ds(row, chunk), :] = value

        for level in (top, top - 1):
            d = levels[level]
            clear_level(g, level, d)
            smooth_weights(g, level, d, limits_of(level), 0, g.rows(level), True)
            residual_step(g, level, d, 0, g.rows(level))
            restrict_into(g, level, d, 0, g.rows(level), set_right if level == top else keep)
        packed = packed_sums(g, edges)
        sums[pl.ds(2 * reach, packed.shape[0]), :] = packed

    @pl.when(level_here < top - 1)
    def _():
        fill_pair(g, rows_ref, own, other, edge, levels, (1, 0), g.patch_rows)
        for level, size in zip((1, 0), lent_rows(g)):
            smooth_weights(g, level, levels[level], limits_of(level), 0, size, False)


def bottom_levels(g, rows_ref, patch, odd, start, stop, fine, coarse, new_sums, store_fine):
    side = g.side
    count, chunk = g.blocks(1), g.chunk(1, stop - start)
    clear_level(g, 1, fine)
    if new_sums is not None:
        reach = g.rows(2) // 2
        for comp in range(2):
            for k in range(count):
                here = pl.ds(0, reach)
                fine.right[comp, k, here, :] = fine.right[comp, k, here, :] + new_sums(comp, k)

    def body(row):
        here = pl.ds(start + row, chunk)
        for comp in range(2):
            for k in range(count):
                fine.cells[comp, k, pl.ds(PAD + start + row, chunk), :] = (
                    fine.weight[comp, k, here, :] * fine.right[comp, k, here, :]
                )

    over_rows(stop - start, chunk, body)
    residual_step(g, 1, fine, start, stop)
    near = near_counts(g, rows_ref, 1, patch, odd)
    covered = lane_limits(g, 0, near, g.half_side)

    def smooth_coarse(comp, k, row, size, value):
        here = pl.ds(row, size)
        ids = row + lax.broadcasted_iota(jnp.int32, (size, side), 0)
        value = jnp.where(ids < covered[0], value, coarse.right[comp, 0, here, :])
        value = coarse.weight[comp, 0, here, :] * value
        coarse.cells[comp, 0, here, :] = value

    restrict_into(g, 1, fine, start, stop, smooth_coarse)

    def load(comp, k, row, size):
        return coarse.cells[comp, 0, pl.ds(row, size), :]

    prolong_from(g, 1, fine, lane_limits(g, 1, near, side), start, stop, load)
    corrected_step(g, 1, fine, start, stop, store_fine)


def up_kernel(
    g, rows_ref, sums, lent, filled, kept, mine, theirs, own_rows, coarse_rows, edges, scratch, low, low_fine,
    low_coarse, finer, coarser,
):
    level_here = lax.axis_index("level")
    patch = lax.axis_index("patch")
    side = g.side
    top = g.levels - 1
    odd = level_here % 2 == 1
    levels = [merged(a, b) for a, b in zip(scratch, filled)]
    for level in (top - 1, top):
        levels[level] = merged(levels[level], kept[level - top + 1])

    def limits_of(level):
        return lane_limits(g, level, near_counts(g, rows_ref, level, patch, odd), side)

    def hand_out():
        def write(first, second):
            for k in range(g.half_slots):
                for comp in range(2):
                    first[k, comp] = finer[k, comp]
                    second[k, comp] = coarser[k, comp]

        pl.when(odd)(lambda: write(mine, theirs))
        pl.when(jnp.logical_not(odd))(lambda: write(theirs, mine))

    @pl.when(level_here >= top - 1)
    def _():
        rows, less = lent_rows(g)
        limits = {level: limits_of(level) for level in (0, 1)}
        clear_pads(low_fine.visc, [(k,) for k in range(g.blocks(1))])
        clear_pads(low_coarse.visc, [(k,) for k in range(g.blocks(0))])
        finer_near = near_counts(g, rows_ref, 2, patch, odd)
        covered = lane_limits(g, 1, finer_near, g.half_side)
        borrow(g, lent, limits, covered, low_fine, low_coarse)
        smooth_weights(g, 1, low_fine, limits[1], 0, rows, False)
        smooth_weights(g, 0, low_coarse, limits[0], 0, less, False)

        def store_fine(comp, k, row, chunk, value):
            low[comp, k, pl.ds(row, chunk), :] = value

        bottom_levels(
            g, rows_ref, patch, odd, 0, rows, low_fine, low_coarse,
            level_sums(g, sums, low_fine.weight), store_fine,
        )

        def load_low(comp, k, row, chunk):
            return low[comp, k, pl.ds(row, chunk), :]

        def load_held(comp, k, row, chunk):
            return edges[comp, k, pl.ds(row, chunk), :]

        def store_in(level, out, hold):
            own = g.own(level)

            def store(comp, k, row, chunk, value):
                if hold:
                    edges[comp, k, pl.ds(row, chunk), :] = value
                if k < own:
                    group, place = row // side, row % side
                    out[group * own + k, comp, pl.ds(pl.multiple_of(place, 8), chunk), :] = value

            return store

        for level, load, out in ((top - 1, load_low, coarser), (top, load_held, finer)):
            d = levels[level]
            clear_level(g, level, d)
            rows = g.rows(level)
            prolong_from(g, level, d, limits_of(level), 0, rows, load)
            corrected_step(g, level, d, 0, rows, store_in(level, out, level < top))
        hand_out()

    @pl.when(level_here < top - 1)
    def _():
        rows = g.rows(1)
        first = g.rows(2) // 2
        fine, coarse = levels[1], levels[0]._replace(cells=coarse_rows)
        smooth_weights(g, 1, fine, limits_of(1), first, rows, False)
        smooth_weights(g, 0, coarse, limits_of(0), first // 2, g.rows(0), False)

        def store_fine(comp, k, row, chunk, value):
            if k == 0:
                own_rows[comp, pl.ds(row, chunk), :] = value

        bottom_levels(g, rows_ref, patch, odd, first, rows, fine, coarse, None, store_fine)
        for r in range(rows // 2 // side, g.patch_rows(0)):
            here = pl.ds(r * side, side)
            for comp in range(2):
                coarse_rows[comp, 0, here, :] = (
                    coarse.weight[comp, 0, here, :] * coarse.right[comp, 0, here, :]
                )


def level_sums(g, sums, weight):
    reach = g.rows(2) // 2

    def value(comp, k):
        if k == 0:
            found = sums[pl.ds(comp * reach, reach), :]
        else:
            count, size = sums_groups(g)
            packed = sums[pl.ds(2 * reach, size), :]
            shifts = [sums_moves(g, group)[comp][0] for group in range(count)]
            parts = [pltpu.roll(packed, -shift % g.side, 1) for shift in shifts]
            found = jnp.concatenate(parts, axis=0)
        return jnp.where(weight[comp, k, pl.ds(0, reach), :] > 0.0, found, 0.0)

    return value


def low_kernel(
    g, rows_ref, sums, filled, kept, mine_in, theirs_in, own_rows, coarse_rows, mine, theirs, scratch, low_coarse, near_rows
):
    level_here = lax.axis_index("level")
    patch = lax.axis_index("patch")
    side = g.side
    top = g.levels - 1
    odd = level_here % 2 == 1

    @pl.when(level_here >= top - 1)
    def _():
        for k in range(g.half_slots):
            for comp in range(2):
                mine[k, comp] = mine_in[k, comp]
                theirs[k, comp] = theirs_in[k, comp]

    @pl.when(level_here < top - 1)
    def _():
        rows, _ = lent_rows(g)
        done = kept_rows(g)
        fine = merged(Level(filled[1].visc, kept[1]), scratch)
        coarse = merged(Level(None, kept[0], filled[0].right), low_coarse)
        for comp in range(2):
            for k in range(g.blocks(1)):
                fine.right[comp, k] = filled[1].right[comp, k, pl.ds(0, rows), :]

        def store_fine(comp, k, row, chunk, value):
            if k == 0:
                near_rows[comp, pl.ds(row, chunk), :] = value

        bottom_levels(
            g, rows_ref, patch, odd, 0, rows, fine, coarse,
            level_sums(g, sums, fine.weight), store_fine,
        )
        lane = lane_ids(side)
        size = rows // 2
        ids = lax.broadcasted_iota(jnp.int32, (size, side), 0)

        def coarse_group(comp, r):
            value = coarse_rows[comp, 0, pl.ds(r * side, side), :]
            if r:
                return value
            near = coarse.cells[comp, 0, pl.ds(0, size), :]
            near = jnp.where(ids < done // 2, near, value[:size])
            return jnp.concatenate([near, value[size:]], axis=0)

        def write(first, second):
            for comp in range(2):
                first[0, comp] = near_rows[comp, pl.ds(0, side), :]
                for r in range(1, g.patch_rows(1)):
                    first[r, comp] = own_rows[comp, pl.ds(r * side, side), :]
                first[1, comp, pl.ds(0, done - side), :] = near_rows[
                    comp, pl.ds(side, done - side), :
                ]
                for k in range(g.half_slots):
                    high = pltpu.roll(coarse_group(comp, k + g.half_slots), g.half_side, 1)
                    second[k, comp] = jnp.where(lane < g.half_side, coarse_group(comp, k), high)

        pl.when(odd)(lambda: write(mine, theirs))
        pl.when(jnp.logical_not(odd))(lambda: write(theirs, mine))


def join_kernel(g, mine, given, speed, fric, adjoint, gradient):
    level_here = lax.axis_index("level")
    lane = lane_ids(g.side)

    def put(slot, parts):
        for comp in range(2):
            adjoint[slot, comp] = parts[comp]
        total = speed[slot, 0].astype(F32) * parts[0] + speed[slot, 1].astype(F32) * parts[1]
        gradient[slot] = (-(fric[slot].astype(F32) * total)).astype(BF16)

    def join_level(level):
        if level == 0:
            for k in range(g.half_slots):
                low = []
                high = []
                for comp in range(2):
                    west, east = given[k, comp], mine[k, comp]
                    low.append(
                        jnp.where(lane < g.half_side, west, pltpu.roll(east, g.half_side, 1))
                    )
                    high.append(
                        jnp.where(lane < g.half_side, pltpu.roll(west, g.half_side, 1), east)
                    )
                put(k, low)
                put(k + g.half_slots, high)
            return
        own = g.own(level)
        west_half, east_half = (mine, given) if level % 2 == 1 else (given, mine)
        for r in range(g.patch_rows(level)):
            for k in range(2 * own):
                source = west_half if k < own else east_half
                put(
                    r * g.columns(level) + k,
                    [source[r * own + k % own, comp] for comp in range(2)],
                )

    for level in range(g.levels):
        pl.when(level_here == level)(lambda level=level: join_level(level))


def run_kernel(body, ins, outs, scratch, grant=VMEM_BYTES):
    in_trees = [jax.tree.flatten(tree) for tree, _ in ins]
    out_trees = [jax.tree.flatten(tree) for tree, _ in outs]
    scratch_trees = [jax.tree.flatten(tree) for tree in scratch]
    sizes = [len(leaves) for leaves, _ in in_trees + out_trees + scratch_trees]
    shapes = [tree for _, tree in in_trees + out_trees + scratch_trees]

    def kernel(*refs):
        given = []
        first = 0
        for size, shape in zip(sizes, shapes):
            given.append(jax.tree.unflatten(shape, refs[first : first + size]))
            first += size
        body(*given)

    def specs(groups, trees):
        return [
            pl.BlockSpec(memory_space=space)
            for (_, space), (leaves, _) in zip(groups, trees)
            for _ in leaves
        ]

    results = pl.pallas_call(
        kernel,
        out_shape=[leaf for leaves, _ in out_trees for leaf in leaves],
        in_specs=specs(ins, in_trees),
        out_specs=specs(outs, out_trees),
        scratch_shapes=[leaf for leaves, _ in scratch_trees for leaf in leaves],
        compiler_params=pltpu.CompilerParams(vmem_limit_bytes=grant),
    )(*[leaf for leaves, _ in in_trees for leaf in leaves])
    answer = []
    first = 0
    for leaves, shape in out_trees:
        answer.append(jax.tree.unflatten(shape, results[first : first + len(leaves)]))
        first += len(leaves)
    return answer


def moved(value, g, step):
    pairs = []
    for patch in range(g.patches):
        for level in range(g.levels):
            to_patch, to_level = step(patch, level)
            if 0 <= to_patch < g.patches and 0 <= to_level < g.levels:
                pairs.append((patch * g.levels + level, to_patch * g.levels + to_level))
    return lax.ppermute(value, ("patch", "level"), pairs)


def per_device(forcing, velocity, viscosity, friction, patch_rows):
    g = Layout(
        forcing.shape[1], forcing.shape[-1], lax.axis_size("level"), lax.axis_size("patch")
    )
    side = g.side
    top = g.levels - 1
    force, speed, visc, fric = forcing[0], velocity[0], viscosity[0], friction[0]
    make = jax.ShapeDtypeStruct
    vmem = pltpu.VMEM
    block = make((side, side), F32)
    half = make((g.half_slots, 2, side, side), F32)
    sums_rows = g.rows(2) + sums_groups(g)[1]

    def array(level, rows, kind, comps, pad):
        return level_array(g, g.blocks(level), rows, kind, comps, pad)

    own = (force, visc, fric)
    other = tuple(moved(value, g, lambda p, l: (p, l ^ 1)) for value in own)
    (edge,) = run_kernel(
        lambda *refs: first_edge_kernel(g, *refs),
        [(own, pltpu.HBM)],
        [(block, VM)],
        [
            pltpu.SemaphoreType.DMA((3 * g.slots,)),
            tuple(vmem(value.shape, value.dtype) for value in own),
        ],
        FIRST_BYTES,
    )
    (edge,) = run_kernel(
        lambda *refs: edge_kernel(g, *refs), [(edge, VM), (other, VM)], [(block, VM)], []
    )
    edge = moved(edge, g, lambda p, l: (p + (-1 if l % 2 else 1), l ^ 1))

    fields = [
        Level(
            array(level, g.rows(level), make, False, True),
            None,
            right=array(level, g.rows(level), make, True, False),
            fric=array(level, g.rows(level), make, False, False),
        )
        for level in range(g.levels)
    ]
    rows, less = lent_rows(g)
    given = [(patch_rows, SM), (own, VM), (other, VM), (edge, VM)]

    upper, lent = run_kernel(
        lambda *refs: fill_kernel(g, *refs),
        given,
        [(fields[top - 1 :], VM), (make((lent_size(g), side), BF16), VM)],
        [],
    )
    lent = moved(lent, g, lambda p, l: (p, l + 2))

    def kept_of(level):
        two = array(level, g.rows(level), make, True, False)
        return Level(None, two, held=two)

    low_weights = [array(0, less, make, True, False), array(1, rows, make, True, False)]

    def down_scratch(level):
        if level < top - 1:
            return Level(None, None)
        both = array(level, g.rows(level), vmem, True, False)
        more = dict(right=both) if level < top else {}
        return Level(None, None, left=both, **more, **step_arrays(g, level, g.rows(level)))

    sums, kept, low_kept, lower = run_kernel(
        lambda *refs: down_kernel(g, *refs),
        [*given, (upper, VM)],
        [
            (make((sums_rows, side), F32), VM),
            ([kept_of(level) for level in (top - 1, top)], VM),
            (low_weights, VM),
            (fields[: top - 1], VM),
        ],
        [vmem((2, side, side), F32), [down_scratch(level) for level in range(g.levels)]],
    )
    filled = [*lower, *upper]
    sums_there = moved(sums, g, lambda p, l: (p, l - 2))

    def up_scratch(level):
        both = array(level, g.rows(level), vmem, True, False)
        if level == 0:
            return Level(None, both)
        steps = step_arrays(g, level, g.rows(level))
        if level == 1:
            return Level(None, both, held=both, left=both, **steps)
        return Level(None, None, **steps)

    low_both = array(1, rows, vmem, True, False)
    low_steps = dict(held=low_both, left=low_both, right=low_both, **step_arrays(g, 1, rows))
    mine, theirs, own_rows, coarse_rows = run_kernel(
        lambda *refs: up_kernel(g, *refs),
        [
            (patch_rows, SM),
            (sums, VM),
            (lent, VM),
            (filled, VM),
            (kept, VM),
        ],
        [
            (half, VM),
            (half, VM),
            (make((2, g.rows(1), side), F32), VM),
            (make((2, 1, g.rows(0), side), F32), VM),
        ],
        [
            array(top - 1, g.rows(top - 1), vmem, True, False),
            [up_scratch(level) for level in range(g.levels)],
            low_both,
            Level(
                array(1, rows, vmem, False, True),
                low_both,
                fric=array(1, rows, vmem, False, False),
                **low_steps,
            ),
            Level(
                array(0, less, vmem, False, True),
                array(0, less, vmem, True, False),
                right=array(0, less, vmem, True, False),
                fric=array(0, less, vmem, False, False),
                cells=array(0, less, vmem, True, False),
            ),
            vmem(half.shape, F32),
            vmem(half.shape, F32),
        ],
    )
    mine, theirs = run_kernel(
        lambda *refs: low_kernel(g, *refs),
        [
            (patch_rows, SM),
            (sums_there, VM),
            (filled[:2], VM),
            (low_kept, VM),
            (mine, VM),
            (theirs, VM),
            (own_rows, VM),
            (coarse_rows, VM),
        ],
        [(half, VM), (half, VM)],
        [
            Level(None, None, **low_steps),
            Level(None, None, cells=array(0, less, vmem, True, False)),
            vmem((2, rows, side), F32),
        ],
    )
    received = moved(theirs, g, lambda p, l: (p, l ^ 1))
    adjoint, gradient = run_kernel(
        lambda *refs: join_kernel(g, *refs),
        [(mine, VM), (received, VM), (speed, VM), (fric, VM)],
        [
            (make((g.slots, 2, side, side), F32), VM),
            (make((g.slots, side, side), BF16), VM),
        ],
        [],
    )
    return (adjoint[None], gradient[None])


def solution(mesh):
    fields = P("level", "patch")
    return jax.shard_map(
        per_device,
        mesh=mesh,
        in_specs=(fields, fields, fields, fields, P()),
        out_specs=(fields, fields),
        check_vma=False,
    )
```

```python
from typing import Any, NamedTuple

import jax
import jax.numpy as jnp
from jax import lax
from jax.experimental import pallas as pl
from jax.experimental.pallas import tpu as pltpu
from jax.sharding import PartitionSpec as P

relaxation = 0.5
PAD = 8
LOW, HIGH, EDGES = 0, 1, 2
VM, SM = pltpu.VMEM, pltpu.SMEM
F32 = jnp.float32
BF16 = jnp.bfloat16
VMEM_BYTES = 30 * 2**20
FIRST_BYTES = 60 * 2**20


class Layout:
    def __init__(self, slots, side, levels, patches):
        self.slots = slots
        self.side = side
        self.levels = levels
        self.patches = patches
        self.half_slots = slots // 2
        self.half_side = side // 2
        self.span = 2 * slots

    def columns(self, level):
        return 1 << level

    def patch_rows(self, level):
        return self.slots >> level

    def rows(self, level):
        return self.patch_rows(level) * self.side

    def margin(self, level):
        return 2 << level

    def own(self, level):
        return max(1, (1 << level) // 2)

    def blocks(self, level):
        return self.own(level) + (1 if level > 0 else 0)

    def chunk(self, level, rows):
        size = 8 * max(1, 112 // self.blocks(level))
        while rows % size or (rows % self.side == 0 and self.side % size):
            size -= 8
        return size


def lane_ids(side):
    return lax.broadcasted_iota(jnp.int32, (1, side), 1)


def near_counts(g, rows_ref, level, patch, odd):
    own = rows_ref[level, patch]
    east = jnp.where(
        patch + 1 < g.patches, rows_ref[level, jnp.minimum(patch + 1, g.patches - 1)], 0
    )
    west = jnp.where(patch > 0, rows_ref[level, jnp.maximum(patch - 1, 0)], 0)
    return own, jnp.where(odd, own, east), jnp.where(odd, west, own)


def lane_limits(g, level, counts, cells):
    own, east, west = (value * cells for value in counts)
    lane = lane_ids(g.side)
    margin = g.margin(level)
    first = 0 if level > 0 else g.half_side
    edges = jnp.where(
        (lane >= first) & (lane < first + margin), east, jnp.where(lane >= g.side - margin, west, 0)
    )
    if level == 0:
        return [jnp.where(lane < g.half_side, own, edges)]
    return [jnp.full((1, g.side), own, jnp.int32)] * g.own(level) + [edges]


def one_side(g, values, east):
    count = len(values)
    turned = [pltpu.roll(value, g.side - 1 if east else 1, 1) for value in values]
    if count == 1:
        return turned
    lane = lax.broadcasted_iota(jnp.int32, values[0].shape, 1)
    last = lane == (g.side - 1 if east else 0)
    step = 1 if east else -1
    return [jnp.where(last, turned[(k + step) % count], turned[k]) for k in range(count)]


def both_sides(g, values):
    return one_side(g, values, True), one_side(g, values, False)


def over_rows(rows, chunk, body):
    def step(index, carry):
        body(pl.multiple_of(index * chunk, chunk))
        return carry

    lax.fori_loop(0, rows // chunk, step, 0)


def clear_pads(ref, lead):
    width = ref.shape[-1]
    last = ref.shape[-2]
    for index in lead:
        ref[index + (slice(0, PAD), slice(None))] = jnp.zeros((PAD, width), F32)
        ref[index + (slice(last - PAD, last), slice(None))] = jnp.zeros((PAD, width), F32)


def off_diagonal_rows(g, d, row, size, count):
    here = pl.ds(row, size)
    inner = pl.ds(PAD + row, size)
    centre = [[d.cells[comp, k, inner, :] for k in range(count)] for comp in range(2)]
    beside = [both_sides(g, centre[comp]) for comp in range(2)]
    products = []
    for k in range(count):
        visc = d.visc[k, inner, :]
        half = 0.5 * visc
        (u, v) = (centre[comp][k] for comp in range(2))
        (u_e, u_w), (v_e, v_w) = ((beside[c][0][k], beside[c][1][k]) for c in range(2))
        u_n, v_n = (d.cells[c, k, pl.ds(PAD + row + 1, size), :] for c in range(2))
        u_s, v_s = (d.cells[c, k, pl.ds(PAD + row - 1, size), :] for c in range(2))
        one_u, one_v = visc * u, visc * v
        four_u, four_v = 4.0 * one_u, 4.0 * one_v
        cross_u, cross_v = half * (v_e - v_w), visc * (u_e - u_w)
        d.north[0, k, inner, :] = one_u + cross_u
        d.south[0, k, inner, :] = one_u - cross_u
        d.north[1, k, inner, :] = four_v + cross_v
        d.south[1, k, inner, :] = four_v - cross_v
        cross_u, cross_v = visc * (v_n - v_s), half * (u_n - u_s)
        products.append(
            (
                four_u + cross_u,
                four_u - cross_u,
                one_v + cross_v,
                one_v - cross_v,
                visc * (4.0 * (u_e + u_w) + (u_n + u_s)),
                visc * (4.0 * (v_n + v_s) + (v_e + v_w)),
            )
        )
    for comp in range(2):
        east = one_side(g, [item[2 * comp] for item in products], True)
        west = one_side(g, [item[2 * comp + 1] for item in products], False)
        for k in range(count):
            d.part[comp, k, here, :] = products[k][4 + comp] + east[k] + west[k]


def off_diagonal_step(g, level, d, start, stop):
    count = g.blocks(level)
    chunk = g.chunk(level, stop - start)

    def body(row):
        for step in range(0, chunk, 8):
            off_diagonal_rows(g, d, start + row + step, 8, count)

    over_rows(stop - start, chunk, body)


def off_diagonal(d, comp, k, row, chunk):
    return (
        d.part[comp, k, pl.ds(row, chunk), :]
        + d.north[comp, k, pl.ds(PAD + row + 1, chunk), :]
        + d.south[comp, k, pl.ds(PAD + row - 1, chunk), :]
    )


def smooth_weights(g, level, d, limits, start, stop, from_zero):
    count = g.blocks(level)
    chunk = g.chunk(level, stop - start)

    def some_rows(row):
        here = pl.ds(row, 8)
        inner = pl.ds(PAD + row, 8)
        centre = [d.visc[k, inner, :] for k in range(count)]
        east, west = both_sides(g, centre)
        for k in range(count):
            north = d.visc[k, pl.ds(PAD + row + 1, 8), :]
            south = d.visc[k, pl.ds(PAD + row - 1, 8), :]
            friction = d.fric[k, here, :]
            twice = 2.0 * centre[k]
            along_row = twice + east[k] + west[k]
            along_col = twice + north + south
            live = jnp.broadcast_to(limits[k], (8, g.side)) > row
            diag_u = 4.0 * along_row + along_col + friction
            diag_v = 4.0 * along_col + along_row + friction
            for comp, diag in ((0, diag_u), (1, diag_v)):
                guess = pl.reciprocal(diag, approx=True)
                weight = guess * (2.0 * relaxation - relaxation * diag * guess)
                weight = jnp.where(live, weight, 0.0)
                d.weight[comp, k, here, :] = weight
                if from_zero:
                    d.cells[comp, k, inner, :] = weight * d.right[comp, k, here, :]

    def body(row):
        for step in range(0, chunk, 8):
            some_rows(start + row + step)

    over_rows(stop - start, chunk, body)


def residual_step(g, level, d, start, stop):
    count = g.blocks(level)
    chunk = g.chunk(level, stop - start)
    off_diagonal_step(g, level, d, start, stop)

    def body(row):
        row = row + start
        here = pl.ds(row, chunk)
        for comp in range(2):
            for k in range(count):
                weight = d.weight[comp, k, here, :]
                left = (1.0 - relaxation) * d.right[comp, k, here, :] + off_diagonal(
                    d, comp, k, row, chunk
                )
                left = jnp.where(weight > 0.0, left, 0.0)
                d.left[comp, k, here, :] = left
                d.held[comp, k, here, :] = (
                    d.cells[comp, k, pl.ds(PAD + row, chunk), :] + weight * left
                )

    over_rows(stop - start, chunk, body)


def corrected_step(g, level, d, start, stop, store):
    count = g.blocks(level)
    chunk = g.chunk(level, stop - start)
    off_diagonal_step(g, level, d, start, stop)

    def body(row):
        row = row + start
        here = pl.ds(row, chunk)
        for comp in range(2):
            for k in range(count):
                value = (
                    d.held[comp, k, here, :]
                    + (1.0 - relaxation) * d.cells[comp, k, pl.ds(PAD + row, chunk), :]
                    + d.weight[comp, k, here, :] * off_diagonal(d, comp, k, row, chunk)
                )
                store(comp, k, row, chunk, value)

    over_rows(stop - start, chunk, body)


def pairings(g, fine):
    if fine == 1:
        return [[(0, LOW), (1, HIGH)]]
    parts = [[(2 * k, LOW), (2 * k + 1, HIGH)] for k in range(g.own(fine) // 2)]
    return parts + [[(g.own(fine), EDGES)]]


def target_lane(g, part, fine_lane):
    halved = jnp.right_shift(fine_lane, 1)
    if part == LOW:
        return halved
    if part == HIGH:
        return g.half_side + halved
    return halved + jnp.where(fine_lane >= g.half_side, g.half_side, 0)


def sum_matrix(g, part):
    fine = lax.broadcasted_iota(jnp.int32, (g.side, g.side), 0)
    coarse = lax.broadcasted_iota(jnp.int32, (g.side, g.side), 1)
    return jnp.where(target_lane(g, part, fine) == coarse, 1.0, 0.0).astype(BF16)


def copy_matrix(g, part):
    coarse = lax.broadcasted_iota(jnp.int32, (g.side, g.side), 0)
    fine = lax.broadcasted_iota(jnp.int32, (g.side, g.side), 1)
    return jnp.where(target_lane(g, part, fine) == coarse, 1.0, 0.0).astype(BF16)


def split_dot(values, matrix):
    high = values.astype(BF16)
    rest = (values - high.astype(F32)).astype(BF16)
    return jnp.dot(high, matrix, preferred_element_type=F32) + jnp.dot(
        rest, matrix, preferred_element_type=F32
    )


def restrict_into(g, fine, d, start, stop, store):
    rows = stop - start
    chunk = min(rows // 2, g.half_side)
    if (rows // 2) % chunk:
        chunk = rows // 2
    parts = pairings(g, fine)
    matrices = {part: sum_matrix(g, part) for members in parts for _, part in members}

    def body(row):
        row = row + start // 2
        for comp in range(2):
            for coarse, members in enumerate(parts):
                total = None
                for k, part in members:
                    first = d.left[comp, k, pl.ds(2 * row, chunk, stride=2), :]
                    second = d.left[comp, k, pl.ds(2 * row + 1, chunk, stride=2), :]
                    term = split_dot(first + second, matrices[part])
                    total = term if total is None else total + term
                store(comp, coarse, row, chunk, total)

    over_rows(rows // 2, chunk, body)


def prolong_from(g, fine, d, limits, start, stop, load):
    rows = stop - start
    chunk = min(rows // 2, g.half_side)
    if (rows // 2) % chunk:
        chunk = rows // 2
    parts = pairings(g, fine)
    matrices = {part: copy_matrix(g, part) for members in parts for _, part in members}

    def body(row):
        row = row + start // 2
        ids = 2 * (row + lax.broadcasted_iota(jnp.int32, (chunk, g.side), 0))
        for comp in range(2):
            for coarse, members in enumerate(parts):
                value = load(comp, coarse, row, chunk)
                for k, part in members:
                    spread = jnp.where(ids < limits[k], split_dot(value, matrices[part]), 0.0)
                    d.cells[comp, k, pl.ds(PAD + 2 * row, chunk, stride=2), :] = spread
                    d.cells[comp, k, pl.ds(PAD + 2 * row + 1, chunk, stride=2), :] = spread

    over_rows(rows // 2, chunk, body)


def sums_groups(g):
    count = g.side // (4 * g.margin(1))
    return count, g.rows(2) // 2 // count


def sums_moves(g, group):
    margin = g.margin(1)
    base = 4 * margin * group
    return (base + margin, base), (base + 3 * margin, base + 2 * margin)


def packed_sums(g, edges):
    lane = lane_ids(g.side)
    count, size = sums_groups(g)
    total = jnp.zeros((size, g.side), F32)
    for group in range(count):
        for comp, (shift, first) in enumerate(sums_moves(g, group)):
            value = pltpu.roll(edges[comp, pl.ds(group * size, size), :], shift % g.side, 1)
            inside = (lane >= first) & (lane < first + 2 * g.margin(1))
            total = jnp.where(inside, value, total)
    return total


def plane(raw, q, slot):
    force, visc, fric = raw
    if q < 2:
        return force[slot, q].astype(F32)
    return (fric if q == 2 else visc)[slot].astype(F32)


def edge_lane(g, level, q, r):
    return (0 if level % 2 else g.half_side) + q * g.span + r * g.margin(level)


def packed_edge(g, here, level, patch_of):
    side = g.side
    lane = lane_ids(side)
    margin = g.margin(level)
    start = 0 if here % 2 else side - margin
    total = jnp.zeros((side, side), F32)
    for r in range(g.patch_rows(level)):
        for q in range(4):
            base = edge_lane(g, level, q, r)
            value = patch_of(q, r)
            if (base - start) % side:
                value = pltpu.roll(value, (base - start) % side, 1)
            total = jnp.where((lane >= base) & (lane < base + margin), value, total)
    return total


def edge_column(g, here, level):
    return 0 if here % 2 else g.columns(level) - 1


def first_edge_kernel(g, own, edge, sems, held):
    level_here = lax.axis_index("level")

    def pack(level):
        copies = Copies(sems)
        rows = g.patch_rows(level)
        if g.columns(level) == 1:
            for source, target in zip(own, held):
                copies.start(source, target)
        else:
            for r in range(rows):
                slot = r * g.columns(level) + edge_column(g, level, level)
                for source, target in zip(own, held):
                    copies.start(source.at[slot], target.at[r])
        copies.finish()
        edge[...] = packed_edge(g, level, level, lambda q, r: plane(held, q, r))

    for level in range(g.levels):
        pl.when(level_here == level)(lambda level=level: pack(level))


def edge_kernel(g, first, other, edge):
    level_here = lax.axis_index("level")

    def pack(here):
        level = here ^ 1
        column = edge_column(g, here, level)

        def patch_of(q, r):
            return plane(other, q, r * g.columns(level) + column)

        edge[...] = first[...] + packed_edge(g, here, level, patch_of)

    for here in range(g.levels):
        pl.when(level_here == here)(lambda here=here: pack(here))


def fill_level(g, level, west_type, d, limits, covered, raw, edge, groups):
    side = g.side
    margin = g.margin(level)
    own = g.own(level)
    columns = g.columns(level)
    lane = lane_ids(side)

    def outer(q, r, place):
        shift = (place - edge_lane(g, level, q, r)) % side
        return pltpu.roll(edge[...], shift, 1) if shift else edge[...]

    def store(q, k, r, value):
        here = pl.ds(r * side, side)
        if q < 2:
            if covered is not None:
                ids = r * side + lax.broadcasted_iota(jnp.int32, (side, side), 0)
                value = jnp.where(ids < covered[k], 0.0, value)
            d.right[q, k, here, :] = value
        elif q == 2:
            d.fric[k, here, :] = value
        else:
            d.visc[k, pl.ds(PAD + r * side, side), :] = jnp.where(
                limits[k] > r * side, 0.5 * value, 0.0
            )

    clear_pads(d.visc, [(k,) for k in range(g.blocks(level))])
    for r in range(groups):
        for q in range(4):
            if level == 0 and west_type:
                west = outer(q, r, side - margin)
                store(q, 0, r, jnp.where(lane >= side - margin, west, plane(raw, q, r)))
            elif level == 0:
                value = pltpu.roll(plane(raw, q, r), g.half_side, 1)
                here = (lane >= g.half_side) & (lane < g.half_side + margin)
                store(q, 0, r, jnp.where(here, outer(q, r, g.half_side), value))
            else:
                for k in range(own):
                    store(q, k, r, plane(raw, q, r * columns + k + (0 if west_type else own)))
                if west_type:
                    east = plane(raw, q, r * columns + own)
                    west = outer(q, r, side - margin)
                else:
                    east = outer(q, r, 0)
                    west = plane(raw, q, r * columns + own - 1)
                store(q, own, r, jnp.where(lane < g.half_side, east, west))


class Level(NamedTuple):
    visc: Any
    weight: Any
    right: Any = None
    held: Any = None
    fric: Any = None
    cells: Any = None
    part: Any = None
    north: Any = None
    south: Any = None
    left: Any = None


def level_array(g, count, rows, make, comps, pad):
    shape = (count, rows + (2 * PAD if pad else 0), g.side)
    return make((2, *shape) if comps else shape, F32)


def step_arrays(g, level, rows):
    count = g.blocks(level)
    padded = level_array(g, count, rows, pltpu.VMEM, True, True)
    return dict(
        cells=padded,
        part=level_array(g, count, rows, pltpu.VMEM, True, False),
        north=padded,
        south=padded,
    )


def clear_level(g, level, d):
    blocks = range(g.blocks(level))
    both = [(c, k) for c in range(2) for k in blocks]
    for ref in (d.cells, d.north, d.south):
        clear_pads(ref, both)


def merged(first, second):
    return Level(*[b if a is None else a for a, b in zip(first, second)])


class Copies:
    def __init__(self, sems, first=0):
        self.sems = sems
        self.used = first
        self.open = []

    def start(self, source, target):
        copy = pltpu.make_async_copy(source, target, self.sems.at[self.used])
        self.used += 1
        copy.start()
        self.open.append(copy)

    def finish(self):
        for copy in self.open:
            copy.wait()
        self.open = []


def low_rows(g):
    return g.rows(2) // 2 + 2 * PAD


def kept_rows(g):
    return g.rows(2) // 2 + PAD


def lent_rows(g):
    return low_rows(g), -(-low_rows(g) // 2 // 16) * 16


def lent_forcing(g):
    return [count * g.half_side for count in range(1, g.patch_rows(2) + 1)]


def lent_size(g):
    rows, less = lent_rows(g)
    return 4 * rows + 2 * 16 * len(lent_forcing(g)) + 2 * less + 16


def pair_of(visc):
    high = visc.astype(BF16)
    return [high, (visc - high.astype(F32)).astype(BF16)]


class Rows:
    def __init__(self, ref):
        self.ref = ref
        self.place = 0

    def put(self, value):
        size = value.shape[0]
        self.ref[pl.ds(self.place, size), :] = value.astype(BF16)
        self.place += size

    def take(self, size):
        value = self.ref[pl.ds(self.place, size), :].astype(F32)
        self.place += size
        return value


def side_by_side(g, low, high):
    lane = lane_ids(g.side)
    return jnp.where(
        lane < g.half_side, low.astype(F32), pltpu.roll(high.astype(F32), g.half_side, 1)
    )


def lend(g, west_type, own, other, edge, out):
    rows, less = lent_rows(g)
    side = g.side
    fine, coarse = (own, other) if west_type else (other, own)
    target = Rows(out)

    def some_rows(raw, q, slot, first, size):
        here = pl.ds(first, size)
        force, visc, fric = raw
        value = force[slot, q, here, :] if q < 2 else (fric if q == 2 else visc)[slot, here, :]
        return 0.5 * value if q == 3 else value

    def fine_rows(q, first, size, column=0 if west_type else g.own(1)):
        parts = []
        while size:
            group, place = first // side, first % side
            part = min(size, side - place)
            slot = group * g.columns(1) + column
            parts.append(some_rows(fine, q, slot, place, part))
            first, size = first + part, size - part
        return parts

    for part in fine_rows(2, 0, rows):
        target.put(part)
    pairs = [pair_of(part) for part in fine_rows(3, 0, rows)]
    for index in range(2):
        for pair in pairs:
            target.put(pair[index])
    for comp in range(2):
        for first in lent_forcing(g):
            for part in fine_rows(comp, first, 16):
                target.put(part)

    def coarse_rows(q, first, size):
        value = some_rows(coarse, q, 0, first, size).astype(F32)
        return value if west_type else pltpu.roll(value, g.half_side, 1)

    high, rest = pair_of(coarse_rows(3, 0, less))
    target.put(side_by_side(g, coarse_rows(2, 0, less), high))
    target.put(rest)
    target.put(
        side_by_side(g, coarse_rows(0, g.half_side, 16), coarse_rows(1, g.half_side, 16))
    )
    lane = lane_ids(side)

    def outer_plane(level, q, size, place):
        parts = []
        for r in range(-(-size // side)):
            part = edge[pl.ds(0, min(side, size - r * side)), :]
            shift = (place - edge_lane(g, level, q, r)) % side
            parts.append(pltpu.roll(part, shift, 1) if shift else part)
        value = jnp.concatenate(parts, axis=0) if len(parts) > 1 else parts[0]
        return 0.5 * value if q == 3 else value

    def margins(level, size):
        column = g.own(1) if west_type else g.own(1) - 1
        total = jnp.zeros((size, side), F32)
        for q in range(4):
            if level:
                parts = fine_rows(q, 0, size, column)
                inner = jnp.concatenate([part.astype(F32) for part in parts], axis=0)
            else:
                inner = coarse_rows(q, 0, size)
            for west in (True, False):
                if west == west_type:
                    place = margin_moves(g, level, q)[0 if west else 1][0]
                    value = outer_plane(level, q, size, place)
                else:
                    value = inner
                for offset, part in enumerate(pair_of(value) if q == 3 else [value]):
                    place, target_lane = margin_moves(g, level, q + offset)[0 if west else 1]
                    shifted = pltpu.roll(part.astype(F32), (target_lane - place) % side, 1)
                    here = (lane >= target_lane) & (lane < target_lane + g.margin(level))
                    total = jnp.where(here, shifted, total)
        return total

    fine_part = margins(1, rows)
    target.put(fine_part[:less] + margins(0, less))
    target.put(fine_part[less:])


def margin_moves(g, level, index):
    margin = g.margin(level)
    base = 2 * margin * index + (0 if level else 2 * g.margin(1) * 5)
    return (g.side - margin, base), ((0 if level else g.half_side), base + margin)


def edges_of(g, level, west, east):
    lane = lane_ids(g.side)
    middle = g.side - g.half_side // 2 if level == 0 else g.half_side
    return jnp.where(lane < middle, east, west)


def borrow(g, lent, limits, covered, fine, coarse):
    rows, less = lent_rows(g)
    side = g.side
    lane = lane_ids(side)
    source = Rows(lent)

    def masked(value, bounds, inside):
        ids = lax.broadcasted_iota(jnp.int32, value.shape, 0)
        return jnp.where((ids < bounds) == inside, value, 0.0)

    fine.fric[0] = source.take(rows)
    high = source.take(rows)
    fine.visc[0, pl.ds(PAD, rows), :] = masked(high + source.take(rows), limits[1][0], True)
    for comp in range(2):
        fine.right[comp, 0] = jnp.zeros((rows, side), F32)
        for first in lent_forcing(g):
            value = masked(source.take(16), covered[0] - first, False)
            fine.right[comp, 0, pl.ds(first, 16), :] = value
    first, rest, window = source.take(less), source.take(less), source.take(16)
    packed = source.take(rows)

    def margins(level, q, size):
        moves = [margin_moves(g, level, index) for index in ((q,) if q < 3 else (3, 4))]
        west, east = (
            sum(
                pltpu.roll(packed[:size], (move[at][0] - move[at][1]) % side, 1)
                for move in moves
            )
            for at in range(2)
        )
        return edges_of(g, level, west, east)

    for comp in range(2):
        fine.right[comp, 1] = masked(margins(1, comp, rows), covered[1], False)
    fine.fric[1] = margins(1, 2, rows)
    fine.visc[1, pl.ds(PAD, rows), :] = masked(margins(1, 3, rows), limits[1][1], True)

    def with_margins(value, q):
        return jnp.where(lane < g.half_side, value, margins(0, q, less))

    coarse.fric[0] = with_margins(first, 2)
    value = with_margins(pltpu.roll(first, g.half_side, 1) + rest, 3)
    coarse.visc[0, pl.ds(PAD, less), :] = masked(value, limits[0][0], True)
    for comp in range(2):
        value = pltpu.roll(window, g.half_side, 1) if comp else window
        value = jnp.concatenate([jnp.zeros((g.half_side, side), F32), value], axis=0)
        coarse.right[comp, 0] = with_margins(value, comp)


def fill_pair(g, rows_ref, own, other, edge, levels, wanted, groups):
    level_here = lax.axis_index("level")
    patch = lax.axis_index("patch")
    odd = level_here % 2 == 1
    for west_type in (True, False):

        @pl.when(odd if west_type else jnp.logical_not(odd))
        def _():
            for level in wanted:
                near = near_counts(g, rows_ref, level, patch, odd)
                limits = lane_limits(g, level, near, g.side)
                covered = None
                if level == 1:
                    finer = near_counts(g, rows_ref, 2, patch, odd)
                    covered = lane_limits(g, 1, finer, g.half_side)
                home = (level % 2 == 1) == west_type
                raw = own if home else other
                fill_level(
                    g, level, west_type, levels[level], limits, covered, raw, edge, groups(level)
                )


def lend_kernel(g, own, other, edge, lent):
    level_here = lax.axis_index("level")
    for level in range(g.levels - 2):
        pl.when(level_here == level)(
            lambda level=level: lend(g, level % 2 == 1, own, other, edge, lent)
        )


def fill_kernel(g, rows_ref, own, other, edge, _, filled):
    level_here = lax.axis_index("level")
    top = g.levels - 1

    @pl.when(level_here >= top - 1)
    def _():
        levels = dict(zip((top - 1, top), filled))
        fill_pair(g, rows_ref, own, other, edge, levels, (top, top - 1), g.patch_rows)


def down_kernel(
    g, rows_ref, own, other, edge, upper, sums, kept, low_kept, lower, edges, scratch
):
    level_here = lax.axis_index("level")
    patch = lax.axis_index("patch")
    side = g.side
    top = g.levels - 1
    odd = level_here % 2 == 1
    filled = [*lower, *upper]
    kept = [*(Level(None, weight) for weight in low_kept), *kept]
    levels = [merged(merged(a, b), c) for a, b, c in zip(scratch, kept, filled)]

    def limits_of(level):
        return lane_limits(g, level, near_counts(g, rows_ref, level, patch, odd), side)

    @pl.when(level_here >= top - 1)
    def _():
        near = near_counts(g, rows_ref, top, patch, odd)
        covered = lane_limits(g, top - 1, near, g.half_side)
        given = filled[top - 1].right
        reach = g.rows(2) // 2
        for comp in range(2):
            for k in range(g.blocks(top - 1)):
                rest = pl.ds(g.half_side, g.rows(top - 1) - g.half_side)
                levels[top - 1].right[comp, k, rest, :] = given[comp, k, rest, :]

        def set_right(comp, k, row, chunk, value):
            here = pl.ds(row, chunk)
            ids = row + lax.broadcasted_iota(jnp.int32, (chunk, side), 0)
            levels[top - 1].right[comp, k, here, :] = jnp.where(
                ids < covered[k], value, given[comp, k, here, :]
            )

        def keep(comp, k, row, chunk, value):
            if k == 0:
                sums[pl.ds(comp * reach + row, chunk), :] = value
            else:
                edges[comp, pl.ds(row, chunk), :] = value

        for level in (top, top - 1):
            d = levels[level]
            clear_level(g, level, d)
            smooth_weights(g, level, d, limits_of(level), 0, g.rows(level), True)
            residual_step(g, level, d, 0, g.rows(level))
            restrict_into(g, level, d, 0, g.rows(level), set_right if level == top else keep)
        packed = packed_sums(g, edges)
        sums[pl.ds(2 * reach, packed.shape[0]), :] = packed

    @pl.when(level_here < top - 1)
    def _():
        fill_pair(g, rows_ref, own, other, edge, levels, (1, 0), g.patch_rows)
        for level, size in zip((1, 0), lent_rows(g)):
            smooth_weights(g, level, levels[level], limits_of(level), 0, size, False)


def bottom_levels(g, rows_ref, patch, odd, start, stop, fine, coarse, new_sums, store_fine):
    side = g.side
    count, chunk = g.blocks(1), g.chunk(1, stop - start)
    clear_level(g, 1, fine)
    if new_sums is not None:
        reach = g.rows(2) // 2
        for comp in range(2):
            for k in range(count):
                here = pl.ds(0, reach)
                fine.right[comp, k, here, :] = fine.right[comp, k, here, :] + new_sums(comp, k)

    def body(row):
        here = pl.ds(start + row, chunk)
        for comp in range(2):
            for k in range(count):
                fine.cells[comp, k, pl.ds(PAD + start + row, chunk), :] = (
                    fine.weight[comp, k, here, :] * fine.right[comp, k, here, :]
                )

    over_rows(stop - start, chunk, body)
    residual_step(g, 1, fine, start, stop)
    near = near_counts(g, rows_ref, 1, patch, odd)
    covered = lane_limits(g, 0, near, g.half_side)

    def smooth_coarse(comp, k, row, size, value):
        here = pl.ds(row, size)
        ids = row + lax.broadcasted_iota(jnp.int32, (size, side), 0)
        value = jnp.where(ids < covered[0], value, coarse.right[comp, 0, here, :])
        value = coarse.weight[comp, 0, here, :] * value
        coarse.cells[comp, 0, here, :] = value

    restrict_into(g, 1, fine, start, stop, smooth_coarse)

    def load(comp, k, row, size):
        return coarse.cells[comp, 0, pl.ds(row, size), :]

    prolong_from(g, 1, fine, lane_limits(g, 1, near, side), start, stop, load)
    corrected_step(g, 1, fine, start, stop, store_fine)


def up_kernel(
    g, rows_ref, sums, lent, filled, kept, mine, theirs, own_rows, coarse_rows, edges, scratch, low, low_fine,
    low_coarse, finer, coarser,
):
    level_here = lax.axis_index("level")
    patch = lax.axis_index("patch")
    side = g.side
    top = g.levels - 1
    odd = level_here % 2 == 1
    levels = [merged(a, b) for a, b in zip(scratch, filled)]
    for level in (top - 1, top):
        levels[level] = merged(levels[level], kept[level - top + 1])

    def limits_of(level):
        return lane_limits(g, level, near_counts(g, rows_ref, level, patch, odd), side)

    def hand_out():
        def write(first, second):
            for k in range(g.half_slots):
                for comp in range(2):
                    first[k, comp] = finer[k, comp]
                    second[k, comp] = coarser[k, comp]

        pl.when(odd)(lambda: write(mine, theirs))
        pl.when(jnp.logical_not(odd))(lambda: write(theirs, mine))

    @pl.when(level_here >= top - 1)
    def _():
        rows, less = lent_rows(g)
        limits = {level: limits_of(level) for level in (0, 1)}
        clear_pads(low_fine.visc, [(k,) for k in range(g.blocks(1))])
        clear_pads(low_coarse.visc, [(k,) for k in range(g.blocks(0))])
        finer_near = near_counts(g, rows_ref, 2, patch, odd)
        covered = lane_limits(g, 1, finer_near, g.half_side)
        borrow(g, lent, limits, covered, low_fine, low_coarse)
        smooth_weights(g, 1, low_fine, limits[1], 0, rows, False)
        smooth_weights(g, 0, low_coarse, limits[0], 0, less, False)

        def store_fine(comp, k, row, chunk, value):
            low[comp, k, pl.ds(row, chunk), :] = value

        bottom_levels(
            g, rows_ref, patch, odd, 0, rows, low_fine, low_coarse,
            level_sums(g, sums, low_fine.weight), store_fine,
        )

        def load_low(comp, k, row, chunk):
            return low[comp, k, pl.ds(row, chunk), :]

        def load_held(comp, k, row, chunk):
            return edges[comp, k, pl.ds(row, chunk), :]

        def store_in(level, out, hold):
            own = g.own(level)

            def store(comp, k, row, chunk, value):
                if hold:
                    edges[comp, k, pl.ds(row, chunk), :] = value
                if k < own:
                    group, place = row // side, row % side
                    out[group * own + k, comp, pl.ds(pl.multiple_of(place, 8), chunk), :] = value

            return store

        for level, load, out in ((top - 1, load_low, coarser), (top, load_held, finer)):
            d = levels[level]
            clear_level(g, level, d)
            rows = g.rows(level)
            prolong_from(g, level, d, limits_of(level), 0, rows, load)
            corrected_step(g, level, d, 0, rows, store_in(level, out, level < top))
        hand_out()

    @pl.when(level_here < top - 1)
    def _():
        rows = g.rows(1)
        first = g.rows(2) // 2
        fine, coarse = levels[1], levels[0]._replace(cells=coarse_rows)
        smooth_weights(g, 1, fine, limits_of(1), first, rows, False)
        smooth_weights(g, 0, coarse, limits_of(0), first // 2, g.rows(0), False)

        def store_fine(comp, k, row, chunk, value):
            if k == 0:
                own_rows[comp, pl.ds(row, chunk), :] = value

        bottom_levels(g, rows_ref, patch, odd, first, rows, fine, coarse, None, store_fine)
        for r in range(rows // 2 // side, g.patch_rows(0)):
            here = pl.ds(r * side, side)
            for comp in range(2):
                coarse_rows[comp, 0, here, :] = (
                    coarse.weight[comp, 0, here, :] * coarse.right[comp, 0, here, :]
                )


def level_sums(g, sums, weight):
    reach = g.rows(2) // 2

    def value(comp, k):
        if k == 0:
            found = sums[pl.ds(comp * reach, reach), :]
        else:
            count, size = sums_groups(g)
            packed = sums[pl.ds(2 * reach, size), :]
            shifts = [sums_moves(g, group)[comp][0] for group in range(count)]
            parts = [pltpu.roll(packed, -shift % g.side, 1) for shift in shifts]
            found = jnp.concatenate(parts, axis=0)
        return jnp.where(weight[comp, k, pl.ds(0, reach), :] > 0.0, found, 0.0)

    return value


def low_kernel(
    g, rows_ref, sums, filled, kept, mine_in, theirs_in, own_rows, coarse_rows, mine, theirs, scratch, low_coarse, near_rows
):
    level_here = lax.axis_index("level")
    patch = lax.axis_index("patch")
    side = g.side
    top = g.levels - 1
    odd = level_here % 2 == 1

    @pl.when(level_here >= top - 1)
    def _():
        for k in range(g.half_slots):
            for comp in range(2):
                mine[k, comp] = mine_in[k, comp]
                theirs[k, comp] = theirs_in[k, comp]

    @pl.when(level_here < top - 1)
    def _():
        rows, _ = lent_rows(g)
        done = kept_rows(g)
        fine = merged(Level(filled[1].visc, kept[1]), scratch)
        coarse = merged(Level(None, kept[0], filled[0].right), low_coarse)
        for comp in range(2):
            for k in range(g.blocks(1)):
                fine.right[comp, k] = filled[1].right[comp, k, pl.ds(0, rows), :]

        def store_fine(comp, k, row, chunk, value):
            if k == 0:
                near_rows[comp, pl.ds(row, chunk), :] = value

        bottom_levels(
            g, rows_ref, patch, odd, 0, rows, fine, coarse,
            level_sums(g, sums, fine.weight), store_fine,
        )
        lane = lane_ids(side)
        size = rows // 2
        ids = lax.broadcasted_iota(jnp.int32, (size, side), 0)

        def coarse_group(comp, r):
            value = coarse_rows[comp, 0, pl.ds(r * side, side), :]
            if r:
                return value
            near = coarse.cells[comp, 0, pl.ds(0, size), :]
            near = jnp.where(ids < done // 2, near, value[:size])
            return jnp.concatenate([near, value[size:]], axis=0)

        def write(first, second):
            for comp in range(2):
                first[0, comp] = near_rows[comp, pl.ds(0, side), :]
                for r in range(1, g.patch_rows(1)):
                    first[r, comp] = own_rows[comp, pl.ds(r * side, side), :]
                first[1, comp, pl.ds(0, done - side), :] = near_rows[
                    comp, pl.ds(side, done - side), :
                ]
                for k in range(g.half_slots):
                    high = pltpu.roll(coarse_group(comp, k + g.half_slots), g.half_side, 1)
                    second[k, comp] = jnp.where(lane < g.half_side, coarse_group(comp, k), high)

        pl.when(odd)(lambda: write(mine, theirs))
        pl.when(jnp.logical_not(odd))(lambda: write(theirs, mine))


def join_kernel(g, mine, given, speed, fric, adjoint, gradient):
    level_here = lax.axis_index("level")
    lane = lane_ids(g.side)

    def put(slot, parts):
        for comp in range(2):
            adjoint[slot, comp] = parts[comp]
        total = speed[slot, 0].astype(F32) * parts[0] + speed[slot, 1].astype(F32) * parts[1]
        gradient[slot] = (-(fric[slot].astype(F32) * total)).astype(BF16)

    def join_level(level):
        if level == 0:
            for k in range(g.half_slots):
                low = []
                high = []
                for comp in range(2):
                    west, east = given[k, comp], mine[k, comp]
                    low.append(
                        jnp.where(lane < g.half_side, west, pltpu.roll(east, g.half_side, 1))
                    )
                    high.append(
                        jnp.where(lane < g.half_side, pltpu.roll(west, g.half_side, 1), east)
                    )
                put(k, low)
                put(k + g.half_slots, high)
            return
        own = g.own(level)
        west_half, east_half = (mine, given) if level % 2 == 1 else (given, mine)
        for r in range(g.patch_rows(level)):
            for k in range(2 * own):
                source = west_half if k < own else east_half
                put(
                    r * g.columns(level) + k,
                    [source[r * own + k % own, comp] for comp in range(2)],
                )

    for level in range(g.levels):
        pl.when(level_here == level)(lambda level=level: join_level(level))


def run_kernel(body, ins, outs, scratch, grant=VMEM_BYTES):
    in_trees = [jax.tree.flatten(tree) for tree, _ in ins]
    out_trees = [jax.tree.flatten(tree) for tree, _ in outs]
    scratch_trees = [jax.tree.flatten(tree) for tree in scratch]
    sizes = [len(leaves) for leaves, _ in in_trees + out_trees + scratch_trees]
    shapes = [tree for _, tree in in_trees + out_trees + scratch_trees]

    def kernel(*refs):
        given = []
        first = 0
        for size, shape in zip(sizes, shapes):
            given.append(jax.tree.unflatten(shape, refs[first : first + size]))
            first += size
        body(*given)

    def specs(groups, trees):
        return [
            pl.BlockSpec(memory_space=space)
            for (_, space), (leaves, _) in zip(groups, trees)
            for _ in leaves
        ]

    results = pl.pallas_call(
        kernel,
        out_shape=[leaf for leaves, _ in out_trees for leaf in leaves],
        in_specs=specs(ins, in_trees),
        out_specs=specs(outs, out_trees),
        scratch_shapes=[leaf for leaves, _ in scratch_trees for leaf in leaves],
        compiler_params=pltpu.CompilerParams(vmem_limit_bytes=grant),
    )(*[leaf for leaves, _ in in_trees for leaf in leaves])
    answer = []
    first = 0
    for leaves, shape in out_trees:
        answer.append(jax.tree.unflatten(shape, results[first : first + len(leaves)]))
        first += len(leaves)
    return answer


def moved(value, g, step):
    pairs = []
    for patch in range(g.patches):
        for level in range(g.levels):
            to_patch, to_level = step(patch, level)
            if 0 <= to_patch < g.patches and 0 <= to_level < g.levels:
                pairs.append((patch * g.levels + level, to_patch * g.levels + to_level))
    return lax.ppermute(value, ("patch", "level"), pairs)


def per_device(forcing, velocity, viscosity, friction, patch_rows):
    g = Layout(
        forcing.shape[1], forcing.shape[-1], lax.axis_size("level"), lax.axis_size("patch")
    )
    side = g.side
    top = g.levels - 1
    force, speed, visc, fric = forcing[0], velocity[0], viscosity[0], friction[0]
    make = jax.ShapeDtypeStruct
    vmem = pltpu.VMEM
    block = make((side, side), F32)
    half = make((g.half_slots, 2, side, side), F32)
    sums_rows = g.rows(2) + sums_groups(g)[1]

    def array(level, rows, kind, comps, pad):
        return level_array(g, g.blocks(level), rows, kind, comps, pad)

    own = (force, visc, fric)
    other = tuple(moved(value, g, lambda p, l: (p, l ^ 1)) for value in own)
    (edge,) = run_kernel(
        lambda *refs: first_edge_kernel(g, *refs),
        [(own, pltpu.HBM)],
        [(block, VM)],
        [
            pltpu.SemaphoreType.DMA((3 * g.slots,)),
            tuple(vmem(value.shape, value.dtype) for value in own),
        ],
        FIRST_BYTES,
    )
    (edge,) = run_kernel(
        lambda *refs: edge_kernel(g, *refs), [(edge, VM), (other, VM)], [(block, VM)], []
    )
    edge = moved(edge, g, lambda p, l: (p + (-1 if l % 2 else 1), l ^ 1))

    fields = [
        Level(
            array(level, g.rows(level), make, False, True),
            None,
            right=array(level, g.rows(level), make, True, False),
            fric=array(level, g.rows(level), make, False, False),
        )
        for level in range(g.levels)
    ]
    rows, less = lent_rows(g)
    given = [(patch_rows, SM), (own, VM), (other, VM), (edge, VM)]

    (lent_here,) = run_kernel(
        lambda *refs: lend_kernel(g, *refs),
        given[1:],
        [(make((lent_size(g), side), BF16), VM)],
        [],
    )
    lent = moved(lent_here, g, lambda p, l: (p, l + 2))
    (upper,) = run_kernel(
        lambda *refs: fill_kernel(g, *refs),
        [*given, (lent_here, VM)],
        [(fields[top - 1 :], VM)],
        [],
    )

    def kept_of(level):
        two = array(level, g.rows(level), make, True, False)
        return Level(None, two, held=two)

    low_weights = [array(0, less, make, True, False), array(1, rows, make, True, False)]

    def down_scratch(level):
        if level < top - 1:
            return Level(None, None)
        both = array(level, g.rows(level), vmem, True, False)
        more = dict(right=both) if level < top else {}
        return Level(None, None, left=both, **more, **step_arrays(g, level, g.rows(level)))

    sums, kept, low_kept, lower = run_kernel(
        lambda *refs: down_kernel(g, *refs),
        [*given, (upper, VM)],
        [
            (make((sums_rows, side), F32), VM),
            ([kept_of(level) for level in (top - 1, top)], VM),
            (low_weights, VM),
            (fields[: top - 1], VM),
        ],
        [vmem((2, side, side), F32), [down_scratch(level) for level in range(g.levels)]],
    )
    filled = [*lower, *upper]
    sums_there = moved(sums, g, lambda p, l: (p, l - 2))

    def up_scratch(level):
        both = array(level, g.rows(level), vmem, True, False)
        if level == 0:
            return Level(None, both)
        steps = step_arrays(g, level, g.rows(level))
        if level == 1:
            return Level(None, both, held=both, left=both, **steps)
        return Level(None, None, **steps)

    low_both = array(1, rows, vmem, True, False)
    low_steps = dict(held=low_both, left=low_both, right=low_both, **step_arrays(g, 1, rows))
    mine, theirs, own_rows, coarse_rows = run_kernel(
        lambda *refs: up_kernel(g, *refs),
        [
            (patch_rows, SM),
            (sums, VM),
            (lent, VM),
            (filled, VM),
            (kept, VM),
        ],
        [
            (half, VM),
            (half, VM),
            (make((2, g.rows(1), side), F32), VM),
            (make((2, 1, g.rows(0), side), F32), VM),
        ],
        [
            array(top - 1, g.rows(top - 1), vmem, True, False),
            [up_scratch(level) for level in range(g.levels)],
            low_both,
            Level(
                array(1, rows, vmem, False, True),
                low_both,
                fric=array(1, rows, vmem, False, False),
                **low_steps,
            ),
            Level(
                array(0, less, vmem, False, True),
                array(0, less, vmem, True, False),
                right=array(0, less, vmem, True, False),
                fric=array(0, less, vmem, False, False),
                cells=array(0, less, vmem, True, False),
            ),
            vmem(half.shape, F32),
            vmem(half.shape, F32),
        ],
    )
    mine, theirs = run_kernel(
        lambda *refs: low_kernel(g, *refs),
        [
            (patch_rows, SM),
            (sums_there, VM),
            (filled[:2], VM),
            (low_kept, VM),
            (mine, VM),
            (theirs, VM),
            (own_rows, VM),
            (coarse_rows, VM),
        ],
        [(half, VM), (half, VM)],
        [
            Level(None, None, **low_steps),
            Level(None, None, cells=array(0, less, vmem, True, False)),
            vmem((2, rows, side), F32),
        ],
    )
    received = moved(theirs, g, lambda p, l: (p, l ^ 1))
    adjoint, gradient = run_kernel(
        lambda *refs: join_kernel(g, *refs),
        [(mine, VM), (received, VM), (speed, VM), (fric, VM)],
        [
            (make((g.slots, 2, side, side), F32), VM),
            (make((g.slots, side, side), BF16), VM),
        ],
        [],
    )
    return (adjoint[None], gradient[None])


def solution(mesh):
    fields = P("level", "patch")
    return jax.shard_map(
        per_device,
        mesh=mesh,
        in_specs=(fields, fields, fields, fields, P()),
        out_specs=(fields, fields),
        check_vma=False,
    )
```

```python
from typing import Any, NamedTuple

import jax
import jax.numpy as jnp
from jax import lax
from jax.experimental import pallas as pl
from jax.experimental.pallas import tpu as pltpu
from jax.sharding import PartitionSpec as P

relaxation = 0.5
PAD = 8
LOW, HIGH, EDGES = 0, 1, 2
VM, SM = pltpu.VMEM, pltpu.SMEM
F32 = jnp.float32
BF16 = jnp.bfloat16
VMEM_BYTES = 30 * 2**20
FIRST_BYTES = 60 * 2**20


class Layout:
    def __init__(self, slots, side, levels, patches):
        self.slots = slots
        self.side = side
        self.levels = levels
        self.patches = patches
        self.half_slots = slots // 2
        self.half_side = side // 2
        self.span = 2 * slots

    def columns(self, level):
        return 1 << level

    def patch_rows(self, level):
        return self.slots >> level

    def rows(self, level):
        return self.patch_rows(level) * self.side

    def margin(self, level):
        return 2 << level

    def own(self, level):
        return max(1, (1 << level) // 2)

    def blocks(self, level):
        return self.own(level) + (1 if level > 0 else 0)

    def chunk(self, level, rows):
        size = 8 * max(1, 112 // self.blocks(level))
        while rows % size or (rows % self.side == 0 and self.side % size):
            size -= 8
        return size


def lane_ids(side):
    return lax.broadcasted_iota(jnp.int32, (1, side), 1)


def near_counts(g, rows_ref, level, patch, odd):
    own = rows_ref[level, patch]
    east = jnp.where(
        patch + 1 < g.patches, rows_ref[level, jnp.minimum(patch + 1, g.patches - 1)], 0
    )
    west = jnp.where(patch > 0, rows_ref[level, jnp.maximum(patch - 1, 0)], 0)
    return own, jnp.where(odd, own, east), jnp.where(odd, west, own)


def lane_limits(g, level, counts, cells):
    own, east, west = (value * cells for value in counts)
    lane = lane_ids(g.side)
    margin = g.margin(level)
    first = 0 if level > 0 else g.half_side
    edges = jnp.where(
        (lane >= first) & (lane < first + margin), east, jnp.where(lane >= g.side - margin, west, 0)
    )
    if level == 0:
        return [jnp.where(lane < g.half_side, own, edges)]
    return [jnp.full((1, g.side), own, jnp.int32)] * g.own(level) + [edges]


def one_side(g, values, east):
    count = len(values)
    turned = [pltpu.roll(value, g.side - 1 if east else 1, 1) for value in values]
    if count == 1:
        return turned
    lane = lax.broadcasted_iota(jnp.int32, values[0].shape, 1)
    last = lane == (g.side - 1 if east else 0)
    step = 1 if east else -1
    return [jnp.where(last, turned[(k + step) % count], turned[k]) for k in range(count)]


def both_sides(g, values):
    return one_side(g, values, True), one_side(g, values, False)


def over_rows(rows, chunk, body):
    def step(index, carry):
        body(pl.multiple_of(index * chunk, chunk))
        return carry

    lax.fori_loop(0, rows // chunk, step, 0)


def clear_pads(ref, lead):
    width = ref.shape[-1]
    last = ref.shape[-2]
    for index in lead:
        ref[index + (slice(0, PAD), slice(None))] = jnp.zeros((PAD, width), F32)
        ref[index + (slice(last - PAD, last), slice(None))] = jnp.zeros((PAD, width), F32)


def off_diagonal_rows(g, d, row, size, count):
    here = pl.ds(row, size)
    inner = pl.ds(PAD + row, size)
    centre = [[d.cells[comp, k, inner, :] for k in range(count)] for comp in range(2)]
    beside = [both_sides(g, centre[comp]) for comp in range(2)]
    products = []
    for k in range(count):
        visc = d.visc[k, inner, :]
        half = 0.5 * visc
        (u, v) = (centre[comp][k] for comp in range(2))
        (u_e, u_w), (v_e, v_w) = ((beside[c][0][k], beside[c][1][k]) for c in range(2))
        u_n, v_n = (d.cells[c, k, pl.ds(PAD + row + 1, size), :] for c in range(2))
        u_s, v_s = (d.cells[c, k, pl.ds(PAD + row - 1, size), :] for c in range(2))
        one_u, one_v = visc * u, visc * v
        four_u, four_v = 4.0 * one_u, 4.0 * one_v
        cross_u, cross_v = half * (v_e - v_w), visc * (u_e - u_w)
        d.north[0, k, inner, :] = one_u + cross_u
        d.south[0, k, inner, :] = one_u - cross_u
        d.north[1, k, inner, :] = four_v + cross_v
        d.south[1, k, inner, :] = four_v - cross_v
        cross_u, cross_v = visc * (v_n - v_s), half * (u_n - u_s)
        products.append(
            (
                four_u + cross_u,
                four_u - cross_u,
                one_v + cross_v,
                one_v - cross_v,
                visc * (4.0 * (u_e + u_w) + (u_n + u_s)),
                visc * (4.0 * (v_n + v_s) + (v_e + v_w)),
            )
        )
    for comp in range(2):
        east = one_side(g, [item[2 * comp] for item in products], True)
        west = one_side(g, [item[2 * comp + 1] for item in products], False)
        for k in range(count):
            d.part[comp, k, here, :] = products[k][4 + comp] + east[k] + west[k]


def off_diagonal_step(g, level, d, start, stop):
    count = g.blocks(level)
    chunk = g.chunk(level, stop - start)

    def body(row):
        for step in range(0, chunk, 8):
            off_diagonal_rows(g, d, start + row + step, 8, count)

    over_rows(stop - start, chunk, body)


def off_diagonal(d, comp, k, row, chunk):
    return (
        d.part[comp, k, pl.ds(row, chunk), :]
        + d.north[comp, k, pl.ds(PAD + row + 1, chunk), :]
        + d.south[comp, k, pl.ds(PAD + row - 1, chunk), :]
    )


def smooth_weights(g, level, d, limits, start, stop, from_zero):
    count = g.blocks(level)
    chunk = g.chunk(level, stop - start)

    def some_rows(row):
        here = pl.ds(row, 8)
        inner = pl.ds(PAD + row, 8)
        centre = [d.visc[k, inner, :] for k in range(count)]
        east, west = both_sides(g, centre)
        for k in range(count):
            north = d.visc[k, pl.ds(PAD + row + 1, 8), :]
            south = d.visc[k, pl.ds(PAD + row - 1, 8), :]
            friction = d.fric[k, here, :]
            twice = 2.0 * centre[k]
            along_row = twice + east[k] + west[k]
            along_col = twice + north + south
            live = jnp.broadcast_to(limits[k], (8, g.side)) > row
            diag_u = 4.0 * along_row + along_col + friction
            diag_v = 4.0 * along_col + along_row + friction
            for comp, diag in ((0, diag_u), (1, diag_v)):
                guess = pl.reciprocal(diag, approx=True)
                weight = guess * (2.0 * relaxation - relaxation * diag * guess)
                weight = jnp.where(live, weight, 0.0)
                d.weight[comp, k, here, :] = weight
                if from_zero:
                    d.cells[comp, k, inner, :] = weight * d.right[comp, k, here, :]

    def body(row):
        for step in range(0, chunk, 8):
            some_rows(start + row + step)

    over_rows(stop - start, chunk, body)


def residual_step(g, level, d, start, stop):
    count = g.blocks(level)
    chunk = g.chunk(level, stop - start)
    off_diagonal_step(g, level, d, start, stop)

    def body(row):
        row = row + start
        here = pl.ds(row, chunk)
        for comp in range(2):
            for k in range(count):
                weight = d.weight[comp, k, here, :]
                left = (1.0 - relaxation) * d.right[comp, k, here, :] + off_diagonal(
                    d, comp, k, row, chunk
                )
                left = jnp.where(weight > 0.0, left, 0.0)
                d.left[comp, k, here, :] = left
                d.held[comp, k, here, :] = (
                    d.cells[comp, k, pl.ds(PAD + row, chunk), :] + weight * left
                )

    over_rows(stop - start, chunk, body)


def corrected_step(g, level, d, start, stop, store):
    count = g.blocks(level)
    chunk = g.chunk(level, stop - start)
    off_diagonal_step(g, level, d, start, stop)

    def body(row):
        row = row + start
        here = pl.ds(row, chunk)
        for comp in range(2):
            for k in range(count):
                value = (
                    d.held[comp, k, here, :]
                    + (1.0 - relaxation) * d.cells[comp, k, pl.ds(PAD + row, chunk), :]
                    + d.weight[comp, k, here, :] * off_diagonal(d, comp, k, row, chunk)
                )
                store(comp, k, row, chunk, value)

    over_rows(stop - start, chunk, body)


def pairings(g, fine):
    if fine == 1:
        return [[(0, LOW), (1, HIGH)]]
    parts = [[(2 * k, LOW), (2 * k + 1, HIGH)] for k in range(g.own(fine) // 2)]
    return parts + [[(g.own(fine), EDGES)]]


def target_lane(g, part, fine_lane):
    halved = jnp.right_shift(fine_lane, 1)
    if part == LOW:
        return halved
    if part == HIGH:
        return g.half_side + halved
    return halved + jnp.where(fine_lane >= g.half_side, g.half_side, 0)


def sum_matrix(g, part):
    fine = lax.broadcasted_iota(jnp.int32, (g.side, g.side), 0)
    coarse = lax.broadcasted_iota(jnp.int32, (g.side, g.side), 1)
    return jnp.where(target_lane(g, part, fine) == coarse, 1.0, 0.0).astype(BF16)


def copy_matrix(g, part):
    coarse = lax.broadcasted_iota(jnp.int32, (g.side, g.side), 0)
    fine = lax.broadcasted_iota(jnp.int32, (g.side, g.side), 1)
    return jnp.where(target_lane(g, part, fine) == coarse, 1.0, 0.0).astype(BF16)


def split_dot(values, matrix):
    high = values.astype(BF16)
    rest = (values - high.astype(F32)).astype(BF16)
    return jnp.dot(high, matrix, preferred_element_type=F32) + jnp.dot(
        rest, matrix, preferred_element_type=F32
    )


def restrict_into(g, fine, d, start, stop, store):
    rows = stop - start
    chunk = min(rows // 2, g.half_side)
    if (rows // 2) % chunk:
        chunk = rows // 2
    parts = pairings(g, fine)
    matrices = {part: sum_matrix(g, part) for members in parts for _, part in members}

    def body(row):
        row = row + start // 2
        for comp in range(2):
            for coarse, members in enumerate(parts):
                total = None
                for k, part in members:
                    first = d.left[comp, k, pl.ds(2 * row, chunk, stride=2), :]
                    second = d.left[comp, k, pl.ds(2 * row + 1, chunk, stride=2), :]
                    term = split_dot(first + second, matrices[part])
                    total = term if total is None else total + term
                store(comp, coarse, row, chunk, total)

    over_rows(rows // 2, chunk, body)


def prolong_from(g, fine, d, limits, start, stop, load):
    rows = stop - start
    chunk = min(rows // 2, g.half_side)
    if (rows // 2) % chunk:
        chunk = rows // 2
    parts = pairings(g, fine)
    matrices = {part: copy_matrix(g, part) for members in parts for _, part in members}

    def body(row):
        row = row + start // 2
        ids = 2 * (row + lax.broadcasted_iota(jnp.int32, (chunk, g.side), 0))
        for comp in range(2):
            for coarse, members in enumerate(parts):
                value = load(comp, coarse, row, chunk)
                for k, part in members:
                    spread = jnp.where(ids < limits[k], split_dot(value, matrices[part]), 0.0)
                    d.cells[comp, k, pl.ds(PAD + 2 * row, chunk, stride=2), :] = spread
                    d.cells[comp, k, pl.ds(PAD + 2 * row + 1, chunk, stride=2), :] = spread

    over_rows(rows // 2, chunk, body)


def sums_groups(g):
    count = g.side // (4 * g.margin(1))
    return count, g.rows(2) // 2 // count


def sums_moves(g, group):
    margin = g.margin(1)
    base = 4 * margin * group
    return (base + margin, base), (base + 3 * margin, base + 2 * margin)


def packed_sums(g, edges):
    lane = lane_ids(g.side)
    count, size = sums_groups(g)
    total = jnp.zeros((size, g.side), F32)
    for group in range(count):
        for comp, (shift, first) in enumerate(sums_moves(g, group)):
            value = pltpu.roll(edges[comp, pl.ds(group * size, size), :], shift % g.side, 1)
            inside = (lane >= first) & (lane < first + 2 * g.margin(1))
            total = jnp.where(inside, value, total)
    return total


def plane(raw, q, slot):
    force, visc, fric = raw
    if q < 2:
        return force[slot, q].astype(F32)
    return (fric if q == 2 else visc)[slot].astype(F32)


def edge_lane(g, level, q, r):
    return (0 if level % 2 else g.half_side) + q * g.span + r * g.margin(level)


def packed_edge(g, here, level, patch_of):
    side = g.side
    lane = lane_ids(side)
    margin = g.margin(level)
    start = 0 if here % 2 else side - margin
    total = jnp.zeros((side, side), F32)
    for r in range(g.patch_rows(level)):
        for q in range(4):
            base = edge_lane(g, level, q, r)
            value = patch_of(q, r)
            if (base - start) % side:
                value = pltpu.roll(value, (base - start) % side, 1)
            total = jnp.where((lane >= base) & (lane < base + margin), value, total)
    return total


def edge_column(g, here, level):
    return 0 if here % 2 else g.columns(level) - 1


def first_edge_kernel(g, own, edge, sems, held):
    level_here = lax.axis_index("level")

    def pack(level):
        copies = Copies(sems)
        rows = g.patch_rows(level)
        if g.columns(level) == 1:
            for source, target in zip(own, held):
                copies.start(source, target)
        else:
            for r in range(rows):
                slot = r * g.columns(level) + edge_column(g, level, level)
                for source, target in zip(own, held):
                    copies.start(source.at[slot], target.at[r])
        copies.finish()
        edge[...] = packed_edge(g, level, level, lambda q, r: plane(held, q, r))

    for level in range(g.levels):
        pl.when(level_here == level)(lambda level=level: pack(level))


def edge_kernel(g, first, other, edge):
    level_here = lax.axis_index("level")

    def pack(here):
        level = here ^ 1
        column = edge_column(g, here, level)

        def patch_of(q, r):
            return plane(other, q, r * g.columns(level) + column)

        edge[...] = first[...] + packed_edge(g, here, level, patch_of)

    for here in range(g.levels):
        pl.when(level_here == here)(lambda here=here: pack(here))


def fill_level(g, level, west_type, d, limits, covered, raw, edge, groups):
    side = g.side
    margin = g.margin(level)
    own = g.own(level)
    columns = g.columns(level)
    lane = lane_ids(side)

    def outer(q, r, place):
        shift = (place - edge_lane(g, level, q, r)) % side
        return pltpu.roll(edge[...], shift, 1) if shift else edge[...]

    def store(q, k, r, value):
        here = pl.ds(r * side, side)
        if q < 2:
            if covered is not None:
                ids = r * side + lax.broadcasted_iota(jnp.int32, (side, side), 0)
                value = jnp.where(ids < covered[k], 0.0, value)
            d.right[q, k, here, :] = value
        elif q == 2:
            d.fric[k, here, :] = value
        else:
            d.visc[k, pl.ds(PAD + r * side, side), :] = jnp.where(
                limits[k] > r * side, 0.5 * value, 0.0
            )

    clear_pads(d.visc, [(k,) for k in range(g.blocks(level))])
    for r in range(groups):
        for q in range(4):
            if level == 0 and west_type:
                west = outer(q, r, side - margin)
                store(q, 0, r, jnp.where(lane >= side - margin, west, plane(raw, q, r)))
            elif level == 0:
                value = pltpu.roll(plane(raw, q, r), g.half_side, 1)
                here = (lane >= g.half_side) & (lane < g.half_side + margin)
                store(q, 0, r, jnp.where(here, outer(q, r, g.half_side), value))
            else:
                for k in range(own):
                    store(q, k, r, plane(raw, q, r * columns + k + (0 if west_type else own)))
                if west_type:
                    east = plane(raw, q, r * columns + own)
                    west = outer(q, r, side - margin)
                else:
                    east = outer(q, r, 0)
                    west = plane(raw, q, r * columns + own - 1)
                store(q, own, r, jnp.where(lane < g.half_side, east, west))


class Level(NamedTuple):
    visc: Any
    weight: Any
    right: Any = None
    held: Any = None
    fric: Any = None
    cells: Any = None
    part: Any = None
    north: Any = None
    south: Any = None
    left: Any = None


def level_array(g, count, rows, make, comps, pad):
    shape = (count, rows + (2 * PAD if pad else 0), g.side)
    return make((2, *shape) if comps else shape, F32)


def step_arrays(g, level, rows):
    count = g.blocks(level)
    padded = level_array(g, count, rows, pltpu.VMEM, True, True)
    return dict(
        cells=padded,
        part=level_array(g, count, rows, pltpu.VMEM, True, False),
        north=padded,
        south=padded,
    )


def clear_level(g, level, d):
    blocks = range(g.blocks(level))
    both = [(c, k) for c in range(2) for k in blocks]
    for ref in (d.cells, d.north, d.south):
        clear_pads(ref, both)


def merged(first, second):
    return Level(*[b if a is None else a for a, b in zip(first, second)])


class Copies:
    def __init__(self, sems, first=0):
        self.sems = sems
        self.used = first
        self.open = []

    def start(self, source, target):
        copy = pltpu.make_async_copy(source, target, self.sems.at[self.used])
        self.used += 1
        copy.start()
        self.open.append(copy)

    def finish(self):
        for copy in self.open:
            copy.wait()
        self.open = []


def low_rows(g):
    return g.rows(2) // 2 + 2 * PAD


def kept_rows(g):
    return g.rows(2) // 2 + PAD


def lent_rows(g):
    return low_rows(g), -(-low_rows(g) // 2 // 16) * 16


def lent_forcing(g):
    return [count * g.half_side for count in range(1, g.patch_rows(2) + 1)]


def lent_size(g):
    rows, less = lent_rows(g)
    return 4 * rows + 2 * 16 * len(lent_forcing(g)) + less + 16


def pair_of(visc):
    high = visc.astype(BF16)
    return [high, (visc - high.astype(F32)).astype(BF16)]


class Rows:
    def __init__(self, ref):
        self.ref = ref
        self.place = 0

    def put(self, value):
        size = value.shape[0]
        self.ref[pl.ds(self.place, size), :] = value.astype(BF16)
        self.place += size

    def take(self, size):
        value = self.ref[pl.ds(self.place, size), :].astype(F32)
        self.place += size
        return value


def side_by_side(g, low, high):
    lane = lane_ids(g.side)
    return jnp.where(
        lane < g.half_side, low.astype(F32), pltpu.roll(high.astype(F32), g.half_side, 1)
    )


def lend(g, west_type, own, other, edge, out):
    rows, less = lent_rows(g)
    side = g.side
    fine, coarse = (own, other) if west_type else (other, own)
    target = Rows(out)

    def some_rows(raw, q, slot, first, size):
        here = pl.ds(first, size)
        force, visc, fric = raw
        value = force[slot, q, here, :] if q < 2 else (fric if q == 2 else visc)[slot, here, :]
        return 0.5 * value if q == 3 else value

    def fine_rows(q, first, size, column=0 if west_type else g.own(1)):
        parts = []
        while size:
            group, place = first // side, first % side
            part = min(size, side - place)
            slot = group * g.columns(1) + column
            parts.append(some_rows(fine, q, slot, place, part))
            first, size = first + part, size - part
        return parts

    for part in fine_rows(2, 0, rows):
        target.put(part)
    pairs = [pair_of(part) for part in fine_rows(3, 0, rows)]
    for index in range(2):
        for pair in pairs:
            target.put(pair[index])
    for comp in range(2):
        for first in lent_forcing(g):
            for part in fine_rows(comp, first, 16):
                target.put(part)

    def coarse_rows(q, first, size):
        value = some_rows(coarse, q, 0, first, size).astype(F32)
        return value if west_type else pltpu.roll(value, g.half_side, 1)

    high, rest = pair_of(coarse_rows(3, 0, less))
    target.put(side_by_side(g, coarse_rows(2, 0, less), high))
    target.put(
        side_by_side(g, coarse_rows(0, g.half_side, 16), coarse_rows(1, g.half_side, 16))
    )
    lane = lane_ids(side)

    def outer_plane(level, q, size, place):
        parts = []
        for r in range(-(-size // side)):
            part = edge[pl.ds(0, min(side, size - r * side)), :]
            shift = (place - edge_lane(g, level, q, r)) % side
            parts.append(pltpu.roll(part, shift, 1) if shift else part)
        value = jnp.concatenate(parts, axis=0) if len(parts) > 1 else parts[0]
        return 0.5 * value if q == 3 else value

    def margins(level, size):
        column = g.own(1) if west_type else g.own(1) - 1
        total = jnp.zeros((size, side), F32)
        for q in range(4):
            if level:
                parts = fine_rows(q, 0, size, column)
                inner = jnp.concatenate([part.astype(F32) for part in parts], axis=0)
            else:
                inner = coarse_rows(q, 0, size)
            for west in (True, False):
                if west == west_type:
                    place = margin_moves(g, level, q)[0 if west else 1][0]
                    value = outer_plane(level, q, size, place)
                else:
                    value = inner
                for offset, part in enumerate(pair_of(value) if q == 3 else [value]):
                    place, target_lane = margin_moves(g, level, q + offset)[0 if west else 1]
                    shifted = pltpu.roll(part.astype(F32), (target_lane - place) % side, 1)
                    here = (lane >= target_lane) & (lane < target_lane + g.margin(level))
                    total = jnp.where(here, shifted, total)
        return total

    fine_part = margins(1, rows)
    target.put(side_by_side(g, rest, fine_part[:less] + margins(0, less)))
    target.put(fine_part[less:])


def margin_moves(g, level, index):
    margin = g.margin(level)
    base = 2 * margin * index + (0 if level else 2 * g.margin(1) * 5)
    return (g.side - margin, base), ((0 if level else g.half_side), base + margin)


def edges_of(g, level, west, east):
    lane = lane_ids(g.side)
    middle = g.side - g.half_side // 2 if level == 0 else g.half_side
    return jnp.where(lane < middle, east, west)


def borrow(g, lent, limits, covered, fine, coarse):
    rows, less = lent_rows(g)
    side = g.side
    lane = lane_ids(side)
    source = Rows(lent)

    def masked(value, bounds, inside):
        ids = lax.broadcasted_iota(jnp.int32, value.shape, 0)
        return jnp.where((ids < bounds) == inside, value, 0.0)

    fine.fric[0] = source.take(rows)
    high = source.take(rows)
    fine.visc[0, pl.ds(PAD, rows), :] = masked(high + source.take(rows), limits[1][0], True)
    for comp in range(2):
        fine.right[comp, 0] = jnp.zeros((rows, side), F32)
        for first in lent_forcing(g):
            value = masked(source.take(16), covered[0] - first, False)
            fine.right[comp, 0, pl.ds(first, 16), :] = value
    first, window, rest = source.take(less), source.take(16), source.take(less)
    packed = jnp.concatenate(
        [pltpu.roll(rest, g.half_side, 1), source.take(rows - less)], axis=0
    )

    def margins(level, q, size):
        moves = [margin_moves(g, level, index) for index in ((q,) if q < 3 else (3, 4))]
        west, east = (
            sum(
                pltpu.roll(packed[:size], (move[at][0] - move[at][1]) % side, 1)
                for move in moves
            )
            for at in range(2)
        )
        return edges_of(g, level, west, east)

    for comp in range(2):
        fine.right[comp, 1] = masked(margins(1, comp, rows), covered[1], False)
    fine.fric[1] = margins(1, 2, rows)
    fine.visc[1, pl.ds(PAD, rows), :] = masked(margins(1, 3, rows), limits[1][1], True)

    def with_margins(value, q):
        return jnp.where(lane < g.half_side, value, margins(0, q, less))

    coarse.fric[0] = with_margins(first, 2)
    value = with_margins(pltpu.roll(first, g.half_side, 1) + rest, 3)
    coarse.visc[0, pl.ds(PAD, less), :] = masked(value, limits[0][0], True)
    for comp in range(2):
        value = pltpu.roll(window, g.half_side, 1) if comp else window
        value = jnp.concatenate([jnp.zeros((g.half_side, side), F32), value], axis=0)
        coarse.right[comp, 0] = with_margins(value, comp)


def fill_pair(g, rows_ref, own, other, edge, levels, wanted, groups):
    level_here = lax.axis_index("level")
    patch = lax.axis_index("patch")
    odd = level_here % 2 == 1
    for west_type in (True, False):

        @pl.when(odd if west_type else jnp.logical_not(odd))
        def _():
            for level in wanted:
                near = near_counts(g, rows_ref, level, patch, odd)
                limits = lane_limits(g, level, near, g.side)
                covered = None
                if level == 1:
                    finer = near_counts(g, rows_ref, 2, patch, odd)
                    covered = lane_limits(g, 1, finer, g.half_side)
                home = (level % 2 == 1) == west_type
                raw = own if home else other
                fill_level(
                    g, level, west_type, levels[level], limits, covered, raw, edge, groups(level)
                )


def lend_kernel(g, own, other, edge, lent):
    level_here = lax.axis_index("level")
    for level in range(g.levels - 2):
        pl.when(level_here == level)(
            lambda level=level: lend(g, level % 2 == 1, own, other, edge, lent)
        )


def fill_kernel(g, rows_ref, own, other, edge, _, filled):
    level_here = lax.axis_index("level")
    top = g.levels - 1

    @pl.when(level_here >= top - 1)
    def _():
        levels = dict(zip((top - 1, top), filled))
        fill_pair(g, rows_ref, own, other, edge, levels, (top, top - 1), g.patch_rows)


def down_kernel(
    g, rows_ref, own, other, edge, upper, sums, kept, low_kept, lower, edges, scratch
):
    level_here = lax.axis_index("level")
    patch = lax.axis_index("patch")
    side = g.side
    top = g.levels - 1
    odd = level_here % 2 == 1
    filled = [*lower, *upper]
    kept = [*(Level(None, weight) for weight in low_kept), *kept]
    levels = [merged(merged(a, b), c) for a, b, c in zip(scratch, kept, filled)]

    def limits_of(level):
        return lane_limits(g, level, near_counts(g, rows_ref, level, patch, odd), side)

    @pl.when(level_here >= top - 1)
    def _():
        near = near_counts(g, rows_ref, top, patch, odd)
        covered = lane_limits(g, top - 1, near, g.half_side)
        given = filled[top - 1].right
        reach = g.rows(2) // 2
        for comp in range(2):
            for k in range(g.blocks(top - 1)):
                rest = pl.ds(g.half_side, g.rows(top - 1) - g.half_side)
                levels[top - 1].right[comp, k, rest, :] = given[comp, k, rest, :]

        def set_right(comp, k, row, chunk, value):
            here = pl.ds(row, chunk)
            ids = row + lax.broadcasted_iota(jnp.int32, (chunk, side), 0)
            levels[top - 1].right[comp, k, here, :] = jnp.where(
                ids < covered[k], value, given[comp, k, here, :]
            )

        def keep(comp, k, row, chunk, value):
            if k == 0:
                sums[pl.ds(comp * reach + row, chunk), :] = value
            else:
                edges[comp, pl.ds(row, chunk), :] = value

        for level in (top, top - 1):
            d = levels[level]
            clear_level(g, level, d)
            smooth_weights(g, level, d, limits_of(level), 0, g.rows(level), True)
            residual_step(g, level, d, 0, g.rows(level))
            restrict_into(g, level, d, 0, g.rows(level), set_right if level == top else keep)
        packed = packed_sums(g, edges)
        sums[pl.ds(2 * reach, packed.shape[0]), :] = packed

    @pl.when(level_here < top - 1)
    def _():
        fill_pair(g, rows_ref, own, other, edge, levels, (1, 0), g.patch_rows)
        for level, size in zip((1, 0), lent_rows(g)):
            smooth_weights(g, level, levels[level], limits_of(level), 0, size, False)


def bottom_levels(g, rows_ref, patch, odd, start, stop, fine, coarse, new_sums, store_fine):
    side = g.side
    count, chunk = g.blocks(1), g.chunk(1, stop - start)
    clear_level(g, 1, fine)
    if new_sums is not None:
        reach = g.rows(2) // 2
        for comp in range(2):
            for k in range(count):
                here = pl.ds(0, reach)
                fine.right[comp, k, here, :] = fine.right[comp, k, here, :] + new_sums(comp, k)

    def body(row):
        here = pl.ds(start + row, chunk)
        for comp in range(2):
            for k in range(count):
                fine.cells[comp, k, pl.ds(PAD + start + row, chunk), :] = (
                    fine.weight[comp, k, here, :] * fine.right[comp, k, here, :]
                )

    over_rows(stop - start, chunk, body)
    residual_step(g, 1, fine, start, stop)
    near = near_counts(g, rows_ref, 1, patch, odd)
    covered = lane_limits(g, 0, near, g.half_side)

    def smooth_coarse(comp, k, row, size, value):
        here = pl.ds(row, size)
        ids = row + lax.broadcasted_iota(jnp.int32, (size, side), 0)
        value = jnp.where(ids < covered[0], value, coarse.right[comp, 0, here, :])
        value = coarse.weight[comp, 0, here, :] * value
        coarse.cells[comp, 0, here, :] = value

    restrict_into(g, 1, fine, start, stop, smooth_coarse)

    def load(comp, k, row, size):
        return coarse.cells[comp, 0, pl.ds(row, size), :]

    prolong_from(g, 1, fine, lane_limits(g, 1, near, side), start, stop, load)
    corrected_step(g, 1, fine, start, stop, store_fine)


def weigh_kernel(g, rows_ref, filled, weights):
    level_here = lax.axis_index("level")
    patch = lax.axis_index("patch")
    odd = level_here % 2 == 1

    @pl.when(level_here < g.levels - 2)
    def _():
        first = g.rows(2) // 2
        for level, start in ((1, first), (0, first // 2)):
            d = Level(filled[level].visc, weights[level], fric=filled[level].fric)
            limits = lane_limits(g, level, near_counts(g, rows_ref, level, patch, odd), g.side)
            smooth_weights(g, level, d, limits, start, g.rows(level), False)


def up_kernel(
    g, rows_ref, sums, lent, filled, kept, rest_weights, mine, theirs, own_rows, coarse_rows, edges, scratch, low, low_fine,
    low_coarse, finer, coarser,
):
    level_here = lax.axis_index("level")
    patch = lax.axis_index("patch")
    side = g.side
    top = g.levels - 1
    odd = level_here % 2 == 1
    levels = [merged(a, b) for a, b in zip(scratch, filled)]
    for level in (top - 1, top):
        levels[level] = merged(levels[level], kept[level - top + 1])

    def limits_of(level):
        return lane_limits(g, level, near_counts(g, rows_ref, level, patch, odd), side)

    def hand_out():
        def write(first, second):
            for k in range(g.half_slots):
                for comp in range(2):
                    first[k, comp] = finer[k, comp]
                    second[k, comp] = coarser[k, comp]

        pl.when(odd)(lambda: write(mine, theirs))
        pl.when(jnp.logical_not(odd))(lambda: write(theirs, mine))

    @pl.when(level_here >= top - 1)
    def _():
        rows, less = lent_rows(g)
        limits = {level: limits_of(level) for level in (0, 1)}
        clear_pads(low_fine.visc, [(k,) for k in range(g.blocks(1))])
        clear_pads(low_coarse.visc, [(k,) for k in range(g.blocks(0))])
        finer_near = near_counts(g, rows_ref, 2, patch, odd)
        covered = lane_limits(g, 1, finer_near, g.half_side)
        borrow(g, lent, limits, covered, low_fine, low_coarse)
        smooth_weights(g, 1, low_fine, limits[1], 0, rows, False)
        smooth_weights(g, 0, low_coarse, limits[0], 0, less, False)

        def store_fine(comp, k, row, chunk, value):
            low[comp, k, pl.ds(row, chunk), :] = value

        bottom_levels(
            g, rows_ref, patch, odd, 0, rows, low_fine, low_coarse,
            level_sums(g, sums, low_fine.weight), store_fine,
        )

        def load_low(comp, k, row, chunk):
            return low[comp, k, pl.ds(row, chunk), :]

        def load_held(comp, k, row, chunk):
            return edges[comp, k, pl.ds(row, chunk), :]

        def store_in(level, out, hold):
            own = g.own(level)

            def store(comp, k, row, chunk, value):
                if hold:
                    edges[comp, k, pl.ds(row, chunk), :] = value
                if k < own:
                    group, place = row // side, row % side
                    out[group * own + k, comp, pl.ds(pl.multiple_of(place, 8), chunk), :] = value

            return store

        for level, load, out in ((top - 1, load_low, coarser), (top, load_held, finer)):
            d = levels[level]
            clear_level(g, level, d)
            rows = g.rows(level)
            prolong_from(g, level, d, limits_of(level), 0, rows, load)
            corrected_step(g, level, d, 0, rows, store_in(level, out, level < top))
        hand_out()

    @pl.when(level_here < top - 1)
    def _():
        rows = g.rows(1)
        first = g.rows(2) // 2
        fine = levels[1]._replace(weight=rest_weights[1])
        coarse = levels[0]._replace(weight=rest_weights[0], cells=coarse_rows)

        def store_fine(comp, k, row, chunk, value):
            if k == 0:
                own_rows[comp, pl.ds(row, chunk), :] = value

        bottom_levels(g, rows_ref, patch, odd, first, rows, fine, coarse, None, store_fine)
        for r in range(rows // 2 // side, g.patch_rows(0)):
            here = pl.ds(r * side, side)
            for comp in range(2):
                coarse_rows[comp, 0, here, :] = (
                    coarse.weight[comp, 0, here, :] * coarse.right[comp, 0, here, :]
                )


def level_sums(g, sums, weight):
    reach = g.rows(2) // 2

    def value(comp, k):
        if k == 0:
            found = sums[pl.ds(comp * reach, reach), :]
        else:
            count, size = sums_groups(g)
            packed = sums[pl.ds(2 * reach, size), :]
            shifts = [sums_moves(g, group)[comp][0] for group in range(count)]
            parts = [pltpu.roll(packed, -shift % g.side, 1) for shift in shifts]
            found = jnp.concatenate(parts, axis=0)
        return jnp.where(weight[comp, k, pl.ds(0, reach), :] > 0.0, found, 0.0)

    return value


def low_kernel(
    g, rows_ref, sums, filled, kept, mine_in, theirs_in, own_rows, coarse_rows, mine, theirs, scratch, low_coarse, near_rows
):
    level_here = lax.axis_index("level")
    patch = lax.axis_index("patch")
    side = g.side
    top = g.levels - 1
    odd = level_here % 2 == 1

    @pl.when(level_here >= top - 1)
    def _():
        for k in range(g.half_slots):
            for comp in range(2):
                mine[k, comp] = mine_in[k, comp]
                theirs[k, comp] = theirs_in[k, comp]

    @pl.when(level_here < top - 1)
    def _():
        rows, _ = lent_rows(g)
        done = kept_rows(g)
        fine = merged(Level(filled[1].visc, kept[1]), scratch)
        coarse = merged(Level(None, kept[0], filled[0].right), low_coarse)
        for comp in range(2):
            for k in range(g.blocks(1)):
                fine.right[comp, k] = filled[1].right[comp, k, pl.ds(0, rows), :]

        def store_fine(comp, k, row, chunk, value):
            if k == 0:
                near_rows[comp, pl.ds(row, chunk), :] = value

        bottom_levels(
            g, rows_ref, patch, odd, 0, rows, fine, coarse,
            level_sums(g, sums, fine.weight), store_fine,
        )
        lane = lane_ids(side)
        size = rows // 2
        ids = lax.broadcasted_iota(jnp.int32, (size, side), 0)

        def coarse_group(comp, r):
            value = coarse_rows[comp, 0, pl.ds(r * side, side), :]
            if r:
                return value
            near = coarse.cells[comp, 0, pl.ds(0, size), :]
            near = jnp.where(ids < done // 2, near, value[:size])
            return jnp.concatenate([near, value[size:]], axis=0)

        def write(first, second):
            for comp in range(2):
                first[0, comp] = near_rows[comp, pl.ds(0, side), :]
                for r in range(1, g.patch_rows(1)):
                    first[r, comp] = own_rows[comp, pl.ds(r * side, side), :]
                first[1, comp, pl.ds(0, done - side), :] = near_rows[
                    comp, pl.ds(side, done - side), :
                ]
                for k in range(g.half_slots):
                    high = pltpu.roll(coarse_group(comp, k + g.half_slots), g.half_side, 1)
                    second[k, comp] = jnp.where(lane < g.half_side, coarse_group(comp, k), high)

        pl.when(odd)(lambda: write(mine, theirs))
        pl.when(jnp.logical_not(odd))(lambda: write(theirs, mine))


def join_kernel(g, mine, given, speed, fric, adjoint, gradient):
    level_here = lax.axis_index("level")
    lane = lane_ids(g.side)

    def put(slot, parts):
        for comp in range(2):
            adjoint[slot, comp] = parts[comp]
        total = speed[slot, 0].astype(F32) * parts[0] + speed[slot, 1].astype(F32) * parts[1]
        gradient[slot] = (-(fric[slot].astype(F32) * total)).astype(BF16)

    def join_level(level):
        if level == 0:
            for k in range(g.half_slots):
                low = []
                high = []
                for comp in range(2):
                    west, east = given[k, comp], mine[k, comp]
                    low.append(
                        jnp.where(lane < g.half_side, west, pltpu.roll(east, g.half_side, 1))
                    )
                    high.append(
                        jnp.where(lane < g.half_side, pltpu.roll(west, g.half_side, 1), east)
                    )
                put(k, low)
                put(k + g.half_slots, high)
            return
        own = g.own(level)
        west_half, east_half = (mine, given) if level % 2 == 1 else (given, mine)
        for r in range(g.patch_rows(level)):
            for k in range(2 * own):
                source = west_half if k < own else east_half
                put(
                    r * g.columns(level) + k,
                    [source[r * own + k % own, comp] for comp in range(2)],
                )

    for level in range(g.levels):
        pl.when(level_here == level)(lambda level=level: join_level(level))


def run_kernel(body, ins, outs, scratch, grant=VMEM_BYTES):
    in_trees = [jax.tree.flatten(tree) for tree, _ in ins]
    out_trees = [jax.tree.flatten(tree) for tree, _ in outs]
    scratch_trees = [jax.tree.flatten(tree) for tree in scratch]
    sizes = [len(leaves) for leaves, _ in in_trees + out_trees + scratch_trees]
    shapes = [tree for _, tree in in_trees + out_trees + scratch_trees]

    def kernel(*refs):
        given = []
        first = 0
        for size, shape in zip(sizes, shapes):
            given.append(jax.tree.unflatten(shape, refs[first : first + size]))
            first += size
        body(*given)

    def specs(groups, trees):
        return [
            pl.BlockSpec(memory_space=space)
            for (_, space), (leaves, _) in zip(groups, trees)
            for _ in leaves
        ]

    results = pl.pallas_call(
        kernel,
        out_shape=[leaf for leaves, _ in out_trees for leaf in leaves],
        in_specs=specs(ins, in_trees),
        out_specs=specs(outs, out_trees),
        scratch_shapes=[leaf for leaves, _ in scratch_trees for leaf in leaves],
        compiler_params=pltpu.CompilerParams(vmem_limit_bytes=grant),
    )(*[leaf for leaves, _ in in_trees for leaf in leaves])
    answer = []
    first = 0
    for leaves, shape in out_trees:
        answer.append(jax.tree.unflatten(shape, results[first : first + len(leaves)]))
        first += len(leaves)
    return answer


def moved(value, g, step):
    pairs = []
    for patch in range(g.patches):
        for level in range(g.levels):
            to_patch, to_level = step(patch, level)
            if 0 <= to_patch < g.patches and 0 <= to_level < g.levels:
                pairs.append((patch * g.levels + level, to_patch * g.levels + to_level))
    return lax.ppermute(value, ("patch", "level"), pairs)


def per_device(forcing, velocity, viscosity, friction, patch_rows):
    g = Layout(
        forcing.shape[1], forcing.shape[-1], lax.axis_size("level"), lax.axis_size("patch")
    )
    side = g.side
    top = g.levels - 1
    force, speed, visc, fric = forcing[0], velocity[0], viscosity[0], friction[0]
    make = jax.ShapeDtypeStruct
    vmem = pltpu.VMEM
    block = make((side, side), F32)
    half = make((g.half_slots, 2, side, side), F32)
    sums_rows = g.rows(2) + sums_groups(g)[1]

    def array(level, rows, kind, comps, pad):
        return level_array(g, g.blocks(level), rows, kind, comps, pad)

    own = (force, visc, fric)
    other = tuple(moved(value, g, lambda p, l: (p, l ^ 1)) for value in own)
    (edge,) = run_kernel(
        lambda *refs: first_edge_kernel(g, *refs),
        [(own, pltpu.HBM)],
        [(block, VM)],
        [
            pltpu.SemaphoreType.DMA((3 * g.slots,)),
            tuple(vmem(value.shape, value.dtype) for value in own),
        ],
        FIRST_BYTES,
    )
    (edge,) = run_kernel(
        lambda *refs: edge_kernel(g, *refs), [(edge, VM), (other, VM)], [(block, VM)], []
    )
    edge = moved(edge, g, lambda p, l: (p + (-1 if l % 2 else 1), l ^ 1))

    fields = [
        Level(
            array(level, g.rows(level), make, False, True),
            None,
            right=array(level, g.rows(level), make, True, False),
            fric=array(level, g.rows(level), make, False, False),
        )
        for level in range(g.levels)
    ]
    rows, less = lent_rows(g)
    given = [(patch_rows, SM), (own, VM), (other, VM), (edge, VM)]

    (lent_here,) = run_kernel(
        lambda *refs: lend_kernel(g, *refs),
        given[1:],
        [(make((lent_size(g), side), BF16), VM)],
        [],
    )
    lent = moved(lent_here, g, lambda p, l: (p, l + 2))
    (upper,) = run_kernel(
        lambda *refs: fill_kernel(g, *refs),
        [*given, (lent_here, VM)],
        [(fields[top - 1 :], VM)],
        [],
    )

    def kept_of(level):
        two = array(level, g.rows(level), make, True, False)
        return Level(None, two, held=two)

    low_weights = [array(0, less, make, True, False), array(1, rows, make, True, False)]

    def down_scratch(level):
        if level < top - 1:
            return Level(None, None)
        both = array(level, g.rows(level), vmem, True, False)
        more = dict(right=both) if level < top else {}
        return Level(None, None, left=both, **more, **step_arrays(g, level, g.rows(level)))

    sums, kept, low_kept, lower = run_kernel(
        lambda *refs: down_kernel(g, *refs),
        [*given, (upper, VM)],
        [
            (make((sums_rows, side), F32), VM),
            ([kept_of(level) for level in (top - 1, top)], VM),
            (low_weights, VM),
            (fields[: top - 1], VM),
        ],
        [vmem((2, side, side), F32), [down_scratch(level) for level in range(g.levels)]],
    )
    filled = [*lower, *upper]
    sums_there = moved(sums, g, lambda p, l: (p, l - 2))

    (rest_weights,) = run_kernel(
        lambda *refs: weigh_kernel(g, *refs),
        [(patch_rows, SM), (lower, VM)],
        [([array(level, g.rows(level), make, True, False) for level in (0, 1)], VM)],
        [],
    )

    def up_scratch(level):
        both = array(level, g.rows(level), vmem, True, False)
        if level == 0:
            return Level(None, None)
        steps = step_arrays(g, level, g.rows(level))
        if level == 1:
            return Level(None, None, held=both, left=both, **steps)
        return Level(None, None, **steps)

    low_both = array(1, rows, vmem, True, False)
    low_steps = dict(held=low_both, left=low_both, right=low_both, **step_arrays(g, 1, rows))
    mine, theirs, own_rows, coarse_rows = run_kernel(
        lambda *refs: up_kernel(g, *refs),
        [
            (patch_rows, SM),
            (sums, VM),
            (lent, VM),
            (filled, VM),
            (kept, VM),
            (rest_weights, VM),
        ],
        [
            (half, VM),
            (half, VM),
            (make((2, g.rows(1), side), F32), VM),
            (make((2, 1, g.rows(0), side), F32), VM),
        ],
        [
            array(top - 1, g.rows(top - 1), vmem, True, False),
            [up_scratch(level) for level in range(g.levels)],
            low_both,
            Level(
                array(1, rows, vmem, False, True),
                low_both,
                fric=array(1, rows, vmem, False, False),
                **low_steps,
            ),
            Level(
                array(0, less, vmem, False, True),
                array(0, less, vmem, True, False),
                right=array(0, less, vmem, True, False),
                fric=array(0, less, vmem, False, False),
                cells=array(0, less, vmem, True, False),
            ),
            vmem(half.shape, F32),
            vmem(half.shape, F32),
        ],
    )
    mine, theirs = run_kernel(
        lambda *refs: low_kernel(g, *refs),
        [
            (patch_rows, SM),
            (sums_there, VM),
            (filled[:2], VM),
            (low_kept, VM),
            (mine, VM),
            (theirs, VM),
            (own_rows, VM),
            (coarse_rows, VM),
        ],
        [(half, VM), (half, VM)],
        [
            Level(None, None, **low_steps),
            Level(None, None, cells=array(0, less, vmem, True, False)),
            vmem((2, rows, side), F32),
        ],
    )
    received = moved(theirs, g, lambda p, l: (p, l ^ 1))
    adjoint, gradient = run_kernel(
        lambda *refs: join_kernel(g, *refs),
        [(mine, VM), (received, VM), (speed, VM), (fric, VM)],
        [
            (make((g.slots, 2, side, side), F32), VM),
            (make((g.slots, side, side), BF16), VM),
        ],
        [],
    )
    return (adjoint[None], gradient[None])


def solution(mesh):
    fields = P("level", "patch")
    return jax.shard_map(
        per_device,
        mesh=mesh,
        in_specs=(fields, fields, fields, fields, P()),
        out_specs=(fields, fields),
        check_vma=False,
    )
```
